32 devices in a mesh: dp: 8 (over z, y), bal: 4 (over x, core).
Axes of the slice: x: 2, y: 2, z: 4, core: 2. Of those that a mesh axis runs over, the one named last changes fastest.
Arguments:
- patches: bfloat16 [32, 784, 512], P(('dp', 'bal')), may hold values from -6 to 6
- tag_rows: bfloat16 [32, 1024, 512], P(('dp', 'bal')), may hold values from -6 to 6
- cotangent: bfloat16 [32, 1024, 512], P(('dp', 'bal')), may hold values from -6 to 6
- tag_length: int32 [32], P(('dp', 'bal')), may hold values from 1 to 768, as said below
- cell_count: int32 [32], P(('dp', 'bal')), may hold values from 0 to 256
- destination: int32 [32, 8], P(('dp', 'bal')), may hold values from 0 to 3, as said below
- slot_index: int32 [32, 8], P(('dp', 'bal')), may hold values from 0 to 1
- encoder_attention: bfloat16 [512, 4, 512], replicated, may hold values from -1.41421356 to 1.41421356
- encoder_up: bfloat16 [512, 1024], replicated, may hold values from -0.25 to 0.25
- encoder_up_bias: float32 [1024], replicated, may hold values from -3 to 3
- encoder_down: bfloat16 [1024, 512], replicated, may hold values from -0.1875 to 0.1875
- encoder_gains: float32 [512, 2], replicated, may hold values from 0.5 to 1.5
- encoder_shifts: float32 [512, 3], replicated, may hold values from -2 to 2
- decoder_self: bfloat16 [512, 4, 512], replicated, may hold values from -1.41421356 to 1.41421356
- decoder_cross: bfloat16 [512, 4, 512], replicated, may hold values from -1.41421356 to 1.41421356
- decoder_up: bfloat16 [512, 1024], replicated, may hold values from -0.25 to 0.25
- decoder_up_bias: float32 [1024], replicated, may hold values from -3 to 3
- decoder_down: bfloat16 [1024, 512], replicated, may hold values from -0.1875 to 0.1875
- decoder_gains: float32 [512, 3], replicated, may hold values from 0.5 to 1.5
- decoder_shifts: float32 [512, 4], replicated, may hold values from -2 to 2
Outputs:
- decoded: bfloat16 [32, 1024, 512], P(('dp', 'bal'))
- patches_grad: float32 [32, 784, 512], P(('dp', 'bal'))
- tag_rows_grad: float32 [32, 1024, 512], P(('dp', 'bal'))
- encoder_attention_grad: float32 [512, 4, 512], P('dp')
- encoder_up_grad: float32 [512, 1024], P('dp')
- encoder_up_bias_grad: float32 [1024], P('dp')
- encoder_down_grad: float32 [1024, 512], P('dp')
- encoder_gains_grad: float32 [512, 2], P('dp')
- encoder_shifts_grad: float32 [512, 3], P('dp')
- decoder_self_grad: float32 [512, 4, 512], P('dp')
- decoder_cross_grad: float32 [512, 4, 512], P('dp')
- decoder_up_grad: float32 [512, 1024], P('dp')
- decoder_up_bias_grad: float32 [1024], P('dp')
- decoder_down_grad: float32 [1024, 512], P('dp')
- decoder_gains_grad: float32 [512, 3], P('dp')
- decoder_shifts_grad: float32 [512, 4], P('dp')
The draws below stay inside these ranges and needn't reach their ends.
Inputs may be any that keep to these rules, and one draw needn't show every extreme that they name: Table t has tag_length[t] + cell_count[t] query rows, at most 1024; in every aligned group of 4 tables one table has exactly 1024 rows. For each table, destination * 2 + slot_index takes every value from 0 to 7 exactly once over its 8 blocks.
All inputs are finite; a program needn't handle non-finite values.
Results may differ from the reference program's by a relative error of at most 0.02.
Values may be sent and summed in bfloat16 or wider, within the bound.
A program may use at most 320 MiB of HBM per device.

```python
import jax
import jax.numpy as jnp
from jax import lax

D = 512
HEADS = 8
FF = 1024
HEAD = 64
PATCH = 784
BLK = 128
NB = 8
LMAX = 1024
CAP = 2
TABLES = 32
N_BAL = 4


def row_split(key):
    group_size = NB // CAP
    groups = TABLES // group_size
    first_key, second_key, third_key = jax.random.split(jax.random.fold_in(key, 101), 3)
    longest = jax.random.randint(first_key, (groups,), 0, group_size)
    short_rows = jax.random.randint(second_key, (groups, group_size), 1, 5 * NB * BLK // 8 + 1)
    is_long = (jnp.arange(group_size)[None, :] == longest[:, None]).reshape(TABLES)
    totals = jnp.where(is_long, NB * BLK, short_rows.reshape(TABLES))
    surplus = jax.random.randint(third_key, (TABLES,), 0, 1 << 20) % (totals // 8 + 1)
    cell_rows = jnp.where(is_long, NB * BLK // 4, totals // 4 + surplus)
    return ((totals - cell_rows).astype(jnp.int32), cell_rows.astype(jnp.int32))


def block_places(key):
    scores = jax.random.randint(jax.random.fold_in(key, 202), (TABLES, NB), 0, 1 << 20) * NB + jnp.arange(NB)[None, :]
    places = jnp.argsort(scores, axis=1)
    return ((places // CAP).astype(jnp.int32), (places % CAP).astype(jnp.int32))


def attention_draw(key, out_scale):
    columns = jax.random.truncated_normal(key, -4.0, 4.0, (D, 4, D), jnp.float32) * D ** (-0.5)
    factors = jnp.array([1.0, 1.0, 1.0, out_scale], jnp.float32)
    return columns * factors[None, :, None]


def draw_tag_length(key, part):
    lengths, counts = row_split(key)
    return lengths


def draw_cell_count(key, part):
    lengths, counts = row_split(key)
    return counts


def draw_destination(key, part):
    devices, slots = block_places(key)
    return devices


def draw_slot_index(key, part):
    devices, slots = block_places(key)
    return slots


def draw_encoder_attention(key, part):
    key = jax.random.fold_in(key, 5)
    return attention_draw(key, 8.0).astype(jnp.bfloat16)


def draw_decoder_self(key, part):
    key = jax.random.fold_in(key, 6)
    return attention_draw(key, 6.0).astype(jnp.bfloat16)


def draw_decoder_cross(key, part):
    key = jax.random.fold_in(key, 7)
    return attention_draw(key, 8.0).astype(jnp.bfloat16)


def with_spikes(values, key, source, target, shards_of, factor):
    def block_of(dim):
        return (jnp.arange(values.shape[dim]) // (values.shape[dim] // shards_of)).reshape((-1,) + (1,) * (values.ndim - 1 - dim))

    near = jax.random.permutation(key, shards_of)[block_of(target)]
    second = (block_of(target) + shards_of // 2) % shards_of
    return jnp.where((block_of(source) == near) | (block_of(source) == second), factor * values, values)


def steps_of(own_key, shape, cuts, smallest, top_value):
    factor_of = 1.0
    for dim, shards_of in cuts:
        heights = jax.random.uniform(jax.random.fold_in(jax.random.fold_in(own_key, 6), dim), (shards_of,), jnp.float32, smallest / len(cuts), top_value / len(cuts))
        factor_of = factor_of * jnp.repeat(jnp.exp(heights), shape[dim] // shards_of).reshape((-1,) + (1,) * (len(shape) - 1 - dim))
    return factor_of


def gaussian(stream_key, extent, scale, reach, shards=(), dtype=jnp.bfloat16):
    values = scale * jax.random.normal(stream_key, extent, jnp.float32)
    if shards:
        values = values * steps_of(stream_key, extent, shards, -0.22, 0.18)
    return jnp.clip(values, -reach, reach).astype(dtype)


def bell_draw_with(own_key, extent, scale, bound, shards, heavy, held_as=jnp.bfloat16):
    values = scale * jax.random.normal(own_key, extent, jnp.float32)
    if shards:
        values = values * steps_of(own_key, extent, shards, -0.22, 0.18)
    return jnp.clip(with_spikes(values, jax.random.fold_in(own_key, 3), *heavy), -bound, bound).astype(held_as)


def setup_inputs(seed: int = 0) -> dict:
    key_of = jax.random.split(jax.random.key(seed), 21)
    patches = bell_draw_with(key_of[0], (TABLES, PATCH, D), 1.0, 6.0, ((0, 32),), (0, 2, 32, 2.75))
    tag_rows = bell_draw_with(key_of[1], (TABLES, LMAX, D), 1.0, 6.0, ((0, 32),), (0, 2, 32, 2.75))
    cotangent = gaussian(key_of[2], (TABLES, LMAX, D), 1.0, 6.0, ((0, 32),))
    tag_length = draw_tag_length(jax.random.fold_in(key_of[20], 71), 0)
    cell_count = draw_cell_count(jax.random.fold_in(key_of[20], 71), 0)
    destination = draw_destination(jax.random.fold_in(key_of[20], 71), 0)
    slot_index = draw_slot_index(jax.random.fold_in(key_of[20], 71), 0)
    encoder_attention = draw_encoder_attention(jax.random.fold_in(key_of[20], 71), 0)
    encoder_up = gaussian(key_of[8], (D, FF), D ** -0.5, 0.25)
    encoder_up_bias = gaussian(key_of[9], (FF,), 0.5, 3.0, (), jnp.float32)
    encoder_down = gaussian(key_of[10], (FF, D), FF ** -0.5, 0.1875)
    encoder_gains = jnp.clip(1.0 + 0.1 * jax.random.normal(key_of[11], (D, 2), jnp.float32), 0.5, 1.5)
    encoder_shifts = gaussian(key_of[12], (D, 3), 0.3, 2.0, (), jnp.float32)
    decoder_self = draw_decoder_self(jax.random.fold_in(key_of[20], 71), 0)
    decoder_cross = draw_decoder_cross(jax.random.fold_in(key_of[20], 71), 0)
    decoder_up = gaussian(key_of[15], (D, FF), D ** -0.5, 0.25)
    decoder_up_bias = gaussian(key_of[16], (FF,), 0.5, 3.0, (), jnp.float32)
    decoder_down = gaussian(key_of[17], (FF, D), FF ** -0.5, 0.1875)
    decoder_gains = jnp.clip(1.0 + 0.1 * jax.random.normal(key_of[18], (D, 3), jnp.float32), 0.5, 1.5)
    decoder_shifts = gaussian(key_of[19], (D, 4), 0.3, 2.0, (), jnp.float32)
    return {"patches": patches, "tag_rows": tag_rows, "cotangent": cotangent, "tag_length": tag_length, "cell_count": cell_count, "destination": destination, "slot_index": slot_index, "encoder_attention": encoder_attention, "encoder_up": encoder_up, "encoder_up_bias": encoder_up_bias, "encoder_down": encoder_down, "encoder_gains": encoder_gains, "encoder_shifts": encoder_shifts, "decoder_self": decoder_self, "decoder_cross": decoder_cross, "decoder_up": decoder_up, "decoder_up_bias": decoder_up_bias, "decoder_down": decoder_down, "decoder_gains": decoder_gains, "decoder_shifts": decoder_shifts}


HIGHEST = lax.Precision.HIGHEST
EPSILON = 1e-05
NEGATIVE = -1e+30

@jax.custom_vjp
def low(v):
    return lax.optimization_barrier(v.astype(jnp.bfloat16)).astype(jnp.float32)

@jax.custom_vjp
def low_back(v):
    return v

def low_keep(v):
    return (low(v), None)

def low_pass(kept, grad):
    return (grad,)

def back_keep(v):
    return (v, None)

def back_low(kept, grad):
    return (low(grad),)
low.defvjp(low_keep, low_pass)
low_back.defvjp(back_keep, back_low)

def coarse(signal):
    return low_back(low(signal))

def project(left, right):
    return jnp.dot(left, right, precision=HIGHEST)

def layer_norm(signal, gains_row, shifts_row):
    centre = lax.optimization_barrier(jnp.mean(signal, axis=-1, keepdims=True))
    centered = signal - centre
    spread = lax.optimization_barrier(jnp.mean(centered * centered, axis=-1, keepdims=True))
    return centered * lax.rsqrt(spread + EPSILON) * gains_row + shifts_row

def attend(inputs, sources, weights, score_bias):
    factor = HEAD ** (-0.5)
    queries = coarse(project(inputs, weights[:, 0])).reshape(-1, HEADS, HEAD)
    key_rows = coarse(project(sources, weights[:, 1])).reshape(-1, HEADS, HEAD)
    value_rows = coarse(project(sources, weights[:, 2])).reshape(-1, HEADS, HEAD)
    scores = low_back(jnp.einsum('qhe,khe->hqk', queries, key_rows, precision=HIGHEST) * factor) + score_bias
    row_peak = lax.optimization_barrier(jnp.max(scores, axis=-1, keepdims=True))
    lifted = jnp.exp(scores - row_peak)
    shares = low(lifted / lax.optimization_barrier(jnp.sum(lifted, axis=-1, keepdims=True)))
    mixture = coarse(jnp.einsum('hqk,khe->qhe', shares, value_rows, precision=HIGHEST).reshape(-1, D))
    return low_back(project(mixture, weights[:, 3]))

def feed_forward(inputs, up_weight, up_offset, down_weight, down_offset):
    hidden = low_back(project(low(inputs), up_weight) + up_offset)
    active = low(jax.nn.gelu(hidden, approximate=True))
    return low_back(project(active, down_weight) + down_offset)

def encode(patches_table, weights):
    first_sum = patches_table + attend(patches_table, patches_table, weights[0], 0.0)
    normed = layer_norm(first_sum, weights[4][:, 0], weights[5][:, 0])
    second = normed + feed_forward(normed, weights[1], weights[2], weights[3], weights[5][:, 2])
    return low(layer_norm(second, weights[4][:, 1], weights[5][:, 1]))

def decode(tags_table, memory, rows_table, weights):
    position = jnp.arange(LMAX)
    causal = jnp.where(position[None, :] <= position[:, None], 0.0, NEGATIVE).astype(jnp.float32)
    first_sum = tags_table + attend(tags_table, tags_table, weights[6], causal)
    normed = coarse(layer_norm(first_sum, weights[11][:, 0], weights[12][:, 0]))
    second = layer_norm(normed + attend(normed, memory, weights[7], 0.0), weights[11][:, 1], weights[12][:, 1])
    third_sum = second + feed_forward(second, weights[8], weights[9], weights[10], weights[12][:, 3])
    final_rows = layer_norm(third_sum, weights[11][:, 2], weights[12][:, 2])
    live_rows = (position < rows_table).astype(jnp.float32)
    return final_rows * live_rows[:, None]

def reference(patches, tag_rows, cotangent, tag_length, cell_count, destination, slot_index, encoder_attention, encoder_up, encoder_up_bias, encoder_down, encoder_gains, encoder_shifts, decoder_self, decoder_cross, decoder_up, decoder_up_bias, decoder_down, decoder_gains, decoder_shifts):
    row_totals = (tag_length + cell_count).astype(jnp.int32)
    params = (encoder_attention.astype(jnp.float32), encoder_up.astype(jnp.float32), encoder_up_bias.astype(jnp.float32), encoder_down.astype(jnp.float32), encoder_gains.astype(jnp.float32), encoder_shifts.astype(jnp.float32), decoder_self.astype(jnp.float32), decoder_cross.astype(jnp.float32), decoder_up.astype(jnp.float32), decoder_up_bias.astype(jnp.float32), decoder_down.astype(jnp.float32), decoder_gains.astype(jnp.float32), decoder_shifts.astype(jnp.float32))
    block_order = jnp.argsort(destination * CAP + slot_index, axis=1).astype(jnp.int32)

    def forward(image_wide, tags_wide, weights):

        def one_table(table_items):
            image_table, tags_table, rows_table = table_items
            memory = encode(image_table, weights)
            return decode(tags_table, memory, rows_table, weights)
        outputs = lax.map(jax.checkpoint(one_table), (image_wide, tags_wide, row_totals))
        blocked = outputs.reshape(TABLES, NB, BLK, D)
        placed = jnp.take_along_axis(blocked, block_order[:, :, None, None], axis=1)
        placed = placed.reshape(TABLES // N_BAL, N_BAL, N_BAL, CAP * BLK, D)
        return jnp.swapaxes(placed, 1, 2).reshape(TABLES, LMAX, D)
    decoded, pullback = jax.vjp(forward, patches.astype(jnp.float32), tag_rows.astype(jnp.float32), params)
    patches_grad, tag_rows_grad, weight_grads = pullback(cotangent.astype(jnp.float32))
    return (decoded.astype(jnp.bfloat16), patches_grad, tag_rows_grad, weight_grads[0], weight_grads[1], weight_grads[2], weight_grads[3], weight_grads[4], weight_grads[5], weight_grads[6], weight_grads[7], weight_grads[8], weight_grads[9], weight_grads[10], weight_grads[11], weight_grads[12])
```

```python
import functools

import jax
import jax.numpy as jnp
from jax import lax
from jax.experimental import pallas as pl
from jax.experimental.pallas import tpu as pltpu
from jax.sharding import PartitionSpec as P

HEADS = 8
HEAD = 64
EPSILON = 1e-05
NEGATIVE = -1e30
BF = jnp.bfloat16
F32 = jnp.float32
NN = (((1,), (0,)), ((), ()))
NT = (((1,), (1,)), ((), ()))
TN = (((0,), (0,)), ((), ()))
TT = (((0,), (1,)), ((), ()))
VM = pl.BlockSpec(memory_space=pltpu.VMEM)
SM = pl.BlockSpec(memory_space=pltpu.SMEM)
ANY = pl.BlockSpec(memory_space=pl.ANY)
LIMIT = 1e18
PARAMS = pltpu.CompilerParams(vmem_limit_bytes=60 << 20)
Shape = jax.ShapeDtypeStruct


def mm(left, right, dims=NN):
    return lax.dot_general(left, right, dims, preferred_element_type=F32)


def cut(rows):
    half = (rows // 2 + 15) // 16 * 16
    return [(0, half), (half, rows - half)]


class Copies:
    def __init__(self, sems):
        self.sems, self.used, self.open = sems, 0, []

    def start(self, source, target):
        copy = pltpu.make_async_copy(source, target, self.sems.at[self.used])
        self.used += 1
        copy.start()
        return copy

    def out(self, source, target):
        self.open.append(self.start(source, target))

    def finish(self):
        for copy in self.open:
            copy.wait()


def split_weights(raw, parts):
    def step(i, carry):
        rows = pl.ds(pl.multiple_of(i * 128, 128), 128)
        parts[:, rows, :] = pltpu.einshape("abc->bac", raw[rows])
        return carry

    lax.fori_loop(0, raw.shape[0] // 128, step, 0)


def normalise(signal):
    centre = jnp.mean(signal, axis=-1, keepdims=True)
    centered = signal - centre
    spread = jnp.mean(centered * centered, axis=-1, keepdims=True)
    rate = lax.rsqrt(spread + EPSILON)
    return centered * rate, rate


def norm_back(unit, rate, gain, gradient):
    inner = gradient * gain
    first = jnp.mean(inner, axis=-1, keepdims=True)
    second = jnp.mean(inner * unit, axis=-1, keepdims=True)
    return rate * (inner - first - unit * second)


def colsum(signal):
    return jnp.sum(signal, axis=0, keepdims=True)


def smooth(hidden):
    scale = 0.7978845608028654
    square = hidden * hidden
    curve = jnp.tanh(scale * hidden * (1.0 + 0.044715 * square))
    half = 0.5 + 0.5 * curve
    slope = half + 0.5 * hidden * (1.0 - curve * curve) * (scale + (3 * 0.044715 * scale) * square)
    return hidden * half, slope


def half_mask(shape, axis, which):
    index = lax.broadcasted_iota(jnp.int32, shape, axis)
    return (index < HEAD) if which == 0 else (index >= HEAD)


def keep_half(pair, axis, which):
    return jnp.where(half_mask(pair.shape, axis, which), pair, jnp.zeros_like(pair))


def project_qkv(x, sources, w4, q, qt, k, v, vt):
    rows = x.shape[0]
    for start, size in cut(rows):
        part = slice(start, start + size)
        q[part] = (mm(x[part], w4[0]) * HEAD ** (-0.5)).astype(BF)
    if q.shape[0] > rows:
        q[rows:] = jnp.zeros((q.shape[0] - rows, q.shape[1]), BF)
    for start, size in cut(sources.shape[0]):
        part = slice(start, start + size)
        k[part] = mm(sources[part], w4[1]).astype(BF)
        v[part] = mm(sources[part], w4[2]).astype(BF)
    qt[...] = q[...].T
    vt[...] = v[...].T


def shifted_exp(scores, exact, causal_rows):
    if causal_rows:
        size, width = scores.shape
        key = lax.broadcasted_iota(jnp.int32, (width, width), 0)
        query = lax.broadcasted_iota(jnp.int32, (width, width), 1)
        last = jnp.where(key <= query, scores[size - width :], NEGATIVE)
        scores = last if size == width else jnp.concatenate([scores[: size - width], last], axis=0)
        exact = exact or size == width
    sample = scores if exact else scores[:128]
    return jnp.exp(scores - jnp.max(sample, axis=0, keepdims=True))


def attend_heads(exact, causal, q_tile, qt, k, vt, ot, rate, store):
    keys, queries = k.shape[0], qt.shape[1]

    def pair(p, carry):
        lanes = pl.ds(pl.multiple_of(p * 128, 128), 128)
        for u in range(2):
            rows = pl.ds(pl.multiple_of(p * 128 + u * HEAD, HEAD), HEAD)
            place, done = store(p, u)
            for start in range(0, queries, q_tile):
                cols = slice(start, start + q_tile)
                depth = start + q_tile if causal else keys
                scores = mm(k[:depth, lanes], keep_half(qt[lanes, cols], 0, u))
                raised = shifted_exp(scores, exact, causal)
                total = jnp.sum(raised, axis=0, keepdims=True)
                low = raised.astype(BF)
                place[:depth, cols] = low
                inverse = 1.0 / total
                rate[2 * p + u, :, cols] = inverse
                ot[rows, cols] = (mm(vt[rows, :depth], low) * inverse).astype(BF)
            done()
        return carry

    lax.fori_loop(0, HEADS // 2, pair, 0)


def attend(causal, q_tile, qt, k, vt, ot, rate, store, drain):
    attend_heads(False, causal, q_tile, qt, k, vt, ot, rate, store)
    drain()
    fine = jnp.min(rate[...]) > 1.0 / LIMIT

    @pl.when(jnp.logical_not(fine))
    def _():
        attend_heads(True, causal, q_tile, qt, k, vt, ot, rate, store)
        drain()


def back_heads(causal, q_tile, q, kt, v, dot_, d_o, rowdot, fetch, ds, dqt, dk, dv):
    keys, queries = v.shape[0], dqt.shape[1]

    def pair(p, carry):
        lanes = pl.ds(pl.multiple_of(p * 128, 128), 128)
        for u in range(2):
            rows = pl.ds(pl.multiple_of(p * 128 + u * HEAD, HEAD), HEAD)
            place = fetch(p, u)
            for start in range(0, queries, q_tile):
                cols = slice(start, start + q_tile)
                depth = start + q_tile if causal else keys
                grad = mm(v[:depth, lanes], keep_half(dot_[lanes, cols], 0, u))
                scaled = place[:depth, cols].astype(F32) * (grad - rowdot[2 * p + u, :, cols])
                low = scaled.astype(BF)
                ds[u][:depth, cols] = low
                dqt[rows, cols] = (mm(kt[rows, :depth], low) * HEAD ** (-0.5)).astype(BF)
            qm = q[:, lanes]
            dm = d_o[:, lanes]
            steps = range(0, keys, q_tile) if causal else (0,)
            for start in steps:
                key = slice(start, start + q_tile) if causal else slice(0, keys)
                more_k = mm(ds[u][key, start:], qm[start:])
                more_v = mm(place[key, start:], dm[start:])
                if u == 0:
                    dk[key, lanes] = more_k.astype(BF)
                    dv[key, lanes] = more_v.astype(BF)
                else:
                    dk[key, lanes] = jnp.where(half_mask(more_k.shape, 1, 1), more_k.astype(BF), dk[key, lanes])
                    dv[key, lanes] = jnp.where(half_mask(more_v.shape, 1, 1), more_v.astype(BF), dv[key, lanes])
        return carry

    lax.fori_loop(0, HEADS // 2, pair, 0)


def back_outputs(grad_low, w4, ot, rate, dot_, d_o, rowdot):
    rows, wide = grad_low.shape[0], dot_.shape[1]
    raw = mm(w4[3], grad_low[...], NT)
    for h in range(HEADS):
        part = slice(h * HEAD, (h + 1) * HEAD)
        low = (raw[part] * rate[h][:, :rows]).astype(BF)
        if wide > rows:
            low = jnp.concatenate([low, jnp.zeros((HEAD, wide - rows), BF)], axis=1)
        dot_[part] = low
        rowdot[h] = jnp.sum(low.astype(F32) * ot[part].astype(F32), axis=0, keepdims=True)
    d_o[...] = dot_[...].T


def ring(buffers, hbm, sems, spans, out):
    def copies(h, slot):
        made = []
        for i, (rows, cols) in enumerate(spans):
            here = buffers.at[slot, pl.ds(0, rows), cols]
            there = hbm.at[h, pl.ds(0, rows), cols]
            made.append(
                pltpu.make_async_copy(here, there, sems.at[slot, i])
                if out
                else pltpu.make_async_copy(there, here, sems.at[slot, i])
            )
        return made

    return copies


def out_ring(buffers, hbm, sems, spans):
    copies = ring(buffers, hbm, sems, spans, True)

    def store(p, u):
        slot = (p % 2) * 2 + u

        @pl.when(p >= 2)
        def _():
            for copy in copies(2 * p + u, slot):
                copy.wait()

        def done():
            for copy in copies(2 * p + u, slot):
                copy.start()

        return buffers.at[slot], done

    def drain():
        for slot in range(4):
            for copy in copies(slot, slot):
                copy.wait()

    return store, drain


def in_ring(buffers, hbm, sems, spans):
    copies = ring(buffers, hbm, sems, spans, False)

    def begin():
        for h in range(4):
            for copy in copies(h, h):
                copy.start()

    def fetch(p, u):
        slot = (p % 2) * 2 + u
        for copy in copies(2 * p + u, slot):
            copy.wait()
        if u == 0:
            @pl.when((p >= 1) & (p < HEADS // 2 - 1))
            def _():
                other = (1 - p % 2) * 2
                for v in range(2):
                    for copy in copies(2 * p + 2 + v, other + v):
                        copy.start()
        return buffers.at[slot]

    return begin, fetch


def encoder_forward(x_h, w_h, up_h, bias, down_h, gains, shifts,
                    memory, w4_h, qkv_h, ot_h, e_h, rate, e1_h, e2_h, zb_h, act_h, slope_h,
                    x, raw, w4, up, down, q, k, v, qt, vt, ot, e1, e2, zb, act, slope, ering, sems, esems):
    c = Copies(sems)
    load_w = c.start(w_h, raw)
    load_x = c.start(x_h, x)
    load_up = c.start(up_h, up)
    load_down = c.start(down_h, down)
    load_w.wait()
    split_weights(raw, w4)
    c.out(w4, w4_h)
    load_x.wait()
    project_qkv(x, x, w4, q, qt, k, v, vt)
    n, wide = x.shape[0], qt.shape[1]
    for i, item in enumerate((q.at[pl.ds(0, n)], k, v)):
        c.out(item, qkv_h.at[i])
    store, drain = out_ring(ering, e_h, esems, [(n, slice(None))])
    attend(False, wide, qt, k, vt, ot, rate, store, drain)
    c.out(ot, ot_h)
    load_up.wait()
    load_down.wait()
    for start, size in cut(n):
        part = slice(start, start + size)
        first = x[part].astype(F32) + mm(ot[:, part], w4[3], TN)
        e1[part] = first
        unit, _ = normalise(first)
        z = unit * gains[0:1] + shifts[0:1]
        low = z.astype(BF)
        zb[part] = low
        active, bend = smooth(mm(low, up[...]) + bias[...])
        act[part] = active.astype(BF)
        slope[part] = bend.astype(BF)
        second = z + mm(act[part], down[...]) + shifts[2:3]
        e2[part] = second
        unit, _ = normalise(second)
        memory[part] = (unit * gains[1:2] + shifts[1:2]).astype(BF)
    for here, there in ((e1, e1_h), (e2, e2_h), (zb, zb_h), (act, act_h), (slope, slope_h)):
        c.out(here, there)
    c.finish()


def tags_forward(x_h, w_h, gains, shifts,
                 x1, w4_h, qkv_h, ot_h, e_h, rate, a1_h,
                 x, raw, w4, q, k, v, qt, vt, ot, a1, ering, sems, esems):
    c = Copies(sems)
    load_w = c.start(w_h, raw)
    load_x = c.start(x_h, x)
    load_w.wait()
    split_weights(raw, w4)
    c.out(w4, w4_h)
    load_x.wait()
    project_qkv(x, x, w4, q, qt, k, v, vt)
    n = x.shape[0]
    for i, item in enumerate((q, k, v)):
        c.out(item, qkv_h.at[i])
    tile = 256
    spans = [(start + tile, slice(start, start + tile)) for start in range(0, n, tile)]
    store, drain = out_ring(ering, e_h, esems, spans)
    attend(True, tile, qt, k, vt, ot, rate, store, drain)
    c.out(ot, ot_h)
    for start, size in cut(n):
        part = slice(start, start + size)
        first = x[part].astype(F32) + mm(ot[:, part], w4[3], TN)
        a1[part] = first
        unit, _ = normalise(first)
        x1[part] = (unit * gains[0:1] + shifts[0:1]).astype(BF)
    c.out(a1, a1_h)
    c.finish()


def decoder_tail(live_rows, places, x1_h, mem_h, w_h, up_h, bias, down_h, gains, shifts, cot_h,
                 y, dx1, dmem, d_w, d_up, d_bias, d_down, d_gains, d_shifts,
                 x1, mem, raw, w4, up, down, q, k, v, qt, vt, ot, kt, e, rate,
                 unit2, rate2, xb2, act, slope, da, gb, rowdot, dqt, dk, dv, sems):
    cot, dh, dot_, d_o, ds = y, slope, qt, xb2, (act, slope)
    c = Copies(sems)
    load_w = c.start(w_h, raw)
    load_mem = c.start(mem_h, mem)
    load_x = c.start(x1_h, x1)
    load_up = c.start(up_h, up)
    load_down = c.start(down_h, down)
    load_cot = c.start(cot_h, cot)
    load_w.wait()
    split_weights(raw, w4)
    load_mem.wait()
    load_x.wait()
    project_qkv(x1, mem, w4, q, qt, k, v, vt)
    kt[...] = k[...].T
    n, blocks = x1.shape[0], y.shape[0]
    block = n // blocks

    def store(p, u):
        return e.at[2 * p + u], lambda: None

    attend(False, n, qt, k, vt, ot, rate, store, lambda: None)
    load_up.wait()
    load_down.wait()
    load_cot.wait()
    live = live_rows[0] + live_rows[1]
    zero = jnp.zeros((1, x1.shape[1]), F32)
    gain3, shift3 = zero, zero
    for start, size in cut(n):
        part = slice(start, start + size)
        second = x1[part].astype(F32) + mm(ot[:, part], w4[3], TN)
        unit, pace = normalise(second)
        unit2[part] = unit
        rate2[part] = pace
        x2 = unit * gains[1:2] + shifts[1:2]
        low = x2.astype(BF)
        xb2[part] = low
        active, bend = smooth(mm(low, up[...]) + bias[...])
        act[part] = active.astype(BF)
        slope[part] = bend.astype(BF)
        third = x2 + mm(act[part], down[...]) + shifts[3:4]
        unit, pace = normalise(third)
        row = lax.broadcasted_iota(jnp.int32, (size, 1), 0) + start
        alive = (row < live).astype(F32)
        final = ((unit * gains[2:3] + shifts[2:3]) * alive).astype(BF)
        picked = []
        for b in range(start // block, (start + size) // block):
            picked.append(cot[places[b]])
            y[places[b]] = final[b * block - start : (b + 1) * block - start]
        dy = jnp.concatenate(picked, axis=0).astype(F32) * alive
        gain3 += colsum(dy * unit)
        shift3 += colsum(dy)
        d3 = norm_back(unit, pace, gains[2:3], dy)
        da[part] = d3
        gb[part] = d3.astype(BF)
    d_gains[2:3] = gain3
    d_shifts[2:3] = shift3
    ffn_back(xb2, up, down, act, slope, gb, dh, d_up, d_bias, d_down, d_shifts, 3)
    gain2, shift2 = zero, zero
    for start, size in cut(n):
        part = slice(start, start + size)
        dx2 = da[part] + mm(dh[part], up[...], NT)
        gain2 += colsum(dx2 * unit2[part])
        shift2 += colsum(dx2)
        d2 = norm_back(unit2[part], rate2[part], gains[1:2], dx2)
        da[part] = d2
        gb[part] = d2.astype(BF)
    d_gains[1:2] = gain2
    d_shifts[1:2] = shift2
    d_w[3] = mm(ot[...], gb[...]).astype(BF)
    back_outputs(gb, w4, ot, rate, dot_, d_o, rowdot)
    back_heads(False, n, q, kt, v, dot_, d_o, rowdot, lambda p, u: e.at[2 * p + u], ds, dqt, dk, dv)
    d_w[0] = mm(x1[...], dqt[...], TT).astype(BF)
    d_w[1] = mm(mem[...], dk[...], TN).astype(BF)
    d_w[2] = mm(mem[...], dv[...], TN).astype(BF)
    for start, size in cut(n):
        part = slice(start, start + size)
        dx1[part] = (da[part] + mm(dqt[:, part], w4[0], TT)).astype(BF)
    for start, size in cut(mem.shape[0]):
        part = slice(start, start + size)
        dmem[part] = mm(dk[part], w4[1], NT) + mm(dv[part], w4[2], NT)


def ffn_back(xb, up, down, act, slope, gb, dh, d_up, d_bias, d_down, d_shifts, row):
    n = xb.shape[0]
    offset = jnp.zeros((1, up.shape[1]), F32)
    for start, size in cut(n):
        part = slice(start, start + size)
        low = (mm(gb[part], down[...], NT) * slope[part].astype(F32)).astype(BF)
        dh[part] = low
        offset += colsum(low.astype(F32))
    d_bias[...] = offset
    d_shifts[row : row + 1] = colsum(gb[...].astype(F32))
    d_down[...] = mm(act[...], gb[...], TN).astype(BF)
    d_up[...] = mm(xb[...], dh[...], TN).astype(BF)


def tags_backward(dx1_h, a1_h, x_h, w4_h, qkv_h, ot_h, e_h, rate, gains,
                  dx, d_w, d_gains, d_shifts,
                  dx1, a1, x, w4, q, k, v, ot, kt, ering, da, gb, dot_, d_o, rowdot, ds, dqt, dk, dv, sems, esems):
    c = Copies(sems)
    load_dx1 = c.start(dx1_h, dx1)
    load_a1 = c.start(a1_h, a1)
    load_w = c.start(w4_h, w4)
    load_ot = c.start(ot_h, ot)
    load_qkv = [c.start(qkv_h.at[i], item) for i, item in enumerate((q, k, v))]
    load_x = c.start(x_h, x)
    n = q.shape[0]
    tile = 256
    spans = [(start + tile, slice(start, start + tile)) for start in range(0, n, tile)]
    begin, fetch = in_ring(ering, e_h, esems, spans)
    begin()
    load_dx1.wait()
    load_a1.wait()
    zero = jnp.zeros((1, x.shape[1]), F32)
    gain, shift = zero, zero
    for start, size in cut(n):
        part = slice(start, start + size)
        unit, pace = normalise(a1[part])
        grad = dx1[part].astype(F32)
        gain += colsum(grad * unit)
        shift += colsum(grad)
        d1 = norm_back(unit, pace, gains[0:1], grad)
        da[part] = d1
        gb[part] = d1.astype(BF)
    d_gains[...] = gain
    d_shifts[...] = shift
    attention_back(True, tile, x, w4, q, k, v, ot, kt, rate, fetch, da, gb, dot_, d_o, rowdot, ds, dqt, dk, dv,
                   (load_w, load_ot, *load_qkv, load_x), d_w, dx)


def attention_back(causal, tile, x, w4, q, k, v, ot, kt, rate, fetch, da, gb, dot_, d_o, rowdot, ds, dqt, dk, dv,
                   loads, d_w, dx):
    for load in loads:
        load.wait()
    n = x.shape[0]
    kt[...] = k[...].T
    d_w[3] = mm(ot[:, :n], gb[...]).astype(BF)
    back_outputs(gb, w4, ot, rate, dot_, d_o, rowdot)
    back_heads(causal, tile, q, kt, v, dot_, d_o, rowdot, fetch, (ds.at[0], ds.at[1]), dqt, dk, dv)
    d_w[0] = mm(x[...], dqt[:, :n], TT).astype(BF)
    d_w[1] = mm(x[...], dk[...], TN).astype(BF)
    d_w[2] = mm(x[...], dv[...], TN).astype(BF)
    for start, size in cut(n):
        part = slice(start, start + size)
        dx[part] = (da[part] + mm(dqt[:, part], w4[0], TT) + mm(dk[part], w4[1], NT) + mm(dv[part], w4[2], NT))


def encoder_backward(dmem_h, e2_h, e1_h, zb_h, act_h, slope_h, up_h, down_h, x_h, w4_h, qkv_h, ot_h, e_h, rate, gains,
                     dx, d_w, d_up, d_bias, d_down, d_gains, d_shifts,
                     dmem, e2, e1, zb, act, slope, up, down, x, w4, q, k, v, ot, kt, ering, da, gb,
                     dot_, d_o, rowdot, ds, dqt, dk, dv, sems, esems):
    c = Copies(sems)
    load_first = [c.start(a, b) for a, b in ((dmem_h, dmem), (e2_h, e2))]
    load_ffn = [c.start(a, b) for a, b in ((down_h, down), (slope_h, slope), (act_h, act), (zb_h, zb), (up_h, up))]
    load_e1 = c.start(e1_h, e1)
    load_w = c.start(w4_h, w4)
    load_ot = c.start(ot_h, ot)
    n, wide = x.shape[0], dot_.shape[1]
    load_qkv = [c.start(qkv_h.at[i], item) for i, item in enumerate((q.at[pl.ds(0, n)], k, v))]
    load_x = c.start(x_h, x)
    begin, fetch = in_ring(ering, e_h, esems, [(n, slice(None))])
    begin()
    q[n:] = jnp.zeros((wide - n, q.shape[1]), BF)
    for load in load_first:
        load.wait()
    zero = jnp.zeros((1, x.shape[1]), F32)
    gain, shift = zero, zero
    for start, size in cut(n):
        part = slice(start, start + size)
        unit, pace = normalise(e2[part])
        grad = dmem[part]
        gain += colsum(grad * unit)
        shift += colsum(grad)
        d2 = norm_back(unit, pace, gains[1:2], grad)
        da[part] = d2
        gb[part] = d2.astype(BF)
    d_gains[1:2] = gain
    d_shifts[1:2] = shift
    for load in load_ffn:
        load.wait()
    dh = slope
    ffn_back(zb, up, down, act, slope, gb, dh, d_up, d_bias, d_down, d_shifts, 2)
    load_e1.wait()
    gain, shift = zero, zero
    for start, size in cut(n):
        part = slice(start, start + size)
        unit, pace = normalise(e1[part])
        dz = da[part] + mm(dh[part], up[...], NT)
        gain += colsum(dz * unit)
        shift += colsum(dz)
        d1 = norm_back(unit, pace, gains[0:1], dz)
        da[part] = d1
        gb[part] = d1.astype(BF)
    d_gains[0:1] = gain
    d_shifts[0:1] = shift
    attention_back(False, wide, x, w4, q, k, v, ot, kt, rate, fetch, da, gb, dot_, d_o, rowdot, ds, dqt, dk, dv,
                   (load_w, load_ot, *load_qkv, load_x), d_w, dx)


def call(kernel, ins, outs, out_specs, scratch, name):
    specs = [spec for spec, _ in ins]
    return pl.pallas_call(
        kernel,
        out_shape=outs,
        in_specs=specs,
        out_specs=out_specs,
        scratch_shapes=scratch,
        compiler_params=PARAMS,
        name=name,
    )(*[value for _, value in ins])


def run_encoder_forward(x, w, up, bias, down, gains, shifts):
    n, width = x.shape
    hidden = up.shape[1]
    wide = (n + 127) // 128 * 128
    bf = lambda *s: Shape(s, BF)
    f32 = lambda *s: Shape(s, F32)
    vb = lambda *s: pltpu.VMEM(s, BF)
    vf = lambda *s: pltpu.VMEM(s, F32)
    outs = [bf(n, width), bf(4, width, width), bf(3, n, width), bf(width, wide), bf(HEADS, n, wide), f32(HEADS, 1, wide),
            f32(n, width), f32(n, width), bf(n, width), bf(n, hidden), bf(n, hidden)]
    return call(
        encoder_forward,
        [(ANY, x), (ANY, w), (ANY, up), (VM, bias), (ANY, down), (VM, gains), (VM, shifts)],
        outs,
        [VM, ANY, ANY, ANY, ANY, VM, ANY, ANY, ANY, ANY, ANY],
        [vb(n, width), vb(width, 4, width), vb(4, width, width), vb(width, hidden), vb(hidden, width),
         vb(wide, width), vb(n, width), vb(n, width), vb(width, wide), vb(width, n), vb(width, wide),
         vf(n, width), vf(n, width), vb(n, width), vb(n, hidden), vb(n, hidden), vb(4, n, wide),
         pltpu.SemaphoreType.DMA((20,)), pltpu.SemaphoreType.DMA((4, 1))],
        "encoder_forward",
    )


def run_tags_forward(x, w, gains, shifts):
    n, width = x.shape
    bf = lambda *s: Shape(s, BF)
    f32 = lambda *s: Shape(s, F32)
    vb = lambda *s: pltpu.VMEM(s, BF)
    vf = lambda *s: pltpu.VMEM(s, F32)
    return call(
        tags_forward,
        [(ANY, x), (ANY, w), (VM, gains), (VM, shifts)],
        [bf(n, width), bf(4, width, width), bf(3, n, width), bf(width, n), bf(HEADS, n, n), f32(HEADS, 1, n), f32(n, width)],
        [VM, ANY, ANY, ANY, ANY, VM, ANY],
        [vb(n, width), vb(width, 4, width), vb(4, width, width), vb(n, width), vb(n, width), vb(n, width),
         vb(width, n), vb(width, n), vb(width, n), vf(n, width), vb(4, n, n),
         pltpu.SemaphoreType.DMA((20,)), pltpu.SemaphoreType.DMA((4, n // 256))],
        "tags_forward",
    )


def run_decoder_tail(live, places, x1, mem, w, up, bias, down, gains, shifts, cot):
    n, width = x1.shape
    m = mem.shape[0]
    hidden = up.shape[1]
    bf = lambda *s: Shape(s, BF)
    f32 = lambda *s: Shape(s, F32)
    vb = lambda *s: pltpu.VMEM(s, BF)
    vf = lambda *s: pltpu.VMEM(s, F32)
    return call(
        decoder_tail,
        [(SM, live), (SM, places), (ANY, x1), (ANY, mem), (ANY, w), (ANY, up), (VM, bias), (ANY, down), (VM, gains),
         (VM, shifts), (ANY, cot)],
        [bf(*cot.shape), bf(n, width), f32(m, width), bf(4, width, width), bf(width, hidden), f32(1, hidden),
         bf(hidden, width), f32(3, width), f32(4, width)],
        [VM] * 9,
        [vb(n, width), vb(m, width), vb(width, 4, width), vb(4, width, width), vb(width, hidden), vb(hidden, width),
         vb(n, width), vb(m, width), vb(m, width), vb(width, n), vb(width, m), vb(width, n), vb(width, m),
         vb(HEADS, m, n), vf(HEADS, 1, n), vf(n, width), vf(n, 1), vb(n, width), vb(n, hidden), vb(n, hidden),
         vf(n, width), vb(n, width), vf(HEADS, 1, n), vb(width, n), vb(m, width), vb(m, width), pltpu.SemaphoreType.DMA((20,))],
        "decoder_tail",
    )


def run_tags_backward(dx1, a1, x, w4, qkv, ot, e, rate, gains):
    n, width = x.shape
    bf = lambda *s: Shape(s, BF)
    f32 = lambda *s: Shape(s, F32)
    vb = lambda *s: pltpu.VMEM(s, BF)
    vf = lambda *s: pltpu.VMEM(s, F32)
    return call(
        tags_backward,
        [(ANY, dx1), (ANY, a1), (ANY, x), (ANY, w4), (ANY, qkv), (ANY, ot), (ANY, e), (VM, rate), (VM, gains)],
        [f32(n, width), bf(4, width, width), f32(1, width), f32(1, width)],
        [VM] * 4,
        [vb(n, width), vf(n, width), vb(n, width), vb(4, width, width), vb(n, width), vb(n, width), vb(n, width),
         vb(width, n), vb(width, n), vb(4, n, n), vf(n, width), vb(n, width), vb(width, n), vb(n, width),
         vf(HEADS, 1, n), vb(2, n, n), vb(width, n), vb(n, width), vb(n, width),
         pltpu.SemaphoreType.DMA((20,)), pltpu.SemaphoreType.DMA((4, n // 256))],
        "tags_backward",
    )


def run_encoder_backward(dmem, e2, e1, zb, act, slope, up, down, x, w4, qkv, ot, e, rate, gains):
    n, width = x.shape
    hidden = up.shape[1]
    wide = ot.shape[1]
    bf = lambda *s: Shape(s, BF)
    f32 = lambda *s: Shape(s, F32)
    vb = lambda *s: pltpu.VMEM(s, BF)
    vf = lambda *s: pltpu.VMEM(s, F32)
    return call(
        encoder_backward,
        [(ANY, v) for v in (dmem, e2, e1, zb, act, slope, up, down, x, w4, qkv, ot, e)] + [(VM, rate), (VM, gains)],
        [f32(n, width), bf(4, width, width), bf(width, hidden), f32(1, hidden), bf(hidden, width), f32(2, width),
         f32(3, width)],
        [VM] * 7,
        [vf(n, width), vf(n, width), vf(n, width), vb(n, width), vb(n, hidden), vb(n, hidden), vb(width, hidden),
         vb(hidden, width), vb(n, width), vb(4, width, width), vb(wide, width), vb(n, width), vb(n, width),
         vb(width, wide), vb(width, n), vb(4, n, wide), vf(n, width), vb(n, width),
         vb(width, wide), vb(wide, width), vf(HEADS, 1, wide), vb(2, n, wide), vb(width, wide), vb(n, width),
         vb(n, width), pltpu.SemaphoreType.DMA((20,)), pltpu.SemaphoreType.DMA((4, 1))],
        "encoder_backward",
    )


def local_step(patches, tag_rows, cot, live, places, enc, dec):
    ew, eu, eb, ed, eg, es = enc
    sw, cw, du, db, dd, dg, dsh = dec
    memory, ew4, eqkv, eot, ee, erate, e1, e2, zb, eact, eslope = run_encoder_forward(patches, ew, eu, eb, ed, eg, es)
    x1, sw4, sqkv, sot, se, srate, a1 = run_tags_forward(tag_rows, sw, dg, dsh)
    y, dx1, dmem, d_cw, d_du, d_db, d_dd, d_dg, d_ds = run_decoder_tail(
        live, places, x1, memory, cw, du, db, dd, dg, dsh, cot)
    d_tags, d_sw, d_dg0, d_ds0 = run_tags_backward(dx1, a1, tag_rows, sw4, sqkv, sot, se, srate, dg)
    d_patches, d_ew, d_eu, d_eb, d_ed, d_eg, d_es = run_encoder_backward(
        dmem, e2, e1, zb, eact, eslope, eu, ed, patches, ew4, eqkv, eot, ee, erate, eg)
    d_dg = d_dg.at[0:1].set(d_dg0)
    d_ds = d_ds.at[0:1].set(d_ds0)
    return y, d_patches, d_tags, (d_ew, d_eu, d_eb, d_ed, d_eg, d_es), (d_sw, d_cw, d_du, d_db, d_dd, d_dg, d_ds)


def per_device(
    patches, tag_rows, cotangent, tag_length, cell_count, destination, slot_index,
    encoder_attention, encoder_up, encoder_up_bias, encoder_down, encoder_gains, encoder_shifts,
    decoder_self, decoder_cross, decoder_up, decoder_up_bias, decoder_down, decoder_gains, decoder_shifts,
):
    group = lax.axis_size("bal")
    length, width = tag_rows.shape[1:]
    blocks = destination.shape[1]
    capacity = blocks // group
    span = length // blocks
    live = jnp.concatenate([tag_length, cell_count])
    places = destination[0] * capacity + slot_index[0]
    cot = lax.all_to_all(cotangent[0].reshape(group, capacity * span, width), "bal", 0, 0, tiled=True)
    y, d_patches, d_tags, enc, dec = local_step(
        patches[0], tag_rows[0], cot.reshape(blocks, span, width), live, places,
        (encoder_attention, encoder_up, encoder_up_bias[None], encoder_down, encoder_gains.T, encoder_shifts.T),
        (decoder_self, decoder_cross, decoder_up, decoder_up_bias[None], decoder_down, decoder_gains.T, decoder_shifts.T),
    )
    decoded = lax.all_to_all(y.reshape(group, capacity * span, width), "bal", 0, 0, tiled=True)

    def total(part, axis=0):
        rows = lax.psum_scatter(part.astype(BF), "dp", scatter_dimension=axis, tiled=True)
        return lax.psum(rows, "bal").astype(F32)

    def small(part, rows):
        whole = lax.psum(part, ("dp", "bal"))
        at = lax.axis_index("dp") * rows
        return lax.dynamic_slice_in_dim(whole, at, rows, axis=1)

    n_dp = lax.axis_size("dp")

    def layer(w):
        return jnp.swapaxes(total(w, 1), 0, 1)

    ew, eu, eb, ed, eg, es = enc
    sw, cw, du, db, dd, dg, ds = dec
    pads = [eb.reshape(2, width), db.reshape(2, width), eg, es, dg, ds]
    whole = lax.psum(jnp.concatenate(pads, axis=0), ("dp", "bal"))
    at = lax.axis_index("dp")
    bias_rows = 2 * width // n_dp
    pick = lambda block, rows: lax.dynamic_slice_in_dim(block, at * rows, rows, axis=0)
    gain_rows = width // n_dp
    return (
        decoded.reshape(1, length, width),
        d_patches[None],
        d_tags[None],
        layer(ew),
        total(eu),
        pick(whole[0:2].reshape(-1), bias_rows),
        total(ed),
        pick(whole[4:6].T, gain_rows),
        pick(whole[6:9].T, gain_rows),
        layer(sw),
        layer(cw),
        total(du),
        pick(whole[2:4].reshape(-1), bias_rows),
        total(dd),
        pick(whole[9:12].T, gain_rows),
        pick(whole[12:16].T, gain_rows),
    )


def solution(mesh):
    split = P(("dp", "bal"))
    in_specs = (split,) * 7 + (P(),) * 13
    out_specs = (split,) * 3 + (P("dp"),) * 13
    return jax.shard_map(per_device, mesh=mesh, in_specs=in_specs, out_specs=out_specs, check_vma=False)
```

```python
import functools

import jax
import jax.numpy as jnp
from jax import lax
from jax.experimental import pallas as pl
from jax.experimental.pallas import tpu as pltpu
from jax.sharding import PartitionSpec as P

HEADS = 8
HEAD = 64
EPSILON = 1e-05
NEGATIVE = -1e30
BF = jnp.bfloat16
F32 = jnp.float32
NN = (((1,), (0,)), ((), ()))
NT = (((1,), (1,)), ((), ()))
TN = (((0,), (0,)), ((), ()))
TT = (((0,), (1,)), ((), ()))
VM = pl.BlockSpec(memory_space=pltpu.VMEM)
SM = pl.BlockSpec(memory_space=pltpu.SMEM)
ANY = pl.BlockSpec(memory_space=pl.ANY)
LIMIT = 1e18
PARAMS = pltpu.CompilerParams(vmem_limit_bytes=60 << 20)
Shape = jax.ShapeDtypeStruct


def mm(left, right, dims=NN):
    return lax.dot_general(left, right, dims, preferred_element_type=F32)


def cut(rows):
    half = (rows // 2 + 15) // 16 * 16
    return [(0, half), (half, rows - half)]


class Copies:
    def __init__(self, sems):
        self.sems, self.used, self.open = sems, 0, []

    def start(self, source, target):
        copy = pltpu.make_async_copy(source, target, self.sems.at[self.used])
        self.used += 1
        copy.start()
        return copy

    def out(self, source, target):
        self.open.append(self.start(source, target))

    def finish(self):
        for copy in self.open:
            copy.wait()


def split_weights(raw, parts):
    def step(i, carry):
        rows = pl.ds(pl.multiple_of(i * 128, 128), 128)
        parts[:, rows, :] = pltpu.einshape("abc->bac", raw[rows])
        return carry

    lax.fori_loop(0, raw.shape[0] // 128, step, 0)


def normalise(signal):
    centre = jnp.mean(signal, axis=-1, keepdims=True)
    centered = signal - centre
    spread = jnp.mean(centered * centered, axis=-1, keepdims=True)
    rate = lax.rsqrt(spread + EPSILON)
    return centered * rate, rate


def norm_back(unit, rate, gain, gradient):
    inner = gradient * gain
    first = jnp.mean(inner, axis=-1, keepdims=True)
    second = jnp.mean(inner * unit, axis=-1, keepdims=True)
    return rate * (inner - first - unit * second)


def colsum(signal):
    return jnp.sum(signal, axis=0, keepdims=True)


def smooth(hidden):
    scale = 0.7978845608028654
    square = hidden * hidden
    curve = jnp.tanh(scale * hidden * (1.0 + 0.044715 * square))
    half = 0.5 + 0.5 * curve
    slope = half + 0.5 * hidden * (1.0 - curve * curve) * (scale + (3 * 0.044715 * scale) * square)
    return hidden * half, slope


def half_mask(shape, axis, which):
    index = lax.broadcasted_iota(jnp.int32, shape, axis)
    return (index < HEAD) if which == 0 else (index >= HEAD)


def keep_half(pair, axis, which):
    return jnp.where(half_mask(pair.shape, axis, which), pair, jnp.zeros_like(pair))


def project_qkv(x, sources, w4, q, qt, k, v, vt):
    rows = x.shape[0]
    for start, size in cut(rows):
        part = slice(start, start + size)
        q[part] = (mm(x[part], w4[0]) * HEAD ** (-0.5)).astype(BF)
    if q.shape[0] > rows:
        q[rows:] = jnp.zeros((q.shape[0] - rows, q.shape[1]), BF)
    for start, size in cut(sources.shape[0]):
        part = slice(start, start + size)
        k[part] = mm(sources[part], w4[1]).astype(BF)
        v[part] = mm(sources[part], w4[2]).astype(BF)
    qt[...] = q[...].T
    vt[...] = v[...].T


def shifted_exp(scores, exact, causal_rows):
    if causal_rows:
        size, width = scores.shape
        key = lax.broadcasted_iota(jnp.int32, (width, width), 0)
        query = lax.broadcasted_iota(jnp.int32, (width, width), 1)
        last = jnp.where(key <= query, scores[size - width :], NEGATIVE)
        scores = last if size == width else jnp.concatenate([scores[: size - width], last], axis=0)
        exact = exact or size == width
    sample = scores if exact else scores[:128]
    return jnp.exp(scores - jnp.max(sample, axis=0, keepdims=True))


def attend_heads(exact, causal, q_tile, qt, k, vt, ot, rate, store):
    keys, queries = k.shape[0], qt.shape[1]

    def pair(p, carry):
        lanes = pl.ds(pl.multiple_of(p * 128, 128), 128)
        for u in range(2):
            rows = pl.ds(pl.multiple_of(p * 128 + u * HEAD, HEAD), HEAD)
            place, done = store(p, u)
            for start in range(0, queries, q_tile):
                cols = slice(start, start + q_tile)
                depth = start + q_tile if causal else keys
                scores = mm(k[:depth, lanes], keep_half(qt[lanes, cols], 0, u))
                raised = shifted_exp(scores, exact, causal)
                total = jnp.sum(raised, axis=0, keepdims=True)
                low = raised.astype(BF)
                place[:depth, cols] = low
                inverse = 1.0 / total
                rate[2 * p + u, :, cols] = inverse
                ot[rows, cols] = (mm(vt[rows, :depth], low) * inverse).astype(BF)
            done()
        return carry

    lax.fori_loop(0, HEADS // 2, pair, 0)


def attend(causal, q_tile, qt, k, vt, ot, rate, store, drain):
    attend_heads(False, causal, q_tile, qt, k, vt, ot, rate, store)
    drain()
    fine = jnp.min(rate[...]) > 1.0 / LIMIT

    @pl.when(jnp.logical_not(fine))
    def _():
        attend_heads(True, causal, q_tile, qt, k, vt, ot, rate, store)
        drain()


def back_heads(causal, q_tile, q, kt, v, dot_, d_o, rowdot, fetch, ds, dqt, dk, dv, hook=None):
    keys, queries = v.shape[0], dqt.shape[1]

    def pair(p, carry):
        lanes = pl.ds(pl.multiple_of(p * 128, 128), 128)
        for u in range(2):
            rows = pl.ds(pl.multiple_of(p * 128 + u * HEAD, HEAD), HEAD)
            place = fetch(p, u)
            for start in range(0, queries, q_tile):
                cols = slice(start, start + q_tile)
                depth = start + q_tile if causal else keys
                grad = mm(v[:depth, lanes], keep_half(dot_[lanes, cols], 0, u))
                scaled = place[:depth, cols].astype(F32) * (grad - rowdot[2 * p + u, :, cols])
                low = scaled.astype(BF)
                ds[u][:depth, cols] = low
                dqt[rows, cols] = (mm(kt[rows, :depth], low) * HEAD ** (-0.5)).astype(BF)
            qm = q[:, lanes]
            dm = d_o[:, lanes]
            steps = range(0, keys, q_tile) if causal else (0,)
            for start in steps:
                key = slice(start, start + q_tile) if causal else slice(0, keys)
                more_k = mm(ds[u][key, start:], qm[start:])
                more_v = mm(place[key, start:], dm[start:])
                if u == 0:
                    dk[key, lanes] = more_k.astype(BF)
                    dv[key, lanes] = more_v.astype(BF)
                else:
                    dk[key, lanes] = jnp.where(half_mask(more_k.shape, 1, 1), more_k.astype(BF), dk[key, lanes])
                    dv[key, lanes] = jnp.where(half_mask(more_v.shape, 1, 1), more_v.astype(BF), dv[key, lanes])
        if hook is not None:
            hook(p)
        return carry

    lax.fori_loop(0, HEADS // 2, pair, 0)


def back_outputs(grad_low, w4, ot, rate, dot_, d_o, rowdot):
    rows, wide = grad_low.shape[0], dot_.shape[1]
    raw = mm(w4[3], grad_low[...], NT)
    for h in range(HEADS):
        part = slice(h * HEAD, (h + 1) * HEAD)
        low = (raw[part] * rate[h][:, :rows]).astype(BF)
        if wide > rows:
            low = jnp.concatenate([low, jnp.zeros((HEAD, wide - rows), BF)], axis=1)
        dot_[part] = low
        rowdot[h] = jnp.sum(low.astype(F32) * ot[part].astype(F32), axis=0, keepdims=True)
    d_o[...] = dot_[...].T


def ring(buffers, hbm, sems, spans, out):
    def copies(h, slot):
        made = []
        for i, (rows, cols) in enumerate(spans):
            here = buffers.at[slot, pl.ds(0, rows), cols]
            there = hbm.at[h, pl.ds(0, rows), cols]
            made.append(
                pltpu.make_async_copy(here, there, sems.at[slot, i])
                if out
                else pltpu.make_async_copy(there, here, sems.at[slot, i])
            )
        return made

    return copies


def out_ring(buffers, hbm, sems, spans):
    copies = ring(buffers, hbm, sems, spans, True)

    def store(p, u):
        slot = (p % 2) * 2 + u

        @pl.when(p >= 2)
        def _():
            for copy in copies(2 * p + u, slot):
                copy.wait()

        def done():
            for copy in copies(2 * p + u, slot):
                copy.start()

        return buffers.at[slot], done

    def drain():
        for slot in range(4):
            for copy in copies(slot, slot):
                copy.wait()

    return store, drain


def in_ring(buffers, hbm, sems, spans):
    copies = ring(buffers, hbm, sems, spans, False)

    def begin():
        for h in range(4):
            for copy in copies(h, h):
                copy.start()

    def fetch(p, u):
        slot = (p % 2) * 2 + u
        for copy in copies(2 * p + u, slot):
            copy.wait()
        if u == 0:
            @pl.when((p >= 1) & (p < HEADS // 2 - 1))
            def _():
                other = (1 - p % 2) * 2
                for v in range(2):
                    for copy in copies(2 * p + 2 + v, other + v):
                        copy.start()
        return buffers.at[slot]

    return begin, fetch


MESH = pl.DeviceIdType.MESH


class Spot:
    def __init__(self, n, m):
        self.n, self.m = n, m
        self.d, self.b = lax.axis_index("dp"), lax.axis_index("bal")
        self.core, self.far = self.b % 2, self.b // 2
        self.parity, self.row = self.d % 2, self.d // 2
        self.by_core = (self.d, self.b + 1 - 2 * self.core)
        self.by_far = (self.d, self.b + 2 - 4 * self.far)
        self.by_parity = (self.d + 1 - 2 * self.parity, self.b)

    def greet(self, everyone):
        barrier = pltpu.get_barrier_semaphore()

        def call(device):
            pl.semaphore_signal(barrier, inc=1, device_id=device, device_id_type=MESH)

        for k in range(1, self.m):
            call((self.d, (self.b + k) % self.m))
        count = self.m - 1
        if not everyone:
            call(self.by_parity)
            count += 1
        else:

            def along(k, carry):
                call(((self.d + k) % self.n, self.b))
                return carry

            def across(k, carry):
                call((((self.row + k) % (self.n // 2)) * 2 + self.parity, self.by_far[1]))
                return carry

            lax.fori_loop(1, self.n, along, 0)
            lax.fori_loop(1, self.n // 2, across, 0)
            count += self.n - 1 + self.n // 2 - 1
        pl.semaphore_wait(barrier, count)


def remote(source, target, sent, received, device):
    return pltpu.make_async_remote_copy(
        src_ref=source, dst_ref=target, send_sem=sent, recv_sem=received, device_id=device, device_id_type=MESH
    )


class Piece:
    def __init__(self, spot, along_x, source, acc, land_a, kept, land_b, slots, result, gathered, sems):
        self.spot, self.along_x, self.source = spot, along_x, source
        self.acc, self.land_a, self.kept, self.land_b = acc, land_a, kept, land_b
        self.slots, self.result, self.gathered, self.sems = slots, result, gathered, sems

    def a_copies(self):
        half = self.acc.shape[3]
        mine = pl.ds(pl.multiple_of(self.spot.core * half, half), half)
        other = pl.ds(pl.multiple_of((1 - self.spot.core) * half, half), half)
        return [
            pltpu.make_async_copy(self.source.at[:, :, :, mine], self.acc, self.sems.at[0]),
            remote(self.source.at[:, :, :, other], self.land_a, self.sems.at[1], self.sems.at[2], self.spot.by_core),
        ]

    def a_start(self):
        for copy in self.a_copies():
            copy.start()

    def a_wait(self):
        for copy in self.a_copies():
            copy.wait()

        def add(i, carry):
            self.acc[i] = self.acc[i] + self.land_a[i]
            return carry

        lax.fori_loop(0, self.acc.shape[0], add, 0)

    def b_copy(self):
        spot = self.spot
        if self.along_x:
            quarter = self.kept.shape[3]
            out = self.acc.at[:, :, :, pl.ds(pl.multiple_of((1 - spot.far) * quarter, quarter), quarter)]
            return remote(out, self.land_b, self.sems.at[3], self.sems.at[4], spot.by_far)
        return remote(self.acc.at[:, 1 - spot.parity], self.land_b, self.sems.at[3], self.sems.at[4], spot.by_parity)

    def b_start(self):
        self.b_copy().start()

    def b_wait(self):
        self.b_copy().wait()
        spot = self.spot

        def add(i, carry):
            if self.along_x:
                quarter = self.kept.shape[3]
                mine = self.acc[i, :, :, pl.ds(pl.multiple_of(spot.far * quarter, quarter), quarter)]
            else:
                mine = self.acc[i, spot.parity]
            self.kept[i] = mine + self.land_b[i]
            return carry

        lax.fori_loop(0, self.kept.shape[0], add, 0)

    def chunk(self, t):
        spot, half = self.spot, self.spot.n // 2
        if self.along_x:
            return (t // 2, t % 2, slice(None), slice(None)), (t, spot.b)
        lanes = self.slots.shape[2]
        far, row = t // half, t % half
        return (row, slice(None), pl.ds(pl.multiple_of(far * lanes, lanes), lanes)), (row * 2 + spot.parity, spot.core + 2 * far)

    def me(self):
        return self.spot.d if self.along_x else self.spot.far * (self.spot.n // 2) + self.spot.row

    def c_copy(self, k):
        n, me = self.spot.n, self.me()
        where, device = self.chunk((me + k) % n)
        return remote(self.kept.at[where], self.slots.at[me], self.sems.at[5 + k], self.sems.at[5 + n + me], device)

    def c_arrival(self, k):
        n, me = self.spot.n, self.me()
        source = (me + k) % n
        where, device = self.chunk(source)
        return remote(self.kept.at[where], self.slots.at[source], self.sems.at[5 + k], self.sems.at[5 + n + source], device)

    def c_start(self):
        def step(k, carry):
            self.c_copy(k).start()
            return carry

        lax.fori_loop(1, self.spot.n, step, 0)

    def c_wait(self):
        n, me = self.spot.n, self.me()

        def step(k, total):
            self.c_copy(k).wait_send()
            self.c_arrival(k).wait_recv()
            return total + self.slots[(me + k) % n].astype(F32)

        where, _ = self.chunk(me)
        total = lax.fori_loop(1, n, step, self.kept[where].astype(F32))
        self.result[...] = total.astype(BF)

    def d_copies(self, arriving):
        spot, base = self.spot, 5 + 2 * self.spot.n
        made = []
        for k in range(1, spot.m):
            peer = (spot.b + k) % spot.m
            slot = peer if arriving else spot.b
            made.append(remote(self.result, self.gathered.at[slot], self.sems.at[base + k], self.sems.at[base + spot.m + slot], (spot.d, peer)))
        return made

    def d_start(self):
        for copy in self.d_copies(False):
            copy.start()
        self.gathered[self.spot.b] = self.result[...]

    def d_wait(self):
        for copy in self.d_copies(False):
            copy.wait_send()
        for copy in self.d_copies(True):
            copy.wait_recv()


def piece_sems(n, m):
    return pltpu.SemaphoreType.DMA((5 + 2 * n + 2 * m,))


def piece_first(n, rows, along_x):
    half = (n // 2, 2, rows, 256)
    return [pltpu.VMEM(half, BF), pltpu.VMEM(half, BF), pltpu.VMEM(kept_shape(n, rows, along_x), BF)]


def kept_shape(n, rows, along_x):
    return (n // 2, 2, rows, 128) if along_x else (n // 2, rows, 256)


def piece_second(n, rows):
    return [pltpu.VMEM((n, rows, 128), BF), pltpu.VMEM((rows, 128), BF)]


class VectorSum:
    def __init__(self, spot, v, land_a, land_b, slots, result, sems):
        self.spot, self.v, self.lands, self.slots, self.result, self.sems = spot, v, (land_a, land_b), slots, result, sems

    def swap(self, step):
        device = (self.spot.by_core, self.spot.by_far)[step]
        return remote(self.v, self.lands[step], self.sems.at[2 * step], self.sems.at[2 * step + 1], device)

    def swap_start(self, step):
        self.swap(step).start()

    def swap_wait(self, step):
        self.swap(step).wait()
        self.v[...] = self.v[...] + self.lands[step][...]

    def copy(self, k, arriving):
        n, d = self.spot.n, self.spot.d
        peer = (d + k) % n
        slot = peer if arriving else d
        return remote(self.v.at[peer], self.slots.at[slot], self.sems.at[4 + k], self.sems.at[4 + n + slot], (peer, self.spot.b))

    def c_start(self):
        def step(k, carry):
            self.copy(k, False).start()
            return carry

        lax.fori_loop(1, self.spot.n, step, 0)

    def c_wait(self):
        n, d = self.spot.n, self.spot.d

        def step(k, total):
            self.copy(k, False).wait_send()
            self.copy(k, True).wait_recv()
            return total + self.slots[(d + k) % n]

        self.result[...] = lax.fori_loop(1, n, step, self.v[d])


def put(piece, row, value):
    halves, two, _, width = piece.shape
    rows = value.shape[0] // (halves * two)
    piece[:, :, row : row + rows, :] = value.reshape(halves, two, rows, width).astype(BF)


def encoder_forward(x_h, w_h, up_h, bias, down_h, gains, shifts,
                    memory, w4_h, qkv_h, ot_h, e_h, rate, e1_h, e2_h, zb_h, act_h, slope_h,
                    x, raw, w4, up, down, q, k, v, qt, vt, ot, e1, e2, zb, act, slope, ering, sems, esems):
    c = Copies(sems)
    load_w = c.start(w_h, raw)
    load_x = c.start(x_h, x)
    load_up = c.start(up_h, up)
    load_down = c.start(down_h, down)
    load_w.wait()
    split_weights(raw, w4)
    c.out(w4, w4_h)
    load_x.wait()
    project_qkv(x, x, w4, q, qt, k, v, vt)
    n, wide = x.shape[0], qt.shape[1]
    for i, item in enumerate((q.at[pl.ds(0, n)], k, v)):
        c.out(item, qkv_h.at[i])
    store, drain = out_ring(ering, e_h, esems, [(n, slice(None))])
    attend(False, wide, qt, k, vt, ot, rate, store, drain)
    c.out(ot, ot_h)
    load_up.wait()
    load_down.wait()
    for start, size in cut(n):
        part = slice(start, start + size)
        first = x[part].astype(F32) + mm(ot[:, part], w4[3], TN)
        e1[part] = first
        unit, _ = normalise(first)
        z = unit * gains[0:1] + shifts[0:1]
        low = z.astype(BF)
        zb[part] = low
        active, bend = smooth(mm(low, up[...]) + bias[...])
        act[part] = active.astype(BF)
        slope[part] = bend.astype(BF)
        second = z + mm(act[part], down[...]) + shifts[2:3]
        e2[part] = second
        unit, _ = normalise(second)
        memory[part] = (unit * gains[1:2] + shifts[1:2]).astype(BF)
    for here, there in ((e1, e1_h), (e2, e2_h), (zb, zb_h), (act, act_h), (slope, slope_h)):
        c.out(here, there)
    c.finish()


def tags_forward(x_h, w_h, gains, shifts,
                 x1, w4_h, qkv_h, ot_h, e_h, rate, a1_h,
                 x, raw, w4, q, k, v, qt, vt, ot, a1, ering, sems, esems):
    c = Copies(sems)
    load_w = c.start(w_h, raw)
    load_x = c.start(x_h, x)
    load_w.wait()
    split_weights(raw, w4)
    c.out(w4, w4_h)
    load_x.wait()
    project_qkv(x, x, w4, q, qt, k, v, vt)
    n = x.shape[0]
    for i, item in enumerate((q, k, v)):
        c.out(item, qkv_h.at[i])
    tile = 256
    spans = [(start + tile, slice(start, start + tile)) for start in range(0, n, tile)]
    store, drain = out_ring(ering, e_h, esems, spans)
    attend(True, tile, qt, k, vt, ot, rate, store, drain)
    c.out(ot, ot_h)
    for start, size in cut(n):
        part = slice(start, start + size)
        first = x[part].astype(F32) + mm(ot[:, part], w4[3], TN)
        a1[part] = first
        unit, _ = normalise(first)
        x1[part] = (unit * gains[0:1] + shifts[0:1]).astype(BF)
    c.out(a1, a1_h)
    c.finish()


def decoder_tail(live_rows, places, x1_h, mem_h, w_h, up_h, bias, down_h, gains, shifts, cot_h,
                 y, dx1, dmem, g_cross, g_ffn, d_bias, d_gains, d_shifts,
                 x1, mem, raw, w4, up, down, q, k, v, qt, vt, ot, kt, e, rate,
                 unit2, rate2, xb2, act, slope, da, gb, rowdot, dqt, dk, dv, sems):
    cot, dh, dot_, d_o, ds = y, slope, qt, xb2, (act, slope)
    c = Copies(sems)
    load_w = c.start(w_h, raw)
    load_mem = c.start(mem_h, mem)
    load_x = c.start(x1_h, x1)
    load_up = c.start(up_h, up)
    load_down = c.start(down_h, down)
    load_cot = c.start(cot_h, cot)
    load_w.wait()
    split_weights(raw, w4)
    load_mem.wait()
    load_x.wait()
    project_qkv(x1, mem, w4, q, qt, k, v, vt)
    kt[...] = k[...].T
    n, blocks = x1.shape[0], y.shape[0]
    block = n // blocks

    def store(p, u):
        return e.at[2 * p + u], lambda: None

    attend(False, n, qt, k, vt, ot, rate, store, lambda: None)
    load_up.wait()
    load_down.wait()
    load_cot.wait()
    live = live_rows[0] + live_rows[1]
    zero = jnp.zeros((1, x1.shape[1]), F32)
    gain3, shift3 = zero, zero
    for start, size in cut(n):
        part = slice(start, start + size)
        second = x1[part].astype(F32) + mm(ot[:, part], w4[3], TN)
        unit, pace = normalise(second)
        unit2[part] = unit
        rate2[part] = pace
        x2 = unit * gains[1:2] + shifts[1:2]
        low = x2.astype(BF)
        xb2[part] = low
        active, bend = smooth(mm(low, up[...]) + bias[...])
        act[part] = active.astype(BF)
        slope[part] = bend.astype(BF)
        third = x2 + mm(act[part], down[...]) + shifts[3:4]
        unit, pace = normalise(third)
        row = lax.broadcasted_iota(jnp.int32, (size, 1), 0) + start
        alive = (row < live).astype(F32)
        final = ((unit * gains[2:3] + shifts[2:3]) * alive).astype(BF)
        picked = []
        for b in range(start // block, (start + size) // block):
            picked.append(cot[places[b]])
            y[places[b]] = final[b * block - start : (b + 1) * block - start]
        dy = jnp.concatenate(picked, axis=0).astype(F32) * alive
        gain3 += colsum(dy * unit)
        shift3 += colsum(dy)
        d3 = norm_back(unit, pace, gains[2:3], dy)
        da[part] = d3
        gb[part] = d3.astype(BF)
    d_gains[2:3] = gain3
    d_shifts[2:3] = shift3
    ffn_back(xb2, up, down, act, slope, gb, dh, g_ffn, d_bias, d_shifts, 3)
    gain2, shift2 = zero, zero
    for start, size in cut(n):
        part = slice(start, start + size)
        dx2 = da[part] + mm(dh[part], up[...], NT)
        gain2 += colsum(dx2 * unit2[part])
        shift2 += colsum(dx2)
        d2 = norm_back(unit2[part], rate2[part], gains[1:2], dx2)
        da[part] = d2
        gb[part] = d2.astype(BF)
    d_gains[1:2] = gain2
    d_shifts[1:2] = shift2
    piece_rows = g_cross.shape[2] // 4
    put(g_cross, 3 * piece_rows, mm(ot[...], gb[...]))
    back_outputs(gb, w4, ot, rate, dot_, d_o, rowdot)
    back_heads(False, n, q, kt, v, dot_, d_o, rowdot, lambda p, u: e.at[2 * p + u], ds, dqt, dk, dv)
    put(g_cross, 0, mm(x1[...], dqt[...], TT))
    put(g_cross, piece_rows, mm(mem[...], dk[...], TN))
    put(g_cross, 2 * piece_rows, mm(mem[...], dv[...], TN))
    for start, size in cut(n):
        part = slice(start, start + size)
        dx1[part] = (da[part] + mm(dqt[:, part], w4[0], TT)).astype(BF)
    for start, size in cut(mem.shape[0]):
        part = slice(start, start + size)
        dmem[part] = mm(dk[part], w4[1], NT) + mm(dv[part], w4[2], NT)


def ffn_back(xb, up, down, act, slope, gb, dh, g_ffn, d_bias, d_shifts, row):
    n, width = xb.shape
    offset = jnp.zeros((1, up.shape[1]), F32)
    for start, size in cut(n):
        part = slice(start, start + size)
        low = (mm(gb[part], down[...], NT) * slope[part].astype(F32)).astype(BF)
        dh[part] = low
        offset += colsum(low.astype(F32))
    d_bias[...] = offset
    d_shifts[row : row + 1] = colsum(gb[...].astype(F32))
    rows = g_ffn.shape[2] // 4
    put(g_ffn, 2 * rows, mm(act[...], gb[...], TN))
    for j in range(up.shape[1] // width):
        put(g_ffn, j * rows, mm(xb[...], dh[:, j * width : (j + 1) * width], TN))


def tags_backward(n_dp, n_bal, dx1_h, a1_h, x_h, w4_h, qkv_h, ot_h, e_h, rate, gains, y_h, g_cross, g_ffn,
                  dx, g_self, d_gains, d_shifts, decoded, kept_cross, kept_ffn,
                  dx1, a1, x, w4, q, k, v, ot, kt, ering, da, gb, dot_, d_o, rowdot, ds, dqt, dk, dv,
                  acc0, land0, next0, acc1, land1, next1, sems, esems, sems0, sems1, moves):
    spot = Spot(n_dp, n_bal)
    cross = Piece(spot, True, g_cross, acc0, land0, kept_cross, next0, None, None, None, sems0)
    branch = Piece(spot, False, g_ffn, acc1, land1, kept_ffn, next1, None, None, None, sems1)
    c = Copies(sems)
    load_dx1 = c.start(dx1_h, dx1)
    load_a1 = c.start(a1_h, a1)
    load_w = c.start(w4_h, w4)
    load_ot = c.start(ot_h, ot)
    load_qkv = [c.start(qkv_h.at[i], item) for i, item in enumerate((q, k, v))]
    load_x = c.start(x_h, x)
    n = q.shape[0]
    tile = 256
    spans = [(start + tile, slice(start, start + tile)) for start in range(0, n, tile)]
    begin, fetch = in_ring(ering, e_h, esems, spans)
    begin()
    spot.greet(False)
    cross.a_start()
    branch.a_start()
    load_dx1.wait()
    load_a1.wait()
    zero = jnp.zeros((1, x.shape[1]), F32)
    gain, shift = zero, zero
    for start, size in cut(n):
        part = slice(start, start + size)
        unit, pace = normalise(a1[part])
        grad = dx1[part].astype(F32)
        gain += colsum(grad * unit)
        shift += colsum(grad)
        d1 = norm_back(unit, pace, gains[0:1], grad)
        da[part] = d1
        gb[part] = d1.astype(BF)
    d_gains[...] = gain
    d_shifts[...] = shift
    cross.a_wait()
    cross.b_start()
    branch.a_wait()
    branch.b_start()
    share = y_h.shape[0] // n_bal

    def moved(k, arriving):
        peer = (spot.b + k) % n_bal
        slot = peer if arriving else spot.b
        return remote(y_h.at[pl.ds(peer * share, share)], decoded.at[pl.ds(slot * share, share)], moves.at[k],
                      moves.at[n_bal + slot], (spot.d, peer))

    own = pltpu.make_async_copy(y_h.at[pl.ds(spot.b * share, share)], decoded.at[pl.ds(spot.b * share, share)], moves.at[0])
    own.start()
    for step in range(1, n_bal):
        moved(step, False).start()
    attention_back(True, tile, x, w4, q, k, v, ot, kt, rate, fetch, da, gb, dot_, d_o, rowdot, ds, dqt, dk, dv,
                   (load_w, load_ot, *load_qkv, load_x), (g_self, g_self), dx, None, None, None)
    cross.b_wait()
    branch.b_wait()
    own.wait()
    for step in range(1, n_bal):
        moved(step, False).wait_send()
        moved(step, True).wait_recv()


def attention_back(causal, tile, x, w4, q, k, v, ot, kt, rate, fetch, da, gb, dot_, d_o, rowdot, ds, dqt, dk, dv,
                   loads, pieces, dx, hook, after_first, after_second):
    for load in loads:
        load.wait()
    n, width = x.shape
    whole = pieces[0] is pieces[1]
    rows = pieces[0].shape[2] // (4 if whole else 2)
    kt[...] = k[...].T
    put(pieces[1], 3 * rows if whole else rows, mm(ot[:, :n], gb[...]))
    back_outputs(gb, w4, ot, rate, dot_, d_o, rowdot)
    back_heads(causal, tile, q, kt, v, dot_, d_o, rowdot, fetch, (ds.at[0], ds.at[1]), dqt, dk, dv, hook)
    put(pieces[0], 0, mm(x[...], dqt[:, :n], TT))
    put(pieces[0], rows, mm(x[...], dk[...], TN))
    if after_first is not None:
        after_first()
    put(pieces[1], 2 * rows if whole else 0, mm(x[...], dv[...], TN))
    if after_second is not None:
        after_second()
    for start, size in cut(n):
        part = slice(start, start + size)
        dx[part] = (da[part] + mm(dqt[:, part], w4[0], TT) + mm(dk[part], w4[1], NT) + mm(dv[part], w4[2], NT))


def encoder_backward(n_dp, n_bal, dmem_h, e2_h, e1_h, zb_h, act_h, slope_h, up_h, down_h, x_h, w4_h, qkv_h, ot_h, e_h,
                     rate, gains, kept_cross, kept_dffn, g_self, d_gains0, d_shifts0, d_bias_d, d_gains_d, d_shifts_d,
                     dx, all_cross, all_dffn, all_self, all_effn, all_enc0, all_enc1, v_total,
                     dmem, e2, e1, zb, act, slope, up, down, x, w4, q, k, v, ot, kt, ering, da, gb,
                     dot_, d_o, rowdot, ds, dqt, dk, dv, d_bias, d_gains, d_shifts,
                     g_effn, g_enc0, g_enc1,
                     slots0, result0, slots1, result1,
                     acc2, land2, next2, kept2, slots2, result2,
                     acc3, land3, next3, kept3, slots3, result3,
                     acc4, land4, next4, kept4, slots4, result4,
                     acc5, land5, next5, kept5, slots5, result5,
                     vec, vec_a, vec_b, vec_slots,
                     sems, esems, sems0, sems1, sems2, sems3, sems4, sems5, sems6):
    spot = Spot(n_dp, n_bal)
    cross = Piece(spot, True, None, None, None, kept_cross, None, slots0, result0, all_cross, sems0)
    dffn = Piece(spot, False, None, None, None, kept_dffn, None, slots1, result1, all_dffn, sems1)
    selfs = Piece(spot, False, g_self, acc2, land2, kept2, next2, slots2, result2, all_self, sems2)
    effn = Piece(spot, False, g_effn, acc3, land3, kept3, next3, slots3, result3, all_effn, sems3)
    enc0 = Piece(spot, True, g_enc0, acc4, land4, kept4, next4, slots4, result4, all_enc0, sems4)
    enc1 = Piece(spot, False, g_enc1, acc5, land5, kept5, next5, slots5, result5, all_enc1, sems5)
    vector = VectorSum(spot, vec, vec_a, vec_b, vec_slots, v_total, sems6)
    c = Copies(sems)
    load_first = [c.start(a, b) for a, b in ((dmem_h, dmem), (e2_h, e2))]
    load_ffn = [c.start(a, b) for a, b in ((down_h, down), (slope_h, slope), (act_h, act), (zb_h, zb), (up_h, up))]
    load_e1 = c.start(e1_h, e1)
    load_w = c.start(w4_h, w4)
    load_ot = c.start(ot_h, ot)
    n, wide = x.shape[0], dot_.shape[1]
    load_qkv = [c.start(qkv_h.at[i], item) for i, item in enumerate((q.at[pl.ds(0, n)], k, v))]
    load_x = c.start(x_h, x)
    begin, fetch = in_ring(ering, e_h, esems, [(n, slice(None))])
    begin()
    spot.greet(True)
    selfs.a_start()
    cross.c_start()
    dffn.c_start()
    q[n:] = jnp.zeros((wide - n, q.shape[1]), BF)
    for load in load_first:
        load.wait()
    zero = jnp.zeros((1, x.shape[1]), F32)
    gain, shift = zero, zero
    for start, size in cut(n):
        part = slice(start, start + size)
        unit, pace = normalise(e2[part])
        grad = dmem[part]
        gain += colsum(grad * unit)
        shift += colsum(grad)
        d2 = norm_back(unit, pace, gains[1:2], grad)
        da[part] = d2
        gb[part] = d2.astype(BF)
    d_gains[1:2] = gain
    d_shifts[1:2] = shift
    selfs.a_wait()
    selfs.b_start()
    for load in load_ffn:
        load.wait()
    dh = slope
    ffn_back(zb, up, down, act, slope, gb, dh, g_effn, d_bias, d_shifts, 2)
    effn.a_start()
    load_e1.wait()
    gain, shift = zero, zero
    for start, size in cut(n):
        part = slice(start, start + size)
        unit, pace = normalise(e1[part])
        dz = da[part] + mm(dh[part], up[...], NT)
        gain += colsum(dz * unit)
        shift += colsum(dz)
        d1 = norm_back(unit, pace, gains[0:1], dz)
        da[part] = d1
        gb[part] = d1.astype(BF)
    d_gains[0:1] = gain
    d_shifts[0:1] = shift
    share = x.shape[1] // n_dp
    vec[...] = jnp.zeros_like(vec)
    for i in range(n_dp):
        lanes = slice(i * share, (i + 1) * share)
        for j in range(2):
            wide_lanes = slice((2 * i + j) * share, (2 * i + j + 1) * share)
            vec[i, j : j + 1, :share] = d_bias[:, wide_lanes]
            vec[i, 2 + j : 3 + j, :share] = d_bias_d[:, wide_lanes]
        vec[i, 4:6, :share] = d_gains[:, lanes]
        vec[i, 6:9, :share] = d_shifts[:, lanes]
        vec[i, 9:10, :share] = d_gains0[:, lanes]
        vec[i, 10:12, :share] = d_gains_d[1:3, lanes]
        vec[i, 12:13, :share] = d_shifts0[:, lanes]
        vec[i, 13:16, :share] = d_shifts_d[1:4, lanes]
    vector.swap_start(0)
    effn.a_wait()
    effn.b_start()
    cross.c_wait()
    cross.d_start()
    dffn.c_wait()
    dffn.d_start()
    vector.swap_wait(0)
    vector.swap_start(1)

    def hook(p):
        @pl.when(p == 0)
        def _():
            selfs.b_wait()
            selfs.c_start()
            vector.swap_wait(1)
            vector.c_start()

        @pl.when(p == 2)
        def _():
            effn.b_wait()
            effn.c_start()
            selfs.c_wait()
            selfs.d_start()

    def after_second():
        enc0.a_wait()
        enc0.b_start()
        enc1.a_start()

    attention_back(False, wide, x, w4, q, k, v, ot, kt, rate, fetch, da, gb, dot_, d_o, rowdot, ds, dqt, dk, dv,
                   (load_w, load_ot, *load_qkv, load_x), (g_enc0, g_enc1), dx, hook, enc0.a_start, after_second)
    enc1.a_wait()
    enc1.b_start()
    effn.c_wait()
    effn.d_start()
    vector.c_wait()
    enc0.b_wait()
    enc0.c_start()
    enc1.b_wait()
    enc1.c_start()
    cross.d_wait()
    dffn.d_wait()
    selfs.d_wait()
    effn.d_wait()
    enc0.c_wait()
    enc0.d_start()
    enc1.c_wait()
    enc1.d_start()
    enc0.d_wait()
    enc1.d_wait()


def finish(all_cross, all_dffn, all_self, all_effn, all_enc0, all_enc1, v_total,
           o_enc, o_eup, o_ebias, o_edown, o_egains, o_eshifts,
           o_self, o_cross, o_dup, o_dbias, o_ddown, o_dgains, o_dshifts):
    def joined(gathered):
        return jnp.concatenate([gathered[b].astype(F32) for b in (0, 2, 1, 3)], axis=1)

    def layer(out, parts, first):
        rows = out.shape[0]
        for j in range(parts.shape[0] // rows):
            out[:, first + j, :] = parts[j * rows : (j + 1) * rows]

    def branch(up, down, parts):
        rows, width = up.shape[0], parts.shape[1]
        for j in range(up.shape[1] // width):
            up[:, j * width : (j + 1) * width] = parts[j * rows : (j + 1) * rows]
        down[...] = parts[2 * rows :]

    layer(o_enc, joined(all_enc0), 0)
    layer(o_enc, joined(all_enc1), 2)
    layer(o_self, joined(all_self), 0)
    layer(o_cross, joined(all_cross), 0)
    branch(o_eup, o_edown, joined(all_effn))
    branch(o_dup, o_ddown, joined(all_dffn))
    share = o_egains.shape[1]
    for j in range(2):
        o_ebias[:, j * share : (j + 1) * share] = v_total[j : j + 1, :share]
        o_dbias[:, j * share : (j + 1) * share] = v_total[2 + j : 3 + j, :share]
    o_egains[...] = v_total[4:6, :share]
    o_eshifts[...] = v_total[6:9, :share]
    o_dgains[...] = v_total[9:12, :share]
    o_dshifts[...] = v_total[12:16, :share]


def call(kernel, ins, outs, out_specs, scratch, name, params=PARAMS):
    specs = [spec for spec, _ in ins]
    return pl.pallas_call(
        kernel,
        out_shape=outs,
        in_specs=specs,
        out_specs=out_specs,
        scratch_shapes=scratch,
        compiler_params=params,
        name=name,
    )(*[value for _, value in ins])


def run_encoder_forward(x, w, up, bias, down, gains, shifts):
    n, width = x.shape
    hidden = up.shape[1]
    wide = (n + 127) // 128 * 128
    bf = lambda *s: Shape(s, BF)
    f32 = lambda *s: Shape(s, F32)
    vb = lambda *s: pltpu.VMEM(s, BF)
    vf = lambda *s: pltpu.VMEM(s, F32)
    outs = [bf(n, width), bf(4, width, width), bf(3, n, width), bf(width, wide), bf(HEADS, n, wide), f32(HEADS, 1, wide),
            f32(n, width), f32(n, width), bf(n, width), bf(n, hidden), bf(n, hidden)]
    return call(
        encoder_forward,
        [(ANY, x), (ANY, w), (ANY, up), (VM, bias), (ANY, down), (VM, gains), (VM, shifts)],
        outs,
        [VM, ANY, ANY, ANY, ANY, VM, ANY, ANY, ANY, ANY, ANY],
        [vb(n, width), vb(width, 4, width), vb(4, width, width), vb(width, hidden), vb(hidden, width),
         vb(wide, width), vb(n, width), vb(n, width), vb(width, wide), vb(width, n), vb(width, wide),
         vf(n, width), vf(n, width), vb(n, width), vb(n, hidden), vb(n, hidden), vb(4, n, wide),
         pltpu.SemaphoreType.DMA((20,)), pltpu.SemaphoreType.DMA((4, 1))],
        "encoder_forward",
    )


def run_tags_forward(x, w, gains, shifts):
    n, width = x.shape
    bf = lambda *s: Shape(s, BF)
    f32 = lambda *s: Shape(s, F32)
    vb = lambda *s: pltpu.VMEM(s, BF)
    vf = lambda *s: pltpu.VMEM(s, F32)
    return call(
        tags_forward,
        [(ANY, x), (ANY, w), (VM, gains), (VM, shifts)],
        [bf(n, width), bf(4, width, width), bf(3, n, width), bf(width, n), bf(HEADS, n, n), f32(HEADS, 1, n), f32(n, width)],
        [VM, ANY, ANY, ANY, ANY, VM, ANY],
        [vb(n, width), vb(width, 4, width), vb(4, width, width), vb(n, width), vb(n, width), vb(n, width),
         vb(width, n), vb(width, n), vb(width, n), vf(n, width), vb(4, n, n),
         pltpu.SemaphoreType.DMA((20,)), pltpu.SemaphoreType.DMA((4, n // 256))],
        "tags_forward",
    )


def run_decoder_tail(n_dp, live, places, x1, mem, w, up, bias, down, gains, shifts, cot):
    n, width = x1.shape
    m = mem.shape[0]
    hidden = up.shape[1]
    piece = (n_dp // 2, 2, 4 * width // n_dp, width)
    bf = lambda *s: Shape(s, BF)
    f32 = lambda *s: Shape(s, F32)
    vb = lambda *s: pltpu.VMEM(s, BF)
    vf = lambda *s: pltpu.VMEM(s, F32)
    return call(
        decoder_tail,
        [(SM, live), (SM, places), (ANY, x1), (ANY, mem), (ANY, w), (ANY, up), (VM, bias), (ANY, down), (VM, gains),
         (VM, shifts), (ANY, cot)],
        [bf(*cot.shape), bf(n, width), f32(m, width), bf(*piece), bf(*piece), f32(1, hidden), f32(3, width),
         f32(4, width)],
        [VM] * 8,
        [vb(n, width), vb(m, width), vb(width, 4, width), vb(4, width, width), vb(width, hidden), vb(hidden, width),
         vb(n, width), vb(m, width), vb(m, width), vb(width, n), vb(width, m), vb(width, n), vb(width, m),
         vb(HEADS, m, n), vf(HEADS, 1, n), vf(n, width), vf(n, 1), vb(n, width), vb(n, hidden), vb(n, hidden),
         vf(n, width), vb(n, width), vf(HEADS, 1, n), vb(width, n), vb(m, width), vb(m, width), pltpu.SemaphoreType.DMA((20,))],
        "decoder_tail",
    )


def talking(number):
    return pltpu.CompilerParams(vmem_limit_bytes=60 << 20, collective_id=number, has_side_effects=True)


def run_tags_backward(n_dp, n_bal, dx1, a1, x, w4, qkv, ot, e, rate, gains, y, g_cross, g_ffn):
    n, width = x.shape
    rows = 4 * width // n_dp
    bf = lambda *s: Shape(s, BF)
    f32 = lambda *s: Shape(s, F32)
    vb = lambda *s: pltpu.VMEM(s, BF)
    vf = lambda *s: pltpu.VMEM(s, F32)
    return call(
        functools.partial(tags_backward, n_dp, n_bal),
        [(ANY, dx1), (ANY, a1), (ANY, x), (ANY, w4), (ANY, qkv), (ANY, ot), (ANY, e), (VM, rate), (VM, gains),
         (ANY, y), (ANY, g_cross), (ANY, g_ffn)],
        [f32(n, width), bf(*g_cross.shape), f32(1, width), f32(1, width), bf(*y.shape),
         bf(*kept_shape(n_dp, rows, True)), bf(*kept_shape(n_dp, rows, False))],
        [VM, VM, VM, VM, ANY, VM, VM],
        [vb(n, width), vf(n, width), vb(n, width), vb(4, width, width), vb(n, width), vb(n, width), vb(n, width),
         vb(width, n), vb(width, n), vb(4, n, n), vf(n, width), vb(n, width), vb(width, n), vb(n, width),
         vf(HEADS, 1, n), vb(2, n, n), vb(width, n), vb(n, width), vb(n, width),
         *piece_first(n_dp, rows, True), *piece_first(n_dp, rows, False),
         pltpu.SemaphoreType.DMA((20,)), pltpu.SemaphoreType.DMA((4, n // 256)),
         piece_sems(n_dp, n_bal), piece_sems(n_dp, n_bal), pltpu.SemaphoreType.DMA((2 * n_bal,))],
        "tags_backward",
        talking(1),
    )


def run_encoder_backward(n_dp, n_bal, dmem, e2, e1, zb, act, slope, up, down, x, w4, qkv, ot, e, rate, gains,
                         kept_cross, kept_dffn, g_self, *vectors):
    n, width = x.shape
    hidden = up.shape[1]
    wide = ot.shape[1]
    rows = 4 * width // n_dp
    bf = lambda *s: Shape(s, BF)
    f32 = lambda *s: Shape(s, F32)
    vb = lambda *s: pltpu.VMEM(s, BF)
    vf = lambda *s: pltpu.VMEM(s, F32)
    gathered = [bf(n_bal, rows, 128)] * 4 + [bf(n_bal, rows // 2, 128)] * 2

    def first(size, along_x):
        return [*piece_first(n_dp, size, along_x), pltpu.VMEM(kept_shape(n_dp, size, along_x), BF), *piece_second(n_dp, size)]

    return call(
        functools.partial(encoder_backward, n_dp, n_bal),
        [(ANY, v) for v in (dmem, e2, e1, zb, act, slope, up, down, x, w4, qkv, ot, e)]
        + [(VM, rate), (VM, gains), (VM, kept_cross), (VM, kept_dffn), (ANY, g_self)] + [(VM, v) for v in vectors],
        [f32(n, width), *gathered, f32(16, 128)],
        [VM] * 8,
        [vf(n, width), vf(n, width), vf(n, width), vb(n, width), vb(n, hidden), vb(n, hidden), vb(width, hidden),
         vb(hidden, width), vb(n, width), vb(4, width, width), vb(wide, width), vb(n, width), vb(n, width),
         vb(width, wide), vb(width, n), vb(4, n, wide), vf(n, width), vb(n, width),
         vb(width, wide), vb(wide, width), vf(HEADS, 1, wide), vb(2, n, wide), vb(width, wide), vb(n, width),
         vb(n, width), vf(1, hidden), vf(2, width), vf(3, width),
         vb(n_dp // 2, 2, rows, width), vb(n_dp // 2, 2, rows // 2, width), vb(n_dp // 2, 2, rows // 2, width),
         *piece_second(n_dp, rows), *piece_second(n_dp, rows),
         *first(rows, False), *first(rows, False), *first(rows // 2, True), *first(rows // 2, False),
         vf(n_dp, 16, 128), vf(n_dp, 16, 128), vf(n_dp, 16, 128), vf(n_dp, 16, 128),
         pltpu.SemaphoreType.DMA((20,)), pltpu.SemaphoreType.DMA((4, 1)),
         *[piece_sems(n_dp, n_bal)] * 6, pltpu.SemaphoreType.DMA((4 + 2 * n_dp,))],
        "encoder_backward",
        talking(2),
    )


def run_finish(n_dp, hidden, width, *gathered):
    share = width // n_dp
    f32 = lambda *s: Shape(s, F32)
    side = [f32(share, 4, width)]
    branch = [f32(share, hidden), f32(1, hidden // n_dp), f32(hidden // n_dp, width)]
    outs = side + branch + [f32(2, share), f32(3, share)] + side + side + branch + [f32(3, share), f32(4, share)]
    return call(finish, [(VM, v) for v in gathered], outs, [VM] * len(outs), [], "finish")


def per_device(
    patches, tag_rows, cotangent, tag_length, cell_count, destination, slot_index,
    encoder_attention, encoder_up, encoder_up_bias, encoder_down, encoder_gains, encoder_shifts,
    decoder_self, decoder_cross, decoder_up, decoder_up_bias, decoder_down, decoder_gains, decoder_shifts,
):
    n_bal, n_dp = lax.axis_size("bal"), lax.axis_size("dp")
    length, width = tag_rows.shape[1:]
    hidden = encoder_up.shape[1]
    blocks = destination.shape[1]
    capacity = blocks // n_bal
    span = length // blocks
    live = jnp.concatenate([tag_length, cell_count])
    places = destination[0] * capacity + slot_index[0]
    cot = lax.all_to_all(cotangent[0].reshape(n_bal, capacity * span, width), "bal", 0, 0, tiled=True)
    cot = cot.reshape(blocks, span, width)
    eg, es, dg, ds = encoder_gains.T, encoder_shifts.T, decoder_gains.T, decoder_shifts.T
    eb, db = encoder_up_bias[None], decoder_up_bias[None]
    memory, ew4, eqkv, eot, ee, erate, e1, e2, zb, act, slope = run_encoder_forward(
        patches[0], encoder_attention, encoder_up, eb, encoder_down, eg, es)
    x1, sw4, sqkv, sot, se, srate, a1 = run_tags_forward(tag_rows[0], decoder_self, dg, ds)
    y, dx1, dmem, g_cross, g_dffn, d_db, d_dg, d_ds = run_decoder_tail(
        n_dp, live, places, x1, memory, decoder_cross, decoder_up, db, decoder_down, dg, ds, cot)
    d_tags, g_self, d_dg0, d_ds0, decoded, kept_cross, kept_dffn = run_tags_backward(
        n_dp, n_bal, dx1, a1, tag_rows[0], sw4, sqkv, sot, se, srate, dg, y, g_cross, g_dffn)
    d_patches, *gathered = run_encoder_backward(
        n_dp, n_bal, dmem, e2, e1, zb, act, slope, encoder_up, encoder_down, patches[0], ew4, eqkv, eot, ee, erate, eg,
        kept_cross, kept_dffn, g_self, d_dg0, d_ds0, d_db, d_dg, d_ds)
    ew, eu, ebg, ed, egg, esg, sw, cw, du, dbg, dd, dgg, dsg = run_finish(n_dp, hidden, width, *gathered)
    return (
        decoded.reshape(1, length, width), d_patches[None], d_tags[None],
        ew, eu, ebg.reshape(-1), ed, egg.T, esg.T, sw, cw, du, dbg.reshape(-1), dd, dgg.T, dsg.T,
    )


def solution(mesh):
    split = P(("dp", "bal"))
    in_specs = (split,) * 7 + (P(),) * 13
    out_specs = (split,) * 3 + (P("dp"),) * 13
    return jax.shard_map(per_device, mesh=mesh, in_specs=in_specs, out_specs=out_specs, check_vma=False)
```

```python
import functools

import jax
import jax.numpy as jnp
from jax import lax
from jax.experimental import pallas as pl
from jax.experimental.pallas import tpu as pltpu
from jax.sharding import PartitionSpec as P

HEADS = 8
HEAD = 64
EPSILON = 1e-05
NEGATIVE = -1e30
BF = jnp.bfloat16
F32 = jnp.float32
NN = (((1,), (0,)), ((), ()))
NT = (((1,), (1,)), ((), ()))
TN = (((0,), (0,)), ((), ()))
TT = (((0,), (1,)), ((), ()))
VM = pl.BlockSpec(memory_space=pltpu.VMEM)
SM = pl.BlockSpec(memory_space=pltpu.SMEM)
ANY = pl.BlockSpec(memory_space=pl.ANY)
LIMIT = 1e18
PARAMS = pltpu.CompilerParams(vmem_limit_bytes=60 << 20)
Shape = jax.ShapeDtypeStruct


def mm(left, right, dims=NN):
    return lax.dot_general(left, right, dims, preferred_element_type=F32)


def cut(rows):
    half = (rows // 2 + 15) // 16 * 16
    return [(0, half), (half, rows - half)]


class Copies:
    def __init__(self, sems):
        self.sems, self.used, self.open = sems, 0, []

    def start(self, source, target):
        copy = pltpu.make_async_copy(source, target, self.sems.at[self.used])
        self.used += 1
        copy.start()
        return copy

    def out(self, source, target):
        self.open.append(self.start(source, target))

    def finish(self):
        for copy in self.open:
            copy.wait()


def split_weights(raw, parts):
    def step(i, carry):
        rows = pl.ds(pl.multiple_of(i * 128, 128), 128)
        parts[:, rows, :] = pltpu.einshape("abc->bac", raw[rows])
        return carry

    lax.fori_loop(0, raw.shape[0] // 128, step, 0)


def normalise(signal):
    centre = jnp.mean(signal, axis=-1, keepdims=True)
    centered = signal - centre
    spread = jnp.mean(centered * centered, axis=-1, keepdims=True)
    rate = lax.rsqrt(spread + EPSILON)
    return centered * rate, rate


def norm_back(unit, rate, gain, gradient):
    inner = gradient * gain
    first = jnp.mean(inner, axis=-1, keepdims=True)
    second = jnp.mean(inner * unit, axis=-1, keepdims=True)
    return rate * (inner - first - unit * second)


def colsum(signal):
    return jnp.sum(signal, axis=0, keepdims=True)


def smooth(hidden):
    scale = 0.7978845608028654
    square = hidden * hidden
    curve = jnp.tanh(scale * hidden * (1.0 + 0.044715 * square))
    half = 0.5 + 0.5 * curve
    slope = half + 0.5 * hidden * (1.0 - curve * curve) * (scale + (3 * 0.044715 * scale) * square)
    return hidden * half, slope


def half_mask(shape, axis, which):
    index = lax.broadcasted_iota(jnp.int32, shape, axis)
    return (index < HEAD) if which == 0 else (index >= HEAD)


def keep_half(pair, axis, which):
    return jnp.where(half_mask(pair.shape, axis, which), pair, jnp.zeros_like(pair))


def project_qkv(x, sources, w4, q, qt, k, v, vt):
    rows = x.shape[0]
    for start, size in cut(rows):
        part = slice(start, start + size)
        q[part] = (mm(x[part], w4[0]) * HEAD ** (-0.5)).astype(BF)
    if q.shape[0] > rows:
        q[rows:] = jnp.zeros((q.shape[0] - rows, q.shape[1]), BF)
    for start, size in cut(sources.shape[0]):
        part = slice(start, start + size)
        k[part] = mm(sources[part], w4[1]).astype(BF)
        v[part] = mm(sources[part], w4[2]).astype(BF)
    qt[...] = q[...].T
    vt[...] = v[...].T


def shifted_exp(scores, exact, causal_rows):
    if causal_rows:
        size, width = scores.shape
        key = lax.broadcasted_iota(jnp.int32, (width, width), 0)
        query = lax.broadcasted_iota(jnp.int32, (width, width), 1)
        last = jnp.where(key <= query, scores[size - width :], NEGATIVE)
        scores = last if size == width else jnp.concatenate([scores[: size - width], last], axis=0)
        exact = exact or size == width
    sample = scores if exact else scores[:128]
    return jnp.exp(scores - jnp.max(sample, axis=0, keepdims=True))


def attend_heads(exact, causal, q_tile, qt, k, vt, ot, rate, store):
    keys, queries = k.shape[0], qt.shape[1]

    def pair(p, carry):
        lanes = pl.ds(pl.multiple_of(p * 128, 128), 128)
        for u in range(2):
            rows = pl.ds(pl.multiple_of(p * 128 + u * HEAD, HEAD), HEAD)
            place, done = store(p, u)
            for start in range(0, queries, q_tile):
                cols = slice(start, start + q_tile)
                depth = start + q_tile if causal else keys
                scores = mm(k[:depth, lanes], keep_half(qt[lanes, cols], 0, u))
                raised = shifted_exp(scores, exact, causal)
                total = jnp.sum(raised, axis=0, keepdims=True)
                low = raised.astype(BF)
                place[:depth, cols] = low
                inverse = 1.0 / total
                rate[2 * p + u, :, cols] = inverse
                ot[rows, cols] = (mm(vt[rows, :depth], low) * inverse).astype(BF)
            done()
        return carry

    lax.fori_loop(0, HEADS // 2, pair, 0)


def attend(causal, q_tile, qt, k, vt, ot, rate, store, drain):
    attend_heads(False, causal, q_tile, qt, k, vt, ot, rate, store)
    drain()
    fine = jnp.min(rate[...]) > 1.0 / LIMIT

    @pl.when(jnp.logical_not(fine))
    def _():
        attend_heads(True, causal, q_tile, qt, k, vt, ot, rate, store)
        drain()


def back_heads(causal, q_tile, q, kt, v, dot_, d_o, rowdot, fetch, ds, dqt, dk, dv, hook=None):
    keys, queries = v.shape[0], dqt.shape[1]

    def pair(p, carry):
        lanes = pl.ds(pl.multiple_of(p * 128, 128), 128)
        for u in range(2):
            rows = pl.ds(pl.multiple_of(p * 128 + u * HEAD, HEAD), HEAD)
            place = fetch(p, u)
            for start in range(0, queries, q_tile):
                cols = slice(start, start + q_tile)
                depth = start + q_tile if causal else keys
                grad = mm(v[:depth, lanes], keep_half(dot_[lanes, cols], 0, u))
                scaled = place[:depth, cols].astype(F32) * (grad - rowdot[2 * p + u, :, cols])
                low = scaled.astype(BF)
                ds[u][:depth, cols] = low
                dqt[rows, cols] = (mm(kt[rows, :depth], low) * HEAD ** (-0.5)).astype(BF)
            qm = q[:queries, lanes]
            dm = d_o[:queries, lanes]
            steps = range(0, keys, q_tile) if causal else (0,)
            for start in steps:
                key = slice(start, start + q_tile) if causal else slice(0, keys)
                more_k = mm(ds[u][key, start:queries], qm[start:])
                more_v = mm(place[key, start:queries], dm[start:])
                if u == 0:
                    dk[key, lanes] = more_k.astype(BF)
                    dv[key, lanes] = more_v.astype(BF)
                else:
                    dk[key, lanes] = jnp.where(half_mask(more_k.shape, 1, 1), more_k.astype(BF), dk[key, lanes])
                    dv[key, lanes] = jnp.where(half_mask(more_v.shape, 1, 1), more_v.astype(BF), dv[key, lanes])
            if hook is not None:
                for at, act in hook.items():
                    if at % 2 == u:
                        pl.when(p == at // 2)(act)
        return carry

    lax.fori_loop(0, HEADS // 2, pair, 0)


def back_outputs(grad_low, w4, ot, rate, dot_, d_o, rowdot):
    rows, wide = grad_low.shape[0], dot_.shape[1]
    raw = mm(w4[3], grad_low[...], NT)
    for h in range(HEADS):
        part = slice(h * HEAD, (h + 1) * HEAD)
        low = (raw[part] * rate[h][:, :rows]).astype(BF)
        if wide > rows:
            low = jnp.concatenate([low, jnp.zeros((HEAD, wide - rows), BF)], axis=1)
        dot_[part] = low
        rowdot[h] = jnp.sum(low.astype(F32) * ot[part].astype(F32), axis=0, keepdims=True)
    d_o[...] = dot_[...].T


def ring(buffers, hbm, sems, spans, out):
    def copies(h, slot):
        made = []
        for i, (rows, cols) in enumerate(spans):
            here = buffers.at[slot, pl.ds(0, rows), cols]
            there = hbm.at[h, pl.ds(0, rows), cols]
            made.append(
                pltpu.make_async_copy(here, there, sems.at[slot, i])
                if out
                else pltpu.make_async_copy(there, here, sems.at[slot, i])
            )
        return made

    return copies


def out_ring(buffers, hbm, sems, spans):
    copies = ring(buffers, hbm, sems, spans, True)

    def store(p, u):
        slot = (p % 2) * 2 + u

        @pl.when(p >= 2)
        def _():
            for copy in copies(2 * p + u, slot):
                copy.wait()

        def done():
            for copy in copies(2 * p + u, slot):
                copy.start()

        return buffers.at[slot], done

    def drain():
        for slot in range(4):
            for copy in copies(slot, slot):
                copy.wait()

    return store, drain


def in_ring(buffers, hbm, sems, spans):
    copies = ring(buffers, hbm, sems, spans, False)

    def begin():
        for h in range(4):
            for copy in copies(h, h):
                copy.start()

    def fetch(p, u):
        slot = (p % 2) * 2 + u
        for copy in copies(2 * p + u, slot):
            copy.wait()
        if u == 0:
            @pl.when((p >= 1) & (p < HEADS // 2 - 1))
            def _():
                other = (1 - p % 2) * 2
                for v in range(2):
                    for copy in copies(2 * p + 2 + v, other + v):
                        copy.start()
        return buffers.at[slot]

    return begin, fetch


MESH = pl.DeviceIdType.MESH


class Spot:
    def __init__(self, n, m):
        self.n, self.m = n, m
        self.d, self.b = lax.axis_index("dp"), lax.axis_index("bal")
        self.core, self.far = self.b % 2, self.b // 2
        self.parity, self.row = self.d % 2, self.d // 2
        self.by_core = (self.d, self.b + 1 - 2 * self.core)
        self.by_far = (self.d, self.b + 2 - 4 * self.far)
        self.by_parity = (self.d + 1 - 2 * self.parity, self.b)

    def greet(self):
        barrier = pltpu.get_barrier_semaphore()

        def call(device):
            pl.semaphore_signal(barrier, inc=1, device_id=device, device_id_type=MESH)

        for k in range(1, self.m):
            call((self.d, (self.b + k) % self.m))
        call(self.by_parity)

        def along(k, carry):
            call((((self.row + k) % (self.n // 2)) * 2 + self.parity, self.b))
            return carry

        lax.fori_loop(1, self.n // 2, along, 0)

    def await_all(self):
        pl.semaphore_wait(pltpu.get_barrier_semaphore(), self.m - 1 + 1 + self.n // 2 - 1)


def remote(source, target, sent, received, device):
    return pltpu.make_async_remote_copy(
        src_ref=source, dst_ref=target, send_sem=sent, recv_sem=received, device_id=device, device_id_type=MESH
    )


class Piece:
    def __init__(self, spot, along_x, sems, source=None, acc=None, land_a=None, kept=None, land_b=None, kept2=None,
                 land_c=None, slots=None, result=None, gathered=None):
        self.spot, self.along_x, self.source, self.sems = spot, along_x, source, sems
        self.acc, self.land_a, self.kept, self.land_b = acc, land_a, kept, land_b
        self.kept2, self.land_c = kept2, land_c
        self.slots, self.result, self.gathered = slots, result, gathered

    def a_copies(self):
        half = self.acc.shape[3]
        mine = pl.ds(pl.multiple_of(self.spot.core * half, half), half)
        other = pl.ds(pl.multiple_of((1 - self.spot.core) * half, half), half)
        return [
            pltpu.make_async_copy(self.source.at[:, :, :, mine], self.acc, self.sems.at[0]),
            remote(self.source.at[:, :, :, other], self.land_a, self.sems.at[1], self.sems.at[2], self.spot.by_core),
        ]

    def a_start(self):
        for copy in self.a_copies():
            copy.start()

    def a_wait(self):
        for copy in self.a_copies():
            copy.wait()

        def add(i, carry):
            self.acc[i] = self.acc[i] + self.land_a[i]
            return carry

        lax.fori_loop(0, self.acc.shape[0], add, 0)

    def lanes(self, mine, size):
        side = self.spot.far if mine else 1 - self.spot.far
        return pl.ds(pl.multiple_of(side * size, size), size)

    def b_copy(self):
        spot = self.spot
        if self.along_x:
            out, to = self.acc.at[:, :, :, self.lanes(False, self.land_b.shape[3])], spot.by_far
        else:
            out, to = self.acc.at[:, 1 - spot.parity], spot.by_parity
        return remote(out, self.land_b, self.sems.at[3], self.sems.at[4], to)

    def b_start(self):
        self.b_copy().start()

    def b_wait(self):
        self.b_copy().wait()

        def add(i, carry):
            if self.along_x:
                mine = self.acc[i, :, :, self.lanes(True, self.land_b.shape[3])]
            else:
                mine = self.acc[i, self.spot.parity]
            self.kept[i] = mine + self.land_b[i]
            return carry

        lax.fori_loop(0, self.kept.shape[0], add, 0)

    def bb_copy(self):
        spot = self.spot
        if self.along_x:
            out, to = self.kept.at[:, 1 - spot.parity], spot.by_parity
        else:
            out, to = self.kept.at[:, :, self.lanes(False, self.land_c.shape[2])], spot.by_far
        return remote(out, self.land_c, self.sems.at[5], self.sems.at[6], to)

    def bb_start(self):
        self.bb_copy().start()

    def bb_wait(self):
        self.bb_copy().wait()

        def add(i, carry):
            if self.along_x:
                mine = self.kept[i, self.spot.parity]
            else:
                mine = self.kept[i, :, self.lanes(True, self.land_c.shape[2])]
            self.kept2[i] = mine + self.land_c[i]
            return carry

        lax.fori_loop(0, self.kept2.shape[0], add, 0)

    def c_copy(self, k, arriving):
        spot, half = self.spot, self.spot.n // 2
        row = (spot.row + k) % half
        slot = row if arriving else spot.row
        return remote(self.kept2.at[row], self.slots.at[slot], self.sems.at[7 + k], self.sems.at[7 + half + slot],
                      (row * 2 + spot.parity, spot.b))

    def c_start(self):
        def step(k, carry):
            self.c_copy(k, False).start()
            return carry

        lax.fori_loop(1, self.spot.n // 2, step, 0)

    def c_wait(self):
        half, row = self.spot.n // 2, self.spot.row

        def step(k, total):
            self.c_copy(k, False).wait_send()
            self.c_copy(k, True).wait_recv()
            return total + self.slots[(row + k) % half].astype(F32)

        total = lax.fori_loop(1, half, step, self.kept2[row].astype(F32))
        self.result[...] = total.astype(BF)

    def d_copies(self, arriving):
        spot, base = self.spot, 7 + self.spot.n
        made = []
        for k in range(1, spot.m):
            peer = (spot.b + k) % spot.m
            slot = peer if arriving else spot.b
            made.append(remote(self.result, self.gathered.at[slot], self.sems.at[base + k],
                               self.sems.at[base + spot.m + slot], (spot.d, peer)))
        return made

    def d_start(self):
        for copy in self.d_copies(False):
            copy.start()
        self.gathered[self.spot.b] = self.result[...]

    def d_wait(self):
        for copy in self.d_copies(False):
            copy.wait_send()
        for copy in self.d_copies(True):
            copy.wait_recv()


def piece_sems(n, m):
    return pltpu.SemaphoreType.DMA((7 + n + 2 * m,))


def half_shape(n, rows):
    return (n // 2, 2, rows, 256)


def kept_shape(n, rows, along_x):
    return (n // 2, 2, rows, 128) if along_x else (n // 2, rows, 256)


def last_shape(n, rows):
    return (n // 2, rows, 128)


class VectorSum:
    def __init__(self, spot, v, lands, slots, result, sems):
        self.spot, self.v, self.lands, self.slots, self.result, self.sems = spot, v, lands, slots, result, sems

    def swap(self, step):
        device = (self.spot.by_core, self.spot.by_far, self.spot.by_parity)[step]
        return remote(self.v, self.lands.at[step], self.sems.at[2 * step], self.sems.at[2 * step + 1], device)

    def swap_start(self, step):
        self.swap(step).start()

    def swap_wait(self, step):
        self.swap(step).wait()
        self.v[...] = self.v[...] + self.lands[step]

    def copy(self, k, arriving):
        spot, half = self.spot, self.spot.n // 2
        row = (spot.row + k) % half
        slot = row if arriving else spot.row
        return remote(self.v.at[row * 2 + spot.parity], self.slots.at[slot], self.sems.at[6 + k],
                      self.sems.at[6 + half + slot], (row * 2 + spot.parity, spot.b))

    def c_start(self):
        def step(k, carry):
            self.copy(k, False).start()
            return carry

        lax.fori_loop(1, self.spot.n // 2, step, 0)

    def c_wait(self):
        half, row = self.spot.n // 2, self.spot.row

        def step(k, total):
            self.copy(k, False).wait_send()
            self.copy(k, True).wait_recv()
            return total + self.slots[(row + k) % half]

        self.result[...] = lax.fori_loop(1, half, step, self.v[self.spot.d])


def put(piece, row, value, lane=0):
    halves, two, width = piece.shape[0], piece.shape[1], value.shape[1]
    rows = value.shape[0] // (halves * two)
    piece[:, :, row : row + rows, lane : lane + width] = value.reshape(halves, two, rows, width).astype(BF)


def encoder_forward(x_h, w_h, up_h, bias, down_h, gains, shifts,
                    memory, w4_h, qkv_h, ot_h, e_h, rate, e1_h, e2_h, zb_h, act_h, slope_h,
                    x, raw, w4, up, down, q, k, v, qt, vt, ot, e1, e2, zb, act, slope, ering, sems, esems):
    c = Copies(sems)
    load_w = c.start(w_h, raw)
    load_x = c.start(x_h, x)
    load_up = c.start(up_h, up)
    load_down = c.start(down_h, down)
    load_w.wait()
    split_weights(raw, w4)
    c.out(w4, w4_h)
    load_x.wait()
    project_qkv(x, x, w4, q, qt, k, v, vt)
    n, wide = x.shape[0], qt.shape[1]
    for i, item in enumerate((q.at[pl.ds(0, n)], k, v)):
        c.out(item, qkv_h.at[i])
    store, drain = out_ring(ering, e_h, esems, [(n, slice(None))])
    attend(False, wide, qt, k, vt, ot, rate, store, drain)
    c.out(ot, ot_h)
    load_up.wait()
    load_down.wait()
    for start, size in cut(n):
        part = slice(start, start + size)
        first = x[part].astype(F32) + mm(ot[:, part], w4[3], TN)
        e1[part] = first
        unit, _ = normalise(first)
        z = unit * gains[0:1] + shifts[0:1]
        low = z.astype(BF)
        zb[part] = low
        active, bend = smooth(mm(low, up[...]) + bias[...])
        act[part] = active.astype(BF)
        slope[part] = bend.astype(BF)
        second = z + mm(act[part], down[...]) + shifts[2:3]
        e2[part] = second
        unit, _ = normalise(second)
        memory[part] = (unit * gains[1:2] + shifts[1:2]).astype(BF)
    for here, there in ((e1, e1_h), (e2, e2_h), (zb, zb_h), (act, act_h), (slope, slope_h)):
        c.out(here, there)
    c.finish()


def tags_forward(x_h, w_h, gains, shifts,
                 x1, w4_h, qkv_h, ot_h, e_h, rate, a1_h,
                 x, raw, w4, q, k, v, qt, vt, ot, a1, ering, sems, esems):
    c = Copies(sems)
    load_w = c.start(w_h, raw)
    load_x = c.start(x_h, x)
    load_w.wait()
    split_weights(raw, w4)
    c.out(w4, w4_h)
    load_x.wait()
    project_qkv(x, x, w4, q, qt, k, v, vt)
    n = x.shape[0]
    for i, item in enumerate((q, k, v)):
        c.out(item, qkv_h.at[i])
    tile = 256
    spans = [(start + tile, slice(start, start + tile)) for start in range(0, n, tile)]
    store, drain = out_ring(ering, e_h, esems, spans)
    attend(True, tile, qt, k, vt, ot, rate, store, drain)
    c.out(ot, ot_h)
    for start, size in cut(n):
        part = slice(start, start + size)
        first = x[part].astype(F32) + mm(ot[:, part], w4[3], TN)
        a1[part] = first
        unit, _ = normalise(first)
        x1[part] = (unit * gains[0:1] + shifts[0:1]).astype(BF)
    c.out(a1, a1_h)
    c.finish()


def decoder_middle(capacity, tag_length, cell_count, destination, slot_index, x1_h, mem_h, w_h, up_h, bias, down_h, gains,
                   shifts, cot_h,
                   y, da_h, gb_h, w4_h, q_h, k_h, v_h, ot_h, e_h, rate, g_ffn, d_bias, d_gains, d_shifts,
                   x1, mem, raw, w4, up, down, q, k, v, qt, vt, ot, ering,
                   unit2, rate2, xb2, act, slope, da, gb, sems, esems):
    cot, dh = y, slope
    c = Copies(sems)
    load_w = c.start(w_h, raw)
    load_mem = c.start(mem_h, mem)
    load_x = c.start(x1_h, x1)
    load_up = c.start(up_h, up)
    load_down = c.start(down_h, down)
    load_cot = c.start(cot_h, cot)
    load_w.wait()
    split_weights(raw, w4)
    load_mem.wait()
    load_x.wait()
    project_qkv(x1, mem, w4, q, qt, k, v, vt)
    for here, there in ((w4, w4_h), (q, q_h), (k, k_h), (v, v_h)):
        c.out(here, there)
    n, blocks = x1.shape[0], y.shape[0]
    block = n // blocks

    store, drain = out_ring(ering, e_h, esems, [(mem.shape[0], slice(None))])
    attend(False, n, qt, k, vt, ot, rate, store, drain)
    c.out(ot, ot_h)
    load_up.wait()
    load_down.wait()
    load_cot.wait()
    live = tag_length[0] + cell_count[0]
    places = [destination[0, b] * capacity + slot_index[0, b] for b in range(blocks)]
    zero = jnp.zeros((1, x1.shape[1]), F32)
    gain3, shift3 = zero, zero
    for start, size in cut(n):
        part = slice(start, start + size)
        second = x1[part].astype(F32) + mm(ot[:, part], w4[3], TN)
        unit, pace = normalise(second)
        unit2[part] = unit
        rate2[part] = pace
        x2 = unit * gains[1:2] + shifts[1:2]
        low = x2.astype(BF)
        xb2[part] = low
        active, bend = smooth(mm(low, up[...]) + bias[...])
        act[part] = active.astype(BF)
        slope[part] = bend.astype(BF)
        third = x2 + mm(act[part], down[...]) + shifts[3:4]
        unit, pace = normalise(third)
        row = lax.broadcasted_iota(jnp.int32, (size, 1), 0) + start
        alive = (row < live).astype(F32)
        final = ((unit * gains[2:3] + shifts[2:3]) * alive).astype(BF)
        picked = []
        for b in range(start // block, (start + size) // block):
            picked.append(cot[places[b]])
            y[places[b]] = final[b * block - start : (b + 1) * block - start]
        dy = jnp.concatenate(picked, axis=0).astype(F32) * alive
        gain3 += colsum(dy * unit)
        shift3 += colsum(dy)
        d3 = norm_back(unit, pace, gains[2:3], dy)
        da[part] = d3
        gb[part] = d3.astype(BF)
    d_gains[2:3] = gain3
    d_shifts[2:3] = shift3
    ffn_back(xb2, up, down, act, slope, gb, dh, g_ffn, d_bias, d_shifts, 3)
    gain2, shift2 = zero, zero
    for start, size in cut(n):
        part = slice(start, start + size)
        dx2 = da[part] + mm(dh[part], up[...], NT)
        gain2 += colsum(dx2 * unit2[part])
        shift2 += colsum(dx2)
        d2 = norm_back(unit2[part], rate2[part], gains[1:2], dx2)
        da[part] = d2
        gb[part] = d2.astype(BF)
    d_gains[1:2] = gain2
    d_shifts[1:2] = shift2
    c.out(gb, gb_h)
    c.out(da, da_h)
    c.finish()


def ffn_back(xb, up, down, act, slope, gb, dh, g_ffn, d_bias, d_shifts, row, middle=None):
    n, width = xb.shape
    offset = jnp.zeros((1, up.shape[1]), F32)
    for start, size in cut(n):
        part = slice(start, start + size)
        low = (mm(gb[part], down[...], NT) * slope[part].astype(F32)).astype(BF)
        dh[part] = low
        offset += colsum(low.astype(F32))
    d_bias[...] = offset
    d_shifts[row : row + 1] = colsum(gb[...].astype(F32))
    if middle is not None:
        middle()
    rows = g_ffn.shape[2] // 4
    put(g_ffn, 2 * rows, mm(act[...], gb[...], TN))
    for j in range(up.shape[1] // width):
        put(g_ffn, j * rows, mm(xb[...], dh[:, j * width : (j + 1) * width], TN))


class Room:
    def __init__(self, acc, land, kept, next_, kept_x, next_x, kept2, last, slots, result):
        self.acc, self.land, self.kept, self.next = acc, land, kept, next_
        self.kept_x, self.next_x, self.kept2, self.last, self.slots, self.result = kept_x, next_x, kept2, last, slots, result

    def whole(self, spot, sems, source, gathered):
        return Piece(spot, False, sems, source, self.acc, self.land, self.kept, self.next, self.kept2, self.last,
                     self.slots, self.result, gathered)

    def half(self, spot, sems, source, gathered, along_x):
        size = self.acc.shape[2] // 2
        rows = pl.ds(0 if along_x else size, size)
        kept = self.kept_x if along_x else self.kept.at[:, rows]
        next_ = self.next_x if along_x else self.next.at[:, rows]
        return Piece(spot, along_x, sems, source, self.acc.at[:, :, rows], self.land.at[:, :, rows], kept, next_,
                     self.kept2.at[:, rows], self.last.at[:, rows], self.slots.at[:, rows], self.result.at[rows], gathered)


def room_scratch(n, rows):
    vb = lambda shape: pltpu.VMEM(shape, BF)
    last, side = vb(last_shape(n, rows)), vb(kept_shape(n, rows // 2, True))
    kept = vb(kept_shape(n, rows, False))
    return [vb(half_shape(n, rows)), vb(half_shape(n, rows)), kept, kept, side, side, last, last, last, vb((rows, 128))]


def backward(n_dp, n_bal,
             da_h, gb_h, x1_h, mem_h, cw4_h, cq_h, ck_h, cv_h, cot_h, ce_h, y_h, g_dffn,
             e2_h, e1_h, zb_h, act_h, slope_h, up_h, down_h, ex_h, ew4_h, eqkv_h, eot_h, ee_h,
             a1_h, tx_h, tw4_h, tqkv_h, tot_h, te_h,
             crate, erate, trate, egains, dgains, d_bias_d, d_gains_d, d_shifts_d,
             dx_enc_h, dx_tags_h, decoded, all_cross, all_dffn, all_effn, all_enc0, all_enc1, all_self0, all_self1, v_total,
             ering, q, k, v, ot, kt, dot_, d_o, rowdot, dqt, dk, dv, ds, gb, da, wide0, wide1, dx1, x0, x1, up, down, zb,
             wa, wb, g0, g1, d_bias, d_gains, d_shifts, vec, vec_lands, vec_slots, *rest):
    room0, room1 = Room(*rest[:10]), Room(*rest[10:20])
    sems, esems, moves, vsems = rest[20:24]
    psems = rest[24:]
    spot = Spot(n_dp, n_bal)
    spot.greet()
    c = Copies(sems)
    n, width = x0.shape
    m = x1.shape[0]
    wide = eot_h.shape[1]
    hidden = up.shape[1]
    size = g0.shape[2] // 2
    rows = size // 2
    half = width // 2
    low, high = pl.ds(0, size), pl.ds(size, size)
    self_pieces = g1.at[:, :, low], g1.at[:, :, high]
    dffn = room0.whole(spot, psems[0], g_dffn, all_dffn)
    cross = room1.whole(spot, psems[1], g0, all_cross)
    effn = room0.whole(spot, psems[2], g1, all_effn)
    enc0 = room1.half(spot, psems[3], g0.at[:, :, low], all_enc0, True)
    enc1 = room1.half(spot, psems[4], g0.at[:, :, high], all_enc1, False)
    self0 = room0.half(spot, psems[5], self_pieces[0], all_self0, False)
    self1 = room0.half(spot, psems[6], self_pieces[1], all_self1, True)
    vector = VectorSum(spot, vec, vec_lands, vec_slots, v_total, vsems)
    zero = jnp.zeros((1, width), F32)
    pair_ds = ds.at[0], ds.at[1]

    load_gb = c.start(gb_h, gb)
    load_ot = c.start(cot_h, ot)
    load_w = c.start(cw4_h, wa)
    loads = [c.start(a, b) for a, b in ((ck_h, k.at[pl.ds(0, m)]), (cv_h, v.at[pl.ds(0, m)]), (cq_h, q))]
    begin, fetch = in_ring(ering, ce_h, esems.at[0], [(m, slice(0, n))])
    begin()
    last = [c.start(a, b) for a, b in ((x1_h, x0), (mem_h, x1), (da_h, da))]
    load_ew = c.start(ew4_h, wb)
    load_up = [c.start(a, b) for a, b in ((e2_h, wide0.at[pl.ds(0, m)]), (down_h, down), (zb_h, zb), (up_h, up))]
    load_gb.wait()
    load_ot.wait()
    put(g0, 3 * rows, mm(ot[...], gb[...]))
    load_w.wait()
    back_outputs(gb, wa, ot, crate, dot_, d_o, rowdot)
    for load in loads:
        load.wait()
    kt[:, :m] = k[:m].T
    spot.await_all()
    dffn.a_start()
    share = y_h.shape[0] // n_bal

    def moved(step, arriving):
        peer = (spot.b + step) % n_bal
        slot = peer if arriving else spot.b
        return remote(y_h.at[pl.ds(peer * share, share)], decoded.at[pl.ds(slot * share, share)], moves.at[step],
                      moves.at[n_bal + slot], (spot.d, peer))

    own = pl.ds(spot.b * share, share)
    own_copy = pltpu.make_async_copy(y_h.at[own], decoded.at[own], moves.at[0])
    own_copy.start()
    for step in range(1, n_bal):
        moved(step, False).start()

    def cross1():
        dffn.a_wait()
        dffn.b_start()

    def cross7():
        dffn.b_wait()
        dffn.bb_start()

    keys = pl.ds(0, m)
    back_heads(False, n, q, kt, v.at[keys], dot_, d_o, rowdot, fetch, pair_ds, dqt, dk.at[keys], dv.at[keys],
               {1: cross1, 7: cross7})
    for load in last:
        load.wait()
    put(g0, 0, mm(x0[...], dqt[...], TT))
    put(g0, rows, mm(x1[...], dk[:m], TN))
    put(g0, 2 * rows, mm(x1[...], dv[:m], TN))
    cross.a_start()
    for start, count in cut(m):
        part = slice(start, start + count)
        wide1[part] = mm(dk[part], wa[1], NT) + mm(dv[part], wa[2], NT)
    for start, count in cut(n):
        part = slice(start, start + count)
        dx1[part] = (da[part] + mm(dqt[:, part], wa[0], TT)).astype(BF)
    cross.a_wait()
    cross.b_start()

    act, slope = ds.at[0, keys, pl.ds(0, hidden)], ds.at[1, keys, pl.ds(0, hidden)]
    load_ffn = [c.start(a, b) for a, b in ((slope_h, slope), (act_h, act))]
    queries = pl.ds(0, wide)
    eot, eq = ot.at[:, queries], q.at[queries]
    load_ot = c.start(eot_h, eot)
    loads = [c.start(eqkv_h.at[i], item.at[keys]) for i, item in enumerate((q, k, v))]
    load_x = c.start(ex_h, x1)
    load_tw = c.start(tw4_h, wa)
    load_tx = c.start(tx_h, x0)
    begin, fetch = in_ring(ering, ee_h, esems.at[1], [(m, slice(0, wide))])
    begin()
    q[m:wide] = jnp.zeros((wide - m, width), BF)
    for load in load_up:
        load.wait()
    gain, shift = zero, zero
    for start, count in cut(m):
        part = slice(start, start + count)
        unit, pace = normalise(wide0[part])
        grad = wide1[part]
        gain += colsum(grad * unit)
        shift += colsum(grad)
        d2 = norm_back(unit, pace, egains[1:2], grad)
        da[part] = d2
        gb[part] = d2.astype(BF)
    d_gains[1:2] = gain
    d_shifts[1:2] = shift
    load_e1 = c.start(e1_h, wide1)
    load_a1 = c.start(a1_h, wide0)
    dffn.bb_wait()
    dffn.c_start()
    for load in load_ffn:
        load.wait()
    ffn_back(zb, up, down, act, slope, gb.at[keys], slope, g1, d_bias, d_shifts, 2)
    effn.a_start()
    dffn.c_wait()
    dffn.d_start()
    load_e1.wait()
    gain, shift = zero, zero
    for start, count in cut(m):
        part = slice(start, start + count)
        unit, pace = normalise(wide1[part])
        dz = da[part] + mm(slope[part], up[...], NT)
        gain += colsum(dz * unit)
        shift += colsum(dz)
        d1 = norm_back(unit, pace, egains[0:1], dz)
        da[part] = d1
        gb[part] = d1.astype(BF)
    d_gains[0:1] = gain
    d_shifts[0:1] = shift
    effn.a_wait()

    def enc0_():
        cross.b_wait()
        cross.bb_start()
        effn.b_start()

    def enc4():
        cross.bb_wait()
        cross.c_start()

    def enc6():
        effn.b_wait()
        effn.bb_start()

    for load in (load_ew, load_ot, *loads, load_x):
        load.wait()
    kt[:, :m] = k[:m].T
    put(g0, 3 * rows, mm(ot[:, :m], gb[:m]))
    edot, edo, edqt = dot_.at[:, queries], d_o.at[queries], dqt.at[:, queries]
    erowdot = rowdot.at[:, :, queries]
    back_outputs(gb.at[keys], wb, eot, erate, edot, edo, erowdot)
    back_heads(False, wide, eq, kt, v.at[keys], edot, edo, erowdot, fetch, pair_ds, edqt, dk.at[keys], dv.at[keys],
               {0: enc0_, 4: enc4, 6: enc6})
    put(g0, 0, mm(x1[...], dqt[:, :m], TT))
    put(g0, rows, mm(x1[...], dk[:m], TN))
    put(g0, 2 * rows, mm(x1[...], dv[:m], TN))
    cross.c_wait()
    cross.d_start()
    enc0.a_start()
    enc1.a_start()
    for start, count in cut(m):
        part = slice(start, start + count)
        wide1[part] = da[part] + mm(dqt[:, part], wb[0], TT) + mm(dk[part], wb[1], NT) + mm(dv[part], wb[2], NT)
    c.out(wide1, dx_enc_h)
    enc0.a_wait()
    enc0.b_start()
    enc1.a_wait()
    enc1.b_start()

    load_ot = c.start(tot_h, ot)
    loads = [c.start(tqkv_h.at[i], item) for i, item in enumerate((q, k, v))]
    tile = 256
    spans = [(start + tile, slice(start, start + tile)) for start in range(0, n, tile)]
    begin, fetch = in_ring(ering, te_h, esems.at[2], spans)
    begin()
    load_a1.wait()
    gain, shift = zero, zero
    for start, count in cut(n):
        part = slice(start, start + count)
        unit, pace = normalise(wide0[part])
        grad = dx1[part].astype(F32)
        gain += colsum(grad * unit)
        shift += colsum(grad)
        d1 = norm_back(unit, pace, dgains[0:1], grad)
        da[part] = d1
        gb[part] = d1.astype(BF)
    part_lanes = width // n_dp
    vec[...] = jnp.zeros_like(vec)
    for i in range(n_dp):
        lanes = slice(i * part_lanes, (i + 1) * part_lanes)
        for j in range(2):
            wide_lanes = slice((2 * i + j) * part_lanes, (2 * i + j + 1) * part_lanes)
            vec[i, j : j + 1, :part_lanes] = d_bias[:, wide_lanes]
            vec[i, 2 + j : 3 + j, :part_lanes] = d_bias_d[:, wide_lanes]
        vec[i, 4:6, :part_lanes] = d_gains[:, lanes]
        vec[i, 6:9, :part_lanes] = d_shifts[:, lanes]
        vec[i, 9:10, :part_lanes] = gain[:, lanes]
        vec[i, 10:12, :part_lanes] = d_gains_d[1:3, lanes]
        vec[i, 12:13, :part_lanes] = shift[:, lanes]
        vec[i, 13:16, :part_lanes] = d_shifts_d[1:4, lanes]
    vector.swap_start(0)
    effn.bb_wait()
    effn.c_start()

    def put_side(piece, at):
        put(piece, 0, mm(x0[...], dqt[at : at + half], TT))
        put(piece, 0, mm(x0[...], dk[:, at : at + half], TN), half)
        put(piece, rows, mm(x0[...], dv[:, at : at + half], TN))

    def tags0():
        vector.swap_wait(0)
        vector.swap_start(1)
        dffn.d_wait()
        effn.c_wait()
        effn.d_start()

    def tags1():
        enc0.b_wait()
        enc1.b_wait()
        enc0.bb_start()
        enc1.bb_start()
        vector.swap_wait(1)
        vector.swap_start(2)

    def tags3():
        put_side(self_pieces[0], 0)
        self0.a_start()
        enc0.bb_wait()
        enc0.c_start()
        vector.swap_wait(2)
        vector.c_start()

    def tags4():
        self0.a_wait()
        self0.b_start()
        enc1.bb_wait()
        enc1.c_start()

    def tags6():
        cross.d_wait()
        enc0.c_wait()
        enc0.d_start()

    def tags7():
        enc1.c_wait()
        enc1.d_start()
        self0.b_wait()
        self0.bb_start()

    for load in (load_ot, load_tw, load_tx, *loads):
        load.wait()
    kt[...] = k[...].T
    out = mm(ot[...], gb[...])
    put(self_pieces[0], rows, out[:, :half], half)
    put(self_pieces[1], rows, out[:, half:], half)
    back_outputs(gb, wa, ot, trate, dot_, d_o, rowdot)
    back_heads(True, tile, q, kt, v, dot_, d_o, rowdot, fetch, pair_ds, dqt, dk, dv,
               {0: tags0, 1: tags1, 3: tags3, 4: tags4, 6: tags6, 7: tags7})
    put_side(self_pieces[1], half)
    self1.a_start()
    for i, (start, count) in enumerate(cut(n)):
        part = slice(start, start + count)
        wide0[part] = (da[part] + mm(dqt[:, part], wa[0], TT) + mm(dk[part], wa[1], NT) + mm(dv[part], wa[2], NT))
        if i == 0:
            self1.a_wait()
            self1.b_start()
            self0.bb_wait()
            self0.c_start()
    c.out(wide0, dx_tags_h)
    effn.d_wait()
    self0.c_wait()
    self0.d_start()
    vector.c_wait()
    self1.b_wait()
    self1.bb_start()
    for piece in (enc0, enc1, self0):
        piece.d_wait()
    own_copy.wait()
    for step in range(1, n_bal):
        moved(step, False).wait_send()
        moved(step, True).wait_recv()
    self1.bb_wait()
    self1.c_start()
    self1.c_wait()
    self1.d_start()
    c.finish()
    self1.d_wait()


def finish(all_cross, all_dffn, all_effn, all_enc0, all_enc1, all_self0, all_self1, v_total, decoded_h, patches_h, tags_h,
           o_enc, o_eup, o_ebias, o_edown, o_egains, o_eshifts,
           o_self, o_cross, o_dup, o_dbias, o_ddown, o_dgains, o_dshifts, o_decoded, o_patches, o_tags, tags, patches, decoded, sems):
    c = Copies(sems)
    moves = [(c.start(source, here), here, target) for source, here, target in
             ((tags_h, tags, o_tags), (patches_h, patches, o_patches), (decoded_h, decoded, o_decoded))]
    for load, here, target in moves:
        load.wait()
        c.out(here, target)

    def joined(gathered):
        return jnp.concatenate([gathered[b].astype(F32) for b in (0, 2, 1, 3)], axis=1)

    def layer(out, parts):
        rows = out.shape[0]
        for j in range(4):
            out[:, j, :] = parts[j * rows : (j + 1) * rows]

    def branch(up, down, parts):
        rows, width = up.shape[0], parts.shape[1]
        for j in range(up.shape[1] // width):
            up[:, j * width : (j + 1) * width] = parts[j * rows : (j + 1) * rows]
        down[...] = parts[2 * rows :]

    layer(o_enc, jnp.concatenate([joined(all_enc0), joined(all_enc1)], axis=0))
    layer(o_cross, joined(all_cross))
    branch(o_eup, o_edown, joined(all_effn))
    branch(o_dup, o_ddown, joined(all_dffn))
    rows, _, width = o_self.shape
    half = width // 2
    for i, gathered in enumerate((all_self0, all_self1)):
        parts = joined(gathered)
        lanes = slice(i * half, (i + 1) * half)
        o_self[:, 0, lanes] = parts[:rows, :half]
        o_self[:, 1, lanes] = parts[:rows, half:]
        o_self[:, 2, lanes] = parts[rows:, :half]
        o_self[:, 3, lanes] = parts[rows:, half:]
    share = o_egains.shape[1]
    for j in range(2):
        o_ebias[:, j * share : (j + 1) * share] = v_total[j : j + 1, :share]
        o_dbias[:, j * share : (j + 1) * share] = v_total[2 + j : 3 + j, :share]
    o_egains[...] = v_total[4:6, :share]
    o_eshifts[...] = v_total[6:9, :share]
    o_dgains[...] = v_total[9:12, :share]
    o_dshifts[...] = v_total[12:16, :share]
    c.finish()


def call(kernel, ins, outs, out_specs, scratch, name, params=PARAMS):
    specs = [spec for spec, _ in ins]
    return pl.pallas_call(
        kernel,
        out_shape=outs,
        in_specs=specs,
        out_specs=out_specs,
        scratch_shapes=scratch,
        compiler_params=params,
        name=name,
    )(*[value for _, value in ins])


def run_encoder_forward(x, w, up, bias, down, gains, shifts):
    n, width = x.shape
    hidden = up.shape[1]
    wide = (n + 127) // 128 * 128
    bf = lambda *s: Shape(s, BF)
    f32 = lambda *s: Shape(s, F32)
    vb = lambda *s: pltpu.VMEM(s, BF)
    vf = lambda *s: pltpu.VMEM(s, F32)
    outs = [bf(n, width), bf(4, width, width), bf(3, n, width), bf(width, wide), bf(HEADS, n, wide), f32(HEADS, 1, wide),
            f32(n, width), f32(n, width), bf(n, width), bf(n, hidden), bf(n, hidden)]
    return call(
        encoder_forward,
        [(ANY, x), (ANY, w), (ANY, up), (VM, bias), (ANY, down), (VM, gains), (VM, shifts)],
        outs,
        [VM, ANY, ANY, ANY, ANY, VM, ANY, ANY, ANY, ANY, ANY],
        [vb(n, width), vb(width, 4, width), vb(4, width, width), vb(width, hidden), vb(hidden, width),
         vb(wide, width), vb(n, width), vb(n, width), vb(width, wide), vb(width, n), vb(width, wide),
         vf(n, width), vf(n, width), vb(n, width), vb(n, hidden), vb(n, hidden), vb(4, n, wide),
         pltpu.SemaphoreType.DMA((20,)), pltpu.SemaphoreType.DMA((4, 1))],
        "encoder_forward",
    )


def run_tags_forward(x, w, gains, shifts):
    n, width = x.shape
    bf = lambda *s: Shape(s, BF)
    f32 = lambda *s: Shape(s, F32)
    vb = lambda *s: pltpu.VMEM(s, BF)
    vf = lambda *s: pltpu.VMEM(s, F32)
    return call(
        tags_forward,
        [(ANY, x), (ANY, w), (VM, gains), (VM, shifts)],
        [bf(n, width), bf(4, width, width), bf(3, n, width), bf(width, n), bf(HEADS, n, n), f32(HEADS, 1, n), f32(n, width)],
        [VM, ANY, ANY, ANY, ANY, VM, ANY],
        [vb(n, width), vb(width, 4, width), vb(4, width, width), vb(n, width), vb(n, width), vb(n, width),
         vb(width, n), vb(width, n), vb(width, n), vf(n, width), vb(4, n, n),
         pltpu.SemaphoreType.DMA((20,)), pltpu.SemaphoreType.DMA((4, n // 256))],
        "tags_forward",
    )


def run_decoder_middle(n_dp, n_bal, scalars, x1, mem, w, up, bias, down, gains, shifts, cot):
    n, width = x1.shape
    m = mem.shape[0]
    hidden = up.shape[1]
    piece = (n_dp // 2, 2, 4 * width // n_dp, width)
    bf = lambda *s: Shape(s, BF)
    f32 = lambda *s: Shape(s, F32)
    vb = lambda *s: pltpu.VMEM(s, BF)
    vf = lambda *s: pltpu.VMEM(s, F32)
    return call(
        functools.partial(decoder_middle, cot.shape[0] // n_bal),
        [(SM, v) for v in scalars]
        + [(ANY, x1), (ANY, mem), (ANY, w), (ANY, up), (VM, bias), (ANY, down), (VM, gains), (VM, shifts), (ANY, cot)],
        [bf(*cot.shape), f32(n, width), bf(n, width), bf(4, width, width), bf(n, width), bf(m, width), bf(m, width), bf(width, n),
         bf(HEADS, m, n), f32(HEADS, 1, n), bf(*piece), f32(1, hidden), f32(3, width), f32(4, width)],
        [VM] + [ANY] * 8 + [VM] * 5,
        [vb(n, width), vb(m, width), vb(width, 4, width), vb(4, width, width), vb(width, hidden), vb(hidden, width),
         vb(n, width), vb(m, width), vb(m, width), vb(width, n), vb(width, m), vb(width, n), vb(4, m, n),
         vf(n, width), vf(n, 1), vb(n, width), vb(n, hidden), vb(n, hidden), vf(n, width), vb(n, width),
         pltpu.SemaphoreType.DMA((20,)), pltpu.SemaphoreType.DMA((4, 1))],
        "decoder_middle",
    )


def run_backward(n_dp, n_bal, inputs, vectors, shapes):
    n, m, width, hidden, wide, blocks = shapes
    rows = 4 * width // n_dp
    bf = lambda *s: Shape(s, BF)
    f32 = lambda *s: Shape(s, F32)
    vb = lambda *s: pltpu.VMEM(s, BF)
    vf = lambda *s: pltpu.VMEM(s, F32)
    whole, part = bf(n_bal, rows, 128), bf(n_bal, rows // 2, 128)
    line, turned = vb(n, width), vb(width, n)
    piece = vb(n_dp // 2, 2, rows, width)
    return call(
        functools.partial(backward, n_dp, n_bal),
        [(ANY, item) for item in inputs] + [(VM, item) for item in vectors],
        [f32(m, width), f32(n, width), bf(*blocks), whole, whole, whole, part, part, part, part, f32(16, 128)],
        [ANY, ANY] + [VM] * 9,
        [vb(4, n, n), line, line, line, turned, turned, turned, line, vf(HEADS, 1, n), turned, line, line,
         vb(2, n, max(n, hidden)), line, vf(n, width), vf(n, width), vf(m, width), line, line, vb(m, width),
         vb(width, hidden), vb(hidden, width), vb(m, width), vb(4, width, width), vb(4, width, width), piece, piece,
         vf(1, hidden), vf(2, width), vf(3, width), vf(n_dp, 16, 128), vf(3, n_dp, 16, 128), vf(n_dp // 2, 16, 128),
         *room_scratch(n_dp, rows), *room_scratch(n_dp, rows),
         pltpu.SemaphoreType.DMA((40,)), pltpu.SemaphoreType.DMA((3, 4, n // 256)), pltpu.SemaphoreType.DMA((2 * n_bal,)),
         pltpu.SemaphoreType.DMA((6 + n_dp,)), *[piece_sems(n_dp, n_bal)] * 7],
        "backward",
        pltpu.CompilerParams(vmem_limit_bytes=60 << 20, collective_id=1, has_side_effects=True),
    )


def run_finish(n_dp, hidden, width, gathered, moved):
    share = width // n_dp
    f32 = lambda *s: Shape(s, F32)
    side = [f32(share, 4, width)]
    branch = [f32(share, hidden), f32(1, hidden // n_dp), f32(hidden // n_dp, width)]
    outs = side + branch + [f32(2, share), f32(3, share)] + side + side + branch + [f32(3, share), f32(4, share)]
    return call(finish, [(VM, v) for v in gathered] + [(ANY, v) for v in moved],
                outs + [Shape(v.shape, v.dtype) for v in moved], [VM] * len(outs) + [ANY] * 3,
                [pltpu.VMEM(v.shape, v.dtype) for v in moved[::-1]] + [pltpu.SemaphoreType.DMA((6,))], "finish")


def swap_blocks(blocks):
    n = lax.axis_size("bal")
    me = lax.axis_index("bal")
    parts = blocks.reshape(n, blocks.shape[0] // n, *blocks.shape[1:])
    out = jnp.zeros_like(parts)
    out = lax.dynamic_update_index_in_dim(out, lax.dynamic_index_in_dim(parts, me, 0, False), me, 0)
    for k in range(1, n):
        got = lax.ppermute(lax.dynamic_index_in_dim(parts, (me + k) % n, 0, False), "bal", [(i, (i + k) % n) for i in range(n)])
        out = lax.dynamic_update_index_in_dim(out, got, (me - k) % n, 0)
    return out.reshape(blocks.shape)


def per_device(
    patches, tag_rows, cotangent, tag_length, cell_count, destination, slot_index,
    encoder_attention, encoder_up, encoder_up_bias, encoder_down, encoder_gains, encoder_shifts,
    decoder_self, decoder_cross, decoder_up, decoder_up_bias, decoder_down, decoder_gains, decoder_shifts,
):
    n_bal, n_dp = lax.axis_size("bal"), lax.axis_size("dp")
    length, width = tag_rows.shape[1:]
    hidden = encoder_up.shape[1]
    blocks = destination.shape[1]
    span = length // blocks
    cot = lax.all_to_all(cotangent[0].reshape(n_bal, length // n_bal, width), "bal", 0, 0, tiled=True)
    cot = cot.reshape(blocks, span, width)
    eg, es, dg, ds = encoder_gains.T, encoder_shifts.T, decoder_gains.T, decoder_shifts.T
    eb, db = encoder_up_bias[None], decoder_up_bias[None]
    memory, ew4, eqkv, eot, ee, erate, e1, e2, zb, act, slope = run_encoder_forward(
        patches[0], encoder_attention, encoder_up, eb, encoder_down, eg, es)
    x1, sw4, sqkv, sot, se, srate, a1 = run_tags_forward(tag_rows[0], decoder_self, dg, ds)
    y, da2, gb2, cw4, cq, ck, cv, c_ot, ce, crate, g_dffn, d_db, d_dg, d_ds = run_decoder_middle(
        n_dp, n_bal, (tag_length, cell_count, destination, slot_index), x1, memory, decoder_cross, decoder_up, db,
        decoder_down, dg, ds, cot)
    d_patches, d_tags, decoded, all_cross, all_dffn, *gathered = run_backward(
        n_dp, n_bal,
        (da2, gb2, x1, memory, cw4, cq, ck, cv, c_ot, ce, y, g_dffn,
         e2, e1, zb, act, slope, encoder_up, encoder_down, patches[0], ew4, eqkv, eot, ee,
         a1, tag_rows[0], sw4, sqkv, sot, se),
        (crate, erate, srate, eg, dg, d_db, d_dg, d_ds),
        (length, patches.shape[1], width, hidden, eot.shape[1], y.shape))
    ew, eu, ebg, ed, egg, esg, sw, cw, du, dbg, dd, dgg, dsg, decoded, d_patches, d_tags = run_finish(
        n_dp, hidden, width, (all_cross, all_dffn, *gathered), (decoded, d_patches, d_tags))
    return (
        decoded.reshape(1, length, width), d_patches[None], d_tags[None],
        ew, eu, ebg.reshape(-1), ed, egg.T, esg.T, sw, cw, du, dbg.reshape(-1), dd, dgg.T, dsg.T,
    )


def solution(mesh):
    split = P(("dp", "bal"))
    in_specs = (split,) * 7 + (P(),) * 13
    out_specs = (split,) * 3 + (P("dp"),) * 13
    return jax.shard_map(per_device, mesh=mesh, in_specs=in_specs, out_specs=out_specs, check_vma=False)
```

```python
import functools

import jax
import jax.numpy as jnp
from jax import lax
from jax.experimental import pallas as pl
from jax.experimental.pallas import tpu as pltpu
from jax.sharding import PartitionSpec as P

HEADS = 8
HEAD = 64
EPSILON = 1e-05
NEGATIVE = -1e30
BF = jnp.bfloat16
F32 = jnp.float32
NN = (((1,), (0,)), ((), ()))
NT = (((1,), (1,)), ((), ()))
TN = (((0,), (0,)), ((), ()))
TT = (((0,), (1,)), ((), ()))
VM = pl.BlockSpec(memory_space=pltpu.VMEM)
SM = pl.BlockSpec(memory_space=pltpu.SMEM)
ANY = pl.BlockSpec(memory_space=pl.ANY)
LIMIT = 1e18
PARAMS = pltpu.CompilerParams(vmem_limit_bytes=60 << 20)
Shape = jax.ShapeDtypeStruct


def mm(left, right, dims=NN):
    return lax.dot_general(left, right, dims, preferred_element_type=F32)


def cut(rows):
    half = (rows // 2 + 15) // 16 * 16
    return [(0, half), (half, rows - half)]


class Copies:
    def __init__(self, sems):
        self.sems, self.used, self.open = sems, 0, []

    def start(self, source, target):
        copy = pltpu.make_async_copy(source, target, self.sems.at[self.used])
        self.used += 1
        copy.start()
        return copy

    def out(self, source, target):
        self.open.append(self.start(source, target))

    def finish(self):
        for copy in self.open:
            copy.wait()


def split_weights(raw, parts):
    def step(i, carry):
        rows = pl.ds(pl.multiple_of(i * 128, 128), 128)
        parts[:, rows, :] = pltpu.einshape("abc->bac", raw[rows])
        return carry

    lax.fori_loop(0, raw.shape[0] // 128, step, 0)


def normalise(signal):
    centre = jnp.mean(signal, axis=-1, keepdims=True)
    centered = signal - centre
    spread = jnp.mean(centered * centered, axis=-1, keepdims=True)
    rate = lax.rsqrt(spread + EPSILON)
    return centered * rate, rate


def norm_back(unit, rate, gain, gradient):
    inner = gradient * gain
    first = jnp.mean(inner, axis=-1, keepdims=True)
    second = jnp.mean(inner * unit, axis=-1, keepdims=True)
    return rate * (inner - first - unit * second)


def colsum(signal):
    return jnp.sum(signal, axis=0, keepdims=True)


def smooth(hidden):
    scale = 0.7978845608028654
    square = hidden * hidden
    curve = jnp.tanh(scale * hidden * (1.0 + 0.044715 * square))
    half = 0.5 + 0.5 * curve
    slope = half + 0.5 * hidden * (1.0 - curve * curve) * (scale + (3 * 0.044715 * scale) * square)
    return hidden * half, slope


def half_mask(shape, axis, which):
    index = lax.broadcasted_iota(jnp.int32, shape, axis)
    return (index < HEAD) if which == 0 else (index >= HEAD)


def keep_half(pair, axis, which):
    return jnp.where(half_mask(pair.shape, axis, which), pair, jnp.zeros_like(pair))


def project_qkv(x, sources, w4, q, qt, k, v, vt):
    rows = x.shape[0]
    for start, size in cut(rows):
        part = slice(start, start + size)
        q[part] = (mm(x[part], w4[0]) * HEAD ** (-0.5)).astype(BF)
    if q.shape[0] > rows:
        q[rows:] = jnp.zeros((q.shape[0] - rows, q.shape[1]), BF)
    for start, size in cut(sources.shape[0]):
        part = slice(start, start + size)
        k[part] = mm(sources[part], w4[1]).astype(BF)
        v[part] = mm(sources[part], w4[2]).astype(BF)
    qt[...] = q[...].T
    vt[...] = v[...].T


def shifted_exp(scores, exact, causal_rows):
    if causal_rows:
        size, width = scores.shape
        key = lax.broadcasted_iota(jnp.int32, (width, width), 0)
        query = lax.broadcasted_iota(jnp.int32, (width, width), 1)
        last = jnp.where(key <= query, scores[size - width :], NEGATIVE)
        scores = last if size == width else jnp.concatenate([scores[: size - width], last], axis=0)
        exact = exact or size == width
    sample = scores if exact else scores[:128]
    return jnp.exp(scores - jnp.max(sample, axis=0, keepdims=True))


def attend_heads(exact, causal, q_tile, qt, k, vt, ot, rate, store):
    keys, queries = k.shape[0], qt.shape[1]

    def pair(p, carry):
        lanes = pl.ds(pl.multiple_of(p * 128, 128), 128)
        for u in range(2):
            rows = pl.ds(pl.multiple_of(p * 128 + u * HEAD, HEAD), HEAD)
            place, done = store(p, u)
            for start in range(0, queries, q_tile):
                cols = slice(start, start + q_tile)
                depth = start + q_tile if causal else keys
                scores = mm(k[:depth, lanes], keep_half(qt[lanes, cols], 0, u))
                raised = shifted_exp(scores, exact, causal)
                total = jnp.sum(raised, axis=0, keepdims=True)
                low = raised.astype(BF)
                place[:depth, cols] = low
                inverse = 1.0 / total
                rate[2 * p + u, :, cols] = inverse
                ot[rows, cols] = (mm(vt[rows, :depth], low) * inverse).astype(BF)
            done()
        return carry

    lax.fori_loop(0, HEADS // 2, pair, 0)


def attend(causal, q_tile, qt, k, vt, ot, rate, store, drain):
    attend_heads(False, causal, q_tile, qt, k, vt, ot, rate, store)
    drain()
    fine = jnp.min(rate[...]) > 1.0 / LIMIT

    @pl.when(jnp.logical_not(fine))
    def _():
        attend_heads(True, causal, q_tile, qt, k, vt, ot, rate, store)
        drain()


def back_heads(causal, q_tile, q, kt, v, dot_, d_o, rowdot, fetch, ds, dqt, dk, dv, hook=None):
    keys, queries = v.shape[0], dqt.shape[1]

    def pair(p, carry):
        lanes = pl.ds(pl.multiple_of(p * 128, 128), 128)
        for u in range(2):
            rows = pl.ds(pl.multiple_of(p * 128 + u * HEAD, HEAD), HEAD)
            place = fetch(p, u)
            for start in range(0, queries, q_tile):
                cols = slice(start, start + q_tile)
                depth = start + q_tile if causal else keys
                grad = mm(v[:depth, lanes], keep_half(dot_[lanes, cols], 0, u))
                scaled = place[:depth, cols].astype(F32) * (grad - rowdot[2 * p + u, :, cols])
                low = scaled.astype(BF)
                ds[u][:depth, cols] = low
                dqt[rows, cols] = (mm(kt[rows, :depth], low) * HEAD ** (-0.5)).astype(BF)
            qm = q[:queries, lanes]
            dm = d_o[:queries, lanes]
            steps = range(0, keys, q_tile) if causal else (0,)
            for start in steps:
                key = slice(start, start + q_tile) if causal else slice(0, keys)
                more_k = mm(ds[u][key, start:queries], qm[start:])
                more_v = mm(place[key, start:queries], dm[start:])
                if u == 0:
                    dk[key, lanes] = more_k.astype(BF)
                    dv[key, lanes] = more_v.astype(BF)
                else:
                    dk[key, lanes] = jnp.where(half_mask(more_k.shape, 1, 1), more_k.astype(BF), dk[key, lanes])
                    dv[key, lanes] = jnp.where(half_mask(more_v.shape, 1, 1), more_v.astype(BF), dv[key, lanes])
            if hook is not None:
                for at, act in hook.items():
                    if at % 2 == u:
                        pl.when(p == at // 2)(act)
        return carry

    lax.fori_loop(0, HEADS // 2, pair, 0)


def back_outputs(grad_low, w4, ot, rate, dot_, d_o, rowdot):
    rows, wide = grad_low.shape[0], dot_.shape[1]
    raw = mm(w4[3], grad_low[...], NT)
    for h in range(HEADS):
        part = slice(h * HEAD, (h + 1) * HEAD)
        low = (raw[part] * rate[h][:, :rows]).astype(BF)
        if wide > rows:
            low = jnp.concatenate([low, jnp.zeros((HEAD, wide - rows), BF)], axis=1)
        dot_[part] = low
        rowdot[h] = jnp.sum(low.astype(F32) * ot[part].astype(F32), axis=0, keepdims=True)
    d_o[...] = dot_[...].T


def ring(buffers, hbm, sems, spans, out):
    def copies(h, slot):
        made = []
        for i, (rows, cols) in enumerate(spans):
            here = buffers.at[slot, pl.ds(0, rows), cols]
            there = hbm.at[h, pl.ds(0, rows), cols]
            made.append(
                pltpu.make_async_copy(here, there, sems.at[slot, i])
                if out
                else pltpu.make_async_copy(there, here, sems.at[slot, i])
            )
        return made

    return copies


def out_ring(buffers, hbm, sems, spans):
    copies = ring(buffers, hbm, sems, spans, True)

    def store(p, u):
        slot = (p % 2) * 2 + u

        @pl.when(p >= 2)
        def _():
            for copy in copies(2 * p + u, slot):
                copy.wait()

        def done():
            for copy in copies(2 * p + u, slot):
                copy.start()

        return buffers.at[slot], done

    def drain():
        for slot in range(4):
            for copy in copies(slot, slot):
                copy.wait()

    return store, drain


def in_ring(buffers, hbm, sems, spans):
    copies = ring(buffers, hbm, sems, spans, False)
    depth = buffers.shape[0]

    def begin():
        for h in range(depth):
            for copy in copies(h, h):
                copy.start()

    def fetch(p, u):
        h = 2 * p + u
        for copy in copies(h, h % depth):
            copy.wait()

        @pl.when((h >= 1) & (h + depth <= HEADS))
        def _():
            for copy in copies(h + depth - 1, (h + depth - 1) % depth):
                copy.start()

        return buffers.at[h % depth]

    return begin, fetch


MESH = pl.DeviceIdType.MESH


class Spot:
    def __init__(self, n, m):
        self.n, self.m = n, m
        self.d, self.b = lax.axis_index("dp"), lax.axis_index("bal")
        self.core, self.far = self.b % 2, self.b // 2
        self.parity, self.row = self.d % 2, self.d // 2
        self.by_core = (self.d, self.b + 1 - 2 * self.core)
        self.by_far = (self.d, self.b + 2 - 4 * self.far)
        self.by_parity = (self.d + 1 - 2 * self.parity, self.b)

    def greet(self):
        barrier = pltpu.get_barrier_semaphore()

        def call(device):
            pl.semaphore_signal(barrier, inc=1, device_id=device, device_id_type=MESH)

        for k in range(1, self.m):
            call((self.d, (self.b + k) % self.m))

        def along(k, carry):
            call(((self.d + k) % self.n, self.b))
            call(((self.d + k) % self.n, self.by_far[1]))
            return carry

        lax.fori_loop(1, self.n, along, 0)

    def await_all(self):
        pl.semaphore_wait(pltpu.get_barrier_semaphore(), self.m - 1 + 2 * (self.n - 1))


def remote(source, target, sent, received, device):
    return pltpu.make_async_remote_copy(
        src_ref=source, dst_ref=target, send_sem=sent, recv_sem=received, device_id=device, device_id_type=MESH
    )


class Piece:
    def __init__(self, spot, along_x, sems, source=None, acc=None, land_a=None, kept=None, land_b=None, kept2=None,
                 land_c=None, slots=None, result=None, gathered=None):
        self.spot, self.along_x, self.source, self.sems = spot, along_x, source, sems
        self.acc, self.land_a, self.kept, self.land_b = acc, land_a, kept, land_b
        self.kept2, self.land_c = kept2, land_c
        self.slots, self.result, self.gathered = slots, result, gathered

    def a_copies(self):
        half = self.acc.shape[3]
        mine = pl.ds(pl.multiple_of(self.spot.core * half, half), half)
        other = pl.ds(pl.multiple_of((1 - self.spot.core) * half, half), half)
        return [
            pltpu.make_async_copy(self.source.at[:, :, :, mine], self.acc, self.sems.at[0]),
            remote(self.source.at[:, :, :, other], self.land_a, self.sems.at[1], self.sems.at[2], self.spot.by_core),
        ]

    def a_start(self):
        for copy in self.a_copies():
            copy.start()

    def a_wait(self):
        for copy in self.a_copies():
            copy.wait()

        def add(i, carry):
            self.acc[i] = self.acc[i] + self.land_a[i]
            return carry

        lax.fori_loop(0, self.acc.shape[0], add, 0)

    def lanes(self, mine, size):
        side = self.spot.far if mine else 1 - self.spot.far
        return pl.ds(pl.multiple_of(side * size, size), size)

    def b_copy(self):
        spot = self.spot
        if self.along_x:
            out, to = self.acc.at[:, :, :, self.lanes(False, self.land_b.shape[3])], spot.by_far
        else:
            out, to = self.acc.at[:, 1 - spot.parity], spot.by_parity
        return remote(out, self.land_b, self.sems.at[3], self.sems.at[4], to)

    def b_start(self):
        self.b_copy().start()

    def b_wait(self):
        self.b_copy().wait()

        def add(i, carry):
            if self.along_x:
                mine = self.acc[i, :, :, self.lanes(True, self.land_b.shape[3])]
            else:
                mine = self.acc[i, self.spot.parity]
            self.kept[i] = mine + self.land_b[i]
            return carry

        lax.fori_loop(0, self.kept.shape[0], add, 0)

    def bb_copy(self):
        spot = self.spot
        if self.along_x:
            out, to = self.kept.at[:, 1 - spot.parity], spot.by_parity
        else:
            out, to = self.kept.at[:, :, self.lanes(False, self.land_c.shape[2])], spot.by_far
        return remote(out, self.land_c, self.sems.at[5], self.sems.at[6], to)

    def bb_start(self):
        self.bb_copy().start()

    def bb_wait(self):
        self.bb_copy().wait()

        def add(i, carry):
            if self.along_x:
                mine = self.kept[i, self.spot.parity]
            else:
                mine = self.kept[i, :, self.lanes(True, self.land_c.shape[2])]
            self.kept2[i] = mine + self.land_c[i]
            return carry

        lax.fori_loop(0, self.kept2.shape[0], add, 0)

    def c_copy(self, k, arriving):
        spot, half = self.spot, self.spot.n // 2
        row = (spot.row + k) % half
        slot = row if arriving else spot.row
        return remote(self.kept2.at[row], self.slots.at[slot], self.sems.at[7 + k], self.sems.at[7 + half + slot],
                      (row * 2 + spot.parity, spot.b))

    def c_start(self):
        def step(k, carry):
            self.c_copy(k, False).start()
            return carry

        lax.fori_loop(1, self.spot.n // 2, step, 0)

    def c_wait(self):
        half, row = self.spot.n // 2, self.spot.row

        def step(k, total):
            self.c_copy(k, False).wait_send()
            self.c_copy(k, True).wait_recv()
            return total + self.slots[(row + k) % half].astype(F32)

        total = lax.fori_loop(1, half, step, self.kept2[row].astype(F32))
        self.result[...] = total.astype(BF)

    def d_base(self):
        return 7 + self.spot.n

    def d_copies(self, arriving):
        spot, base = self.spot, self.d_base()
        made = []
        for k in range(1, spot.m):
            peer = (spot.b + k) % spot.m
            slot = peer if arriving else spot.b
            made.append(remote(self.result, self.gathered.at[slot], self.sems.at[base + k],
                               self.sems.at[base + spot.m + slot], (spot.d, peer)))
        return made

    def d_start(self):
        for copy in self.d_copies(False):
            copy.start()
        self.gathered[self.spot.b] = self.result[...]

    def d_wait(self):
        for copy in self.d_copies(False):
            copy.wait_send()
        for copy in self.d_copies(True):
            copy.wait_recv()


class LatePiece(Piece):
    def e_place(self, t):
        n, lanes = self.spot.n, self.slots.shape[2]
        far, d = t // n, t % n
        where = (d // 2, d % 2, slice(None), pl.ds(pl.multiple_of(far * lanes, lanes), lanes))
        return where, (d, self.spot.core + 2 * far)

    def e_copy(self, k, arriving):
        count, me = 2 * self.spot.n, self.spot.far * self.spot.n + self.spot.d
        peer = (me + k) % count
        where, device = self.e_place(peer)
        slot = peer if arriving else me
        return remote(self.acc.at[where], self.slots.at[slot], self.sems.at[3 + k], self.sems.at[3 + count + slot], device)

    def e_start(self):
        def step(k, carry):
            self.e_copy(k, False).start()
            return carry

        lax.fori_loop(1, 2 * self.spot.n, step, 0)

    def e_wait(self):
        count, me = 2 * self.spot.n, self.spot.far * self.spot.n + self.spot.d

        def step(k, total):
            self.e_copy(k, False).wait_send()
            self.e_copy(k, True).wait_recv()
            return total + self.slots[(me + k) % count].astype(F32)

        where, _ = self.e_place(me)
        total = lax.fori_loop(1, count, step, self.acc[where].astype(F32))
        self.result[...] = total.astype(BF)

    def d_base(self):
        return 3 + 4 * self.spot.n


def late_scratch(n, m, rows):
    vb = lambda shape: pltpu.VMEM(shape, BF)
    return [vb((n // 2, 2, rows, 512)), vb(half_shape(n, rows)), vb(half_shape(n, rows)), vb((2 * n, rows, 128)),
            vb((rows, 128)), pltpu.SemaphoreType.DMA((3 + 4 * n + 2 * m,))]


def piece_sems(n, m):
    return pltpu.SemaphoreType.DMA((7 + n + 2 * m,))


def half_shape(n, rows):
    return (n // 2, 2, rows, 256)


def kept_shape(n, rows, along_x):
    return (n // 2, 2, rows, 128) if along_x else (n // 2, rows, 256)


def last_shape(n, rows):
    return (n // 2, rows, 128)


class VectorSum:
    def __init__(self, spot, v, lands, slots, result, sems):
        self.spot, self.v, self.lands, self.slots, self.result, self.sems = spot, v, lands, slots, result, sems

    def swap(self, step):
        device = (self.spot.by_core, self.spot.by_far, self.spot.by_parity)[step]
        return remote(self.v, self.lands.at[step], self.sems.at[2 * step], self.sems.at[2 * step + 1], device)

    def swap_start(self, step):
        self.swap(step).start()

    def swap_wait(self, step):
        self.swap(step).wait()
        self.v[...] = self.v[...] + self.lands[step]

    def copy(self, k, arriving):
        spot, half = self.spot, self.spot.n // 2
        row = (spot.row + k) % half
        slot = row if arriving else spot.row
        return remote(self.v.at[row * 2 + spot.parity], self.slots.at[slot], self.sems.at[6 + k],
                      self.sems.at[6 + half + slot], (row * 2 + spot.parity, spot.b))

    def c_start(self):
        def step(k, carry):
            self.copy(k, False).start()
            return carry

        lax.fori_loop(1, self.spot.n // 2, step, 0)

    def c_wait(self):
        half, row = self.spot.n // 2, self.spot.row

        def step(k, total):
            self.copy(k, False).wait_send()
            self.copy(k, True).wait_recv()
            return total + self.slots[(row + k) % half]

        self.result[...] = lax.fori_loop(1, half, step, self.v[self.spot.d])


def put(piece, row, value, lane=0):
    halves, two, width = piece.shape[0], piece.shape[1], value.shape[1]
    rows = value.shape[0] // (halves * two)
    piece[:, :, row : row + rows, lane : lane + width] = value.reshape(halves, two, rows, width).astype(BF)


def encoder_forward(x_h, w_h, up_h, bias, down_h, gains, shifts,
                    memory, w4_h, qkv_h, ot_h, e_h, rate, e1_h, e2_h, zb_h, act_h, slope_h,
                    x, raw, w4, up, down, q, k, v, qt, vt, ot, e1, e2, zb, act, slope, ering, sems, esems):
    c = Copies(sems)
    load_w = c.start(w_h, raw)
    load_x = c.start(x_h, x)
    load_up = c.start(up_h, up)
    load_down = c.start(down_h, down)
    load_w.wait()
    split_weights(raw, w4)
    c.out(w4, w4_h)
    load_x.wait()
    project_qkv(x, x, w4, q, qt, k, v, vt)
    n, wide = x.shape[0], qt.shape[1]
    for i, item in enumerate((q.at[pl.ds(0, n)], k, v)):
        c.out(item, qkv_h.at[i])
    store, drain = out_ring(ering, e_h, esems, [(n, slice(None))])
    attend(False, wide, qt, k, vt, ot, rate, store, drain)
    c.out(ot, ot_h)
    load_up.wait()
    load_down.wait()
    for start, size in cut(n):
        part = slice(start, start + size)
        first = x[part].astype(F32) + mm(ot[:, part], w4[3], TN)
        e1[part] = first
        unit, _ = normalise(first)
        z = unit * gains[0:1] + shifts[0:1]
        low = z.astype(BF)
        zb[part] = low
        active, bend = smooth(mm(low, up[...]) + bias[...])
        act[part] = active.astype(BF)
        slope[part] = bend.astype(BF)
        second = z + mm(act[part], down[...]) + shifts[2:3]
        e2[part] = second
        unit, _ = normalise(second)
        memory[part] = (unit * gains[1:2] + shifts[1:2]).astype(BF)
    for here, there in ((e1, e1_h), (e2, e2_h), (zb, zb_h), (act, act_h), (slope, slope_h)):
        c.out(here, there)
    c.finish()


def tags_forward(x_h, w_h, gains, shifts,
                 x1, w4_h, qkv_h, ot_h, e_h, rate, a1_h,
                 x, raw, w4, q, k, v, qt, vt, ot, a1, ering, sems, esems):
    c = Copies(sems)
    load_w = c.start(w_h, raw)
    load_x = c.start(x_h, x)
    load_w.wait()
    split_weights(raw, w4)
    c.out(w4, w4_h)
    load_x.wait()
    project_qkv(x, x, w4, q, qt, k, v, vt)
    n = x.shape[0]
    for i, item in enumerate((q, k, v)):
        c.out(item, qkv_h.at[i])
    tile = 256
    spans = [(start + tile, slice(start, start + tile)) for start in range(0, n, tile)]
    store, drain = out_ring(ering, e_h, esems, spans)
    attend(True, tile, qt, k, vt, ot, rate, store, drain)
    c.out(ot, ot_h)
    for start, size in cut(n):
        part = slice(start, start + size)
        first = x[part].astype(F32) + mm(ot[:, part], w4[3], TN)
        a1[part] = first
        unit, _ = normalise(first)
        x1[part] = (unit * gains[0:1] + shifts[0:1]).astype(BF)
    c.out(a1, a1_h)
    c.finish()


def decoder_middle(capacity, tag_length, cell_count, destination, slot_index, x1_h, mem_h, w_h, up_h, bias, down_h, gains,
                   shifts, cot_h,
                   y, da_h, gb_h, w4_h, q_h, k_h, v_h, ot_h, e_h, rate, g_ffn, d_bias, d_gains, d_shifts,
                   x1, mem, raw, w4, up, down, q, k, v, qt, vt, ot, ering,
                   unit2, rate2, xb2, act, slope, da, gb, sems, esems):
    cot, dh = y, slope
    c = Copies(sems)
    load_w = c.start(w_h, raw)
    load_mem = c.start(mem_h, mem)
    load_x = c.start(x1_h, x1)
    load_up = c.start(up_h, up)
    load_down = c.start(down_h, down)
    load_cot = c.start(cot_h, cot)
    load_w.wait()
    split_weights(raw, w4)
    load_mem.wait()
    load_x.wait()
    project_qkv(x1, mem, w4, q, qt, k, v, vt)
    for here, there in ((w4, w4_h), (q, q_h), (k, k_h), (v, v_h)):
        c.out(here, there)
    n, blocks = x1.shape[0], y.shape[0]
    block = n // blocks

    store, drain = out_ring(ering, e_h, esems, [(mem.shape[0], slice(None))])
    attend(False, n, qt, k, vt, ot, rate, store, drain)
    c.out(ot, ot_h)
    load_up.wait()
    load_down.wait()
    load_cot.wait()
    live = tag_length[0] + cell_count[0]
    places = [destination[0, b] * capacity + slot_index[0, b] for b in range(blocks)]
    zero = jnp.zeros((1, x1.shape[1]), F32)
    gain3, shift3 = zero, zero
    for start, size in cut(n):
        part = slice(start, start + size)
        second = x1[part].astype(F32) + mm(ot[:, part], w4[3], TN)
        unit, pace = normalise(second)
        unit2[part] = unit
        rate2[part] = pace
        x2 = unit * gains[1:2] + shifts[1:2]
        low = x2.astype(BF)
        xb2[part] = low
        active, bend = smooth(mm(low, up[...]) + bias[...])
        act[part] = active.astype(BF)
        slope[part] = bend.astype(BF)
        third = x2 + mm(act[part], down[...]) + shifts[3:4]
        unit, pace = normalise(third)
        row = lax.broadcasted_iota(jnp.int32, (size, 1), 0) + start
        alive = (row < live).astype(F32)
        final = ((unit * gains[2:3] + shifts[2:3]) * alive).astype(BF)
        picked = []
        for b in range(start // block, (start + size) // block):
            picked.append(cot[places[b]])
            y[places[b]] = final[b * block - start : (b + 1) * block - start]
        dy = jnp.concatenate(picked, axis=0).astype(F32) * alive
        gain3 += colsum(dy * unit)
        shift3 += colsum(dy)
        d3 = norm_back(unit, pace, gains[2:3], dy)
        da[part] = d3
        gb[part] = d3.astype(BF)
    d_gains[2:3] = gain3
    d_shifts[2:3] = shift3
    ffn_back(xb2, up, down, act, slope, gb, dh, g_ffn, d_bias, d_shifts, 3)
    gain2, shift2 = zero, zero
    for start, size in cut(n):
        part = slice(start, start + size)
        dx2 = da[part] + mm(dh[part], up[...], NT)
        gain2 += colsum(dx2 * unit2[part])
        shift2 += colsum(dx2)
        d2 = norm_back(unit2[part], rate2[part], gains[1:2], dx2)
        da[part] = d2
        gb[part] = d2.astype(BF)
    d_gains[1:2] = gain2
    d_shifts[1:2] = shift2
    c.out(gb, gb_h)
    c.out(da, da_h)
    c.finish()


def ffn_back(xb, up, down, act, slope, gb, dh, g_ffn, d_bias, d_shifts, row, middle=None):
    n, width = xb.shape
    offset = jnp.zeros((1, up.shape[1]), F32)
    for start, size in cut(n):
        part = slice(start, start + size)
        low = (mm(gb[part], down[...], NT) * slope[part].astype(F32)).astype(BF)
        dh[part] = low
        offset += colsum(low.astype(F32))
    d_bias[...] = offset
    d_shifts[row : row + 1] = colsum(gb[...].astype(F32))
    if middle is not None:
        middle()
    rows = g_ffn.shape[2] // 4
    put(g_ffn, 2 * rows, mm(act[...], gb[...], TN))
    for j in range(up.shape[1] // width):
        put(g_ffn, j * rows, mm(xb[...], dh[:, j * width : (j + 1) * width], TN))


class Room:
    def __init__(self, acc, land, kept, next_, kept_x, next_x, kept2, last, slots, result):
        self.acc, self.land, self.kept, self.next = acc, land, kept, next_
        self.kept_x, self.next_x, self.kept2, self.last, self.slots, self.result = kept_x, next_x, kept2, last, slots, result

    def whole(self, spot, sems, source, gathered):
        return Piece(spot, False, sems, source, self.acc, self.land, self.kept, self.next, self.kept2, self.last,
                     self.slots, self.result, gathered)

    def part(self, spot, sems, source, gathered, along_x, start, size):
        rows, head = pl.ds(start, size), pl.ds(0, size)
        kept = self.kept_x.at[:, :, head] if along_x else self.kept.at[:, rows]
        next_ = self.next_x.at[:, :, head] if along_x else self.next.at[:, rows]
        return Piece(spot, along_x, sems, source, self.acc.at[:, :, rows], self.land.at[:, :, rows], kept, next_,
                     self.kept2.at[:, rows], self.last.at[:, rows], self.slots.at[:, rows], self.result.at[rows], gathered)


def room_scratch(n, rows):
    vb = lambda shape: pltpu.VMEM(shape, BF)
    last, side = vb(last_shape(n, rows)), vb(kept_shape(n, rows // 2, True))
    kept = vb(kept_shape(n, rows, False))
    return [vb(half_shape(n, rows)), vb(half_shape(n, rows)), kept, kept, side, side, last, last, last, vb((rows, 128))]


def backward(n_dp, n_bal,
             da_h, gb_h, x1_h, mem_h, cw4_h, cq_h, ck_h, cv_h, cot_h, ce_h, y_h, g_dffn,
             e2_h, e1_h, zb_h, act_h, slope_h, up_h, down_h, ex_h, ew4_h, eqkv_h, eot_h, ee_h,
             a1_h, tx_h, tw4_h, tqkv_h, tot_h, te_h,
             crate, erate, trate, egains, dgains, d_bias_d, d_gains_d, d_shifts_d,
             dx_enc_h, dx_tags_h, decoded, all_cross, all_dffn, all_effn, all_enc0, all_enc1, *rest_refs):
    all_self, v_total = rest_refs[:4], rest_refs[4]
    (ering, q, k, v, ot, kt, dot_, d_o, rowdot, dqt, dk, dv, ds, gb, da, wide0, wide1, dx1, x0, x1,
     wa, wb, g0, g1, d_bias, d_gains, d_shifts, vec, vec_lands, vec_slots, next_effn, next_enc1, *rest) = rest_refs[5:]
    room0, room1 = Room(*rest[:10]), Room(*rest[10:20])
    sems, esems, moves, vsems = rest[20:24]
    psems = rest[24:31]
    late = [rest[31:37], rest[37:43]]
    spot = Spot(n_dp, n_bal)
    spot.greet()
    c = Copies(sems)
    n, width = x0.shape
    m = x1.shape[0]
    wide = eot_h.shape[1]
    hidden = up_h.shape[1]
    size = g0.shape[2] // 2
    rows = size // 2
    half = width // 2
    low, high = pl.ds(0, size), pl.ds(size, size)
    least = all_self[0].shape[1]
    dffn = room0.whole(spot, psems[0], g_dffn, all_dffn)
    cross = room1.whole(spot, psems[1], g0, all_cross)
    effn = room0.whole(spot, psems[2], g1, all_effn)
    effn.land_b = next_effn
    enc0 = room1.part(spot, psems[3], g0.at[:, :, low], all_enc0, True, 0, size)
    enc1 = room1.part(spot, psems[4], g0.at[:, :, high], all_enc1, False, size, size)
    enc1.land_b = next_enc1
    pairs = [
        room0.part(spot, psems[5 + i], g1.at[:, :, pl.ds(i * least, least)], all_self[i], i == 1, i * least, least)
        for i in range(2)
    ] + [
        LatePiece(spot, True, sem, source, acc, land, slots=slots, result=result, gathered=gathered)
        for (source, acc, land, slots, result, sem), gathered in zip(late, all_self[2:])
    ]
    pair0, pair1, pair2, pair3 = pairs
    vector = VectorSum(spot, vec, vec_lands, vec_slots, v_total, vsems)
    zero = jnp.zeros((1, width), F32)
    pair_ds = ds.at[0], ds.at[1]

    load_gb = c.start(gb_h, gb)
    load_ot = c.start(cot_h, ot)
    load_w = c.start(cw4_h, wa)
    loads = [c.start(a, b) for a, b in ((ck_h, k.at[pl.ds(0, m)]), (cv_h, v.at[pl.ds(0, m)]), (cq_h, q))]
    begin, fetch = in_ring(ering, ce_h, esems.at[0], [(m, slice(0, n))])
    begin()
    last = [c.start(a, b) for a, b in ((x1_h, x0), (mem_h, x1), (da_h, da))]
    load_ew = c.start(ew4_h, wb)
    load_e2 = c.start(e2_h, wide0.at[pl.ds(0, m)])
    load_gb.wait()
    load_ot.wait()
    put(g0, 3 * rows, mm(ot[...], gb[...]))
    load_w.wait()
    back_outputs(gb, wa, ot, crate, dot_, d_o, rowdot)
    for load in loads:
        load.wait()
    kt[:, :m] = k[:m].T
    spot.await_all()
    dffn.a_start()
    share = y_h.shape[0] // n_bal

    def moved(step, arriving):
        peer = (spot.b + step) % n_bal
        slot = peer if arriving else spot.b
        return remote(y_h.at[pl.ds(peer * share, share)], decoded.at[pl.ds(slot * share, share)], moves.at[step],
                      moves.at[n_bal + slot], (spot.d, peer))

    own = pl.ds(spot.b * share, share)
    own_copy = pltpu.make_async_copy(y_h.at[own], decoded.at[own], moves.at[0])
    own_copy.start()
    for step in range(1, n_bal):
        moved(step, False).start()

    def cross1():
        dffn.a_wait()
        dffn.b_start()

    keys = pl.ds(0, m)
    back_heads(False, n, q, kt, v.at[keys], dot_, d_o, rowdot, fetch, pair_ds, dqt, dk.at[keys], dv.at[keys],
               {1: cross1})
    for load in last:
        load.wait()
    put(g0, 0, mm(x0[...], dqt[...], TT))
    put(g0, rows, mm(x1[...], dk[:m], TN))
    put(g0, 2 * rows, mm(x1[...], dv[:m], TN))
    cross.a_start()
    dffn.b_wait()
    dffn.bb_start()
    for start, count in cut(m):
        part = slice(start, start + count)
        wide1[part] = mm(dk[part], wa[1], NT) + mm(dv[part], wa[2], NT)
    for start, count in cut(n):
        part = slice(start, start + count)
        dx1[part] = (da[part] + mm(dqt[:, part], wa[0], TT)).astype(BF)
    act, slope = ds.at[0, keys, pl.ds(0, hidden)], ds.at[1, keys, pl.ds(0, hidden)]
    up, down, zb = dqt.at[:, pl.ds(0, hidden)], dk.at[pl.ds(0, hidden)], dv.at[keys]
    load_ffn = [c.start(a, b) for a, b in ((down_h, down), (slope_h, slope), (act_h, act), (zb_h, zb), (up_h, up))]
    queries = pl.ds(0, wide)
    eot, eq = ot.at[:, queries], q.at[queries]
    load_ot = c.start(eot_h, eot)
    loads = [c.start(eqkv_h.at[i], item.at[keys]) for i, item in enumerate((q, k, v))]
    load_x = c.start(ex_h, x1)
    load_tw = c.start(tw4_h, wa)
    load_tx = c.start(tx_h, x0)
    begin, fetch = in_ring(ering, ee_h, esems.at[1], [(m, slice(0, wide))])
    begin()
    q[m:wide] = jnp.zeros((wide - m, width), BF)
    load_e2.wait()
    gain, shift = zero, zero
    for start, count in cut(m):
        part = slice(start, start + count)
        unit, pace = normalise(wide0[part])
        grad = wide1[part]
        gain += colsum(grad * unit)
        shift += colsum(grad)
        d2 = norm_back(unit, pace, egains[1:2], grad)
        da[part] = d2
        gb[part] = d2.astype(BF)
    d_gains[1:2] = gain
    d_shifts[1:2] = shift
    load_e1 = c.start(e1_h, wide1)
    load_a1 = c.start(a1_h, wide0)
    cross.a_wait()
    cross.b_start()
    for load in load_ffn:
        load.wait()
    ffn_back(zb, up, down, act, slope, gb.at[keys], slope, g1, d_bias, d_shifts, 2)
    effn.a_start()
    dffn.bb_wait()
    dffn.c_start()
    load_e1.wait()
    gain, shift = zero, zero
    for start, count in cut(m):
        part = slice(start, start + count)
        unit, pace = normalise(wide1[part])
        dz = da[part] + mm(slope[part], up[...], NT)
        gain += colsum(dz * unit)
        shift += colsum(dz)
        d1 = norm_back(unit, pace, egains[0:1], dz)
        da[part] = d1
        gb[part] = d1.astype(BF)
    d_gains[0:1] = gain
    d_shifts[0:1] = shift

    def enc0_():
        effn.a_wait()
        effn.b_start()

    def enc2():
        cross.b_wait()
        cross.bb_start()
        dffn.c_wait()
        dffn.d_start()

    for load in (load_ew, load_ot, *loads, load_x):
        load.wait()
    kt[:, :m] = k[:m].T
    put(g0, 3 * rows, mm(ot[:, :m], gb[:m]))
    edot, edo, edqt = dot_.at[:, queries], d_o.at[queries], dqt.at[:, queries]
    erowdot = rowdot.at[:, :, queries]
    back_outputs(gb.at[keys], wb, eot, erate, edot, edo, erowdot)
    back_heads(False, wide, eq, kt, v.at[keys], edot, edo, erowdot, fetch, pair_ds, edqt, dk.at[keys], dv.at[keys],
               {0: enc0_, 2: enc2})
    cross.bb_wait()
    cross.c_start()
    put(g0, 0, mm(x1[...], dqt[:, :m], TT))
    put(g0, rows, mm(x1[...], dk[:m], TN))
    put(g0, 2 * rows, mm(x1[...], dv[:m], TN))
    enc0.a_start()
    enc1.a_start()
    effn.b_wait()
    effn.bb_start()
    for start, count in cut(m):
        part = slice(start, start + count)
        wide1[part] = da[part] + mm(dqt[:, part], wb[0], TT) + mm(dk[part], wb[1], NT) + mm(dv[part], wb[2], NT)
    c.out(wide1, dx_enc_h)

    load_ot = c.start(tot_h, ot)
    loads = [c.start(tqkv_h.at[i], item) for i, item in enumerate((q, k, v))]
    tile = 256
    spans = [(start + tile, slice(start, start + tile)) for start in range(0, n, tile)]
    begin, fetch = in_ring(ering, te_h, esems.at[2], spans)
    begin()
    load_a1.wait()
    gain, shift = zero, zero
    for start, count in cut(n):
        part = slice(start, start + count)
        unit, pace = normalise(wide0[part])
        grad = dx1[part].astype(F32)
        gain += colsum(grad * unit)
        shift += colsum(grad)
        d1 = norm_back(unit, pace, dgains[0:1], grad)
        da[part] = d1
        gb[part] = d1.astype(BF)
    part_lanes = width // n_dp
    vec[...] = jnp.zeros_like(vec)
    for i in range(n_dp):
        lanes = slice(i * part_lanes, (i + 1) * part_lanes)
        for j in range(2):
            wide_lanes = slice((2 * i + j) * part_lanes, (2 * i + j + 1) * part_lanes)
            vec[i, j : j + 1, :part_lanes] = d_bias[:, wide_lanes]
            vec[i, 2 + j : 3 + j, :part_lanes] = d_bias_d[:, wide_lanes]
        vec[i, 4:6, :part_lanes] = d_gains[:, lanes]
        vec[i, 6:9, :part_lanes] = d_shifts[:, lanes]
        vec[i, 9:10, :part_lanes] = gain[:, lanes]
        vec[i, 10:12, :part_lanes] = d_gains_d[1:3, lanes]
        vec[i, 12:13, :part_lanes] = shift[:, lanes]
        vec[i, 13:16, :part_lanes] = d_shifts_d[1:4, lanes]
    vector.swap_start(0)
    enc0.a_wait()
    enc0.b_start()
    enc1.a_wait()
    enc1.b_start()

    quarter = half // 2

    def put_pair(p):
        lanes = slice(p * quarter, (p + 1) * quarter)
        sides = jnp.concatenate([dqt[lanes].T, dk[:, lanes], dv[:, lanes]], axis=1)
        put(pairs[p].source, 0, mm(x0[...], sides, TN))
        pairs[p].a_start()

    def tags0():
        vector.swap_wait(0)
        vector.swap_start(1)
        cross.c_wait()
        cross.d_start()
        effn.bb_wait()
        effn.c_start()

    def tags1():
        put_pair(0)

    def tags2():
        enc0.b_wait()
        enc1.b_wait()
        enc0.bb_start()
        enc1.bb_start()
        pair0.a_wait()
        pair0.b_start()
        vector.swap_wait(1)
        vector.swap_start(2)

    def tags3():
        put_pair(1)

    def tags4():
        pair1.a_wait()
        pair1.b_start()
        dffn.d_wait()
        effn.c_wait()
        effn.d_start()
        vector.swap_wait(2)
        vector.c_start()

    def tags5():
        put_pair(2)
        enc0.bb_wait()
        enc0.c_start()
        enc1.bb_wait()
        enc1.c_start()
        pair0.b_wait()
        pair0.bb_start()

    def tags6():
        pair2.a_wait()
        pair2.e_start()

    def tags7():
        put_pair(3)
        cross.d_wait()
        enc0.c_wait()
        enc0.d_start()
        enc1.c_wait()
        enc1.d_start()
        pair1.b_wait()
        pair1.bb_start()
        pair0.bb_wait()
        pair0.c_start()

    for load in (load_ot, load_tw, load_tx, *loads):
        load.wait()
    kt[...] = k[...].T
    out = mm(ot[...], gb[...])
    for i, piece in enumerate(pairs):
        put(piece.source, 0, out[:, i * quarter : (i + 1) * quarter], 3 * quarter)
    back_outputs(gb, wa, ot, trate, dot_, d_o, rowdot)
    back_heads(True, tile, q, kt, v, dot_, d_o, rowdot, fetch, pair_ds, dqt, dk, dv,
               dict(enumerate((tags0, tags1, tags2, tags3, tags4, tags5, tags6, tags7))))
    pair3.a_wait()
    pair3.e_start()
    for i, (start, count) in enumerate(cut(n)):
        part = slice(start, start + count)
        wide0[part] = (da[part] + mm(dqt[:, part], wa[0], TT) + mm(dk[part], wa[1], NT) + mm(dv[part], wa[2], NT))
        if i == 0:
            pair1.bb_wait()
            pair1.c_start()
    c.out(wide0, dx_tags_h)
    effn.d_wait()
    pair0.c_wait()
    pair0.d_start()
    pair2.e_wait()
    pair2.d_start()
    pair1.c_wait()
    pair1.d_start()
    vector.c_wait()
    pair3.e_wait()
    pair3.d_start()
    own_copy.wait()
    for step in range(1, n_bal):
        moved(step, False).wait_send()
        moved(step, True).wait_recv()
    c.finish()
    for piece in (enc0, enc1, *pairs):
        piece.d_wait()


def finish(all_cross, all_dffn, all_effn, all_enc0, all_enc1, all_self0, all_self1, all_self2, all_self3, v_total, decoded_h, patches_h, tags_h,
           o_enc, o_eup, o_ebias, o_edown, o_egains, o_eshifts,
           o_self, o_cross, o_dup, o_dbias, o_ddown, o_dgains, o_dshifts, o_decoded, o_patches, o_tags, tags, patches, decoded, sems):
    c = Copies(sems)
    moves = [(c.start(source, here), here, target) for source, here, target in
             ((tags_h, tags, o_tags), (patches_h, patches, o_patches), (decoded_h, decoded, o_decoded))]
    for load, here, target in moves:
        load.wait()
        c.out(here, target)

    def joined(gathered):
        return jnp.concatenate([gathered[b].astype(F32) for b in (0, 2, 1, 3)], axis=1)

    def layer(out, parts):
        rows = out.shape[0]
        for j in range(4):
            out[:, j, :] = parts[j * rows : (j + 1) * rows]

    def branch(up, down, parts):
        rows, width = up.shape[0], parts.shape[1]
        for j in range(up.shape[1] // width):
            up[:, j * width : (j + 1) * width] = parts[j * rows : (j + 1) * rows]
        down[...] = parts[2 * rows :]

    layer(o_enc, jnp.concatenate([joined(all_enc0), joined(all_enc1)], axis=0))
    layer(o_cross, joined(all_cross))
    branch(o_eup, o_edown, joined(all_effn))
    branch(o_dup, o_ddown, joined(all_dffn))
    rows, _, width = o_self.shape
    half = width // 2
    quarter = half // 2
    for i, gathered in enumerate((all_self0, all_self1, all_self2, all_self3)):
        parts = joined(gathered)
        for j in range(4):
            o_self[:, j, i * quarter : (i + 1) * quarter] = parts[:rows, j * quarter : (j + 1) * quarter]
    share = o_egains.shape[1]
    for j in range(2):
        o_ebias[:, j * share : (j + 1) * share] = v_total[j : j + 1, :share]
        o_dbias[:, j * share : (j + 1) * share] = v_total[2 + j : 3 + j, :share]
    o_egains[...] = v_total[4:6, :share]
    o_eshifts[...] = v_total[6:9, :share]
    o_dgains[...] = v_total[9:12, :share]
    o_dshifts[...] = v_total[12:16, :share]
    c.finish()


def call(kernel, ins, outs, out_specs, scratch, name, params=PARAMS):
    specs = [spec for spec, _ in ins]
    return pl.pallas_call(
        kernel,
        out_shape=outs,
        in_specs=specs,
        out_specs=out_specs,
        scratch_shapes=scratch,
        compiler_params=params,
        name=name,
    )(*[value for _, value in ins])


def run_encoder_forward(x, w, up, bias, down, gains, shifts):
    n, width = x.shape
    hidden = up.shape[1]
    wide = (n + 127) // 128 * 128
    bf = lambda *s: Shape(s, BF)
    f32 = lambda *s: Shape(s, F32)
    vb = lambda *s: pltpu.VMEM(s, BF)
    vf = lambda *s: pltpu.VMEM(s, F32)
    outs = [bf(n, width), bf(4, width, width), bf(3, n, width), bf(width, wide), bf(HEADS, n, wide), f32(HEADS, 1, wide),
            f32(n, width), f32(n, width), bf(n, width), bf(n, hidden), bf(n, hidden)]
    return call(
        encoder_forward,
        [(ANY, x), (ANY, w), (ANY, up), (VM, bias), (ANY, down), (VM, gains), (VM, shifts)],
        outs,
        [VM, ANY, ANY, ANY, ANY, VM, ANY, ANY, ANY, ANY, ANY],
        [vb(n, width), vb(width, 4, width), vb(4, width, width), vb(width, hidden), vb(hidden, width),
         vb(wide, width), vb(n, width), vb(n, width), vb(width, wide), vb(width, n), vb(width, wide),
         vf(n, width), vf(n, width), vb(n, width), vb(n, hidden), vb(n, hidden), vb(4, n, wide),
         pltpu.SemaphoreType.DMA((20,)), pltpu.SemaphoreType.DMA((4, 1))],
        "encoder_forward",
    )


def run_tags_forward(x, w, gains, shifts):
    n, width = x.shape
    bf = lambda *s: Shape(s, BF)
    f32 = lambda *s: Shape(s, F32)
    vb = lambda *s: pltpu.VMEM(s, BF)
    vf = lambda *s: pltpu.VMEM(s, F32)
    return call(
        tags_forward,
        [(ANY, x), (ANY, w), (VM, gains), (VM, shifts)],
        [bf(n, width), bf(4, width, width), bf(3, n, width), bf(width, n), bf(HEADS, n, n), f32(HEADS, 1, n), f32(n, width)],
        [VM, ANY, ANY, ANY, ANY, VM, ANY],
        [vb(n, width), vb(width, 4, width), vb(4, width, width), vb(n, width), vb(n, width), vb(n, width),
         vb(width, n), vb(width, n), vb(width, n), vf(n, width), vb(4, n, n),
         pltpu.SemaphoreType.DMA((20,)), pltpu.SemaphoreType.DMA((4, n // 256))],
        "tags_forward",
    )


def run_decoder_middle(n_dp, n_bal, scalars, x1, mem, w, up, bias, down, gains, shifts, cot):
    n, width = x1.shape
    m = mem.shape[0]
    hidden = up.shape[1]
    piece = (n_dp // 2, 2, 4 * width // n_dp, width)
    bf = lambda *s: Shape(s, BF)
    f32 = lambda *s: Shape(s, F32)
    vb = lambda *s: pltpu.VMEM(s, BF)
    vf = lambda *s: pltpu.VMEM(s, F32)
    return call(
        functools.partial(decoder_middle, cot.shape[0] // n_bal),
        [(SM, v) for v in scalars]
        + [(ANY, x1), (ANY, mem), (ANY, w), (ANY, up), (VM, bias), (ANY, down), (VM, gains), (VM, shifts), (ANY, cot)],
        [bf(*cot.shape), f32(n, width), bf(n, width), bf(4, width, width), bf(n, width), bf(m, width), bf(m, width), bf(width, n),
         bf(HEADS, m, n), f32(HEADS, 1, n), bf(*piece), f32(1, hidden), f32(3, width), f32(4, width)],
        [VM] + [ANY] * 8 + [VM] * 5,
        [vb(n, width), vb(m, width), vb(width, 4, width), vb(4, width, width), vb(width, hidden), vb(hidden, width),
         vb(n, width), vb(m, width), vb(m, width), vb(width, n), vb(width, m), vb(width, n), vb(4, m, n),
         vf(n, width), vf(n, 1), vb(n, width), vb(n, hidden), vb(n, hidden), vf(n, width), vb(n, width),
         pltpu.SemaphoreType.DMA((20,)), pltpu.SemaphoreType.DMA((4, 1))],
        "decoder_middle",
    )


def run_backward(n_dp, n_bal, inputs, vectors, shapes):
    n, m, width, hidden, wide, blocks = shapes
    rows = 4 * width // n_dp
    bf = lambda *s: Shape(s, BF)
    f32 = lambda *s: Shape(s, F32)
    vb = lambda *s: pltpu.VMEM(s, BF)
    vf = lambda *s: pltpu.VMEM(s, F32)
    least = max(rows // 4, 16)
    whole, part, small = bf(n_bal, rows, 128), bf(n_bal, rows // 2, 128), bf(n_bal, least, 128)
    line, turned = vb(n, width), vb(width, n)
    piece = vb(n_dp // 2, 2, rows, width)
    return call(
        functools.partial(backward, n_dp, n_bal),
        [(ANY, item) for item in inputs] + [(VM, item) for item in vectors],
        [f32(m, width), f32(n, width), bf(*blocks), whole, whole, whole, part, part, small, small, small, small, f32(16, 128)],
        [ANY, ANY] + [VM] * 11,
        [vb(3, n, n), line, line, line, turned, turned, turned, line, vf(HEADS, 1, n), vb(width, max(n, hidden)), vb(max(n, hidden), width), line,
         vb(2, n, max(n, hidden)), line, vf(n, width), vf(n, width), vf(m, width), line, line, vb(m, width),
         vb(4, width, width), vb(4, width, width), piece, piece,
         vf(1, hidden), vf(2, width), vf(3, width), vf(n_dp, 16, 128), vf(3, n_dp, 16, 128), vf(n_dp // 2, 16, 128),
         vb(*kept_shape(n_dp, rows, False)), vb(*kept_shape(n_dp, rows // 2, False)),
         *room_scratch(n_dp, rows), *room_scratch(n_dp, rows),
         pltpu.SemaphoreType.DMA((40,)), pltpu.SemaphoreType.DMA((3, 4, n // 256)), pltpu.SemaphoreType.DMA((2 * n_bal,)),
         pltpu.SemaphoreType.DMA((6 + n_dp,)), *[piece_sems(n_dp, n_bal)] * 7,
         *late_scratch(n_dp, n_bal, least), *late_scratch(n_dp, n_bal, least)],
        "backward",
        pltpu.CompilerParams(vmem_limit_bytes=60 << 20, collective_id=1, has_side_effects=True),
    )


def run_finish(n_dp, hidden, width, gathered, moved):
    share = width // n_dp
    f32 = lambda *s: Shape(s, F32)
    side = [f32(share, 4, width)]
    branch = [f32(share, hidden), f32(1, hidden // n_dp), f32(hidden // n_dp, width)]
    outs = side + branch + [f32(2, share), f32(3, share)] + side + side + branch + [f32(3, share), f32(4, share)]
    return call(finish, [(VM, v) for v in gathered] + [(ANY, v) for v in moved],
                outs + [Shape(v.shape, v.dtype) for v in moved], [VM] * len(outs) + [ANY] * 3,
                [pltpu.VMEM(v.shape, v.dtype) for v in moved[::-1]] + [pltpu.SemaphoreType.DMA((6,))], "finish")


def swap_blocks(blocks):
    n = lax.axis_size("bal")
    me = lax.axis_index("bal")
    parts = blocks.reshape(n, blocks.shape[0] // n, *blocks.shape[1:])
    out = jnp.zeros_like(parts)
    out = lax.dynamic_update_index_in_dim(out, lax.dynamic_index_in_dim(parts, me, 0, False), me, 0)
    for k in range(1, n):
        got = lax.ppermute(lax.dynamic_index_in_dim(parts, (me + k) % n, 0, False), "bal", [(i, (i + k) % n) for i in range(n)])
        out = lax.dynamic_update_index_in_dim(out, got, (me - k) % n, 0)
    return out.reshape(blocks.shape)


def per_device(
    patches, tag_rows, cotangent, tag_length, cell_count, destination, slot_index,
    encoder_attention, encoder_up, encoder_up_bias, encoder_down, encoder_gains, encoder_shifts,
    decoder_self, decoder_cross, decoder_up, decoder_up_bias, decoder_down, decoder_gains, decoder_shifts,
):
    n_bal, n_dp = lax.axis_size("bal"), lax.axis_size("dp")
    length, width = tag_rows.shape[1:]
    hidden = encoder_up.shape[1]
    blocks = destination.shape[1]
    span = length // blocks
    cot = lax.all_to_all(cotangent[0].reshape(n_bal, length // n_bal, width), "bal", 0, 0, tiled=True)
    cot = cot.reshape(blocks, span, width)
    eg, es, dg, ds = encoder_gains.T, encoder_shifts.T, decoder_gains.T, decoder_shifts.T
    eb, db = encoder_up_bias[None], decoder_up_bias[None]
    memory, ew4, eqkv, eot, ee, erate, e1, e2, zb, act, slope = run_encoder_forward(
        patches[0], encoder_attention, encoder_up, eb, encoder_down, eg, es)
    x1, sw4, sqkv, sot, se, srate, a1 = run_tags_forward(tag_rows[0], decoder_self, dg, ds)
    y, da2, gb2, cw4, cq, ck, cv, c_ot, ce, crate, g_dffn, d_db, d_dg, d_ds = run_decoder_middle(
        n_dp, n_bal, (tag_length, cell_count, destination, slot_index), x1, memory, decoder_cross, decoder_up, db,
        decoder_down, dg, ds, cot)
    d_patches, d_tags, decoded, all_cross, all_dffn, *gathered = run_backward(
        n_dp, n_bal,
        (da2, gb2, x1, memory, cw4, cq, ck, cv, c_ot, ce, y, g_dffn,
         e2, e1, zb, act, slope, encoder_up, encoder_down, patches[0], ew4, eqkv, eot, ee,
         a1, tag_rows[0], sw4, sqkv, sot, se),
        (crate, erate, srate, eg, dg, d_db, d_dg, d_ds),
        (length, patches.shape[1], width, hidden, eot.shape[1], y.shape))
    ew, eu, ebg, ed, egg, esg, sw, cw, du, dbg, dd, dgg, dsg, decoded, d_patches, d_tags = run_finish(
        n_dp, hidden, width, (all_cross, all_dffn, *gathered), (decoded, d_patches, d_tags))
    return (
        decoded.reshape(1, length, width), d_patches[None], d_tags[None],
        ew, eu, ebg.reshape(-1), ed, egg.T, esg.T, sw, cw, du, dbg.reshape(-1), dd, dgg.T, dsg.T,
    )


def solution(mesh):
    split = P(("dp", "bal"))
    in_specs = (split,) * 7 + (P(),) * 13
    out_specs = (split,) * 3 + (P("dp"),) * 13
    return jax.shard_map(per_device, mesh=mesh, in_specs=in_specs, out_specs=out_specs, check_vma=False)
```

```python
import functools

import jax
import jax.numpy as jnp
from jax import lax
from jax.experimental import pallas as pl
from jax.experimental.pallas import tpu as pltpu
from jax.sharding import PartitionSpec as P

HEADS = 8
HEAD = 64
EPSILON = 1e-05
NEGATIVE = -1e30
BF = jnp.bfloat16
F32 = jnp.float32
NN = (((1,), (0,)), ((), ()))
NT = (((1,), (1,)), ((), ()))
TN = (((0,), (0,)), ((), ()))
TT = (((0,), (1,)), ((), ()))
VM = pl.BlockSpec(memory_space=pltpu.VMEM)
SM = pl.BlockSpec(memory_space=pltpu.SMEM)
ANY = pl.BlockSpec(memory_space=pl.ANY)
LIMIT = 1e18
PARAMS = pltpu.CompilerParams(vmem_limit_bytes=60 << 20)
Shape = jax.ShapeDtypeStruct


def mm(left, right, dims=NN):
    return lax.dot_general(left, right, dims, preferred_element_type=F32)


def cut(rows):
    half = (rows // 2 + 15) // 16 * 16
    return [(0, half), (half, rows - half)]


class Copies:
    def __init__(self, sems):
        self.sems, self.used, self.open = sems, 0, []

    def start(self, source, target):
        copy = pltpu.make_async_copy(source, target, self.sems.at[self.used])
        self.used += 1
        copy.start()
        return copy

    def out(self, source, target):
        self.open.append(self.start(source, target))

    def finish(self):
        for copy in self.open:
            copy.wait()


def split_weights(raw, parts):
    def step(i, carry):
        rows = pl.ds(pl.multiple_of(i * 128, 128), 128)
        parts[:, rows, :] = pltpu.einshape("abc->bac", raw[rows])
        return carry

    lax.fori_loop(0, raw.shape[0] // 128, step, 0)


def normalise(signal):
    centre = jnp.mean(signal, axis=-1, keepdims=True)
    centered = signal - centre
    spread = jnp.mean(centered * centered, axis=-1, keepdims=True)
    rate = lax.rsqrt(spread + EPSILON)
    return centered * rate, rate


def norm_back(unit, rate, gain, gradient):
    inner = gradient * gain
    first = jnp.mean(inner, axis=-1, keepdims=True)
    second = jnp.mean(inner * unit, axis=-1, keepdims=True)
    return rate * (inner - first - unit * second)


def colsum(signal):
    return jnp.sum(signal, axis=0, keepdims=True)


def smooth(hidden):
    scale = 0.7978845608028654
    square = hidden * hidden
    curve = jnp.tanh(scale * hidden * (1.0 + 0.044715 * square))
    half = 0.5 + 0.5 * curve
    slope = half + 0.5 * hidden * (1.0 - curve * curve) * (scale + (3 * 0.044715 * scale) * square)
    return hidden * half, slope


def half_mask(shape, axis, which):
    index = lax.broadcasted_iota(jnp.int32, shape, axis)
    return (index < HEAD) if which == 0 else (index >= HEAD)


def keep_half(pair, axis, which):
    return jnp.where(half_mask(pair.shape, axis, which), pair, jnp.zeros_like(pair))


def project_qkv(x, sources, w4, q, qt, k, v, vt):
    rows = x.shape[0]
    for start, size in cut(rows):
        part = slice(start, start + size)
        q[part] = (mm(x[part], w4[0]) * HEAD ** (-0.5)).astype(BF)
    if q.shape[0] > rows:
        q[rows:] = jnp.zeros((q.shape[0] - rows, q.shape[1]), BF)
    for start, size in cut(sources.shape[0]):
        part = slice(start, start + size)
        k[part] = mm(sources[part], w4[1]).astype(BF)
        v[part] = mm(sources[part], w4[2]).astype(BF)
    qt[...] = q[...].T
    vt[...] = v[...].T


def shifted_exp(scores, exact, causal_rows):
    if causal_rows:
        size, width = scores.shape
        key = lax.broadcasted_iota(jnp.int32, (width, width), 0)
        query = lax.broadcasted_iota(jnp.int32, (width, width), 1)
        last = jnp.where(key <= query, scores[size - width :], NEGATIVE)
        scores = last if size == width else jnp.concatenate([scores[: size - width], last], axis=0)
        exact = exact or size == width
    sample = scores if exact else scores[:128]
    return jnp.exp(scores - jnp.max(sample, axis=0, keepdims=True))


def attend_heads(exact, causal, q_tile, qt, k, vt, ot, rate, store, beside=None):
    keys, queries = k.shape[0], qt.shape[1]

    def pair(p, carry):
        lanes = pl.ds(pl.multiple_of(p * 128, 128), 128)
        if beside is not None:
            beside(p)
        for u in range(2):
            rows = pl.ds(pl.multiple_of(p * 128 + u * HEAD, HEAD), HEAD)
            place, done = store(p, u)
            for start in range(0, queries, q_tile):
                cols = slice(start, start + q_tile)
                depth = start + q_tile if causal else keys
                scores = mm(k[:depth, lanes], keep_half(qt[lanes, cols], 0, u))
                raised = shifted_exp(scores, exact, causal)
                total = jnp.sum(raised, axis=0, keepdims=True)
                low = raised.astype(BF)
                place[:depth, cols] = low
                inverse = 1.0 / total
                rate[2 * p + u, :, cols] = inverse
                ot[rows, cols] = (mm(vt[rows, :depth], low) * inverse).astype(BF)
            done()
        return carry

    lax.fori_loop(0, HEADS // 2, pair, 0)


def attend(causal, q_tile, qt, k, vt, ot, rate, store, drain):
    attend_heads(False, causal, q_tile, qt, k, vt, ot, rate, store)
    drain()
    fine = jnp.min(rate[...]) > 1.0 / LIMIT

    @pl.when(jnp.logical_not(fine))
    def _():
        attend_heads(True, causal, q_tile, qt, k, vt, ot, rate, store)
        drain()


def back_heads(causal, q_tile, q, kt, v, dot_, d_o, rowdot, fetch, ds, dqt, dk, dv, hook=None):
    keys, queries = v.shape[0], dqt.shape[1]

    def pair(p, carry):
        lanes = pl.ds(pl.multiple_of(p * 128, 128), 128)
        for u in range(2):
            rows = pl.ds(pl.multiple_of(p * 128 + u * HEAD, HEAD), HEAD)
            place = fetch(p, u)
            for start in range(0, queries, q_tile):
                cols = slice(start, start + q_tile)
                depth = start + q_tile if causal else keys
                grad = mm(v[:depth, lanes], keep_half(dot_[lanes, cols], 0, u))
                scaled = place[:depth, cols].astype(F32) * (grad - rowdot[2 * p + u, :, cols])
                low = scaled.astype(BF)
                ds[u][:depth, cols] = low
                dqt[rows, cols] = (mm(kt[rows, :depth], low) * HEAD ** (-0.5)).astype(BF)
            qm = q[:queries, lanes]
            dm = d_o[:queries, lanes]
            steps = range(0, keys, q_tile) if causal else (0,)
            for start in steps:
                key = slice(start, start + q_tile) if causal else slice(0, keys)
                more_k = mm(ds[u][key, start:queries], qm[start:])
                more_v = mm(place[key, start:queries], dm[start:])
                if u == 0:
                    dk[key, lanes] = more_k.astype(BF)
                    dv[key, lanes] = more_v.astype(BF)
                else:
                    dk[key, lanes] = jnp.where(half_mask(more_k.shape, 1, 1), more_k.astype(BF), dk[key, lanes])
                    dv[key, lanes] = jnp.where(half_mask(more_v.shape, 1, 1), more_v.astype(BF), dv[key, lanes])
            if hook is not None:
                for at, act in hook.items():
                    if at % 2 == u:
                        pl.when(p == at // 2)(act)
        return carry

    lax.fori_loop(0, HEADS // 2, pair, 0)


def back_outputs(grad_low, w4, ot, rate, dot_, d_o, rowdot):
    rows, wide = grad_low.shape[0], dot_.shape[1]
    raw = mm(w4[3], grad_low[...], NT)
    for h in range(HEADS):
        part = slice(h * HEAD, (h + 1) * HEAD)
        low = (raw[part] * rate[h][:, :rows]).astype(BF)
        if wide > rows:
            low = jnp.concatenate([low, jnp.zeros((HEAD, wide - rows), BF)], axis=1)
        dot_[part] = low
        rowdot[h] = jnp.sum(low.astype(F32) * ot[part].astype(F32), axis=0, keepdims=True)
    d_o[...] = dot_[...].T


def ring(buffers, hbm, sems, spans, out):
    def copies(h, slot):
        made = []
        for i, (rows, cols) in enumerate(spans):
            here = buffers.at[slot, pl.ds(0, rows), cols]
            there = hbm.at[h, pl.ds(0, rows), cols]
            made.append(
                pltpu.make_async_copy(here, there, sems.at[slot, i])
                if out
                else pltpu.make_async_copy(there, here, sems.at[slot, i])
            )
        return made

    return copies


def out_ring(buffers, hbm, sems, spans):
    copies = ring(buffers, hbm, sems, spans, True)

    def store(p, u):
        slot = (p % 2) * 2 + u

        @pl.when(p >= 2)
        def _():
            for copy in copies(2 * p + u, slot):
                copy.wait()

        def done():
            for copy in copies(2 * p + u, slot):
                copy.start()

        return buffers.at[slot], done

    def drain():
        for slot in range(4):
            for copy in copies(slot, slot):
                copy.wait()

    return store, drain


def in_ring(buffers, hbm, sems, spans):
    copies = ring(buffers, hbm, sems, spans, False)
    depth = buffers.shape[0]

    def begin():
        for h in range(depth):
            for copy in copies(h, h):
                copy.start()

    def fetch(p, u):
        h = 2 * p + u
        for copy in copies(h, h % depth):
            copy.wait()

        @pl.when((h >= 1) & (h + depth <= HEADS))
        def _():
            for copy in copies(h + depth - 1, (h + depth - 1) % depth):
                copy.start()

        return buffers.at[h % depth]

    return begin, fetch


MESH = pl.DeviceIdType.MESH


class Spot:
    def __init__(self, n, m):
        self.n, self.m = n, m
        self.d, self.b = lax.axis_index("dp"), lax.axis_index("bal")
        self.core, self.far = self.b % 2, self.b // 2
        self.parity, self.row = self.d % 2, self.d // 2
        self.by_core = (self.d, self.b + 1 - 2 * self.core)
        self.by_far = (self.d, self.b + 2 - 4 * self.far)
        self.by_parity = (self.d + 1 - 2 * self.parity, self.b)

    def greet(self, everyone=True):
        barrier = pltpu.get_barrier_semaphore()

        def call(device):
            pl.semaphore_signal(barrier, inc=1, device_id=device, device_id_type=MESH)

        for k in range(1, self.m):
            call((self.d, (self.b + k) % self.m))

        if not everyone:
            return
        call(self.by_parity)
        call((self.by_parity[0], self.by_far[1]))

        def along(k, carry):
            call((((self.row + k) % (self.n // 2)) * 2 + self.parity, self.b))
            return carry

        lax.fori_loop(1, self.n // 2, along, 0)

    def await_all(self, everyone=True):
        pl.semaphore_wait(pltpu.get_barrier_semaphore(), self.m - 1 + (2 + self.n // 2 - 1 if everyone else 0))


def remote(source, target, sent, received, device):
    return pltpu.make_async_remote_copy(
        src_ref=source, dst_ref=target, send_sem=sent, recv_sem=received, device_id=device, device_id_type=MESH
    )


class Piece:
    def __init__(self, spot, along_x, sems, source=None, acc=None, land_a=None, kept=None, land_b=None, kept2=None,
                 land_c=None, slots=None, result=None, gathered=None):
        self.spot, self.along_x, self.source, self.sems = spot, along_x, source, sems
        self.acc, self.land_a, self.kept, self.land_b = acc, land_a, kept, land_b
        self.kept2, self.land_c = kept2, land_c
        self.slots, self.result, self.gathered = slots, result, gathered

    def a_copies(self):
        half = self.acc.shape[3]
        mine = pl.ds(pl.multiple_of(self.spot.core * half, half), half)
        other = pl.ds(pl.multiple_of((1 - self.spot.core) * half, half), half)
        return [
            pltpu.make_async_copy(self.source.at[:, :, :, mine], self.acc, self.sems.at[0]),
            remote(self.source.at[:, :, :, other], self.land_a, self.sems.at[1], self.sems.at[2], self.spot.by_core),
        ]

    def a_start(self):
        for copy in self.a_copies():
            copy.start()

    def a_wait(self):
        for copy in self.a_copies():
            copy.wait()

        def add(i, carry):
            self.acc[i] = self.acc[i] + self.land_a[i]
            return carry

        lax.fori_loop(0, self.acc.shape[0], add, 0)

    def lanes(self, mine, size):
        side = self.spot.far if mine else 1 - self.spot.far
        return pl.ds(pl.multiple_of(side * size, size), size)

    def b_copy(self):
        spot = self.spot
        if self.along_x:
            out, to = self.acc.at[:, :, :, self.lanes(False, self.land_b.shape[3])], spot.by_far
        else:
            out, to = self.acc.at[:, 1 - spot.parity], spot.by_parity
        return remote(out, self.land_b, self.sems.at[3], self.sems.at[4], to)

    def b_start(self):
        self.b_copy().start()

    def b_wait(self):
        self.b_copy().wait()

        def add(i, carry):
            if self.along_x:
                mine = self.acc[i, :, :, self.lanes(True, self.land_b.shape[3])]
            else:
                mine = self.acc[i, self.spot.parity]
            self.kept[i] = mine + self.land_b[i]
            return carry

        lax.fori_loop(0, self.kept.shape[0], add, 0)

    def bb_copy(self):
        spot = self.spot
        if self.along_x:
            out, to = self.kept.at[:, 1 - spot.parity], spot.by_parity
        else:
            out, to = self.kept.at[:, :, self.lanes(False, self.land_c.shape[2])], spot.by_far
        return remote(out, self.land_c, self.sems.at[5], self.sems.at[6], to)

    def bb_start(self):
        self.bb_copy().start()

    def bb_wait(self):
        self.bb_copy().wait()

        def add(i, carry):
            if self.along_x:
                mine = self.kept[i, self.spot.parity]
            else:
                mine = self.kept[i, :, self.lanes(True, self.land_c.shape[2])]
            self.kept2[i] = mine + self.land_c[i]
            return carry

        lax.fori_loop(0, self.kept2.shape[0], add, 0)

    def base(self):
        return 7

    def c_copy(self, k, arriving):
        spot, half = self.spot, self.spot.n // 2
        row = (spot.row + k) % half
        slot = row if arriving else spot.row
        return remote(self.kept2.at[row], self.slots.at[slot], self.sems.at[self.base() + k], self.sems.at[self.base() + half + slot],
                      (row * 2 + spot.parity, spot.b))

    def c_start(self):
        def step(k, carry):
            self.c_copy(k, False).start()
            return carry

        lax.fori_loop(1, self.spot.n // 2, step, 0)

    def c_wait(self):
        half, row = self.spot.n // 2, self.spot.row

        def step(k, total):
            self.c_copy(k, False).wait_send()
            self.c_copy(k, True).wait_recv()
            return total + self.slots[(row + k) % half].astype(F32)

        total = lax.fori_loop(1, half, step, self.kept2[row].astype(F32))
        self.result[...] = total.astype(BF)

    def d_copies(self, arriving):
        spot, base = self.spot, self.base() + self.spot.n
        made = []
        for k in range(1, spot.m):
            peer = (spot.b + k) % spot.m
            slot = peer if arriving else spot.b
            made.append(remote(self.result, self.gathered.at[slot], self.sems.at[base + k],
                               self.sems.at[base + spot.m + slot], (spot.d, peer)))
        return made

    def d_start(self):
        for copy in self.d_copies(False):
            copy.start()
        self.gathered[self.spot.b] = self.result[...]

    def d_wait(self):
        for copy in self.d_copies(False):
            copy.wait_send()
        for copy in self.d_copies(True):
            copy.wait_recv()


class PairPiece(Piece):
    def __init__(self, spot, sems, source, acc, land_a, quads, kept2, slots, result, gathered):
        super().__init__(spot, True, sems, source, acc, land_a, kept2=kept2, slots=slots, result=result, gathered=gathered)
        self.quads = quads

    def base(self):
        return 11

    def quarter(self, far):
        lanes = self.kept2.shape[2]
        return pl.ds(pl.multiple_of(far * lanes, lanes), lanes)

    def q_copy(self, k, arriving):
        spot = self.spot
        me = spot.far * 2 + spot.parity
        peer = (me + k) % 4
        far, parity = peer // 2, peer % 2
        slot = peer if arriving else me
        return remote(self.acc.at[:, parity, :, self.quarter(far)], self.quads.at[slot], self.sems.at[3 + k],
                      self.sems.at[7 + slot], (spot.row * 2 + parity, spot.core + 2 * far))

    def q_start(self):
        for k in range(1, 4):
            self.q_copy(k, False).start()

    def q_wait(self):
        spot = self.spot
        me = spot.far * 2 + spot.parity
        for k in range(1, 4):
            self.q_copy(k, False).wait_send()
            self.q_copy(k, True).wait_recv()

        def add(i, carry):
            total = self.acc[i, spot.parity, :, self.quarter(spot.far)].astype(F32)
            for k in range(1, 4):
                total = total + self.quads[(me + k) % 4, i].astype(F32)
            self.kept2[i] = total.astype(BF)
            return carry

        lax.fori_loop(0, self.kept2.shape[0], add, 0)


def pair_scratch(n, m, rows, whole):
    vb = lambda shape: pltpu.VMEM(shape, BF)
    first = [vb((n // 2, 2, rows, 512)), vb(half_shape(n, rows)), vb(half_shape(n, rows))] if whole else []
    return first + [vb((4, *last_shape(n, rows))), vb(last_shape(n, rows)), vb(last_shape(n, rows)), vb((rows, 128)),
                    pltpu.SemaphoreType.DMA((11 + n + 2 * m,))]


def piece_sems(n, m):
    return pltpu.SemaphoreType.DMA((7 + n + 2 * m,))


def half_shape(n, rows):
    return (n // 2, 2, rows, 256)


def kept_shape(n, rows, along_x):
    return (n // 2, 2, rows, 128) if along_x else (n // 2, rows, 256)


def last_shape(n, rows):
    return (n // 2, rows, 128)


class VectorSum:
    def __init__(self, spot, v, lands, slots, result, sems):
        self.spot, self.v, self.lands, self.slots, self.result, self.sems = spot, v, lands, slots, result, sems

    def swap(self, step):
        device = (self.spot.by_core, self.spot.by_far, self.spot.by_parity)[step]
        return remote(self.v, self.lands.at[step], self.sems.at[2 * step], self.sems.at[2 * step + 1], device)

    def swap_start(self, step):
        self.swap(step).start()

    def swap_wait(self, step):
        self.swap(step).wait()
        self.v[...] = self.v[...] + self.lands[step]

    def copy(self, k, arriving):
        spot, half = self.spot, self.spot.n // 2
        row = (spot.row + k) % half
        slot = row if arriving else spot.row
        return remote(self.v.at[row * 2 + spot.parity], self.slots.at[slot], self.sems.at[6 + k],
                      self.sems.at[6 + half + slot], (row * 2 + spot.parity, spot.b))

    def c_start(self):
        def step(k, carry):
            self.copy(k, False).start()
            return carry

        lax.fori_loop(1, self.spot.n // 2, step, 0)

    def c_wait(self):
        half, row = self.spot.n // 2, self.spot.row

        def step(k, total):
            self.copy(k, False).wait_send()
            self.copy(k, True).wait_recv()
            return total + self.slots[(row + k) % half]

        self.result[...] = lax.fori_loop(1, half, step, self.v[self.spot.d])


def put(piece, row, value, lane=0):
    halves, two, width = piece.shape[0], piece.shape[1], value.shape[1]
    rows = value.shape[0] // (halves * two)
    piece[:, :, row : row + rows, lane : lane + width] = value.reshape(halves, two, rows, width).astype(BF)


def split_part(raw, parts, p):
    rows = pl.ds(pl.multiple_of(p * 128, 128), 128)
    parts[:, rows, :] = pltpu.einshape("abc->bac", raw[rows])


def tags_forward(n_dp, n_bal, x_h, w_h, ew_h, cw_h, cot_h, gains, shifts,
                 x1, cot, rate, w4_h, ew4_h, cw4_h, qkv_h, ot_h, e_h, a1_h,
                 x, raw, w4, raw_e, ew4, raw_c, cw4, q, k, v, qt, vt, ot, a1, ering, sems, esems, moves):
    spot = Spot(n_dp, n_bal)
    spot.greet(False)
    c = Copies(sems)
    load_w = c.start(w_h, raw)
    load_x = c.start(x_h, x)
    load_e, load_c = c.start(ew_h, raw_e), c.start(cw_h, raw_c)
    load_w.wait()
    split_weights(raw, w4)
    c.out(w4, w4_h)
    load_x.wait()
    project_qkv(x, x, w4, q, qt, k, v, vt)
    n = x.shape[0]
    for i, item in enumerate((q, k, v)):
        c.out(item, qkv_h.at[i])
    spot.await_all(False)
    share = cot_h.shape[0] // n_bal

    def moved(step, arriving):
        peer = (spot.b + step) % n_bal
        slot = peer if arriving else spot.b
        return remote(cot_h.at[pl.ds(peer * share, share)], cot.at[pl.ds(slot * share, share)], moves.at[step],
                      moves.at[n_bal + slot], (spot.d, peer))

    own = pl.ds(spot.b * share, share)
    own_copy = pltpu.make_async_copy(cot_h.at[own], cot.at[own], moves.at[0])
    own_copy.start()
    for step in range(1, n_bal):
        moved(step, False).start()
    load_e.wait()
    load_c.wait()

    def beside(p):
        split_part(raw_e, ew4, p)
        split_part(raw_c, cw4, p)

    tile = 256
    spans = [(start + tile, slice(start, start + tile)) for start in range(0, n, tile)]
    store, drain = out_ring(ering, e_h, esems, spans)
    attend_heads(True, True, tile, qt, k, vt, ot, rate, store, beside)
    drain()
    c.out(ew4, ew4_h)
    c.out(cw4, cw4_h)
    c.out(ot, ot_h)
    for start, size in cut(n):
        part = slice(start, start + size)
        first = x[part].astype(F32) + mm(ot[:, part], w4[3], TN)
        a1[part] = first
        unit, _ = normalise(first)
        x1[part] = (unit * gains[0:1] + shifts[0:1]).astype(BF)
    c.out(a1, a1_h)
    own_copy.wait()
    for step in range(1, n_bal):
        moved(step, False).wait_send()
        moved(step, True).wait_recv()
    c.finish()


def forward(capacity, tag_length, cell_count, destination, slot_index,
            x_h, ew4_h, eup_h, ebias, edown_h, egains, eshifts,
            x1_h, cw4_h, up_h, bias, down_h, gains, shifts, cot_h,
            erate, rate, g_ffn, d_bias, d_gains, d_shifts, y,
            mem_h, eqkv_h, eot_h, ee_h, e1_h, e2_h, zb_h, eact_h, eslope_h,
            da_h, gb_h, q_h, k_h, v_h, ot_h, e_h,
            x, ew4, eup, edown, q, k, v, qt, vt, ot, ering, e1, e2, zb, eact, eslope,
            x1, mem, w4, up, down, unit2, rate2, xb2, act, slope, da, gb, sems, esems):
    cot, dh = y, slope
    c = Copies(sems)
    load_w = c.start(ew4_h, ew4)
    load_x = c.start(x_h, x)
    load_eup = c.start(eup_h, eup)
    load_edown = c.start(edown_h, edown)
    load_w.wait()
    load_x.wait()
    m, n = x.shape[0], x1.shape[0]
    wide = eot_h.shape[1]
    eq, eqt, eot = q.at[pl.ds(0, wide)], qt.at[:, pl.ds(0, wide)], ot.at[:, pl.ds(0, wide)]
    project_qkv(x, x, ew4, eq, eqt, k, v, vt)
    spent = [c.start(item, eqkv_h.at[i]) for i, item in enumerate((q.at[pl.ds(0, m)], k, v))]
    load_w = c.start(cw4_h, w4)
    load_x1 = c.start(x1_h, x1)
    load_up = c.start(up_h, up)
    load_down = c.start(down_h, down)
    load_cot = c.start(cot_h, cot)
    view = ering.at[:, :, pl.ds(0, wide)]
    store, drain = out_ring(view, ee_h, esems, [(m, slice(None))])
    attend(False, wide, eqt, k, vt, eot, erate, store, drain)
    spent.append(c.start(eot, eot_h))
    load_eup.wait()
    load_edown.wait()
    for start, size in cut(m):
        part = slice(start, start + size)
        first = x[part].astype(F32) + mm(ot[:, part], ew4[3], TN)
        e1[part] = first
        unit, _ = normalise(first)
        z = unit * egains[0:1] + eshifts[0:1]
        low = z.astype(BF)
        zb[part] = low
        active, bend = smooth(mm(low, eup[...]) + ebias[...])
        eact[part] = active.astype(BF)
        eslope[part] = bend.astype(BF)
        second = z + mm(eact[part], edown[...]) + eshifts[2:3]
        e2[part] = second
        unit, _ = normalise(second)
        mem[part] = (unit * egains[1:2] + eshifts[1:2]).astype(BF)
    for here, there in ((e1, e1_h), (e2, e2_h), (zb, zb_h), (eact, eact_h), (eslope, eslope_h), (mem, mem_h)):
        c.out(here, there)

    load_w.wait()
    load_x1.wait()
    for copy in spent:
        copy.wait()
    project_qkv(x1, mem, w4, q, qt, k, v, vt)
    for here, there in ((q, q_h), (k, k_h), (v, v_h)):
        c.out(here, there)
    blocks = y.shape[0]
    block = n // blocks
    store, drain = out_ring(ering, e_h, esems, [(m, slice(None))])
    attend(False, n, qt, k, vt, ot, rate, store, drain)
    c.out(ot, ot_h)
    load_up.wait()
    load_down.wait()
    load_cot.wait()
    live = tag_length[0] + cell_count[0]
    places = [destination[0, b] * capacity + slot_index[0, b] for b in range(blocks)]
    zero = jnp.zeros((1, x1.shape[1]), F32)
    gain3, shift3 = zero, zero
    for start, size in cut(n):
        part = slice(start, start + size)
        second = x1[part].astype(F32) + mm(ot[:, part], w4[3], TN)
        unit, pace = normalise(second)
        unit2[part] = unit
        rate2[part] = pace
        x2 = unit * gains[1:2] + shifts[1:2]
        low = x2.astype(BF)
        xb2[part] = low
        active, bend = smooth(mm(low, up[...]) + bias[...])
        act[part] = active.astype(BF)
        slope[part] = bend.astype(BF)
        third = x2 + mm(act[part], down[...]) + shifts[3:4]
        unit, pace = normalise(third)
        row = lax.broadcasted_iota(jnp.int32, (size, 1), 0) + start
        alive = (row < live).astype(F32)
        final = ((unit * gains[2:3] + shifts[2:3]) * alive).astype(BF)
        picked = []
        for b in range(start // block, (start + size) // block):
            picked.append(cot[places[b]])
            y[places[b]] = final[b * block - start : (b + 1) * block - start]
        dy = jnp.concatenate(picked, axis=0).astype(F32) * alive
        gain3 += colsum(dy * unit)
        shift3 += colsum(dy)
        d3 = norm_back(unit, pace, gains[2:3], dy)
        da[part] = d3
        gb[part] = d3.astype(BF)
    d_gains[2:3] = gain3
    d_shifts[2:3] = shift3
    ffn_back(xb2, up, down, act, slope, gb, dh, g_ffn, d_bias, d_shifts, 3)
    gain2, shift2 = zero, zero
    for start, size in cut(n):
        part = slice(start, start + size)
        dx2 = da[part] + mm(dh[part], up[...], NT)
        gain2 += colsum(dx2 * unit2[part])
        shift2 += colsum(dx2)
        d2 = norm_back(unit2[part], rate2[part], gains[1:2], dx2)
        da[part] = d2
        gb[part] = d2.astype(BF)
    d_gains[1:2] = gain2
    d_shifts[1:2] = shift2
    c.out(gb, gb_h)
    c.out(da, da_h)
    c.finish()


def ffn_back(xb, up, down, act, slope, gb, dh, g_ffn, d_bias, d_shifts, row, middle=None):
    n, width = xb.shape
    offset = jnp.zeros((1, up.shape[1]), F32)
    for start, size in cut(n):
        part = slice(start, start + size)
        low = (mm(gb[part], down[...], NT) * slope[part].astype(F32)).astype(BF)
        dh[part] = low
        offset += colsum(low.astype(F32))
    d_bias[...] = offset
    d_shifts[row : row + 1] = colsum(gb[...].astype(F32))
    if middle is not None:
        middle()
    rows = g_ffn.shape[2] // 4
    put(g_ffn, 2 * rows, mm(act[...], gb[...], TN))
    for j in range(up.shape[1] // width):
        put(g_ffn, j * rows, mm(xb[...], dh[:, j * width : (j + 1) * width], TN))


class Room:
    def __init__(self, acc, land, kept, next_, kept_x, next_x, kept2, last, slots, result):
        self.acc, self.land, self.kept, self.next = acc, land, kept, next_
        self.kept_x, self.next_x, self.kept2, self.last, self.slots, self.result = kept_x, next_x, kept2, last, slots, result

    def whole(self, spot, sems, source, gathered):
        return Piece(spot, False, sems, source, self.acc, self.land, self.kept, self.next, self.kept2, self.last,
                     self.slots, self.result, gathered)

    def part(self, spot, sems, source, gathered, along_x, start, size):
        rows, head = pl.ds(start, size), pl.ds(0, size)
        kept = self.kept_x.at[:, :, head] if along_x else self.kept.at[:, rows]
        next_ = self.next_x.at[:, :, head] if along_x else self.next.at[:, rows]
        return Piece(spot, along_x, sems, source, self.acc.at[:, :, rows], self.land.at[:, :, rows], kept, next_,
                     self.kept2.at[:, rows], self.last.at[:, rows], self.slots.at[:, rows], self.result.at[rows], gathered)


def room_scratch(n, rows):
    vb = lambda shape: pltpu.VMEM(shape, BF)
    last, side = vb(last_shape(n, rows)), vb(kept_shape(n, rows // 2, True))
    kept = vb(kept_shape(n, rows, False))
    return [vb(half_shape(n, rows)), vb(half_shape(n, rows)), kept, kept, side, side, last, last, last, vb((rows, 128))]


def backward(n_dp, n_bal,
             da_h, gb_h, x1_h, mem_h, cw4_h, cq_h, ck_h, cv_h, cot_h, ce_h, y_h, g_dffn,
             e2_h, e1_h, zb_h, act_h, slope_h, up_h, down_h, ex_h, ew4_h, eqkv_h, eot_h, ee_h,
             a1_h, tx_h, tw4_h, tqkv_h, tot_h, te_h,
             crate, erate, trate, egains, dgains, d_bias_d, d_gains_d, d_shifts_d,
             dx_enc_h, dx_tags_h, dx1_h, decoded, all_cross, all_dffn, all_effn, all_enc0, all_enc1, *rest_refs):
    all_self, v_total = rest_refs[:4], rest_refs[4]
    (ering, q, k, v, ot, kt, dot_, d_o, rowdot, dqt, dk, dv, ds, gb, da, wide0, wide1, x0, x1,
     wa, wb, g0, g1, d_bias, d_gains, d_shifts, vec, vec_lands, vec_slots, next_effn, next_enc1, *rest) = rest_refs[5:]
    room0, room1 = Room(*rest[:10]), Room(*rest[10:20])
    sems, esems, moves, vsems = rest[20:24]
    psems = rest[24:29]
    early, late = [rest[29:34], rest[34:39]], [rest[39:47], rest[47:55]]
    spot = Spot(n_dp, n_bal)
    spot.greet()
    c = Copies(sems)
    n, width = x0.shape
    m = x1.shape[0]
    wide = eot_h.shape[1]
    hidden = up_h.shape[1]
    size = g0.shape[2] // 2
    rows = size // 2
    half = width // 2
    low, high = pl.ds(0, size), pl.ds(size, size)
    least = all_self[0].shape[1]
    dffn = room0.whole(spot, psems[0], g_dffn, all_dffn)
    cross = room1.whole(spot, psems[1], g0, all_cross)
    effn = room0.whole(spot, psems[2], g1, all_effn)
    effn.land_b = next_effn
    enc0 = room1.part(spot, psems[3], g0.at[:, :, low], all_enc0, True, 0, size)
    enc1 = room1.part(spot, psems[4], g0.at[:, :, high], all_enc1, False, size, size)
    enc1.land_b = next_enc1
    pairs = []
    for i, gathered in enumerate(all_self):
        if i < 2:
            where = pl.ds(i * least, least)
            first = g1.at[:, :, where], room0.acc.at[:, :, where], room0.land.at[:, :, where]
            others = early[i]
        else:
            first, others = late[i - 2][:3], late[i - 2][3:]
        pairs.append(PairPiece(spot, others[4], *first, *others[:4], gathered))
    pair0, pair1, pair2, pair3 = pairs
    vector = VectorSum(spot, vec, vec_lands, vec_slots, v_total, vsems)
    zero = jnp.zeros((1, width), F32)
    pair_ds = ds.at[0], ds.at[1]

    load_gb = c.start(gb_h, gb)
    load_ot = c.start(cot_h, ot)
    load_w = c.start(cw4_h, wa)
    loads = [c.start(a, b) for a, b in ((ck_h, k.at[pl.ds(0, m)]), (cv_h, v.at[pl.ds(0, m)]), (cq_h, q))]
    begin, fetch = in_ring(ering, ce_h, esems.at[0], [(m, slice(0, n))])
    begin()
    last = [c.start(a, b) for a, b in ((x1_h, x0), (mem_h, x1), (da_h, da))]
    load_ew = c.start(ew4_h, wb)
    load_e2 = c.start(e2_h, wide0.at[pl.ds(0, m)])
    load_gb.wait()
    load_ot.wait()
    put(g0, 3 * rows, mm(ot[...], gb[...]))
    load_w.wait()
    back_outputs(gb, wa, ot, crate, dot_, d_o, rowdot)
    for load in loads:
        load.wait()
    kt[:, :m] = k[:m].T
    spot.await_all()
    dffn.a_start()
    share = y_h.shape[0] // n_bal

    def moved(step, arriving):
        peer = (spot.b + step) % n_bal
        slot = peer if arriving else spot.b
        return remote(y_h.at[pl.ds(peer * share, share)], decoded.at[pl.ds(slot * share, share)], moves.at[step],
                      moves.at[n_bal + slot], (spot.d, peer))

    own = pl.ds(spot.b * share, share)
    own_copy = pltpu.make_async_copy(y_h.at[own], decoded.at[own], moves.at[0])
    own_copy.start()
    for step in range(1, n_bal):
        moved(step, False).start()

    def cross1():
        dffn.a_wait()
        dffn.b_start()

    keys = pl.ds(0, m)
    back_heads(False, n, q, kt, v.at[keys], dot_, d_o, rowdot, fetch, pair_ds, dqt, dk.at[keys], dv.at[keys],
               {1: cross1})
    for load in last:
        load.wait()
    put(g0, 0, mm(x0[...], dqt[...], TT))
    put(g0, rows, mm(x1[...], dk[:m], TN))
    put(g0, 2 * rows, mm(x1[...], dv[:m], TN))
    cross.a_start()
    dffn.b_wait()
    dffn.bb_start()
    for start, count in cut(m):
        part = slice(start, start + count)
        wide1[part] = mm(dk[part], wa[1], NT) + mm(dv[part], wa[2], NT)
    for start, count in cut(n):
        part = slice(start, start + count)
        d_o[part] = (da[part] + mm(dqt[:, part], wa[0], TT)).astype(BF)
    save_dx1 = c.start(d_o, dx1_h)
    act, slope = ds.at[0, keys, pl.ds(0, hidden)], ds.at[1, keys, pl.ds(0, hidden)]
    up, down, zb = dqt.at[:, pl.ds(0, hidden)], dk.at[pl.ds(0, hidden)], dv.at[keys]
    load_ffn = [c.start(a, b) for a, b in ((down_h, down), (slope_h, slope), (act_h, act), (zb_h, zb), (up_h, up))]
    queries = pl.ds(0, wide)
    eot, eq = ot.at[:, queries], q.at[queries]
    load_ot = c.start(eot_h, eot)
    loads = [c.start(eqkv_h.at[i], item.at[keys]) for i, item in enumerate((q, k, v))]
    load_x = c.start(ex_h, x1)
    load_tw = c.start(tw4_h, wa)
    load_tx = c.start(tx_h, x0)
    begin, fetch = in_ring(ering, ee_h, esems.at[1], [(m, slice(0, wide))])
    begin()
    q[m:wide] = jnp.zeros((wide - m, width), BF)
    load_e2.wait()
    gain, shift = zero, zero
    for start, count in cut(m):
        part = slice(start, start + count)
        unit, pace = normalise(wide0[part])
        grad = wide1[part]
        gain += colsum(grad * unit)
        shift += colsum(grad)
        d2 = norm_back(unit, pace, egains[1:2], grad)
        da[part] = d2
        gb[part] = d2.astype(BF)
    d_gains[1:2] = gain
    d_shifts[1:2] = shift
    load_e1 = c.start(e1_h, wide1)
    load_a1 = c.start(a1_h, wide0)
    cross.a_wait()
    cross.b_start()
    for load in load_ffn:
        load.wait()
    ffn_back(zb, up, down, act, slope, gb.at[keys], slope, g1, d_bias, d_shifts, 2)
    effn.a_start()
    dffn.bb_wait()
    dffn.c_start()
    load_e1.wait()
    gain, shift = zero, zero
    for start, count in cut(m):
        part = slice(start, start + count)
        unit, pace = normalise(wide1[part])
        dz = da[part] + mm(slope[part], up[...], NT)
        gain += colsum(dz * unit)
        shift += colsum(dz)
        d1 = norm_back(unit, pace, egains[0:1], dz)
        da[part] = d1
        gb[part] = d1.astype(BF)
    d_gains[0:1] = gain
    d_shifts[0:1] = shift

    def enc0_():
        effn.a_wait()
        effn.b_start()

    def enc2():
        cross.b_wait()
        cross.bb_start()
        dffn.c_wait()
        dffn.d_start()

    for load in (load_ew, load_ot, *loads, load_x, save_dx1):
        load.wait()
    kt[:, :m] = k[:m].T
    put(g0, 3 * rows, mm(ot[:, :m], gb[:m]))
    edot, edo, edqt = dot_.at[:, queries], d_o.at[queries], dqt.at[:, queries]
    erowdot = rowdot.at[:, :, queries]
    back_outputs(gb.at[keys], wb, eot, erate, edot, edo, erowdot)
    back_heads(False, wide, eq, kt, v.at[keys], edot, edo, erowdot, fetch, pair_ds, edqt, dk.at[keys], dv.at[keys],
               {0: enc0_, 2: enc2})
    load_dx1 = c.start(dx1_h, d_o)
    cross.bb_wait()
    cross.c_start()
    put(g0, 0, mm(x1[...], dqt[:, :m], TT))
    put(g0, rows, mm(x1[...], dk[:m], TN))
    put(g0, 2 * rows, mm(x1[...], dv[:m], TN))
    enc0.a_start()
    enc1.a_start()
    effn.b_wait()
    effn.bb_start()
    for start, count in cut(m):
        part = slice(start, start + count)
        wide1[part] = da[part] + mm(dqt[:, part], wb[0], TT) + mm(dk[part], wb[1], NT) + mm(dv[part], wb[2], NT)
    c.out(wide1, dx_enc_h)

    load_ot = c.start(tot_h, ot)
    loads = [c.start(tqkv_h.at[i], item) for i, item in enumerate((q, k, v))]
    tile = 256
    spans = [(start + tile, slice(start, start + tile)) for start in range(0, n, tile)]
    begin, fetch = in_ring(ering, te_h, esems.at[2], spans)
    begin()
    load_a1.wait()
    load_dx1.wait()
    gain, shift = zero, zero
    for start, count in cut(n):
        part = slice(start, start + count)
        unit, pace = normalise(wide0[part])
        grad = d_o[part].astype(F32)
        gain += colsum(grad * unit)
        shift += colsum(grad)
        d1 = norm_back(unit, pace, dgains[0:1], grad)
        da[part] = d1
        gb[part] = d1.astype(BF)
    part_lanes = width // n_dp
    vec[...] = jnp.zeros_like(vec)
    for i in range(n_dp):
        lanes = slice(i * part_lanes, (i + 1) * part_lanes)
        for j in range(2):
            wide_lanes = slice((2 * i + j) * part_lanes, (2 * i + j + 1) * part_lanes)
            vec[i, j : j + 1, :part_lanes] = d_bias[:, wide_lanes]
            vec[i, 2 + j : 3 + j, :part_lanes] = d_bias_d[:, wide_lanes]
        vec[i, 4:6, :part_lanes] = d_gains[:, lanes]
        vec[i, 6:9, :part_lanes] = d_shifts[:, lanes]
        vec[i, 9:10, :part_lanes] = gain[:, lanes]
        vec[i, 10:12, :part_lanes] = d_gains_d[1:3, lanes]
        vec[i, 12:13, :part_lanes] = shift[:, lanes]
        vec[i, 13:16, :part_lanes] = d_shifts_d[1:4, lanes]
    vector.swap_start(0)
    enc0.a_wait()
    enc0.b_start()
    enc1.a_wait()
    enc1.b_start()

    quarter = half // 2

    def put_pair(p):
        lanes = slice(p * quarter, (p + 1) * quarter)
        sides = jnp.concatenate([dqt[lanes].T, dk[:, lanes], dv[:, lanes]], axis=1)
        put(pairs[p].source, 0, mm(x0[...], sides, TN))
        pairs[p].a_start()

    def tags0():
        vector.swap_wait(0)
        vector.swap_start(1)
        cross.c_wait()
        cross.d_start()
        effn.bb_wait()
        effn.c_start()

    def tags1():
        put_pair(0)

    def tags2():
        enc0.b_wait()
        enc1.b_wait()
        enc0.bb_start()
        enc1.bb_start()
        pair0.a_wait()
        pair0.q_start()
        vector.swap_wait(1)
        vector.swap_start(2)

    def tags3():
        put_pair(1)

    def tags4():
        pair1.a_wait()
        pair1.q_start()
        dffn.d_wait()
        effn.c_wait()
        effn.d_start()
        vector.swap_wait(2)
        vector.c_start()

    def tags5():
        put_pair(2)
        enc0.bb_wait()
        enc0.c_start()
        enc1.bb_wait()
        enc1.c_start()
        pair0.q_wait()
        pair0.c_start()

    def tags6():
        pair2.a_wait()
        pair2.q_start()

    def tags7():
        put_pair(3)
        cross.d_wait()
        enc0.c_wait()
        enc0.d_start()
        enc1.c_wait()
        enc1.d_start()
        pair1.q_wait()
        pair1.c_start()
        pair0.c_wait()
        pair0.d_start()

    for load in (load_ot, load_tw, load_tx, *loads):
        load.wait()
    kt[...] = k[...].T
    out = mm(ot[...], gb[...])
    for i, piece in enumerate(pairs):
        put(piece.source, 0, out[:, i * quarter : (i + 1) * quarter], 3 * quarter)
    back_outputs(gb, wa, ot, trate, dot_, d_o, rowdot)
    back_heads(True, tile, q, kt, v, dot_, d_o, rowdot, fetch, pair_ds, dqt, dk, dv,
               dict(enumerate((tags0, tags1, tags2, tags3, tags4, tags5, tags6, tags7))))
    pair3.a_wait()
    pair3.q_start()
    for i, (start, count) in enumerate(cut(n)):
        part = slice(start, start + count)
        wide0[part] = (da[part] + mm(dqt[:, part], wa[0], TT) + mm(dk[part], wa[1], NT) + mm(dv[part], wa[2], NT))
        if i == 0:
            pair2.q_wait()
            pair2.c_start()
    c.out(wide0, dx_tags_h)
    pair1.c_wait()
    pair1.d_start()
    pair3.q_wait()
    pair3.c_start()
    pair2.c_wait()
    pair2.d_start()
    vector.c_wait()
    effn.d_wait()
    own_copy.wait()
    for step in range(1, n_bal):
        moved(step, False).wait_send()
        moved(step, True).wait_recv()
    c.finish()
    pair3.c_wait()
    pair3.d_start()
    for piece in (enc0, enc1, *pairs):
        piece.d_wait()


def finish(all_cross, all_dffn, all_effn, all_enc0, all_enc1, all_self0, all_self1, all_self2, all_self3, v_total, decoded_h, patches_h, tags_h,
           o_enc, o_eup, o_ebias, o_edown, o_egains, o_eshifts,
           o_self, o_cross, o_dup, o_dbias, o_ddown, o_dgains, o_dshifts, o_decoded, o_patches, o_tags, tags, patches, decoded, sems):
    c = Copies(sems)
    moves = [(c.start(source, here), here, target) for source, here, target in
             ((tags_h, tags, o_tags), (patches_h, patches, o_patches), (decoded_h, decoded, o_decoded))]
    for load, here, target in moves:
        load.wait()
        c.out(here, target)

    def joined(gathered):
        return jnp.concatenate([gathered[b].astype(F32) for b in (0, 2, 1, 3)], axis=1)

    def layer(out, parts):
        rows = out.shape[0]
        for j in range(4):
            out[:, j, :] = parts[j * rows : (j + 1) * rows]

    def branch(up, down, parts):
        rows, width = up.shape[0], parts.shape[1]
        for j in range(up.shape[1] // width):
            up[:, j * width : (j + 1) * width] = parts[j * rows : (j + 1) * rows]
        down[...] = parts[2 * rows :]

    layer(o_enc, jnp.concatenate([joined(all_enc0), joined(all_enc1)], axis=0))
    layer(o_cross, joined(all_cross))
    branch(o_eup, o_edown, joined(all_effn))
    branch(o_dup, o_ddown, joined(all_dffn))
    rows, _, width = o_self.shape
    half = width // 2
    quarter = half // 2
    for i, gathered in enumerate((all_self0, all_self1, all_self2, all_self3)):
        parts = joined(gathered)
        for j in range(4):
            o_self[:, j, i * quarter : (i + 1) * quarter] = parts[:rows, j * quarter : (j + 1) * quarter]
    share = o_egains.shape[1]
    for j in range(2):
        o_ebias[:, j * share : (j + 1) * share] = v_total[j : j + 1, :share]
        o_dbias[:, j * share : (j + 1) * share] = v_total[2 + j : 3 + j, :share]
    o_egains[...] = v_total[4:6, :share]
    o_eshifts[...] = v_total[6:9, :share]
    o_dgains[...] = v_total[9:12, :share]
    o_dshifts[...] = v_total[12:16, :share]
    c.finish()


def call(kernel, ins, outs, out_specs, scratch, name, params=PARAMS):
    specs = [spec for spec, _ in ins]
    return pl.pallas_call(
        kernel,
        out_shape=outs,
        in_specs=specs,
        out_specs=out_specs,
        scratch_shapes=scratch,
        compiler_params=params,
        name=name,
    )(*[value for _, value in ins])


def talking(number):
    return pltpu.CompilerParams(vmem_limit_bytes=60 << 20, collective_id=number, has_side_effects=True)


def run_tags_forward(n_dp, n_bal, x, w, ew, cw, cot, gains, shifts):
    n, width = x.shape
    bf = lambda *s: Shape(s, BF)
    f32 = lambda *s: Shape(s, F32)
    vb = lambda *s: pltpu.VMEM(s, BF)
    vf = lambda *s: pltpu.VMEM(s, F32)
    line, turned, raw, split = vb(n, width), vb(width, n), vb(width, 4, width), vb(4, width, width)
    weights = bf(4, width, width)
    return call(
        functools.partial(tags_forward, n_dp, n_bal),
        [(ANY, x), (ANY, w), (ANY, ew), (ANY, cw), (ANY, cot), (VM, gains), (VM, shifts)],
        [bf(n, width), bf(*cot.shape), f32(HEADS, 1, n), weights, weights, weights, bf(3, n, width), bf(width, n),
         bf(HEADS, n, n), f32(n, width)],
        [VM, VM, VM] + [ANY] * 7,
        [line, raw, split, raw, split, raw, split, line, line, line, turned, turned, turned, vf(n, width), vb(4, n, n),
         pltpu.SemaphoreType.DMA((20,)), pltpu.SemaphoreType.DMA((4, n // 256)), pltpu.SemaphoreType.DMA((2 * n_bal,))],
        "tags_forward",
        talking(2),
    )


def run_forward(n_dp, n_bal, scalars, x, ew4, eup, ebias, edown, egains, eshifts, x1, cw4, up, bias, down, gains, shifts, cot):
    m, width = x.shape
    n = x1.shape[0]
    hidden = up.shape[1]
    wide = (m + 127) // 128 * 128
    piece = (n_dp // 2, 2, 4 * width // n_dp, width)
    bf = lambda *s: Shape(s, BF)
    f32 = lambda *s: Shape(s, F32)
    vb = lambda *s: pltpu.VMEM(s, BF)
    vf = lambda *s: pltpu.VMEM(s, F32)
    split, first, second = vb(4, width, width), vb(width, hidden), vb(hidden, width)
    short, line = vb(m, width), vb(n, width)
    return call(
        functools.partial(forward, cot.shape[0] // n_bal),
        [(SM, v) for v in scalars]
        + [(ANY, x), (ANY, ew4), (ANY, eup), (VM, ebias), (ANY, edown), (VM, egains), (VM, eshifts),
           (ANY, x1), (ANY, cw4), (ANY, up), (VM, bias), (ANY, down), (VM, gains), (VM, shifts), (ANY, cot)],
        [f32(HEADS, 1, wide), f32(HEADS, 1, n), bf(*piece), f32(1, hidden), f32(3, width), f32(4, width), bf(*cot.shape),
         bf(m, width), bf(3, m, width), bf(width, wide), bf(HEADS, m, wide), f32(m, width), f32(m, width), bf(m, width),
         bf(m, hidden), bf(m, hidden),
         f32(n, width), bf(n, width), bf(n, width), bf(m, width), bf(m, width), bf(width, n), bf(HEADS, m, n)],
        [VM] * 7 + [ANY] * 16,
        [short, split, first, second, line, short, short, vb(width, n), vb(width, m), vb(width, n), vb(4, m, n),
         vf(m, width), vf(m, width), short, vb(m, hidden), vb(m, hidden),
         line, short, split, first, second, vf(n, width), vf(n, 1), line, vb(n, hidden), vb(n, hidden), vf(n, width), line,
         pltpu.SemaphoreType.DMA((40,)), pltpu.SemaphoreType.DMA((4, 1))],
        "forward",
    )


def run_backward(n_dp, n_bal, inputs, vectors, shapes):
    n, m, width, hidden, wide, blocks = shapes
    rows = 4 * width // n_dp
    bf = lambda *s: Shape(s, BF)
    f32 = lambda *s: Shape(s, F32)
    vb = lambda *s: pltpu.VMEM(s, BF)
    vf = lambda *s: pltpu.VMEM(s, F32)
    least = max(rows // 4, 16)
    whole, part, small = bf(n_bal, rows, 128), bf(n_bal, rows // 2, 128), bf(n_bal, least, 128)
    line, turned = vb(n, width), vb(width, n)
    piece = vb(n_dp // 2, 2, rows, width)
    return call(
        functools.partial(backward, n_dp, n_bal),
        [(ANY, item) for item in inputs] + [(VM, item) for item in vectors],
        [f32(m, width), f32(n, width), bf(n, width), bf(*blocks), whole, whole, whole, part, part, small, small, small, small, f32(16, 128)],
        [ANY, ANY, ANY] + [VM] * 11,
        [vb(3, n, n), line, line, line, turned, turned, turned, line, vf(HEADS, 1, n), vb(width, max(n, hidden)), vb(max(n, hidden), width), line,
         vb(2, n, max(n, hidden)), line, vf(n, width), vf(n, width), vf(m, width), line, vb(m, width),
         vb(4, width, width), vb(4, width, width), piece, piece,
         vf(1, hidden), vf(2, width), vf(3, width), vf(n_dp, 16, 128), vf(3, n_dp, 16, 128), vf(n_dp // 2, 16, 128),
         vb(*kept_shape(n_dp, rows, False)), vb(*kept_shape(n_dp, rows // 2, False)),
         *room_scratch(n_dp, rows), *room_scratch(n_dp, rows),
         pltpu.SemaphoreType.DMA((40,)), pltpu.SemaphoreType.DMA((3, 4, n // 256)), pltpu.SemaphoreType.DMA((2 * n_bal,)),
         pltpu.SemaphoreType.DMA((6 + n_dp,)), *[piece_sems(n_dp, n_bal)] * 5,
         *pair_scratch(n_dp, n_bal, least, False) * 2, *pair_scratch(n_dp, n_bal, least, True) * 2],
        "backward",
        pltpu.CompilerParams(vmem_limit_bytes=60 << 20, collective_id=1, has_side_effects=True),
    )


def run_finish(n_dp, hidden, width, gathered, moved):
    share = width // n_dp
    f32 = lambda *s: Shape(s, F32)
    side = [f32(share, 4, width)]
    branch = [f32(share, hidden), f32(1, hidden // n_dp), f32(hidden // n_dp, width)]
    outs = side + branch + [f32(2, share), f32(3, share)] + side + side + branch + [f32(3, share), f32(4, share)]
    return call(finish, [(VM, v) for v in gathered] + [(ANY, v) for v in moved],
                outs + [Shape(v.shape, v.dtype) for v in moved], [VM] * len(outs) + [ANY] * 3,
                [pltpu.VMEM(v.shape, v.dtype) for v in moved[::-1]] + [pltpu.SemaphoreType.DMA((6,))], "finish")


def per_device(
    patches, tag_rows, cotangent, tag_length, cell_count, destination, slot_index,
    encoder_attention, encoder_up, encoder_up_bias, encoder_down, encoder_gains, encoder_shifts,
    decoder_self, decoder_cross, decoder_up, decoder_up_bias, decoder_down, decoder_gains, decoder_shifts,
):
    n_bal, n_dp = lax.axis_size("bal"), lax.axis_size("dp")
    length, width = tag_rows.shape[1:]
    hidden = encoder_up.shape[1]
    blocks = destination.shape[1]
    span = length // blocks
    cot = cotangent[0].reshape(blocks, span, width)
    eg, es, dg, ds = encoder_gains.T, encoder_shifts.T, decoder_gains.T, decoder_shifts.T
    eb, db = encoder_up_bias[None], decoder_up_bias[None]
    x1, cot, srate, sw4, ew4, cw4, sqkv, sot, se, a1 = run_tags_forward(
        n_dp, n_bal, tag_rows[0], decoder_self, encoder_attention, decoder_cross, cot, dg, ds)
    (erate, crate, g_dffn, d_db, d_dg, d_ds, y, memory, eqkv, eot, ee, e1, e2, zb, act, slope, da2, gb2, cq, ck, cv, c_ot,
     ce) = run_forward(
        n_dp, n_bal, (tag_length, cell_count, destination, slot_index), patches[0], ew4, encoder_up, eb, encoder_down,
        eg, es, x1, cw4, decoder_up, db, decoder_down, dg, ds, cot)
    d_patches, d_tags, _, decoded, all_cross, all_dffn, *gathered = run_backward(
        n_dp, n_bal,
        (da2, gb2, x1, memory, cw4, cq, ck, cv, c_ot, ce, y, g_dffn,
         e2, e1, zb, act, slope, encoder_up, encoder_down, patches[0], ew4, eqkv, eot, ee,
         a1, tag_rows[0], sw4, sqkv, sot, se),
        (crate, erate, srate, eg, dg, d_db, d_dg, d_ds),
        (length, patches.shape[1], width, hidden, eot.shape[1], y.shape))
    ew, eu, ebg, ed, egg, esg, sw, cw, du, dbg, dd, dgg, dsg, decoded, d_patches, d_tags = run_finish(
        n_dp, hidden, width, (all_cross, all_dffn, *gathered), (decoded, d_patches, d_tags))
    return (
        decoded.reshape(1, length, width), d_patches[None], d_tags[None],
        ew, eu, ebg.reshape(-1), ed, egg.T, esg.T, sw, cw, du, dbg.reshape(-1), dd, dgg.T, dsg.T,
    )


def solution(mesh):
    split = P(("dp", "bal"))
    in_specs = (split,) * 7 + (P(),) * 13
    out_specs = (split,) * 3 + (P("dp"),) * 13
    return jax.shard_map(per_device, mesh=mesh, in_specs=in_specs, out_specs=out_specs, check_vma=False)
```

```python
import functools

import jax
import jax.numpy as jnp
from jax import lax
from jax.experimental import pallas as pl
from jax.experimental.pallas import tpu as pltpu
from jax.sharding import PartitionSpec as P

HEADS = 8
HEAD = 64
EPSILON = 1e-05
NEGATIVE = -1e30
BF = jnp.bfloat16
F32 = jnp.float32
NN = (((1,), (0,)), ((), ()))
NT = (((1,), (1,)), ((), ()))
TN = (((0,), (0,)), ((), ()))
TT = (((0,), (1,)), ((), ()))
VM = pl.BlockSpec(memory_space=pltpu.VMEM)
SM = pl.BlockSpec(memory_space=pltpu.SMEM)
ANY = pl.BlockSpec(memory_space=pl.ANY)
LIMIT = 1e18
PARAMS = pltpu.CompilerParams(vmem_limit_bytes=60 << 20)
Shape = jax.ShapeDtypeStruct


def mm(left, right, dims=NN):
    return lax.dot_general(left, right, dims, preferred_element_type=F32)


def cut(rows):
    half = (rows // 2 + 15) // 16 * 16
    return [(0, half), (half, rows - half)]


class Copies:
    def __init__(self, sems):
        self.sems, self.used, self.open = sems, 0, []

    def start(self, source, target):
        copy = pltpu.make_async_copy(source, target, self.sems.at[self.used])
        self.used += 1
        copy.start()
        return copy

    def out(self, source, target):
        self.open.append(self.start(source, target))

    def finish(self):
        for copy in self.open:
            copy.wait()


def split_weights(raw, parts):
    def step(i, carry):
        rows = pl.ds(pl.multiple_of(i * 128, 128), 128)
        parts[:, rows, :] = pltpu.einshape("abc->bac", raw[rows])
        return carry

    lax.fori_loop(0, raw.shape[0] // 128, step, 0)


def normalise(signal):
    centre = jnp.mean(signal, axis=-1, keepdims=True)
    centered = signal - centre
    spread = jnp.mean(centered * centered, axis=-1, keepdims=True)
    rate = lax.rsqrt(spread + EPSILON)
    return centered * rate, rate


def norm_back(unit, rate, gain, gradient):
    inner = gradient * gain
    first = jnp.mean(inner, axis=-1, keepdims=True)
    second = jnp.mean(inner * unit, axis=-1, keepdims=True)
    return rate * (inner - first - unit * second)


def colsum(signal):
    return jnp.sum(signal, axis=0, keepdims=True)


def smooth(hidden):
    scale = 0.7978845608028654
    square = hidden * hidden
    curve = jnp.tanh(scale * hidden * (1.0 + 0.044715 * square))
    half = 0.5 + 0.5 * curve
    slope = half + 0.5 * hidden * (1.0 - curve * curve) * (scale + (3 * 0.044715 * scale) * square)
    return hidden * half, slope


def half_mask(shape, axis, which):
    index = lax.broadcasted_iota(jnp.int32, shape, axis)
    return (index < HEAD) if which == 0 else (index >= HEAD)


def keep_half(pair, axis, which):
    return jnp.where(half_mask(pair.shape, axis, which), pair, jnp.zeros_like(pair))


def project_qkv(x, sources, w4, q, qt, k, v, vt):
    rows = x.shape[0]
    for start, size in cut(rows):
        part = slice(start, start + size)
        q[part] = (mm(x[part], w4[0]) * HEAD ** (-0.5)).astype(BF)
    if q.shape[0] > rows:
        q[rows:] = jnp.zeros((q.shape[0] - rows, q.shape[1]), BF)
    for start, size in cut(sources.shape[0]):
        part = slice(start, start + size)
        k[part] = mm(sources[part], w4[1]).astype(BF)
        v[part] = mm(sources[part], w4[2]).astype(BF)
    qt[...] = q[...].T
    vt[...] = v[...].T


def shifted_exp(scores, exact, causal_rows):
    if causal_rows:
        size, width = scores.shape
        key = lax.broadcasted_iota(jnp.int32, (width, width), 0)
        query = lax.broadcasted_iota(jnp.int32, (width, width), 1)
        last = jnp.where(key <= query, scores[size - width :], NEGATIVE)
        scores = last if size == width else jnp.concatenate([scores[: size - width], last], axis=0)
        exact = exact or size == width
    sample = scores if exact else scores[:128]
    return jnp.exp(scores - jnp.max(sample, axis=0, keepdims=True))


def attend_heads(exact, causal, q_tile, qt, k, vt, ot, rate, store, beside=None):
    keys, queries = k.shape[0], qt.shape[1]

    def pair(p, carry):
        lanes = pl.ds(pl.multiple_of(p * 128, 128), 128)
        if beside is not None:
            beside(p)
        for u in range(2):
            rows = pl.ds(pl.multiple_of(p * 128 + u * HEAD, HEAD), HEAD)
            place, done = store(p, u)
            for start in range(0, queries, q_tile):
                cols = slice(start, start + q_tile)
                depth = start + q_tile if causal else keys
                scores = mm(k[:depth, lanes], keep_half(qt[lanes, cols], 0, u))
                raised = shifted_exp(scores, exact, causal)
                total = jnp.sum(raised, axis=0, keepdims=True)
                low = raised.astype(BF)
                place[:depth, cols] = low
                inverse = 1.0 / total
                rate[2 * p + u, :, cols] = inverse
                ot[rows, cols] = (mm(vt[rows, :depth], low) * inverse).astype(BF)
            done()
        return carry

    lax.fori_loop(0, HEADS // 2, pair, 0)


def attend(causal, q_tile, qt, k, vt, ot, rate, store, drain):
    attend_heads(False, causal, q_tile, qt, k, vt, ot, rate, store)
    drain()
    fine = jnp.min(rate[...]) > 1.0 / LIMIT

    @pl.when(jnp.logical_not(fine))
    def _():
        attend_heads(True, causal, q_tile, qt, k, vt, ot, rate, store)
        drain()


def back_heads(causal, q_tile, q, kt, v, dot_, d_o, rowdot, fetch, ds, dqt, dk, dv, hook=None):
    keys, queries = v.shape[0], dqt.shape[1]

    def pair(p, carry):
        lanes = pl.ds(pl.multiple_of(p * 128, 128), 128)
        for u in range(2):
            rows = pl.ds(pl.multiple_of(p * 128 + u * HEAD, HEAD), HEAD)
            place = fetch(p, u)
            for start in range(0, queries, q_tile):
                cols = slice(start, start + q_tile)
                depth = start + q_tile if causal else keys
                grad = mm(v[:depth, lanes], keep_half(dot_[lanes, cols], 0, u))
                scaled = place[:depth, cols].astype(F32) * (grad - rowdot[2 * p + u, :, cols])
                low = scaled.astype(BF)
                ds[u][:depth, cols] = low
                dqt[rows, cols] = (mm(kt[rows, :depth], low) * HEAD ** (-0.5)).astype(BF)
            qm = q[:queries, lanes]
            dm = d_o[:queries, lanes]
            steps = range(0, keys, q_tile) if causal else (0,)
            for start in steps:
                key = slice(start, start + q_tile) if causal else slice(0, keys)
                more_k = mm(ds[u][key, start:queries], qm[start:])
                more_v = mm(place[key, start:queries], dm[start:])
                if u == 0:
                    dk[key, lanes] = more_k.astype(BF)
                    dv[key, lanes] = more_v.astype(BF)
                else:
                    dk[key, lanes] = jnp.where(half_mask(more_k.shape, 1, 1), more_k.astype(BF), dk[key, lanes])
                    dv[key, lanes] = jnp.where(half_mask(more_v.shape, 1, 1), more_v.astype(BF), dv[key, lanes])
            if hook is not None:
                for at, act in hook.items():
                    if at % 2 == u:
                        pl.when(p == at // 2)(act)
        return carry

    lax.fori_loop(0, HEADS // 2, pair, 0)


def back_outputs(grad_low, w4, ot, rate, dot_, d_o, rowdot):
    rows, wide = grad_low.shape[0], dot_.shape[1]
    raw = mm(w4[3], grad_low[...], NT)
    for h in range(HEADS):
        part = slice(h * HEAD, (h + 1) * HEAD)
        low = (raw[part] * rate[h][:, :rows]).astype(BF)
        if wide > rows:
            low = jnp.concatenate([low, jnp.zeros((HEAD, wide - rows), BF)], axis=1)
        dot_[part] = low
        rowdot[h] = jnp.sum(low.astype(F32) * ot[part].astype(F32), axis=0, keepdims=True)
    d_o[...] = dot_[...].T


def ring(buffers, hbm, sems, spans, out):
    def copies(h, slot):
        made = []
        for i, (rows, cols) in enumerate(spans):
            here = buffers.at[slot, pl.ds(0, rows), cols]
            there = hbm.at[h, pl.ds(0, rows), cols]
            made.append(
                pltpu.make_async_copy(here, there, sems.at[slot, i])
                if out
                else pltpu.make_async_copy(there, here, sems.at[slot, i])
            )
        return made

    return copies


def out_ring(buffers, hbm, sems, spans):
    copies = ring(buffers, hbm, sems, spans, True)

    def store(p, u):
        slot = (p % 2) * 2 + u

        @pl.when(p >= 2)
        def _():
            for copy in copies(2 * p + u, slot):
                copy.wait()

        def done():
            for copy in copies(2 * p + u, slot):
                copy.start()

        return buffers.at[slot], done

    def drain():
        for slot in range(4):
            for copy in copies(slot, slot):
                copy.wait()

    return store, drain


def in_ring(buffers, hbm, sems, spans):
    copies = ring(buffers, hbm, sems, spans, False)
    depth = buffers.shape[0]

    def begin():
        for h in range(depth):
            for copy in copies(h, h):
                copy.start()

    def fetch(p, u):
        h = 2 * p + u
        for copy in copies(h, h % depth):
            copy.wait()

        @pl.when((h >= 1) & (h + depth <= HEADS))
        def _():
            for copy in copies(h + depth - 1, (h + depth - 1) % depth):
                copy.start()

        return buffers.at[h % depth]

    return begin, fetch


MESH = pl.DeviceIdType.MESH


class Spot:
    def __init__(self, n, m):
        self.n, self.m = n, m
        self.d, self.b = lax.axis_index("dp"), lax.axis_index("bal")
        self.core, self.far = self.b % 2, self.b // 2
        self.parity, self.row = self.d % 2, self.d // 2
        self.by_core = (self.d, self.b + 1 - 2 * self.core)
        self.by_far = (self.d, self.b + 2 - 4 * self.far)
        self.by_parity = (self.d + 1 - 2 * self.parity, self.b)

    def greet(self, everyone=True):
        barrier = pltpu.get_barrier_semaphore()

        def call(device):
            pl.semaphore_signal(barrier, inc=1, device_id=device, device_id_type=MESH)

        for k in range(1, self.m):
            call((self.d, (self.b + k) % self.m))

        if not everyone:
            return
        call(self.by_parity)
        call((self.by_parity[0], self.by_far[1]))

        def along(k, carry):
            call((((self.row + k) % (self.n // 2)) * 2 + self.parity, self.b))
            return carry

        lax.fori_loop(1, self.n // 2, along, 0)

    def await_all(self, everyone=True):
        pl.semaphore_wait(pltpu.get_barrier_semaphore(), self.m - 1 + (2 + self.n // 2 - 1 if everyone else 0))


def remote(source, target, sent, received, device):
    return pltpu.make_async_remote_copy(
        src_ref=source, dst_ref=target, send_sem=sent, recv_sem=received, device_id=device, device_id_type=MESH
    )


class Piece:
    def __init__(self, spot, along_x, sems, source=None, acc=None, land_a=None, kept=None, land_b=None, kept2=None,
                 land_c=None, slots=None, result=None, gathered=None):
        self.spot, self.along_x, self.source, self.sems = spot, along_x, source, sems
        self.acc, self.land_a, self.kept, self.land_b = acc, land_a, kept, land_b
        self.kept2, self.land_c = kept2, land_c
        self.slots, self.result, self.gathered = slots, result, gathered

    def a_copies(self):
        half = self.acc.shape[3]
        mine = pl.ds(pl.multiple_of(self.spot.core * half, half), half)
        other = pl.ds(pl.multiple_of((1 - self.spot.core) * half, half), half)
        return [
            pltpu.make_async_copy(self.source.at[:, :, :, mine], self.acc, self.sems.at[0]),
            remote(self.source.at[:, :, :, other], self.land_a, self.sems.at[1], self.sems.at[2], self.spot.by_core),
        ]

    def a_start(self):
        for copy in self.a_copies():
            copy.start()

    def a_wait(self):
        for copy in self.a_copies():
            copy.wait()

        def add(i, carry):
            self.acc[i] = self.acc[i] + self.land_a[i]
            return carry

        lax.fori_loop(0, self.acc.shape[0], add, 0)

    def lanes(self, mine, size):
        side = self.spot.far if mine else 1 - self.spot.far
        return pl.ds(pl.multiple_of(side * size, size), size)

    def b_copy(self):
        spot = self.spot
        if self.along_x:
            out, to = self.acc.at[:, :, :, self.lanes(False, self.land_b.shape[3])], spot.by_far
        else:
            out, to = self.acc.at[:, 1 - spot.parity], spot.by_parity
        return remote(out, self.land_b, self.sems.at[3], self.sems.at[4], to)

    def b_start(self):
        self.b_copy().start()

    def b_wait(self):
        self.b_copy().wait()

        def add(i, carry):
            if self.along_x:
                mine = self.acc[i, :, :, self.lanes(True, self.land_b.shape[3])]
            else:
                mine = self.acc[i, self.spot.parity]
            self.kept[i] = mine + self.land_b[i]
            return carry

        lax.fori_loop(0, self.kept.shape[0], add, 0)

    def bb_copy(self):
        spot = self.spot
        if self.along_x:
            out, to = self.kept.at[:, 1 - spot.parity], spot.by_parity
        else:
            out, to = self.kept.at[:, :, self.lanes(False, self.land_c.shape[2])], spot.by_far
        return remote(out, self.land_c, self.sems.at[5], self.sems.at[6], to)

    def bb_start(self):
        self.bb_copy().start()

    def bb_wait(self):
        self.bb_copy().wait()

        def add(i, carry):
            if self.along_x:
                mine = self.kept[i, self.spot.parity]
            else:
                mine = self.kept[i, :, self.lanes(True, self.land_c.shape[2])]
            self.kept2[i] = mine + self.land_c[i]
            return carry

        lax.fori_loop(0, self.kept2.shape[0], add, 0)

    def base(self):
        return 7

    def c_copy(self, k, arriving):
        spot, half = self.spot, self.spot.n // 2
        row = (spot.row + k) % half
        slot = row if arriving else spot.row
        return remote(self.kept2.at[row], self.slots.at[slot], self.sems.at[self.base() + k], self.sems.at[self.base() + half + slot],
                      (row * 2 + spot.parity, spot.b))

    def c_start(self):
        def step(k, carry):
            self.c_copy(k, False).start()
            return carry

        lax.fori_loop(1, self.spot.n // 2, step, 0)

    def c_wait(self):
        half, row = self.spot.n // 2, self.spot.row

        def step(k, total):
            self.c_copy(k, False).wait_send()
            self.c_copy(k, True).wait_recv()
            return total + self.slots[(row + k) % half].astype(F32)

        total = lax.fori_loop(1, half, step, self.kept2[row].astype(F32))
        self.result[...] = total.astype(BF)

    def d_copies(self, arriving):
        spot, base = self.spot, self.base() + self.spot.n
        made = []
        for k in range(1, spot.m):
            peer = (spot.b + k) % spot.m
            slot = peer if arriving else spot.b
            made.append(remote(self.result, self.gathered.at[slot], self.sems.at[base + k],
                               self.sems.at[base + spot.m + slot], (spot.d, peer)))
        return made

    def d_start(self):
        for copy in self.d_copies(False):
            copy.start()
        self.gathered[self.spot.b] = self.result[...]

    def d_wait(self):
        for copy in self.d_copies(False):
            copy.wait_send()
        for copy in self.d_copies(True):
            copy.wait_recv()


class PairPiece(Piece):
    def __init__(self, spot, sems, source, acc, land_a, quads, kept2, slots, result, gathered):
        super().__init__(spot, True, sems, source, acc, land_a, kept2=kept2, slots=slots, result=result, gathered=gathered)
        self.quads = quads

    def base(self):
        return 11

    def quarter(self, far):
        lanes = self.kept2.shape[2]
        return pl.ds(pl.multiple_of(far * lanes, lanes), lanes)

    def q_copy(self, k, arriving):
        spot = self.spot
        me = spot.far * 2 + spot.parity
        peer = (me + k) % 4
        far, parity = peer // 2, peer % 2
        slot = peer if arriving else me
        return remote(self.acc.at[:, parity, :, self.quarter(far)], self.quads.at[slot], self.sems.at[3 + k],
                      self.sems.at[7 + slot], (spot.row * 2 + parity, spot.core + 2 * far))

    def q_start(self):
        for k in range(1, 4):
            self.q_copy(k, False).start()

    def q_wait(self):
        spot = self.spot
        me = spot.far * 2 + spot.parity
        for k in range(1, 4):
            self.q_copy(k, False).wait_send()
            self.q_copy(k, True).wait_recv()

        def add(i, carry):
            total = self.acc[i, spot.parity, :, self.quarter(spot.far)].astype(F32)
            for k in range(1, 4):
                total = total + self.quads[(me + k) % 4, i].astype(F32)
            self.kept2[i] = total.astype(BF)
            return carry

        lax.fori_loop(0, self.kept2.shape[0], add, 0)


def pair_scratch(n, m, rows, whole):
    vb = lambda shape: pltpu.VMEM(shape, BF)
    first = [vb((n // 2, 2, rows, 512)), vb(half_shape(n, rows)), vb(half_shape(n, rows))] if whole else []
    return first + [vb((4, *last_shape(n, rows))), vb(last_shape(n, rows)), vb(last_shape(n, rows)), vb((rows, 128)),
                    pltpu.SemaphoreType.DMA((11 + n + 2 * m,))]


def piece_sems(n, m):
    return pltpu.SemaphoreType.DMA((7 + n + 2 * m,))


def half_shape(n, rows):
    return (n // 2, 2, rows, 256)


def kept_shape(n, rows, along_x):
    return (n // 2, 2, rows, 128) if along_x else (n // 2, rows, 256)


def last_shape(n, rows):
    return (n // 2, rows, 128)


class VectorSum:
    def __init__(self, spot, v, lands, slots, result, sems):
        self.spot, self.v, self.lands, self.slots, self.result, self.sems = spot, v, lands, slots, result, sems

    def swap(self, step):
        device = (self.spot.by_core, self.spot.by_far, self.spot.by_parity)[step]
        return remote(self.v, self.lands.at[step], self.sems.at[2 * step], self.sems.at[2 * step + 1], device)

    def swap_start(self, step):
        self.swap(step).start()

    def swap_wait(self, step):
        self.swap(step).wait()
        self.v[...] = self.v[...] + self.lands[step]

    def copy(self, k, arriving):
        spot, half = self.spot, self.spot.n // 2
        row = (spot.row + k) % half
        slot = row if arriving else spot.row
        return remote(self.v.at[row * 2 + spot.parity], self.slots.at[slot], self.sems.at[6 + k],
                      self.sems.at[6 + half + slot], (row * 2 + spot.parity, spot.b))

    def c_start(self):
        def step(k, carry):
            self.copy(k, False).start()
            return carry

        lax.fori_loop(1, self.spot.n // 2, step, 0)

    def c_wait(self):
        half, row = self.spot.n // 2, self.spot.row

        def step(k, total):
            self.copy(k, False).wait_send()
            self.copy(k, True).wait_recv()
            return total + self.slots[(row + k) % half]

        self.result[...] = lax.fori_loop(1, half, step, self.v[self.spot.d])


def put(piece, row, value, lane=0):
    halves, two, width = piece.shape[0], piece.shape[1], value.shape[1]
    rows = value.shape[0] // (halves * two)
    piece[:, :, row : row + rows, lane : lane + width] = value.reshape(halves, two, rows, width).astype(BF)


def split_part(raw, parts, p):
    rows = pl.ds(pl.multiple_of(p * 128, 128), 128)
    parts[:, rows, :] = pltpu.einshape("abc->bac", raw[rows])


def tags_forward(n_dp, n_bal, x_h, w_h, ew_h, cw_h, cot_h, gains, shifts,
                 x1, cot, rate, w4_h, ew4_h, cw4_h, qkv_h, ot_h, e_h, a1_h,
                 x, raw, w4, raw_e, ew4, raw_c, cw4, q, k, v, qt, vt, ot, a1, ering, sems, esems, moves):
    spot = Spot(n_dp, n_bal)
    spot.greet(False)
    c = Copies(sems)
    load_w = c.start(w_h, raw)
    load_x = c.start(x_h, x)
    load_e, load_c = c.start(ew_h, raw_e), c.start(cw_h, raw_c)
    load_w.wait()
    split_weights(raw, w4)
    c.out(w4, w4_h)
    load_x.wait()
    project_qkv(x, x, w4, q, qt, k, v, vt)
    n = x.shape[0]
    for i, item in enumerate((q, k, v)):
        c.out(item, qkv_h.at[i])
    spot.await_all(False)
    share = cot_h.shape[0] // n_bal

    def moved(step, arriving):
        peer = (spot.b + step) % n_bal
        slot = peer if arriving else spot.b
        return remote(cot_h.at[pl.ds(peer * share, share)], cot.at[pl.ds(slot * share, share)], moves.at[step],
                      moves.at[n_bal + slot], (spot.d, peer))

    own = pl.ds(spot.b * share, share)
    own_copy = pltpu.make_async_copy(cot_h.at[own], cot.at[own], moves.at[0])
    own_copy.start()
    for step in range(1, n_bal):
        moved(step, False).start()
    load_e.wait()
    load_c.wait()

    def beside(p):
        split_part(raw_e, ew4, p)
        split_part(raw_c, cw4, p)

    tile = 512
    spans = [(start + tile, slice(start, start + tile)) for start in range(0, n, tile)]
    store, drain = out_ring(ering, e_h, esems, spans)
    attend_heads(True, True, tile, qt, k, vt, ot, rate, store, beside)
    drain()
    c.out(ew4, ew4_h)
    c.out(cw4, cw4_h)
    c.out(ot, ot_h)
    for start, size in cut(n):
        part = slice(start, start + size)
        first = x[part].astype(F32) + mm(ot[:, part], w4[3], TN)
        a1[part] = first
        unit, _ = normalise(first)
        x1[part] = (unit * gains[0:1] + shifts[0:1]).astype(BF)
    c.out(a1, a1_h)
    own_copy.wait()
    for step in range(1, n_bal):
        moved(step, False).wait_send()
        moved(step, True).wait_recv()
    c.finish()


def forward(capacity, tag_length, cell_count, destination, slot_index,
            x_h, ew4_h, eup_h, ebias, edown_h, egains, eshifts,
            x1_h, cw4_h, up_h, bias, down_h, gains, shifts, cot_h,
            erate, rate, g_ffn, d_bias, d_gains, d_shifts, y,
            mem_h, eqkv_h, eot_h, ee_h, e1_h, e2_h, zb_h, eact_h, eslope_h,
            da_h, gb_h, q_h, k_h, v_h, ot_h, e_h,
            x, ew4, eup, edown, q, k, v, qt, vt, ot, ering, e1, e2, zb, eact, eslope,
            x1, mem, w4, up, down, unit2, rate2, xb2, act, slope, da, gb, sems, esems):
    cot, dh = y, slope
    c = Copies(sems)
    load_w = c.start(ew4_h, ew4)
    load_x = c.start(x_h, x)
    load_eup = c.start(eup_h, eup)
    load_edown = c.start(edown_h, edown)
    load_w.wait()
    load_x.wait()
    m, n = x.shape[0], x1.shape[0]
    wide = eot_h.shape[1]
    eq, eqt, eot = q.at[pl.ds(0, wide)], qt.at[:, pl.ds(0, wide)], ot.at[:, pl.ds(0, wide)]
    project_qkv(x, x, ew4, eq, eqt, k, v, vt)
    spent = [c.start(item, eqkv_h.at[i]) for i, item in enumerate((q.at[pl.ds(0, m)], k, v))]
    load_w = c.start(cw4_h, w4)
    load_x1 = c.start(x1_h, x1)
    load_up = c.start(up_h, up)
    load_down = c.start(down_h, down)
    load_cot = c.start(cot_h, cot)
    view = ering.at[:, :, pl.ds(0, wide)]
    store, drain = out_ring(view, ee_h, esems, [(m, slice(None))])
    attend(False, wide, eqt, k, vt, eot, erate, store, drain)
    spent.append(c.start(eot, eot_h))
    load_eup.wait()
    load_edown.wait()
    for start, size in cut(m):
        part = slice(start, start + size)
        first = x[part].astype(F32) + mm(ot[:, part], ew4[3], TN)
        e1[part] = first
        unit, _ = normalise(first)
        z = unit * egains[0:1] + eshifts[0:1]
        low = z.astype(BF)
        zb[part] = low
        active, bend = smooth(mm(low, eup[...]) + ebias[...])
        eact[part] = active.astype(BF)
        eslope[part] = bend.astype(BF)
        second = z + mm(eact[part], edown[...]) + eshifts[2:3]
        e2[part] = second
        unit, _ = normalise(second)
        mem[part] = (unit * egains[1:2] + eshifts[1:2]).astype(BF)
    for here, there in ((e1, e1_h), (e2, e2_h), (zb, zb_h), (eact, eact_h), (eslope, eslope_h), (mem, mem_h)):
        c.out(here, there)

    load_w.wait()
    load_x1.wait()
    for copy in spent:
        copy.wait()
    project_qkv(x1, mem, w4, q, qt, k, v, vt)
    for here, there in ((q, q_h), (k, k_h), (v, v_h)):
        c.out(here, there)
    blocks = y.shape[0]
    block = n // blocks
    store, drain = out_ring(ering, e_h, esems, [(m, slice(None))])
    attend(False, n, qt, k, vt, ot, rate, store, drain)
    c.out(ot, ot_h)
    load_up.wait()
    load_down.wait()
    load_cot.wait()
    live = tag_length[0] + cell_count[0]
    places = [destination[0, b] * capacity + slot_index[0, b] for b in range(blocks)]
    zero = jnp.zeros((1, x1.shape[1]), F32)
    gain3, shift3 = zero, zero
    for start, size in cut(n):
        part = slice(start, start + size)
        second = x1[part].astype(F32) + mm(ot[:, part], w4[3], TN)
        unit, pace = normalise(second)
        unit2[part] = unit
        rate2[part] = pace
        x2 = unit * gains[1:2] + shifts[1:2]
        low = x2.astype(BF)
        xb2[part] = low
        active, bend = smooth(mm(low, up[...]) + bias[...])
        act[part] = active.astype(BF)
        slope[part] = bend.astype(BF)
        third = x2 + mm(act[part], down[...]) + shifts[3:4]
        unit, pace = normalise(third)
        row = lax.broadcasted_iota(jnp.int32, (size, 1), 0) + start
        alive = (row < live).astype(F32)
        final = ((unit * gains[2:3] + shifts[2:3]) * alive).astype(BF)
        picked = []
        for b in range(start // block, (start + size) // block):
            picked.append(cot[places[b]])
            y[places[b]] = final[b * block - start : (b + 1) * block - start]
        dy = jnp.concatenate(picked, axis=0).astype(F32) * alive
        gain3 += colsum(dy * unit)
        shift3 += colsum(dy)
        d3 = norm_back(unit, pace, gains[2:3], dy)
        da[part] = d3
        gb[part] = d3.astype(BF)
    d_gains[2:3] = gain3
    d_shifts[2:3] = shift3
    ffn_back(xb2, up, down, act, slope, gb, dh, g_ffn, d_bias, d_shifts, 3)
    gain2, shift2 = zero, zero
    for start, size in cut(n):
        part = slice(start, start + size)
        dx2 = da[part] + mm(dh[part], up[...], NT)
        gain2 += colsum(dx2 * unit2[part])
        shift2 += colsum(dx2)
        d2 = norm_back(unit2[part], rate2[part], gains[1:2], dx2)
        da[part] = d2
        gb[part] = d2.astype(BF)
    d_gains[1:2] = gain2
    d_shifts[1:2] = shift2
    c.out(gb, gb_h)
    c.out(da, da_h)
    c.finish()


def ffn_back(xb, up, down, act, slope, gb, dh, g_ffn, d_bias, d_shifts, row, middle=None):
    n, width = xb.shape
    offset = jnp.zeros((1, up.shape[1]), F32)
    for start, size in cut(n):
        part = slice(start, start + size)
        low = (mm(gb[part], down[...], NT) * slope[part].astype(F32)).astype(BF)
        dh[part] = low
        offset += colsum(low.astype(F32))
    d_bias[...] = offset
    d_shifts[row : row + 1] = colsum(gb[...].astype(F32))
    if middle is not None:
        middle()
    rows = g_ffn.shape[2] // 4
    put(g_ffn, 2 * rows, mm(act[...], gb[...], TN))
    for j in range(up.shape[1] // width):
        put(g_ffn, j * rows, mm(xb[...], dh[:, j * width : (j + 1) * width], TN))


class Room:
    def __init__(self, acc, land, kept, next_, kept_x, next_x, kept2, last, slots, result):
        self.acc, self.land, self.kept, self.next = acc, land, kept, next_
        self.kept_x, self.next_x, self.kept2, self.last, self.slots, self.result = kept_x, next_x, kept2, last, slots, result

    def whole(self, spot, sems, source, gathered):
        return Piece(spot, False, sems, source, self.acc, self.land, self.kept, self.next, self.kept2, self.last,
                     self.slots, self.result, gathered)

    def part(self, spot, sems, source, gathered, along_x, start, size):
        rows, head = pl.ds(start, size), pl.ds(0, size)
        kept = self.kept_x.at[:, :, head] if along_x else self.kept.at[:, rows]
        next_ = self.next_x.at[:, :, head] if along_x else self.next.at[:, rows]
        return Piece(spot, along_x, sems, source, self.acc.at[:, :, rows], self.land.at[:, :, rows], kept, next_,
                     self.kept2.at[:, rows], self.last.at[:, rows], self.slots.at[:, rows], self.result.at[rows], gathered)


def room_scratch(n, rows):
    vb = lambda shape: pltpu.VMEM(shape, BF)
    last, side = vb(last_shape(n, rows)), vb(kept_shape(n, rows // 2, True))
    kept = vb(kept_shape(n, rows, False))
    return [vb(half_shape(n, rows)), vb(half_shape(n, rows)), kept, kept, side, side, last, last, last, vb((rows, 128))]


def backward(n_dp, n_bal,
             da_h, gb_h, x1_h, mem_h, cw4_h, cq_h, ck_h, cv_h, cot_h, ce_h, y_h, g_dffn,
             e2_h, e1_h, zb_h, act_h, slope_h, up_h, down_h, ex_h, ew4_h, eqkv_h, eot_h, ee_h,
             a1_h, tx_h, tw4_h, tqkv_h, tot_h, te_h,
             crate, erate, trate, egains, dgains, d_bias_d, d_gains_d, d_shifts_d,
             dx_enc_h, dx_tags_h, dx1_h, decoded, all_cross, all_dffn, all_effn, all_enc0, all_enc1, *rest_refs):
    all_self, v_total = rest_refs[:4], rest_refs[4]
    (ering, q, k, v, ot, kt, dot_, d_o, rowdot, dqt, dk, dv, ds, gb, da, wide0, wide1, x0, x1,
     wa, wb, g0, g1, d_bias, d_gains, d_shifts, vec, vec_lands, vec_slots, next_effn, next_enc1, *rest) = rest_refs[5:]
    room0, room1 = Room(*rest[:10]), Room(*rest[10:20])
    sems, esems, moves, vsems = rest[20:24]
    psems = rest[24:29]
    early, late = [rest[29:34], rest[34:39]], [rest[39:47], rest[47:55]]
    spot = Spot(n_dp, n_bal)
    spot.greet()
    c = Copies(sems)
    n, width = x0.shape
    m = x1.shape[0]
    wide = eot_h.shape[1]
    hidden = up_h.shape[1]
    size = g0.shape[2] // 2
    rows = size // 2
    half = width // 2
    low, high = pl.ds(0, size), pl.ds(size, size)
    least = all_self[0].shape[1]
    dffn = room0.whole(spot, psems[0], g_dffn, all_dffn)
    cross = room1.whole(spot, psems[1], g0, all_cross)
    effn = room0.whole(spot, psems[2], g1, all_effn)
    effn.land_b = next_effn
    enc0 = room1.part(spot, psems[3], g0.at[:, :, low], all_enc0, True, 0, size)
    enc1 = room1.part(spot, psems[4], g0.at[:, :, high], all_enc1, False, size, size)
    enc1.land_b = next_enc1
    pairs = []
    for i, gathered in enumerate(all_self):
        if i < 2:
            where = pl.ds(i * least, least)
            first = g1.at[:, :, where], room0.acc.at[:, :, where], room0.land.at[:, :, where]
            others = early[i]
        else:
            first, others = late[i - 2][:3], late[i - 2][3:]
        pairs.append(PairPiece(spot, others[4], *first, *others[:4], gathered))
    pair0, pair1, pair2, pair3 = pairs
    vector = VectorSum(spot, vec, vec_lands, vec_slots, v_total, vsems)
    zero = jnp.zeros((1, width), F32)
    pair_ds = ds.at[0], ds.at[1]

    load_gb = c.start(gb_h, gb)
    load_ot = c.start(cot_h, ot)
    load_w = c.start(cw4_h, wa)
    loads = [c.start(a, b) for a, b in ((ck_h, k.at[pl.ds(0, m)]), (cv_h, v.at[pl.ds(0, m)]), (cq_h, q))]
    begin, fetch = in_ring(ering, ce_h, esems.at[0], [(m, slice(0, n))])
    begin()
    last = [c.start(a, b) for a, b in ((x1_h, x0), (mem_h, x1), (da_h, da))]
    load_ew = c.start(ew4_h, wb)
    load_e2 = c.start(e2_h, wide0.at[pl.ds(0, m)])
    load_gb.wait()
    load_ot.wait()
    put(g0, 3 * rows, mm(ot[...], gb[...]))
    load_w.wait()
    back_outputs(gb, wa, ot, crate, dot_, d_o, rowdot)
    for load in loads:
        load.wait()
    kt[:, :m] = k[:m].T
    spot.await_all()
    dffn.a_start()
    share = y_h.shape[0] // n_bal

    def moved(step, arriving):
        peer = (spot.b + step) % n_bal
        slot = peer if arriving else spot.b
        return remote(y_h.at[pl.ds(peer * share, share)], decoded.at[pl.ds(slot * share, share)], moves.at[step],
                      moves.at[n_bal + slot], (spot.d, peer))

    own = pl.ds(spot.b * share, share)
    own_copy = pltpu.make_async_copy(y_h.at[own], decoded.at[own], moves.at[0])
    own_copy.start()
    for step in range(1, n_bal):
        moved(step, False).start()

    def cross1():
        dffn.a_wait()
        dffn.b_start()

    keys = pl.ds(0, m)
    back_heads(False, n, q, kt, v.at[keys], dot_, d_o, rowdot, fetch, pair_ds, dqt, dk.at[keys], dv.at[keys],
               {1: cross1})
    for load in last:
        load.wait()
    put(g0, 0, mm(x0[...], dqt[...], TT))
    put(g0, rows, mm(x1[...], dk[:m], TN))
    put(g0, 2 * rows, mm(x1[...], dv[:m], TN))
    cross.a_start()
    dffn.b_wait()
    dffn.bb_start()
    for start, count in cut(m):
        part = slice(start, start + count)
        wide1[part] = mm(dk[part], wa[1], NT) + mm(dv[part], wa[2], NT)
    for start, count in cut(n):
        part = slice(start, start + count)
        d_o[part] = (da[part] + mm(dqt[:, part], wa[0], TT)).astype(BF)
    save_dx1 = c.start(d_o, dx1_h)
    act, slope = ds.at[0, keys, pl.ds(0, hidden)], ds.at[1, keys, pl.ds(0, hidden)]
    up, down, zb = dqt.at[:, pl.ds(0, hidden)], dk.at[pl.ds(0, hidden)], dv.at[keys]
    load_ffn = [c.start(a, b) for a, b in ((down_h, down), (slope_h, slope), (act_h, act), (zb_h, zb), (up_h, up))]
    queries = pl.ds(0, wide)
    eot, eq = ot.at[:, queries], q.at[queries]
    load_ot = c.start(eot_h, eot)
    loads = [c.start(eqkv_h.at[i], item.at[keys]) for i, item in enumerate((q, k, v))]
    load_x = c.start(ex_h, x1)
    load_tw = c.start(tw4_h, wa)
    load_tx = c.start(tx_h, x0)
    begin, fetch = in_ring(ering, ee_h, esems.at[1], [(m, slice(0, wide))])
    begin()
    q[m:wide] = jnp.zeros((wide - m, width), BF)
    load_e2.wait()
    gain, shift = zero, zero
    for start, count in cut(m):
        part = slice(start, start + count)
        unit, pace = normalise(wide0[part])
        grad = wide1[part]
        gain += colsum(grad * unit)
        shift += colsum(grad)
        d2 = norm_back(unit, pace, egains[1:2], grad)
        da[part] = d2
        gb[part] = d2.astype(BF)
    d_gains[1:2] = gain
    d_shifts[1:2] = shift
    load_e1 = c.start(e1_h, wide1)
    load_a1 = c.start(a1_h, wide0)
    cross.a_wait()
    cross.b_start()
    for load in load_ffn:
        load.wait()
    ffn_back(zb, up, down, act, slope, gb.at[keys], slope, g1, d_bias, d_shifts, 2)
    effn.a_start()
    dffn.bb_wait()
    dffn.c_start()
    load_e1.wait()
    gain, shift = zero, zero
    for start, count in cut(m):
        part = slice(start, start + count)
        unit, pace = normalise(wide1[part])
        dz = da[part] + mm(slope[part], up[...], NT)
        gain += colsum(dz * unit)
        shift += colsum(dz)
        d1 = norm_back(unit, pace, egains[0:1], dz)
        da[part] = d1
        gb[part] = d1.astype(BF)
    d_gains[0:1] = gain
    d_shifts[0:1] = shift

    def enc0_():
        effn.a_wait()
        effn.b_start()

    def enc2():
        cross.b_wait()
        cross.bb_start()
        dffn.c_wait()
        dffn.d_start()

    for load in (load_ew, load_ot, *loads, load_x, save_dx1):
        load.wait()
    kt[:, :m] = k[:m].T
    put(g0, 3 * rows, mm(ot[:, :m], gb[:m]))
    edot, edo, edqt = dot_.at[:, queries], d_o.at[queries], dqt.at[:, queries]
    erowdot = rowdot.at[:, :, queries]
    back_outputs(gb.at[keys], wb, eot, erate, edot, edo, erowdot)
    back_heads(False, wide, eq, kt, v.at[keys], edot, edo, erowdot, fetch, pair_ds, edqt, dk.at[keys], dv.at[keys],
               {0: enc0_, 2: enc2})
    load_dx1 = c.start(dx1_h, d_o)
    cross.bb_wait()
    cross.c_start()
    put(g0, 0, mm(x1[...], dqt[:, :m], TT))
    put(g0, rows, mm(x1[...], dk[:m], TN))
    put(g0, 2 * rows, mm(x1[...], dv[:m], TN))
    enc0.a_start()
    enc1.a_start()
    effn.b_wait()
    effn.bb_start()
    for start, count in cut(m):
        part = slice(start, start + count)
        wide1[part] = da[part] + mm(dqt[:, part], wb[0], TT) + mm(dk[part], wb[1], NT) + mm(dv[part], wb[2], NT)
    c.out(wide1, dx_enc_h)

    load_ot = c.start(tot_h, ot)
    loads = [c.start(tqkv_h.at[i], item) for i, item in enumerate((q, k, v))]
    tile = 512
    spans = [(start + tile, slice(start, start + tile)) for start in range(0, n, tile)]
    begin, fetch = in_ring(ering, te_h, esems.at[2], spans)
    begin()
    load_a1.wait()
    load_dx1.wait()
    gain, shift = zero, zero
    for start, count in cut(n):
        part = slice(start, start + count)
        unit, pace = normalise(wide0[part])
        grad = d_o[part].astype(F32)
        gain += colsum(grad * unit)
        shift += colsum(grad)
        d1 = norm_back(unit, pace, dgains[0:1], grad)
        da[part] = d1
        gb[part] = d1.astype(BF)
    part_lanes = width // n_dp
    vec[...] = jnp.zeros_like(vec)
    for i in range(n_dp):
        lanes = slice(i * part_lanes, (i + 1) * part_lanes)
        for j in range(2):
            wide_lanes = slice((2 * i + j) * part_lanes, (2 * i + j + 1) * part_lanes)
            vec[i, j : j + 1, :part_lanes] = d_bias[:, wide_lanes]
            vec[i, 2 + j : 3 + j, :part_lanes] = d_bias_d[:, wide_lanes]
        vec[i, 4:6, :part_lanes] = d_gains[:, lanes]
        vec[i, 6:9, :part_lanes] = d_shifts[:, lanes]
        vec[i, 9:10, :part_lanes] = gain[:, lanes]
        vec[i, 10:12, :part_lanes] = d_gains_d[1:3, lanes]
        vec[i, 12:13, :part_lanes] = shift[:, lanes]
        vec[i, 13:16, :part_lanes] = d_shifts_d[1:4, lanes]
    vector.swap_start(0)
    enc0.a_wait()
    enc0.b_start()
    enc1.a_wait()
    enc1.b_start()

    quarter = half // 2

    def put_pair(p):
        lanes = slice(p * quarter, (p + 1) * quarter)
        sides = jnp.concatenate([dqt[lanes].T, dk[:, lanes], dv[:, lanes]], axis=1)
        put(pairs[p].source, 0, mm(x0[...], sides, TN))
        pairs[p].a_start()

    def tags0():
        vector.swap_wait(0)
        vector.swap_start(1)
        cross.c_wait()
        cross.d_start()
        effn.bb_wait()
        effn.c_start()

    def tags1():
        put_pair(0)

    def tags2():
        enc0.b_wait()
        enc1.b_wait()
        enc0.bb_start()
        enc1.bb_start()
        pair0.a_wait()
        pair0.q_start()
        vector.swap_wait(1)
        vector.swap_start(2)

    def tags3():
        put_pair(1)

    def tags4():
        pair1.a_wait()
        pair1.q_start()
        dffn.d_wait()
        effn.c_wait()
        effn.d_start()
        vector.swap_wait(2)
        vector.c_start()

    def tags5():
        put_pair(2)
        enc0.bb_wait()
        enc0.c_start()
        enc1.bb_wait()
        enc1.c_start()
        pair0.q_wait()
        pair0.c_start()

    def tags6():
        pair2.a_wait()
        pair2.q_start()

    def tags7():
        put_pair(3)
        cross.d_wait()
        enc0.c_wait()
        enc0.d_start()
        enc1.c_wait()
        enc1.d_start()
        pair1.q_wait()
        pair1.c_start()
        pair0.c_wait()
        pair0.d_start()

    for load in (load_ot, load_tw, load_tx, *loads):
        load.wait()
    kt[...] = k[...].T
    out = mm(ot[...], gb[...])
    for i, piece in enumerate(pairs):
        put(piece.source, 0, out[:, i * quarter : (i + 1) * quarter], 3 * quarter)
    back_outputs(gb, wa, ot, trate, dot_, d_o, rowdot)
    back_heads(True, tile, q, kt, v, dot_, d_o, rowdot, fetch, pair_ds, dqt, dk, dv,
               dict(enumerate((tags0, tags1, tags2, tags3, tags4, tags5, tags6, tags7))))
    pair3.a_wait()
    pair3.q_start()
    for i, (start, count) in enumerate(cut(n)):
        part = slice(start, start + count)
        wide0[part] = (da[part] + mm(dqt[:, part], wa[0], TT) + mm(dk[part], wa[1], NT) + mm(dv[part], wa[2], NT))
        if i == 0:
            pair2.q_wait()
            pair2.c_start()
    c.out(wide0, dx_tags_h)
    pair1.c_wait()
    pair1.d_start()
    pair3.q_wait()
    pair3.c_start()
    pair2.c_wait()
    pair2.d_start()
    vector.c_wait()
    effn.d_wait()
    own_copy.wait()
    for step in range(1, n_bal):
        moved(step, False).wait_send()
        moved(step, True).wait_recv()
    c.finish()
    pair3.c_wait()
    pair3.d_start()
    for piece in (enc0, enc1, *pairs):
        piece.d_wait()


def finish(all_cross, all_dffn, all_effn, all_enc0, all_enc1, all_self0, all_self1, all_self2, all_self3, v_total, decoded_h, patches_h, tags_h,
           o_enc, o_eup, o_ebias, o_edown, o_egains, o_eshifts,
           o_self, o_cross, o_dup, o_dbias, o_ddown, o_dgains, o_dshifts, o_decoded, o_patches, o_tags, tags, patches, decoded, sems):
    c = Copies(sems)
    moves = [(c.start(source, here), here, target) for source, here, target in
             ((tags_h, tags, o_tags), (patches_h, patches, o_patches), (decoded_h, decoded, o_decoded))]
    for load, here, target in moves:
        load.wait()
        c.out(here, target)

    def joined(gathered):
        return jnp.concatenate([gathered[b].astype(F32) for b in (0, 2, 1, 3)], axis=1)

    def layer(out, parts):
        rows = out.shape[0]
        for j in range(4):
            out[:, j, :] = parts[j * rows : (j + 1) * rows]

    def branch(up, down, parts):
        rows, width = up.shape[0], parts.shape[1]
        for j in range(up.shape[1] // width):
            up[:, j * width : (j + 1) * width] = parts[j * rows : (j + 1) * rows]
        down[...] = parts[2 * rows :]

    layer(o_enc, jnp.concatenate([joined(all_enc0), joined(all_enc1)], axis=0))
    layer(o_cross, joined(all_cross))
    branch(o_eup, o_edown, joined(all_effn))
    branch(o_dup, o_ddown, joined(all_dffn))
    rows, _, width = o_self.shape
    half = width // 2
    quarter = half // 2
    for i, gathered in enumerate((all_self0, all_self1, all_self2, all_self3)):
        parts = joined(gathered)
        for j in range(4):
            o_self[:, j, i * quarter : (i + 1) * quarter] = parts[:rows, j * quarter : (j + 1) * quarter]
    share = o_egains.shape[1]
    for j in range(2):
        o_ebias[:, j * share : (j + 1) * share] = v_total[j : j + 1, :share]
        o_dbias[:, j * share : (j + 1) * share] = v_total[2 + j : 3 + j, :share]
    o_egains[...] = v_total[4:6, :share]
    o_eshifts[...] = v_total[6:9, :share]
    o_dgains[...] = v_total[9:12, :share]
    o_dshifts[...] = v_total[12:16, :share]
    c.finish()


def call(kernel, ins, outs, out_specs, scratch, name, params=PARAMS):
    specs = [spec for spec, _ in ins]
    return pl.pallas_call(
        kernel,
        out_shape=outs,
        in_specs=specs,
        out_specs=out_specs,
        scratch_shapes=scratch,
        compiler_params=params,
        name=name,
    )(*[value for _, value in ins])


def talking(number):
    return pltpu.CompilerParams(vmem_limit_bytes=60 << 20, collective_id=number, has_side_effects=True)


def run_tags_forward(n_dp, n_bal, x, w, ew, cw, cot, gains, shifts):
    n, width = x.shape
    bf = lambda *s: Shape(s, BF)
    f32 = lambda *s: Shape(s, F32)
    vb = lambda *s: pltpu.VMEM(s, BF)
    vf = lambda *s: pltpu.VMEM(s, F32)
    line, turned, raw, split = vb(n, width), vb(width, n), vb(width, 4, width), vb(4, width, width)
    weights = bf(4, width, width)
    return call(
        functools.partial(tags_forward, n_dp, n_bal),
        [(ANY, x), (ANY, w), (ANY, ew), (ANY, cw), (ANY, cot), (VM, gains), (VM, shifts)],
        [bf(n, width), bf(*cot.shape), f32(HEADS, 1, n), weights, weights, weights, bf(3, n, width), bf(width, n),
         bf(HEADS, n, n), f32(n, width)],
        [VM, VM, VM] + [ANY] * 7,
        [line, raw, split, raw, split, raw, split, line, line, line, turned, turned, turned, vf(n, width), vb(4, n, n),
         pltpu.SemaphoreType.DMA((20,)), pltpu.SemaphoreType.DMA((4, n // 512)), pltpu.SemaphoreType.DMA((2 * n_bal,))],
        "tags_forward",
        talking(2),
    )


def run_forward(n_dp, n_bal, scalars, x, ew4, eup, ebias, edown, egains, eshifts, x1, cw4, up, bias, down, gains, shifts, cot):
    m, width = x.shape
    n = x1.shape[0]
    hidden = up.shape[1]
    wide = (m + 127) // 128 * 128
    piece = (n_dp // 2, 2, 4 * width // n_dp, width)
    bf = lambda *s: Shape(s, BF)
    f32 = lambda *s: Shape(s, F32)
    vb = lambda *s: pltpu.VMEM(s, BF)
    vf = lambda *s: pltpu.VMEM(s, F32)
    split, first, second = vb(4, width, width), vb(width, hidden), vb(hidden, width)
    short, line = vb(m, width), vb(n, width)
    return call(
        functools.partial(forward, cot.shape[0] // n_bal),
        [(SM, v) for v in scalars]
        + [(ANY, x), (ANY, ew4), (ANY, eup), (VM, ebias), (ANY, edown), (VM, egains), (VM, eshifts),
           (ANY, x1), (ANY, cw4), (ANY, up), (VM, bias), (ANY, down), (VM, gains), (VM, shifts), (ANY, cot)],
        [f32(HEADS, 1, wide), f32(HEADS, 1, n), bf(*piece), f32(1, hidden), f32(3, width), f32(4, width), bf(*cot.shape),
         bf(m, width), bf(3, m, width), bf(width, wide), bf(HEADS, m, wide), f32(m, width), f32(m, width), bf(m, width),
         bf(m, hidden), bf(m, hidden),
         f32(n, width), bf(n, width), bf(n, width), bf(m, width), bf(m, width), bf(width, n), bf(HEADS, m, n)],
        [VM] * 7 + [ANY] * 16,
        [short, split, first, second, line, short, short, vb(width, n), vb(width, m), vb(width, n), vb(4, m, n),
         vf(m, width), vf(m, width), short, vb(m, hidden), vb(m, hidden),
         line, short, split, first, second, vf(n, width), vf(n, 1), line, vb(n, hidden), vb(n, hidden), vf(n, width), line,
         pltpu.SemaphoreType.DMA((40,)), pltpu.SemaphoreType.DMA((4, 1))],
        "forward",
    )


def run_backward(n_dp, n_bal, inputs, vectors, shapes):
    n, m, width, hidden, wide, blocks = shapes
    rows = 4 * width // n_dp
    bf = lambda *s: Shape(s, BF)
    f32 = lambda *s: Shape(s, F32)
    vb = lambda *s: pltpu.VMEM(s, BF)
    vf = lambda *s: pltpu.VMEM(s, F32)
    least = max(rows // 4, 16)
    whole, part, small = bf(n_bal, rows, 128), bf(n_bal, rows // 2, 128), bf(n_bal, least, 128)
    line, turned = vb(n, width), vb(width, n)
    piece = vb(n_dp // 2, 2, rows, width)
    return call(
        functools.partial(backward, n_dp, n_bal),
        [(ANY, item) for item in inputs] + [(VM, item) for item in vectors],
        [f32(m, width), f32(n, width), bf(n, width), bf(*blocks), whole, whole, whole, part, part, small, small, small, small, f32(16, 128)],
        [ANY, ANY, ANY] + [VM] * 11,
        [vb(3, n, n), line, line, line, turned, turned, turned, line, vf(HEADS, 1, n), vb(width, max(n, hidden)), vb(max(n, hidden), width), line,
         vb(2, n, max(n, hidden)), line, vf(n, width), vf(n, width), vf(m, width), line, vb(m, width),
         vb(4, width, width), vb(4, width, width), piece, piece,
         vf(1, hidden), vf(2, width), vf(3, width), vf(n_dp, 16, 128), vf(3, n_dp, 16, 128), vf(n_dp // 2, 16, 128),
         vb(*kept_shape(n_dp, rows, False)), vb(*kept_shape(n_dp, rows // 2, False)),
         *room_scratch(n_dp, rows), *room_scratch(n_dp, rows),
         pltpu.SemaphoreType.DMA((40,)), pltpu.SemaphoreType.DMA((3, 4, n // 512)), pltpu.SemaphoreType.DMA((2 * n_bal,)),
         pltpu.SemaphoreType.DMA((6 + n_dp,)), *[piece_sems(n_dp, n_bal)] * 5,
         *pair_scratch(n_dp, n_bal, least, False) * 2, *pair_scratch(n_dp, n_bal, least, True) * 2],
        "backward",
        pltpu.CompilerParams(vmem_limit_bytes=60 << 20, collective_id=1, has_side_effects=True),
    )


def run_finish(n_dp, hidden, width, gathered, moved):
    share = width // n_dp
    f32 = lambda *s: Shape(s, F32)
    side = [f32(share, 4, width)]
    branch = [f32(share, hidden), f32(1, hidden // n_dp), f32(hidden // n_dp, width)]
    outs = side + branch + [f32(2, share), f32(3, share)] + side + side + branch + [f32(3, share), f32(4, share)]
    return call(finish, [(VM, v) for v in gathered] + [(ANY, v) for v in moved],
                outs + [Shape(v.shape, v.dtype) for v in moved], [VM] * len(outs) + [ANY] * 3,
                [pltpu.VMEM(v.shape, v.dtype) for v in moved[::-1]] + [pltpu.SemaphoreType.DMA((6,))], "finish")


def per_device(
    patches, tag_rows, cotangent, tag_length, cell_count, destination, slot_index,
    encoder_attention, encoder_up, encoder_up_bias, encoder_down, encoder_gains, encoder_shifts,
    decoder_self, decoder_cross, decoder_up, decoder_up_bias, decoder_down, decoder_gains, decoder_shifts,
):
    n_bal, n_dp = lax.axis_size("bal"), lax.axis_size("dp")
    length, width = tag_rows.shape[1:]
    hidden = encoder_up.shape[1]
    blocks = destination.shape[1]
    span = length // blocks
    cot = cotangent[0].reshape(blocks, span, width)
    eg, es, dg, ds = encoder_gains.T, encoder_shifts.T, decoder_gains.T, decoder_shifts.T
    eb, db = encoder_up_bias[None], decoder_up_bias[None]
    x1, cot, srate, sw4, ew4, cw4, sqkv, sot, se, a1 = run_tags_forward(
        n_dp, n_bal, tag_rows[0], decoder_self, encoder_attention, decoder_cross, cot, dg, ds)
    (erate, crate, g_dffn, d_db, d_dg, d_ds, y, memory, eqkv, eot, ee, e1, e2, zb, act, slope, da2, gb2, cq, ck, cv, c_ot,
     ce) = run_forward(
        n_dp, n_bal, (tag_length, cell_count, destination, slot_index), patches[0], ew4, encoder_up, eb, encoder_down,
        eg, es, x1, cw4, decoder_up, db, decoder_down, dg, ds, cot)
    d_patches, d_tags, _, decoded, all_cross, all_dffn, *gathered = run_backward(
        n_dp, n_bal,
        (da2, gb2, x1, memory, cw4, cq, ck, cv, c_ot, ce, y, g_dffn,
         e2, e1, zb, act, slope, encoder_up, encoder_down, patches[0], ew4, eqkv, eot, ee,
         a1, tag_rows[0], sw4, sqkv, sot, se),
        (crate, erate, srate, eg, dg, d_db, d_dg, d_ds),
        (length, patches.shape[1], width, hidden, eot.shape[1], y.shape))
    ew, eu, ebg, ed, egg, esg, sw, cw, du, dbg, dd, dgg, dsg, decoded, d_patches, d_tags = run_finish(
        n_dp, hidden, width, (all_cross, all_dffn, *gathered), (decoded, d_patches, d_tags))
    return (
        decoded.reshape(1, length, width), d_patches[None], d_tags[None],
        ew, eu, ebg.reshape(-1), ed, egg.T, esg.T, sw, cw, du, dbg.reshape(-1), dd, dgg.T, dsg.T,
    )


def solution(mesh):
    split = P(("dp", "bal"))
    in_specs = (split,) * 7 + (P(),) * 13
    out_specs = (split,) * 3 + (P("dp"),) * 13
    return jax.shard_map(per_device, mesh=mesh, in_specs=in_specs, out_specs=out_specs, check_vma=False)
```

```python
import functools

import jax
import jax.numpy as jnp
from jax import lax
from jax.experimental import pallas as pl
from jax.experimental.pallas import tpu as pltpu
from jax.sharding import PartitionSpec as P

HEADS = 8
HEAD = 64
EPSILON = 1e-05
NEGATIVE = -1e30
BF = jnp.bfloat16
F32 = jnp.float32
NN = (((1,), (0,)), ((), ()))
NT = (((1,), (1,)), ((), ()))
TN = (((0,), (0,)), ((), ()))
TT = (((0,), (1,)), ((), ()))
VM = pl.BlockSpec(memory_space=pltpu.VMEM)
SM = pl.BlockSpec(memory_space=pltpu.SMEM)
ANY = pl.BlockSpec(memory_space=pl.ANY)
LIMIT = 1e18
PARAMS = pltpu.CompilerParams(vmem_limit_bytes=60 << 20)
Shape = jax.ShapeDtypeStruct


def mm(left, right, dims=NN):
    return lax.dot_general(left, right, dims, preferred_element_type=F32)


def cut(rows):
    half = (rows // 2 + 15) // 16 * 16
    return [(0, half), (half, rows - half)]


class Copies:
    def __init__(self, sems):
        self.sems, self.used, self.open = sems, 0, []

    def start(self, source, target):
        copy = pltpu.make_async_copy(source, target, self.sems.at[self.used])
        self.used += 1
        copy.start()
        return copy

    def out(self, source, target):
        self.open.append(self.start(source, target))

    def finish(self):
        for copy in self.open:
            copy.wait()


def split_weights(raw, parts):
    def step(i, carry):
        rows = pl.ds(pl.multiple_of(i * 128, 128), 128)
        parts[:, rows, :] = pltpu.einshape("abc->bac", raw[rows])
        return carry

    lax.fori_loop(0, raw.shape[0] // 128, step, 0)


def normalise(signal):
    centre = jnp.mean(signal, axis=-1, keepdims=True)
    centered = signal - centre
    spread = jnp.mean(centered * centered, axis=-1, keepdims=True)
    rate = lax.rsqrt(spread + EPSILON)
    return centered * rate, rate


def norm_back(unit, rate, gain, gradient):
    inner = gradient * gain
    first = jnp.mean(inner, axis=-1, keepdims=True)
    second = jnp.mean(inner * unit, axis=-1, keepdims=True)
    return rate * (inner - first - unit * second)


def colsum(signal):
    return jnp.sum(signal, axis=0, keepdims=True)


def smooth(hidden):
    scale = 0.7978845608028654
    square = hidden * hidden
    curve = jnp.tanh(scale * hidden * (1.0 + 0.044715 * square))
    half = 0.5 + 0.5 * curve
    slope = half + 0.5 * hidden * (1.0 - curve * curve) * (scale + (3 * 0.044715 * scale) * square)
    return hidden * half, slope


def half_mask(shape, axis, which):
    index = lax.broadcasted_iota(jnp.int32, shape, axis)
    return (index < HEAD) if which == 0 else (index >= HEAD)


def keep_half(pair, axis, which):
    return jnp.where(half_mask(pair.shape, axis, which), pair, jnp.zeros_like(pair))


def project_qkv(x, sources, w4, q, qt, k, v, vt):
    rows = x.shape[0]
    for start, size in cut(rows):
        part = slice(start, start + size)
        q[part] = (mm(x[part], w4[0]) * HEAD ** (-0.5)).astype(BF)
    if q.shape[0] > rows:
        q[rows:] = jnp.zeros((q.shape[0] - rows, q.shape[1]), BF)
    for start, size in cut(sources.shape[0]):
        part = slice(start, start + size)
        k[part] = mm(sources[part], w4[1]).astype(BF)
        v[part] = mm(sources[part], w4[2]).astype(BF)
    qt[...] = q[...].T
    vt[...] = v[...].T


def shifted_exp(scores, exact, causal_rows):
    if causal_rows:
        size, width = scores.shape
        key = lax.broadcasted_iota(jnp.int32, (width, width), 0)
        query = lax.broadcasted_iota(jnp.int32, (width, width), 1)
        last = jnp.where(key <= query, scores[size - width :], NEGATIVE)
        scores = last if size == width else jnp.concatenate([scores[: size - width], last], axis=0)
        exact = exact or size == width
    sample = scores if exact else scores[:128]
    return jnp.exp(scores - jnp.max(sample, axis=0, keepdims=True))


def attend_heads(exact, causal, q_tile, qt, k, vt, ot, rate, store, beside=None):
    keys, queries = k.shape[0], qt.shape[1]

    def pair(p, carry):
        lanes = pl.ds(pl.multiple_of(p * 128, 128), 128)
        if beside is not None:
            beside(p)
        for u in range(2):
            rows = pl.ds(pl.multiple_of(p * 128 + u * HEAD, HEAD), HEAD)
            place, done = store(p, u)
            for start in range(0, queries, q_tile):
                cols = slice(start, start + q_tile)
                depth = start + q_tile if causal else keys
                scores = mm(k[:depth, lanes], keep_half(qt[lanes, cols], 0, u))
                raised = shifted_exp(scores, exact, causal)
                total = jnp.sum(raised, axis=0, keepdims=True)
                low = raised.astype(BF)
                place[:depth, cols] = low
                inverse = 1.0 / total
                rate[2 * p + u, :, cols] = inverse
                ot[rows, cols] = (mm(vt[rows, :depth], low) * inverse).astype(BF)
            done()
        return carry

    lax.fori_loop(0, HEADS // 2, pair, 0)


def attend(causal, q_tile, qt, k, vt, ot, rate, store, drain):
    attend_heads(False, causal, q_tile, qt, k, vt, ot, rate, store)
    drain()
    fine = jnp.min(rate[...]) > 1.0 / LIMIT

    @pl.when(jnp.logical_not(fine))
    def _():
        attend_heads(True, causal, q_tile, qt, k, vt, ot, rate, store)
        drain()


def back_heads(causal, q_tile, q, kt, v, dot_, d_o, rowdot, fetch, ds, dqt, dk, dv, hook=None):
    keys, queries = v.shape[0], dqt.shape[1]

    def pair(p, carry):
        lanes = pl.ds(pl.multiple_of(p * 128, 128), 128)
        for u in range(2):
            rows = pl.ds(pl.multiple_of(p * 128 + u * HEAD, HEAD), HEAD)
            place = fetch(p, u)
            for start in range(0, queries, q_tile):
                cols = slice(start, start + q_tile)
                depth = start + q_tile if causal else keys
                grad = mm(v[:depth, lanes], keep_half(dot_[lanes, cols], 0, u))
                scaled = place[:depth, cols].astype(F32) * (grad - rowdot[2 * p + u, :, cols])
                low = scaled.astype(BF)
                ds[u][:depth, cols] = low
                dqt[rows, cols] = (mm(kt[rows, :depth], low) * HEAD ** (-0.5)).astype(BF)
            qm = q[:queries, lanes]
            dm = d_o[:queries, lanes]
            steps = range(0, keys, q_tile) if causal else (0,)
            for start in steps:
                key = slice(start, start + q_tile) if causal else slice(0, keys)
                more_k = mm(ds[u][key, start:queries], qm[start:])
                more_v = mm(place[key, start:queries], dm[start:])
                if u == 0:
                    dk[key, lanes] = more_k.astype(BF)
                    dv[key, lanes] = more_v.astype(BF)
                else:
                    dk[key, lanes] = jnp.where(half_mask(more_k.shape, 1, 1), more_k.astype(BF), dk[key, lanes])
                    dv[key, lanes] = jnp.where(half_mask(more_v.shape, 1, 1), more_v.astype(BF), dv[key, lanes])
            if hook is not None:
                for at, act in hook.items():
                    if at % 2 == u:
                        pl.when(p == at // 2)(act)
        return carry

    lax.fori_loop(0, HEADS // 2, pair, 0)


def back_outputs(grad_low, w4, ot, rate, dot_, d_o, rowdot):
    rows, wide = grad_low.shape[0], dot_.shape[1]
    raw = mm(w4[3], grad_low[...], NT)
    for h in range(HEADS):
        part = slice(h * HEAD, (h + 1) * HEAD)
        low = (raw[part] * rate[h][:, :rows]).astype(BF)
        if wide > rows:
            low = jnp.concatenate([low, jnp.zeros((HEAD, wide - rows), BF)], axis=1)
        dot_[part] = low
        rowdot[h] = jnp.sum(low.astype(F32) * ot[part].astype(F32), axis=0, keepdims=True)
    d_o[...] = dot_[...].T


def ring(buffers, hbm, sems, spans, out):
    def copies(h, slot):
        made = []
        for i, (rows, cols) in enumerate(spans):
            here = buffers.at[slot, pl.ds(0, rows), cols]
            there = hbm.at[h, pl.ds(0, rows), cols]
            made.append(
                pltpu.make_async_copy(here, there, sems.at[slot, i])
                if out
                else pltpu.make_async_copy(there, here, sems.at[slot, i])
            )
        return made

    return copies


def out_ring(buffers, hbm, sems, spans):
    copies = ring(buffers, hbm, sems, spans, True)

    def store(p, u):
        slot = (p % 2) * 2 + u

        @pl.when(p >= 2)
        def _():
            for copy in copies(2 * p + u, slot):
                copy.wait()

        def done():
            for copy in copies(2 * p + u, slot):
                copy.start()

        return buffers.at[slot], done

    def drain():
        for slot in range(4):
            for copy in copies(slot, slot):
                copy.wait()

    return store, drain


def in_ring(buffers, hbm, sems, spans):
    copies = ring(buffers, hbm, sems, spans, False)
    depth = buffers.shape[0]

    def begin():
        for h in range(depth):
            for copy in copies(h, h):
                copy.start()

    def fetch(p, u):
        h = 2 * p + u
        for copy in copies(h, h % depth):
            copy.wait()

        @pl.when((h >= 1) & (h + depth <= HEADS))
        def _():
            for copy in copies(h + depth - 1, (h + depth - 1) % depth):
                copy.start()

        return buffers.at[h % depth]

    return begin, fetch


MESH = pl.DeviceIdType.MESH


class Spot:
    def __init__(self, n, m):
        self.n, self.m = n, m
        self.d, self.b = lax.axis_index("dp"), lax.axis_index("bal")
        self.core, self.far = self.b % 2, self.b // 2
        self.parity, self.row = self.d % 2, self.d // 2
        self.by_core = (self.d, self.b + 1 - 2 * self.core)
        self.by_far = (self.d, self.b + 2 - 4 * self.far)
        self.by_parity = (self.d + 1 - 2 * self.parity, self.b)

    def greet(self, everyone=True):
        barrier = pltpu.get_barrier_semaphore()

        def call(device):
            pl.semaphore_signal(barrier, inc=1, device_id=device, device_id_type=MESH)

        for k in range(1, self.m):
            call((self.d, (self.b + k) % self.m))

        if not everyone:
            return
        call(self.by_parity)
        call((self.by_parity[0], self.by_far[1]))

        def along(k, carry):
            call((((self.row + k) % (self.n // 2)) * 2 + self.parity, self.b))
            return carry

        lax.fori_loop(1, self.n // 2, along, 0)

    def await_all(self, everyone=True):
        pl.semaphore_wait(pltpu.get_barrier_semaphore(), self.m - 1 + (2 + self.n // 2 - 1 if everyone else 0))


def remote(source, target, sent, received, device):
    return pltpu.make_async_remote_copy(
        src_ref=source, dst_ref=target, send_sem=sent, recv_sem=received, device_id=device, device_id_type=MESH
    )


class Piece:
    def __init__(self, spot, along_x, sems, source=None, acc=None, land_a=None, kept=None, land_b=None, kept2=None,
                 land_c=None, slots=None, result=None, gathered=None):
        self.spot, self.along_x, self.source, self.sems = spot, along_x, source, sems
        self.acc, self.land_a, self.kept, self.land_b = acc, land_a, kept, land_b
        self.kept2, self.land_c = kept2, land_c
        self.slots, self.result, self.gathered = slots, result, gathered

    def a_copies(self):
        half = self.acc.shape[3]
        mine = pl.ds(pl.multiple_of(self.spot.core * half, half), half)
        other = pl.ds(pl.multiple_of((1 - self.spot.core) * half, half), half)
        return [
            pltpu.make_async_copy(self.source.at[:, :, :, mine], self.acc, self.sems.at[0]),
            remote(self.source.at[:, :, :, other], self.land_a, self.sems.at[1], self.sems.at[2], self.spot.by_core),
        ]

    def a_start(self):
        for copy in self.a_copies():
            copy.start()

    def a_wait(self):
        for copy in self.a_copies():
            copy.wait()

        def add(i, carry):
            self.acc[i] = self.acc[i] + self.land_a[i]
            return carry

        lax.fori_loop(0, self.acc.shape[0], add, 0)

    def lanes(self, mine, size):
        side = self.spot.far if mine else 1 - self.spot.far
        return pl.ds(pl.multiple_of(side * size, size), size)

    def b_copy(self):
        spot = self.spot
        if self.along_x:
            out, to = self.acc.at[:, :, :, self.lanes(False, self.land_b.shape[3])], spot.by_far
        else:
            out, to = self.acc.at[:, 1 - spot.parity], spot.by_parity
        return remote(out, self.land_b, self.sems.at[3], self.sems.at[4], to)

    def b_start(self):
        self.b_copy().start()

    def b_wait(self):
        self.b_copy().wait()

        def add(i, carry):
            if self.along_x:
                mine = self.acc[i, :, :, self.lanes(True, self.land_b.shape[3])]
            else:
                mine = self.acc[i, self.spot.parity]
            self.kept[i] = mine + self.land_b[i]
            return carry

        lax.fori_loop(0, self.kept.shape[0], add, 0)

    def bb_copy(self):
        spot = self.spot
        if self.along_x:
            out, to = self.kept.at[:, 1 - spot.parity], spot.by_parity
        else:
            out, to = self.kept.at[:, :, self.lanes(False, self.land_c.shape[2])], spot.by_far
        return remote(out, self.land_c, self.sems.at[5], self.sems.at[6], to)

    def bb_start(self):
        self.bb_copy().start()

    def bb_wait(self):
        self.bb_copy().wait()

        def add(i, carry):
            if self.along_x:
                mine = self.kept[i, self.spot.parity]
            else:
                mine = self.kept[i, :, self.lanes(True, self.land_c.shape[2])]
            self.kept2[i] = mine + self.land_c[i]
            return carry

        lax.fori_loop(0, self.kept2.shape[0], add, 0)

    def base(self):
        return 7

    def c_copy(self, k, arriving):
        spot, half = self.spot, self.spot.n // 2
        row = (spot.row + k) % half
        slot = row if arriving else spot.row
        return remote(self.kept2.at[row], self.slots.at[slot], self.sems.at[self.base() + k], self.sems.at[self.base() + half + slot],
                      (row * 2 + spot.parity, spot.b))

    def c_start(self):
        def step(k, carry):
            self.c_copy(k, False).start()
            return carry

        lax.fori_loop(1, self.spot.n // 2, step, 0)

    def c_wait(self):
        half, row = self.spot.n // 2, self.spot.row

        def step(k, total):
            self.c_copy(k, False).wait_send()
            self.c_copy(k, True).wait_recv()
            return total + self.slots[(row + k) % half].astype(F32)

        total = lax.fori_loop(1, half, step, self.kept2[row].astype(F32))
        self.result[...] = total.astype(BF)

    def d_copies(self, arriving):
        spot, base = self.spot, self.base() + self.spot.n
        made = []
        for k in range(1, spot.m):
            peer = (spot.b + k) % spot.m
            slot = peer if arriving else spot.b
            made.append(remote(self.result, self.gathered.at[slot], self.sems.at[base + k],
                               self.sems.at[base + spot.m + slot], (spot.d, peer)))
        return made

    def d_start(self):
        for copy in self.d_copies(False):
            copy.start()
        self.gathered[self.spot.b] = self.result[...]

    def d_wait(self):
        for copy in self.d_copies(False):
            copy.wait_send()
        for copy in self.d_copies(True):
            copy.wait_recv()


class PairPiece(Piece):
    def __init__(self, spot, sems, source, acc, land_a, quads, kept2, slots, result, gathered):
        super().__init__(spot, True, sems, source, acc, land_a, kept2=kept2, slots=slots, result=result, gathered=gathered)
        self.quads = quads

    def base(self):
        return 11

    def quarter(self, far):
        lanes = self.kept2.shape[2]
        return pl.ds(pl.multiple_of(far * lanes, lanes), lanes)

    def q_copy(self, k, arriving):
        spot = self.spot
        me = spot.far * 2 + spot.parity
        peer = (me + k) % 4
        far, parity = peer // 2, peer % 2
        slot = peer if arriving else me
        return remote(self.acc.at[:, parity, :, self.quarter(far)], self.quads.at[slot], self.sems.at[3 + k],
                      self.sems.at[7 + slot], (spot.row * 2 + parity, spot.core + 2 * far))

    def q_start(self):
        for k in range(1, 4):
            self.q_copy(k, False).start()

    def q_wait(self):
        spot = self.spot
        me = spot.far * 2 + spot.parity
        for k in range(1, 4):
            self.q_copy(k, False).wait_send()
            self.q_copy(k, True).wait_recv()

        def add(i, carry):
            total = self.acc[i, spot.parity, :, self.quarter(spot.far)].astype(F32)
            for k in range(1, 4):
                total = total + self.quads[(me + k) % 4, i].astype(F32)
            self.kept2[i] = total.astype(BF)
            return carry

        lax.fori_loop(0, self.kept2.shape[0], add, 0)


def pair_scratch(n, m, rows, whole):
    vb = lambda shape: pltpu.VMEM(shape, BF)
    first = [vb((n // 2, 2, rows, 512)), vb(half_shape(n, rows)), vb(half_shape(n, rows))] if whole else []
    return first + [vb((4, *last_shape(n, rows))), vb(last_shape(n, rows)), vb(last_shape(n, rows)), vb((rows, 128)),
                    pltpu.SemaphoreType.DMA((11 + n + 2 * m,))]


def piece_sems(n, m):
    return pltpu.SemaphoreType.DMA((7 + n + 2 * m,))


def half_shape(n, rows):
    return (n // 2, 2, rows, 256)


def kept_shape(n, rows, along_x):
    return (n // 2, 2, rows, 128) if along_x else (n // 2, rows, 256)


def last_shape(n, rows):
    return (n // 2, rows, 128)


class VectorSum:
    def __init__(self, spot, v, lands, slots, result, sems):
        self.spot, self.v, self.lands, self.slots, self.result, self.sems = spot, v, lands, slots, result, sems

    def swap(self, step):
        device = (self.spot.by_core, self.spot.by_far, self.spot.by_parity)[step]
        return remote(self.v, self.lands.at[step], self.sems.at[2 * step], self.sems.at[2 * step + 1], device)

    def swap_start(self, step):
        self.swap(step).start()

    def swap_wait(self, step):
        self.swap(step).wait()
        self.v[...] = self.v[...] + self.lands[step]

    def copy(self, k, arriving):
        spot, half = self.spot, self.spot.n // 2
        row = (spot.row + k) % half
        slot = row if arriving else spot.row
        return remote(self.v.at[row * 2 + spot.parity], self.slots.at[slot], self.sems.at[6 + k],
                      self.sems.at[6 + half + slot], (row * 2 + spot.parity, spot.b))

    def c_start(self):
        def step(k, carry):
            self.copy(k, False).start()
            return carry

        lax.fori_loop(1, self.spot.n // 2, step, 0)

    def c_wait(self):
        half, row = self.spot.n // 2, self.spot.row

        def step(k, total):
            self.copy(k, False).wait_send()
            self.copy(k, True).wait_recv()
            return total + self.slots[(row + k) % half]

        self.result[...] = lax.fori_loop(1, half, step, self.v[self.spot.d])


def put(piece, row, value, lane=0):
    halves, two, width = piece.shape[0], piece.shape[1], value.shape[1]
    rows = value.shape[0] // (halves * two)
    piece[:, :, row : row + rows, lane : lane + width] = value.reshape(halves, two, rows, width).astype(BF)


def split_part(raw, parts, p):
    rows = pl.ds(pl.multiple_of(p * 128, 128), 128)
    parts[:, rows, :] = pltpu.einshape("abc->bac", raw[rows])


def tags_forward(n_dp, n_bal, x_h, w_h, ew_h, cw_h, cot_h, gains, shifts,
                 x1, cot, rate, w4_h, ew4_h, cw4_h, qkv_h, ot_h, e_h, a1_h,
                 x, raw, w4, raw_e, ew4, raw_c, cw4, q, k, v, qt, vt, ot, a1, ering, sems, esems, moves):
    spot = Spot(n_dp, n_bal)
    spot.greet(False)
    c = Copies(sems)
    load_w = c.start(w_h, raw)
    load_x = c.start(x_h, x)
    load_e, load_c = c.start(ew_h, raw_e), c.start(cw_h, raw_c)
    load_w.wait()
    split_weights(raw, w4)
    c.out(w4, w4_h)
    load_x.wait()
    project_qkv(x, x, w4, q, qt, k, v, vt)
    n = x.shape[0]
    for i, item in enumerate((q, k, v)):
        c.out(item, qkv_h.at[i])
    spot.await_all(False)
    share = cot_h.shape[0] // n_bal

    def moved(step, arriving):
        peer = (spot.b + step) % n_bal
        slot = peer if arriving else spot.b
        return remote(cot_h.at[pl.ds(peer * share, share)], cot.at[pl.ds(slot * share, share)], moves.at[step],
                      moves.at[n_bal + slot], (spot.d, peer))

    own = pl.ds(spot.b * share, share)
    own_copy = pltpu.make_async_copy(cot_h.at[own], cot.at[own], moves.at[0])
    own_copy.start()
    for step in range(1, n_bal):
        moved(step, False).start()
    load_e.wait()
    load_c.wait()

    def beside(p):
        split_part(raw_e, ew4, p)
        split_part(raw_c, cw4, p)

    tile = 512
    spans = [(start + tile, slice(start, start + tile)) for start in range(0, n, tile)]
    store, drain = out_ring(ering, e_h, esems, spans)
    attend_heads(True, True, tile, qt, k, vt, ot, rate, store, beside)
    drain()
    c.out(ew4, ew4_h)
    c.out(cw4, cw4_h)
    c.out(ot, ot_h)
    for start, size in cut(n):
        part = slice(start, start + size)
        first = x[part].astype(F32) + mm(ot[:, part], w4[3], TN)
        a1[part] = first
        unit, _ = normalise(first)
        x1[part] = (unit * gains[0:1] + shifts[0:1]).astype(BF)
    c.out(a1, a1_h)
    own_copy.wait()
    for step in range(1, n_bal):
        moved(step, False).wait_send()
        moved(step, True).wait_recv()
    c.finish()


def forward(capacity, tag_length, cell_count, destination, slot_index,
            x_h, ew4_h, eup_h, ebias, edown_h, egains, eshifts,
            x1_h, cw4_h, up_h, bias, down_h, gains, shifts, cot_h,
            erate, rate, g_ffn, d_bias, d_gains, d_shifts, y,
            mem_h, eqkv_h, eot_h, ee_h, e1_h, e2_h, zb_h, eact_h, eslope_h,
            da_h, gb_h, q_h, k_h, v_h, ot_h, e_h,
            x, ew4, eup, edown, q, k, v, qt, vt, ot, ering, e1, e2, zb, eact, eslope,
            x1, mem, w4, up, down, unit2, rate2, xb2, act, slope, da, gb, sems, esems):
    cot, dh = y, slope
    c = Copies(sems)
    load_w = c.start(ew4_h, ew4)
    load_x = c.start(x_h, x)
    load_eup = c.start(eup_h, eup)
    load_edown = c.start(edown_h, edown)
    load_w.wait()
    load_x.wait()
    m, n = x.shape[0], x1.shape[0]
    wide = eot_h.shape[1]
    eq, eqt, eot = q.at[pl.ds(0, wide)], qt.at[:, pl.ds(0, wide)], ot.at[:, pl.ds(0, wide)]
    project_qkv(x, x, ew4, eq, eqt, k, v, vt)
    spent = [c.start(item, eqkv_h.at[i]) for i, item in enumerate((q.at[pl.ds(0, m)], k, v))]
    load_w = c.start(cw4_h, w4)
    load_x1 = c.start(x1_h, x1)
    load_up = c.start(up_h, up)
    load_down = c.start(down_h, down)
    load_cot = c.start(cot_h, cot)
    view = ering.at[:, :, pl.ds(0, wide)]
    store, drain = out_ring(view, ee_h, esems, [(m, slice(None))])
    attend(False, wide, eqt, k, vt, eot, erate, store, drain)
    spent.append(c.start(eot, eot_h))
    load_eup.wait()
    load_edown.wait()
    for start, size in cut(m):
        part = slice(start, start + size)
        first = x[part].astype(F32) + mm(ot[:, part], ew4[3], TN)
        e1[part] = first
        unit, _ = normalise(first)
        z = unit * egains[0:1] + eshifts[0:1]
        low = z.astype(BF)
        zb[part] = low
        active, bend = smooth(mm(low, eup[...]) + ebias[...])
        eact[part] = active.astype(BF)
        eslope[part] = bend.astype(BF)
        second = z + mm(eact[part], edown[...]) + eshifts[2:3]
        e2[part] = second
        unit, _ = normalise(second)
        mem[part] = (unit * egains[1:2] + eshifts[1:2]).astype(BF)
    for here, there in ((e1, e1_h), (e2, e2_h), (zb, zb_h), (eact, eact_h), (eslope, eslope_h), (mem, mem_h)):
        c.out(here, there)

    load_w.wait()
    load_x1.wait()
    for copy in spent:
        copy.wait()
    project_qkv(x1, mem, w4, q, qt, k, v, vt)
    for here, there in ((q, q_h), (k, k_h), (v, v_h)):
        c.out(here, there)
    blocks = y.shape[0]
    block = n // blocks
    store, drain = out_ring(ering, e_h, esems, [(m, slice(None))])
    attend(False, n, qt, k, vt, ot, rate, store, drain)
    c.out(ot, ot_h)
    load_up.wait()
    load_down.wait()
    load_cot.wait()
    live = tag_length[0] + cell_count[0]
    places = [destination[0, b] * capacity + slot_index[0, b] for b in range(blocks)]
    zero = jnp.zeros((1, x1.shape[1]), F32)
    gain3, shift3 = zero, zero
    for start, size in cut(n):
        part = slice(start, start + size)
        second = x1[part].astype(F32) + mm(ot[:, part], w4[3], TN)
        unit, pace = normalise(second)
        unit2[part] = unit
        rate2[part] = pace
        x2 = unit * gains[1:2] + shifts[1:2]
        low = x2.astype(BF)
        xb2[part] = low
        active, bend = smooth(mm(low, up[...]) + bias[...])
        act[part] = active.astype(BF)
        slope[part] = bend.astype(BF)
        third = x2 + mm(act[part], down[...]) + shifts[3:4]
        unit, pace = normalise(third)
        row = lax.broadcasted_iota(jnp.int32, (size, 1), 0) + start
        alive = (row < live).astype(F32)
        final = ((unit * gains[2:3] + shifts[2:3]) * alive).astype(BF)
        picked = []
        for b in range(start // block, (start + size) // block):
            picked.append(cot[places[b]])
            y[places[b]] = final[b * block - start : (b + 1) * block - start]
        dy = jnp.concatenate(picked, axis=0).astype(F32) * alive
        gain3 += colsum(dy * unit)
        shift3 += colsum(dy)
        d3 = norm_back(unit, pace, gains[2:3], dy)
        da[part] = d3
        gb[part] = d3.astype(BF)
    d_gains[2:3] = gain3
    d_shifts[2:3] = shift3
    ffn_back(xb2, up, down, act, slope, gb, dh, g_ffn, d_bias, d_shifts, 3)
    gain2, shift2 = zero, zero
    for start, size in cut(n):
        part = slice(start, start + size)
        dx2 = da[part] + mm(dh[part], up[...], NT)
        gain2 += colsum(dx2 * unit2[part])
        shift2 += colsum(dx2)
        d2 = norm_back(unit2[part], rate2[part], gains[1:2], dx2)
        da[part] = d2
        gb[part] = d2.astype(BF)
    d_gains[1:2] = gain2
    d_shifts[1:2] = shift2
    c.out(gb, gb_h)
    c.out(da, da_h)
    c.finish()


def ffn_back(xb, up, down, act, slope, gb, dh, g_ffn, d_bias, d_shifts, row, middle=None):
    n, width = xb.shape
    offset = jnp.zeros((1, up.shape[1]), F32)
    for start, size in cut(n):
        part = slice(start, start + size)
        low = (mm(gb[part], down[...], NT) * slope[part].astype(F32)).astype(BF)
        dh[part] = low
        offset += colsum(low.astype(F32))
    d_bias[...] = offset
    d_shifts[row : row + 1] = colsum(gb[...].astype(F32))
    if middle is not None:
        middle()
    rows = g_ffn.shape[2] // 4
    put(g_ffn, 2 * rows, mm(act[...], gb[...], TN))
    for j in range(up.shape[1] // width):
        put(g_ffn, j * rows, mm(xb[...], dh[:, j * width : (j + 1) * width], TN))


class Room:
    def __init__(self, acc, land, kept, next_, kept_x, next_x, kept2, last, slots, result):
        self.acc, self.land, self.kept, self.next = acc, land, kept, next_
        self.kept_x, self.next_x, self.kept2, self.last, self.slots, self.result = kept_x, next_x, kept2, last, slots, result

    def whole(self, spot, sems, source, gathered):
        return Piece(spot, False, sems, source, self.acc, self.land, self.kept, self.next, self.kept2, self.last,
                     self.slots, self.result, gathered)

    def part(self, spot, sems, source, gathered, along_x, start, size):
        rows, head = pl.ds(start, size), pl.ds(0, size)
        kept = self.kept_x.at[:, :, head] if along_x else self.kept.at[:, rows]
        next_ = self.next_x.at[:, :, head] if along_x else self.next.at[:, rows]
        return Piece(spot, along_x, sems, source, self.acc.at[:, :, rows], self.land.at[:, :, rows], kept, next_,
                     self.kept2.at[:, rows], self.last.at[:, rows], self.slots.at[:, rows], self.result.at[rows], gathered)


def room_scratch(n, rows):
    vb = lambda shape: pltpu.VMEM(shape, BF)
    last, side = vb(last_shape(n, rows)), vb(kept_shape(n, rows // 2, True))
    kept = vb(kept_shape(n, rows, False))
    return [vb(half_shape(n, rows)), vb(half_shape(n, rows)), kept, kept, side, side, last, last, last, vb((rows, 128))]


def backward(n_dp, n_bal,
             da_h, gb_h, x1_h, mem_h, cw4_h, cq_h, ck_h, cv_h, cot_h, ce_h, y_h, g_dffn,
             e2_h, e1_h, zb_h, act_h, slope_h, up_h, down_h, ex_h, ew4_h, eqkv_h, eot_h, ee_h,
             a1_h, tx_h, tw4_h, tqkv_h, tot_h, te_h,
             crate, erate, trate, egains, dgains, d_bias_d, d_gains_d, d_shifts_d,
             dx_enc_h, dx_tags_h, dx1_h, decoded, all_cross, all_dffn, all_effn, all_enc0, all_enc1, *rest_refs):
    all_self, v_total = rest_refs[:4], rest_refs[4]
    (ering, q, k, v, ot, kt, dot_, d_o, rowdot, dqt, dk, dv, ds, gb, da, wide0, wide1, x0, x1,
     wa, wb, g0, g1, d_bias, d_gains, d_shifts, vec, vec_lands, vec_slots, next_effn, next_enc1, *rest) = rest_refs[5:]
    room0, room1 = Room(*rest[:10]), Room(*rest[10:20])
    sems, esems, moves, vsems = rest[20:24]
    psems = rest[24:29]
    early, late = [rest[29:34], rest[34:39]], [rest[39:47], rest[47:55]]
    spot = Spot(n_dp, n_bal)
    spot.greet()
    c = Copies(sems)
    n, width = x0.shape
    m = x1.shape[0]
    wide = eot_h.shape[1]
    hidden = up_h.shape[1]
    size = g0.shape[2] // 2
    rows = size // 2
    half = width // 2
    low, high = pl.ds(0, size), pl.ds(size, size)
    least = all_self[0].shape[1]
    dffn = room0.whole(spot, psems[0], g_dffn, all_dffn)
    cross = room1.whole(spot, psems[1], g0, all_cross)
    effn = room0.whole(spot, psems[2], g1, all_effn)
    effn.land_b = next_effn
    enc0 = room1.part(spot, psems[3], g0.at[:, :, low], all_enc0, True, 0, size)
    enc1 = room1.part(spot, psems[4], g0.at[:, :, high], all_enc1, False, size, size)
    enc1.land_b = next_enc1
    pairs = []
    for i, gathered in enumerate(all_self):
        if i < 2:
            where = pl.ds(i * least, least)
            first = g1.at[:, :, where], room0.acc.at[:, :, where], room0.land.at[:, :, where]
            others = early[i]
        else:
            first, others = late[i - 2][:3], late[i - 2][3:]
        pairs.append(PairPiece(spot, others[4], *first, *others[:4], gathered))
    pair0, pair1, pair2, pair3 = pairs
    vector = VectorSum(spot, vec, vec_lands, vec_slots, v_total, vsems)
    zero = jnp.zeros((1, width), F32)
    pair_ds = ds.at[0], ds.at[1]

    load_gb = c.start(gb_h, gb)
    load_ot = c.start(cot_h, ot)
    load_w = c.start(cw4_h, wa)
    loads = [c.start(a, b) for a, b in ((ck_h, k.at[pl.ds(0, m)]), (cv_h, v.at[pl.ds(0, m)]), (cq_h, q))]
    begin, fetch = in_ring(ering, ce_h, esems.at[0], [(m, slice(0, n))])
    begin()
    last = [c.start(a, b) for a, b in ((x1_h, x0), (mem_h, x1), (da_h, da))]
    load_ew = c.start(ew4_h, wb)
    load_e2 = c.start(e2_h, wide0.at[pl.ds(0, m)])
    load_gb.wait()
    load_ot.wait()
    put(g0, 3 * rows, mm(ot[...], gb[...]))
    load_w.wait()
    back_outputs(gb, wa, ot, crate, dot_, d_o, rowdot)
    for load in loads:
        load.wait()
    kt[:, :m] = k[:m].T
    spot.await_all()
    dffn.a_start()
    share = y_h.shape[0] // n_bal

    def moved(step, arriving):
        peer = (spot.b + step) % n_bal
        slot = peer if arriving else spot.b
        return remote(y_h.at[pl.ds(peer * share, share)], decoded.at[pl.ds(slot * share, share)], moves.at[step],
                      moves.at[n_bal + slot], (spot.d, peer))

    own = pl.ds(spot.b * share, share)
    own_copy = pltpu.make_async_copy(y_h.at[own], decoded.at[own], moves.at[0])
    own_copy.start()
    for step in range(1, n_bal):
        moved(step, False).start()

    def cross1():
        dffn.a_wait()
        dffn.b_start()

    keys = pl.ds(0, m)
    back_heads(False, n, q, kt, v.at[keys], dot_, d_o, rowdot, fetch, pair_ds, dqt, dk.at[keys], dv.at[keys],
               {1: cross1})
    for load in last:
        load.wait()
    put(g0, 0, mm(x0[...], dqt[...], TT))
    put(g0, rows, mm(x1[...], dk[:m], TN))
    put(g0, 2 * rows, mm(x1[...], dv[:m], TN))
    cross.a_start()
    dffn.b_wait()
    dffn.bb_start()
    for start, count in cut(m):
        part = slice(start, start + count)
        wide1[part] = mm(dk[part], wa[1], NT) + mm(dv[part], wa[2], NT)
    for start, count in cut(n):
        part = slice(start, start + count)
        d_o[part] = (da[part] + mm(dqt[:, part], wa[0], TT)).astype(BF)
    save_dx1 = c.start(d_o, dx1_h)
    act, slope = ds.at[0, keys, pl.ds(0, hidden)], ds.at[1, keys, pl.ds(0, hidden)]
    up, down, zb = dqt.at[:, pl.ds(0, hidden)], dk.at[pl.ds(0, hidden)], dv.at[keys]
    load_ffn = [c.start(a, b) for a, b in ((down_h, down), (slope_h, slope), (act_h, act), (zb_h, zb), (up_h, up))]
    queries = pl.ds(0, wide)
    eot, eq = ot.at[:, queries], q.at[queries]
    load_ot = c.start(eot_h, eot)
    loads = [c.start(eqkv_h.at[i], item.at[keys]) for i, item in enumerate((q, k, v))]
    load_x = c.start(ex_h, x1)
    load_tw = c.start(tw4_h, wa)
    load_tx = c.start(tx_h, x0)
    begin, fetch = in_ring(ering, ee_h, esems.at[1], [(m, slice(0, wide))])
    begin()
    q[m:wide] = jnp.zeros((wide - m, width), BF)
    load_e2.wait()
    gain, shift = zero, zero
    for start, count in cut(m):
        part = slice(start, start + count)
        unit, pace = normalise(wide0[part])
        grad = wide1[part]
        gain += colsum(grad * unit)
        shift += colsum(grad)
        d2 = norm_back(unit, pace, egains[1:2], grad)
        da[part] = d2
        gb[part] = d2.astype(BF)
    d_gains[1:2] = gain
    d_shifts[1:2] = shift
    load_e1 = c.start(e1_h, wide1)
    load_a1 = c.start(a1_h, wide0)
    cross.a_wait()
    cross.b_start()
    for load in load_ffn:
        load.wait()
    ffn_back(zb, up, down, act, slope, gb.at[keys], slope, g1, d_bias, d_shifts, 2)
    effn.a_start()
    dffn.bb_wait()
    dffn.c_start()
    load_e1.wait()
    gain, shift = zero, zero
    for start, count in cut(m):
        part = slice(start, start + count)
        unit, pace = normalise(wide1[part])
        dz = da[part] + mm(slope[part], up[...], NT)
        gain += colsum(dz * unit)
        shift += colsum(dz)
        d1 = norm_back(unit, pace, egains[0:1], dz)
        da[part] = d1
        gb[part] = d1.astype(BF)
    d_gains[0:1] = gain
    d_shifts[0:1] = shift

    def enc0_():
        effn.a_wait()
        effn.b_start()

    def enc2():
        cross.b_wait()
        cross.bb_start()
        dffn.c_wait()
        dffn.d_start()

    for load in (load_ew, load_ot, *loads, load_x, save_dx1):
        load.wait()
    kt[:, :m] = k[:m].T
    put(g0, 3 * rows, mm(ot[:, :m], gb[:m]))
    edot, edo, edqt = dot_.at[:, queries], d_o.at[queries], dqt.at[:, queries]
    erowdot = rowdot.at[:, :, queries]
    back_outputs(gb.at[keys], wb, eot, erate, edot, edo, erowdot)
    back_heads(False, wide, eq, kt, v.at[keys], edot, edo, erowdot, fetch, pair_ds, edqt, dk.at[keys], dv.at[keys],
               {0: enc0_, 2: enc2})
    load_dx1 = c.start(dx1_h, d_o)
    cross.bb_wait()
    cross.c_start()
    put(g0, 0, mm(x1[...], dqt[:, :m], TT))
    put(g0, rows, mm(x1[...], dk[:m], TN))
    put(g0, 2 * rows, mm(x1[...], dv[:m], TN))
    enc0.a_start()
    enc1.a_start()
    effn.b_wait()
    effn.bb_start()
    for start, count in cut(m):
        part = slice(start, start + count)
        wide1[part] = da[part] + mm(dqt[:, part], wb[0], TT) + mm(dk[part], wb[1], NT) + mm(dv[part], wb[2], NT)
    c.out(wide1, dx_enc_h)

    load_ot = c.start(tot_h, ot)
    loads = [c.start(tqkv_h.at[i], item) for i, item in enumerate((q, k, v))]
    tile = 512
    spans = [(start + tile, slice(start, start + tile)) for start in range(0, n, tile)]
    begin, fetch = in_ring(ering, te_h, esems.at[2], spans)
    begin()
    load_a1.wait()
    load_dx1.wait()
    gain, shift = zero, zero
    for start, count in cut(n):
        part = slice(start, start + count)
        unit, pace = normalise(wide0[part])
        grad = d_o[part].astype(F32)
        gain += colsum(grad * unit)
        shift += colsum(grad)
        d1 = norm_back(unit, pace, dgains[0:1], grad)
        da[part] = d1
        gb[part] = d1.astype(BF)
    part_lanes = width // n_dp
    vec[...] = jnp.zeros_like(vec)
    for i in range(n_dp):
        lanes = slice(i * part_lanes, (i + 1) * part_lanes)
        for j in range(2):
            wide_lanes = slice((2 * i + j) * part_lanes, (2 * i + j + 1) * part_lanes)
            vec[i, j : j + 1, :part_lanes] = d_bias[:, wide_lanes]
            vec[i, 2 + j : 3 + j, :part_lanes] = d_bias_d[:, wide_lanes]
        vec[i, 4:6, :part_lanes] = d_gains[:, lanes]
        vec[i, 6:9, :part_lanes] = d_shifts[:, lanes]
        vec[i, 9:10, :part_lanes] = gain[:, lanes]
        vec[i, 10:12, :part_lanes] = d_gains_d[1:3, lanes]
        vec[i, 12:13, :part_lanes] = shift[:, lanes]
        vec[i, 13:16, :part_lanes] = d_shifts_d[1:4, lanes]
    vector.swap_start(0)
    enc0.a_wait()
    enc0.b_start()
    enc1.a_wait()
    enc1.b_start()

    quarter = half // 2

    def put_pair(p):
        lanes = slice(p * quarter, (p + 1) * quarter)
        sides = jnp.concatenate([dqt[lanes].T, dk[:, lanes], dv[:, lanes]], axis=1)
        put(pairs[p].source, 0, mm(x0[...], sides, TN))
        pairs[p].a_start()

    def tags0():
        vector.swap_wait(0)
        vector.swap_start(1)
        cross.c_wait()
        cross.d_start()
        effn.bb_wait()
        effn.c_start()

    def tags1():
        put_pair(0)

    def tags2():
        pair0.a_wait()
        pair0.q_start()
        vector.swap_wait(1)
        vector.swap_start(2)

    def tags3():
        put_pair(1)
        enc0.b_wait()
        enc1.b_wait()
        enc0.bb_start()
        enc1.bb_start()

    def tags4():
        pair1.a_wait()
        pair1.q_start()
        dffn.d_wait()
        effn.c_wait()
        effn.d_start()
        vector.swap_wait(2)
        vector.c_start()

    def tags5():
        put_pair(2)

    def tags6():
        pair2.a_wait()
        pair2.q_start()
        pair0.q_wait()
        pair0.c_start()
        enc0.bb_wait()
        enc0.c_start()
        enc1.bb_wait()
        enc1.c_start()

    def tags7():
        put_pair(3)

    for load in (load_ot, load_tw, load_tx, *loads):
        load.wait()
    kt[...] = k[...].T
    out = mm(ot[...], gb[...])
    for i, piece in enumerate(pairs):
        put(piece.source, 0, out[:, i * quarter : (i + 1) * quarter], 3 * quarter)
    back_outputs(gb, wa, ot, trate, dot_, d_o, rowdot)
    back_heads(True, tile, q, kt, v, dot_, d_o, rowdot, fetch, pair_ds, dqt, dk, dv,
               dict(enumerate((tags0, tags1, tags2, tags3, tags4, tags5, tags6, tags7))))
    pair3.a_wait()
    pair3.q_start()
    pair1.q_wait()
    pair1.c_start()
    for i, (start, count) in enumerate(cut(n)):
        part = slice(start, start + count)
        wide0[part] = (da[part] + mm(dqt[:, part], wa[0], TT) + mm(dk[part], wa[1], NT) + mm(dv[part], wa[2], NT))
        if i == 0:
            pair2.q_wait()
            pair2.c_start()
            pair0.c_wait()
            pair0.d_start()
            cross.d_wait()
            enc0.c_wait()
            enc0.d_start()
    c.out(wide0, dx_tags_h)
    pair3.q_wait()
    pair3.c_start()
    enc1.c_wait()
    enc1.d_start()
    pair1.c_wait()
    pair1.d_start()
    pair2.c_wait()
    pair2.d_start()
    vector.c_wait()
    effn.d_wait()
    own_copy.wait()
    for step in range(1, n_bal):
        moved(step, False).wait_send()
        moved(step, True).wait_recv()
    c.finish()
    pair3.c_wait()
    pair3.d_start()
    for piece in (enc0, enc1, *pairs):
        piece.d_wait()


def finish(all_cross, all_dffn, all_effn, all_enc0, all_enc1, all_self0, all_self1, all_self2, all_self3, v_total, decoded_h, patches_h, tags_h,
           o_enc, o_eup, o_ebias, o_edown, o_egains, o_eshifts,
           o_self, o_cross, o_dup, o_dbias, o_ddown, o_dgains, o_dshifts, o_decoded, o_patches, o_tags, tags, patches, decoded, sems):
    c = Copies(sems)
    moves = [(c.start(source, here), here, target) for source, here, target in
             ((tags_h, tags, o_tags), (patches_h, patches, o_patches), (decoded_h, decoded, o_decoded))]
    for load, here, target in moves:
        load.wait()
        c.out(here, target)

    def joined(gathered):
        return jnp.concatenate([gathered[b].astype(F32) for b in (0, 2, 1, 3)], axis=1)

    def layer(out, parts):
        rows = out.shape[0]
        for j in range(4):
            out[:, j, :] = parts[j * rows : (j + 1) * rows]

    def branch(up, down, parts):
        rows, width = up.shape[0], parts.shape[1]
        for j in range(up.shape[1] // width):
            up[:, j * width : (j + 1) * width] = parts[j * rows : (j + 1) * rows]
        down[...] = parts[2 * rows :]

    layer(o_enc, jnp.concatenate([joined(all_enc0), joined(all_enc1)], axis=0))
    layer(o_cross, joined(all_cross))
    branch(o_eup, o_edown, joined(all_effn))
    branch(o_dup, o_ddown, joined(all_dffn))
    rows, _, width = o_self.shape
    half = width // 2
    quarter = half // 2
    for i, gathered in enumerate((all_self0, all_self1, all_self2, all_self3)):
        parts = joined(gathered)
        for j in range(4):
            o_self[:, j, i * quarter : (i + 1) * quarter] = parts[:rows, j * quarter : (j + 1) * quarter]
    share = o_egains.shape[1]
    for j in range(2):
        o_ebias[:, j * share : (j + 1) * share] = v_total[j : j + 1, :share]
        o_dbias[:, j * share : (j + 1) * share] = v_total[2 + j : 3 + j, :share]
    o_egains[...] = v_total[4:6, :share]
    o_eshifts[...] = v_total[6:9, :share]
    o_dgains[...] = v_total[9:12, :share]
    o_dshifts[...] = v_total[12:16, :share]
    c.finish()


def call(kernel, ins, outs, out_specs, scratch, name, params=PARAMS):
    specs = [spec for spec, _ in ins]
    return pl.pallas_call(
        kernel,
        out_shape=outs,
        in_specs=specs,
        out_specs=out_specs,
        scratch_shapes=scratch,
        compiler_params=params,
        name=name,
    )(*[value for _, value in ins])


def talking(number):
    return pltpu.CompilerParams(vmem_limit_bytes=60 << 20, collective_id=number, has_side_effects=True)


def run_tags_forward(n_dp, n_bal, x, w, ew, cw, cot, gains, shifts):
    n, width = x.shape
    bf = lambda *s: Shape(s, BF)
    f32 = lambda *s: Shape(s, F32)
    vb = lambda *s: pltpu.VMEM(s, BF)
    vf = lambda *s: pltpu.VMEM(s, F32)
    line, turned, raw, split = vb(n, width), vb(width, n), vb(width, 4, width), vb(4, width, width)
    weights = bf(4, width, width)
    return call(
        functools.partial(tags_forward, n_dp, n_bal),
        [(ANY, x), (ANY, w), (ANY, ew), (ANY, cw), (ANY, cot), (VM, gains), (VM, shifts)],
        [bf(n, width), bf(*cot.shape), f32(HEADS, 1, n), weights, weights, weights, bf(3, n, width), bf(width, n),
         bf(HEADS, n, n), f32(n, width)],
        [VM, VM, VM] + [ANY] * 7,
        [line, raw, split, raw, split, raw, split, line, line, line, turned, turned, turned, vf(n, width), vb(4, n, n),
         pltpu.SemaphoreType.DMA((20,)), pltpu.SemaphoreType.DMA((4, n // 512)), pltpu.SemaphoreType.DMA((2 * n_bal,))],
        "tags_forward",
        talking(2),
    )


def run_forward(n_dp, n_bal, scalars, x, ew4, eup, ebias, edown, egains, eshifts, x1, cw4, up, bias, down, gains, shifts, cot):
    m, width = x.shape
    n = x1.shape[0]
    hidden = up.shape[1]
    wide = (m + 127) // 128 * 128
    piece = (n_dp // 2, 2, 4 * width // n_dp, width)
    bf = lambda *s: Shape(s, BF)
    f32 = lambda *s: Shape(s, F32)
    vb = lambda *s: pltpu.VMEM(s, BF)
    vf = lambda *s: pltpu.VMEM(s, F32)
    split, first, second = vb(4, width, width), vb(width, hidden), vb(hidden, width)
    short, line = vb(m, width), vb(n, width)
    return call(
        functools.partial(forward, cot.shape[0] // n_bal),
        [(SM, v) for v in scalars]
        + [(ANY, x), (ANY, ew4), (ANY, eup), (VM, ebias), (ANY, edown), (VM, egains), (VM, eshifts),
           (ANY, x1), (ANY, cw4), (ANY, up), (VM, bias), (ANY, down), (VM, gains), (VM, shifts), (ANY, cot)],
        [f32(HEADS, 1, wide), f32(HEADS, 1, n), bf(*piece), f32(1, hidden), f32(3, width), f32(4, width), bf(*cot.shape),
         bf(m, width), bf(3, m, width), bf(width, wide), bf(HEADS, m, wide), f32(m, width), f32(m, width), bf(m, width),
         bf(m, hidden), bf(m, hidden),
         f32(n, width), bf(n, width), bf(n, width), bf(m, width), bf(m, width), bf(width, n), bf(HEADS, m, n)],
        [VM] * 7 + [ANY] * 16,
        [short, split, first, second, line, short, short, vb(width, n), vb(width, m), vb(width, n), vb(4, m, n),
         vf(m, width), vf(m, width), short, vb(m, hidden), vb(m, hidden),
         line, short, split, first, second, vf(n, width), vf(n, 1), line, vb(n, hidden), vb(n, hidden), vf(n, width), line,
         pltpu.SemaphoreType.DMA((40,)), pltpu.SemaphoreType.DMA((4, 1))],
        "forward",
    )


def run_backward(n_dp, n_bal, inputs, vectors, shapes):
    n, m, width, hidden, wide, blocks = shapes
    rows = 4 * width // n_dp
    bf = lambda *s: Shape(s, BF)
    f32 = lambda *s: Shape(s, F32)
    vb = lambda *s: pltpu.VMEM(s, BF)
    vf = lambda *s: pltpu.VMEM(s, F32)
    least = max(rows // 4, 16)
    whole, part, small = bf(n_bal, rows, 128), bf(n_bal, rows // 2, 128), bf(n_bal, least, 128)
    line, turned = vb(n, width), vb(width, n)
    piece = vb(n_dp // 2, 2, rows, width)
    return call(
        functools.partial(backward, n_dp, n_bal),
        [(ANY, item) for item in inputs] + [(VM, item) for item in vectors],
        [f32(m, width), f32(n, width), bf(n, width), bf(*blocks), whole, whole, whole, part, part, small, small, small, small, f32(16, 128)],
        [ANY, ANY, ANY] + [VM] * 11,
        [vb(3, n, n), line, line, line, turned, turned, turned, line, vf(HEADS, 1, n), vb(width, max(n, hidden)), vb(max(n, hidden), width), line,
         vb(2, n, max(n, hidden)), line, vf(n, width), vf(n, width), vf(m, width), line, vb(m, width),
         vb(4, width, width), vb(4, width, width), piece, piece,
         vf(1, hidden), vf(2, width), vf(3, width), vf(n_dp, 16, 128), vf(3, n_dp, 16, 128), vf(n_dp // 2, 16, 128),
         vb(*kept_shape(n_dp, rows, False)), vb(*kept_shape(n_dp, rows // 2, False)),
         *room_scratch(n_dp, rows), *room_scratch(n_dp, rows),
         pltpu.SemaphoreType.DMA((40,)), pltpu.SemaphoreType.DMA((3, 4, n // 512)), pltpu.SemaphoreType.DMA((2 * n_bal,)),
         pltpu.SemaphoreType.DMA((6 + n_dp,)), *[piece_sems(n_dp, n_bal)] * 5,
         *pair_scratch(n_dp, n_bal, least, False) * 2, *pair_scratch(n_dp, n_bal, least, True) * 2],
        "backward",
        pltpu.CompilerParams(vmem_limit_bytes=60 << 20, collective_id=1, has_side_effects=True),
    )


def run_finish(n_dp, hidden, width, gathered, moved):
    share = width // n_dp
    f32 = lambda *s: Shape(s, F32)
    side = [f32(share, 4, width)]
    branch = [f32(share, hidden), f32(1, hidden // n_dp), f32(hidden // n_dp, width)]
    outs = side + branch + [f32(2, share), f32(3, share)] + side + side + branch + [f32(3, share), f32(4, share)]
    return call(finish, [(VM, v) for v in gathered] + [(ANY, v) for v in moved],
                outs + [Shape(v.shape, v.dtype) for v in moved], [VM] * len(outs) + [ANY] * 3,
                [pltpu.VMEM(v.shape, v.dtype) for v in moved[::-1]] + [pltpu.SemaphoreType.DMA((6,))], "finish")


def per_device(
    patches, tag_rows, cotangent, tag_length, cell_count, destination, slot_index,
    encoder_attention, encoder_up, encoder_up_bias, encoder_down, encoder_gains, encoder_shifts,
    decoder_self, decoder_cross, decoder_up, decoder_up_bias, decoder_down, decoder_gains, decoder_shifts,
):
    n_bal, n_dp = lax.axis_size("bal"), lax.axis_size("dp")
    length, width = tag_rows.shape[1:]
    hidden = encoder_up.shape[1]
    blocks = destination.shape[1]
    span = length // blocks
    cot = cotangent[0].reshape(blocks, span, width)
    eg, es, dg, ds = encoder_gains.T, encoder_shifts.T, decoder_gains.T, decoder_shifts.T
    eb, db = encoder_up_bias[None], decoder_up_bias[None]
    x1, cot, srate, sw4, ew4, cw4, sqkv, sot, se, a1 = run_tags_forward(
        n_dp, n_bal, tag_rows[0], decoder_self, encoder_attention, decoder_cross, cot, dg, ds)
    (erate, crate, g_dffn, d_db, d_dg, d_ds, y, memory, eqkv, eot, ee, e1, e2, zb, act, slope, da2, gb2, cq, ck, cv, c_ot,
     ce) = run_forward(
        n_dp, n_bal, (tag_length, cell_count, destination, slot_index), patches[0], ew4, encoder_up, eb, encoder_down,
        eg, es, x1, cw4, decoder_up, db, decoder_down, dg, ds, cot)
    d_patches, d_tags, _, decoded, all_cross, all_dffn, *gathered = run_backward(
        n_dp, n_bal,
        (da2, gb2, x1, memory, cw4, cq, ck, cv, c_ot, ce, y, g_dffn,
         e2, e1, zb, act, slope, encoder_up, encoder_down, patches[0], ew4, eqkv, eot, ee,
         a1, tag_rows[0], sw4, sqkv, sot, se),
        (crate, erate, srate, eg, dg, d_db, d_dg, d_ds),
        (length, patches.shape[1], width, hidden, eot.shape[1], y.shape))
    ew, eu, ebg, ed, egg, esg, sw, cw, du, dbg, dd, dgg, dsg, decoded, d_patches, d_tags = run_finish(
        n_dp, hidden, width, (all_cross, all_dffn, *gathered), (decoded, d_patches, d_tags))
    return (
        decoded.reshape(1, length, width), d_patches[None], d_tags[None],
        ew, eu, ebg.reshape(-1), ed, egg.T, esg.T, sw, cw, du, dbg.reshape(-1), dd, dgg.T, dsg.T,
    )


def solution(mesh):
    split = P(("dp", "bal"))
    in_specs = (split,) * 7 + (P(),) * 13
    out_specs = (split,) * 3 + (P("dp"),) * 13
    return jax.shard_map(per_device, mesh=mesh, in_specs=in_specs, out_specs=out_specs, check_vma=False)
```

```python
import functools

import jax
import jax.numpy as jnp
from jax import lax
from jax.experimental import pallas as pl
from jax.experimental.pallas import tpu as pltpu
from jax.sharding import PartitionSpec as P

HEADS = 8
HEAD = 64
EPSILON = 1e-05
NEGATIVE = -1e30
BF = jnp.bfloat16
F32 = jnp.float32
NN = (((1,), (0,)), ((), ()))
NT = (((1,), (1,)), ((), ()))
TN = (((0,), (0,)), ((), ()))
TT = (((0,), (1,)), ((), ()))
VM = pl.BlockSpec(memory_space=pltpu.VMEM)
SM = pl.BlockSpec(memory_space=pltpu.SMEM)
ANY = pl.BlockSpec(memory_space=pl.ANY)
LIMIT = 1e18
PARAMS = pltpu.CompilerParams(vmem_limit_bytes=60 << 20)
Shape = jax.ShapeDtypeStruct


def mm(left, right, dims=NN):
    return lax.dot_general(left, right, dims, preferred_element_type=F32)


def cut(rows):
    half = (rows // 2 + 15) // 16 * 16
    return [(0, half), (half, rows - half)]


class Copies:
    def __init__(self, sems):
        self.sems, self.used, self.open = sems, 0, []

    def start(self, source, target):
        copy = pltpu.make_async_copy(source, target, self.sems.at[self.used])
        self.used += 1
        copy.start()
        return copy

    def out(self, source, target):
        self.open.append(self.start(source, target))

    def finish(self):
        for copy in self.open:
            copy.wait()


def split_weights(raw, parts):
    def step(i, carry):
        rows = pl.ds(pl.multiple_of(i * 128, 128), 128)
        parts[:, rows, :] = pltpu.einshape("abc->bac", raw[rows])
        return carry

    lax.fori_loop(0, raw.shape[0] // 128, step, 0)


def normalise(signal):
    centre = jnp.mean(signal, axis=-1, keepdims=True)
    centered = signal - centre
    spread = jnp.mean(centered * centered, axis=-1, keepdims=True)
    rate = lax.rsqrt(spread + EPSILON)
    return centered * rate, rate


def norm_back(unit, rate, gain, gradient):
    inner = gradient * gain
    first = jnp.mean(inner, axis=-1, keepdims=True)
    second = jnp.mean(inner * unit, axis=-1, keepdims=True)
    return rate * (inner - first - unit * second)


def colsum(signal):
    return jnp.sum(signal, axis=0, keepdims=True)


def smooth(hidden):
    scale = 0.7978845608028654
    curve = scale + (0.044715 * scale) * (hidden * hidden)
    half = 0.5 + 0.5 * jnp.tanh(hidden * curve)
    active = hidden * half
    slope = half + active * (1.0 - half) * (6.0 * curve - 4.0 * scale)
    return active, slope


def half_mask(shape, axis, which):
    index = lax.broadcasted_iota(jnp.int32, shape, axis)
    return (index < HEAD) if which == 0 else (index >= HEAD)


def keep_half(pair, axis, which):
    return jnp.where(half_mask(pair.shape, axis, which), pair, jnp.zeros_like(pair))


def project_qkv(x, sources, w4, q, qt, k, v, vt):
    rows = x.shape[0]
    for start, size in cut(rows):
        part = slice(start, start + size)
        q[part] = (mm(x[part], w4[0]) * HEAD ** (-0.5)).astype(BF)
    if q.shape[0] > rows:
        q[rows:] = jnp.zeros((q.shape[0] - rows, q.shape[1]), BF)
    for start, size in cut(sources.shape[0]):
        part = slice(start, start + size)
        k[part] = mm(sources[part], w4[1]).astype(BF)
        v[part] = mm(sources[part], w4[2]).astype(BF)
    qt[...] = q[...].T
    vt[...] = v[...].T


def shifted_exp(scores, exact, causal_rows):
    if causal_rows:
        size, width = scores.shape
        key = lax.broadcasted_iota(jnp.int32, (width, width), 0)
        query = lax.broadcasted_iota(jnp.int32, (width, width), 1)
        last = jnp.where(key <= query, scores[size - width :], NEGATIVE)
        scores = last if size == width else jnp.concatenate([scores[: size - width], last], axis=0)
        exact = exact or size == width
    sample = scores if exact else scores[:128]
    return jnp.exp(scores - jnp.max(sample, axis=0, keepdims=True))


def attend_heads(exact, causal, q_tile, qt, k, vt, ot, rate, store, beside=None):
    keys, queries = k.shape[0], qt.shape[1]

    def pair(p, carry):
        lanes = pl.ds(pl.multiple_of(p * 128, 128), 128)
        if beside is not None:
            beside(p)
        for u in range(2):
            rows = pl.ds(pl.multiple_of(p * 128 + u * HEAD, HEAD), HEAD)
            place, done = store(p, u)
            for start in range(0, queries, q_tile):
                cols = slice(start, start + q_tile)
                depth = start + q_tile if causal else keys
                scores = mm(k[:depth, lanes], keep_half(qt[lanes, cols], 0, u))
                raised = shifted_exp(scores, exact, causal)
                total = jnp.sum(raised, axis=0, keepdims=True)
                low = raised.astype(BF)
                place[:depth, cols] = low
                inverse = 1.0 / total
                rate[2 * p + u, :, cols] = inverse
                ot[rows, cols] = (mm(vt[rows, :depth], low) * inverse).astype(BF)
            done()
        return carry

    lax.fori_loop(0, HEADS // 2, pair, 0)


def attend(causal, q_tile, qt, k, vt, ot, rate, store, drain):
    attend_heads(False, causal, q_tile, qt, k, vt, ot, rate, store)
    drain()
    fine = jnp.min(rate[...]) > 1.0 / LIMIT

    @pl.when(jnp.logical_not(fine))
    def _():
        attend_heads(True, causal, q_tile, qt, k, vt, ot, rate, store)
        drain()


def back_heads(causal, q_tile, q, kt, v, dot_, d_o, rowdot, fetch, ds, dqt, dk, dv, hook=None):
    keys, queries = v.shape[0], dqt.shape[1]

    def pair(p, carry):
        lanes = pl.ds(pl.multiple_of(p * 128, 128), 128)
        for u in range(2):
            rows = pl.ds(pl.multiple_of(p * 128 + u * HEAD, HEAD), HEAD)
            place = fetch(p, u)
            for start in range(0, queries, q_tile):
                cols = slice(start, start + q_tile)
                depth = start + q_tile if causal else keys
                grad = mm(v[:depth, lanes], keep_half(dot_[lanes, cols], 0, u))
                scaled = place[:depth, cols].astype(F32) * (grad - rowdot[2 * p + u, :, cols])
                low = scaled.astype(BF)
                ds[u][:depth, cols] = low
                dqt[rows, cols] = (mm(kt[rows, :depth], low) * HEAD ** (-0.5)).astype(BF)
            qm = q[:queries, lanes]
            dm = d_o[:queries, lanes]
            steps = range(0, keys, q_tile) if causal else (0,)
            for start in steps:
                key = slice(start, start + q_tile) if causal else slice(0, keys)
                more_k = mm(ds[u][key, start:queries], qm[start:])
                more_v = mm(place[key, start:queries], dm[start:])
                if u == 0:
                    dk[key, lanes] = more_k.astype(BF)
                    dv[key, lanes] = more_v.astype(BF)
                else:
                    dk[key, lanes] = jnp.where(half_mask(more_k.shape, 1, 1), more_k.astype(BF), dk[key, lanes])
                    dv[key, lanes] = jnp.where(half_mask(more_v.shape, 1, 1), more_v.astype(BF), dv[key, lanes])
            if hook is not None:
                for at, act in hook.items():
                    if at % 2 == u:
                        pl.when(p == at // 2)(act)
        return carry

    lax.fori_loop(0, HEADS // 2, pair, 0)


def back_outputs(grad_low, w4, ot, rate, dot_, d_o, rowdot):
    rows, wide = grad_low.shape[0], dot_.shape[1]
    raw = mm(w4[3], grad_low[...], NT)
    for h in range(HEADS):
        part = slice(h * HEAD, (h + 1) * HEAD)
        low = (raw[part] * rate[h][:, :rows]).astype(BF)
        if wide > rows:
            low = jnp.concatenate([low, jnp.zeros((HEAD, wide - rows), BF)], axis=1)
        dot_[part] = low
        rowdot[h] = jnp.sum(low.astype(F32) * ot[part].astype(F32), axis=0, keepdims=True)
    d_o[...] = dot_[...].T


def ring(buffers, hbm, sems, spans, out):
    def copies(h, slot):
        made = []
        for i, (rows, cols) in enumerate(spans):
            here = buffers.at[slot, pl.ds(0, rows), cols]
            there = hbm.at[h, pl.ds(0, rows), cols]
            made.append(
                pltpu.make_async_copy(here, there, sems.at[slot, i])
                if out
                else pltpu.make_async_copy(there, here, sems.at[slot, i])
            )
        return made

    return copies


def out_ring(buffers, hbm, sems, spans):
    copies = ring(buffers, hbm, sems, spans, True)

    def store(p, u):
        slot = (p % 2) * 2 + u

        @pl.when(p >= 2)
        def _():
            for copy in copies(2 * p + u, slot):
                copy.wait()

        def done():
            for copy in copies(2 * p + u, slot):
                copy.start()

        return buffers.at[slot], done

    def drain():
        for slot in range(4):
            for copy in copies(slot, slot):
                copy.wait()

    return store, drain


def in_ring(buffers, hbm, sems, spans):
    copies = ring(buffers, hbm, sems, spans, False)
    depth = buffers.shape[0]

    def begin():
        for h in range(depth):
            for copy in copies(h, h):
                copy.start()

    def fetch(p, u):
        h = 2 * p + u
        for copy in copies(h, h % depth):
            copy.wait()

        @pl.when((h >= 1) & (h + depth <= HEADS))
        def _():
            for copy in copies(h + depth - 1, (h + depth - 1) % depth):
                copy.start()

        return buffers.at[h % depth]

    return begin, fetch


MESH = pl.DeviceIdType.MESH


class Spot:
    def __init__(self, n, m):
        self.n, self.m = n, m
        self.d, self.b = lax.axis_index("dp"), lax.axis_index("bal")
        self.core, self.far = self.b % 2, self.b // 2
        self.parity, self.row = self.d % 2, self.d // 2
        self.by_core = (self.d, self.b + 1 - 2 * self.core)
        self.by_far = (self.d, self.b + 2 - 4 * self.far)
        self.by_parity = (self.d + 1 - 2 * self.parity, self.b)

    def greet(self, everyone=True):
        barrier = pltpu.get_barrier_semaphore()

        def call(device):
            pl.semaphore_signal(barrier, inc=1, device_id=device, device_id_type=MESH)

        for k in range(1, self.m):
            call((self.d, (self.b + k) % self.m))

        if not everyone:
            return
        call(self.by_parity)
        call((self.by_parity[0], self.by_far[1]))

        def along(k, carry):
            call((((self.row + k) % (self.n // 2)) * 2 + self.parity, self.b))
            return carry

        lax.fori_loop(1, self.n // 2, along, 0)

    def await_all(self, everyone=True):
        pl.semaphore_wait(pltpu.get_barrier_semaphore(), self.m - 1 + (2 + self.n // 2 - 1 if everyone else 0))


def remote(source, target, sent, received, device):
    return pltpu.make_async_remote_copy(
        src_ref=source, dst_ref=target, send_sem=sent, recv_sem=received, device_id=device, device_id_type=MESH
    )


class Piece:
    def __init__(self, spot, along_x, sems, source=None, acc=None, land_a=None, kept=None, land_b=None, kept2=None,
                 land_c=None, slots=None, result=None, gathered=None):
        self.spot, self.along_x, self.source, self.sems = spot, along_x, source, sems
        self.acc, self.land_a, self.kept, self.land_b = acc, land_a, kept, land_b
        self.kept2, self.land_c = kept2, land_c
        self.slots, self.result, self.gathered = slots, result, gathered

    def a_copies(self):
        half = self.acc.shape[3]
        mine = pl.ds(pl.multiple_of(self.spot.core * half, half), half)
        other = pl.ds(pl.multiple_of((1 - self.spot.core) * half, half), half)
        return [
            pltpu.make_async_copy(self.source.at[:, :, :, mine], self.acc, self.sems.at[0]),
            remote(self.source.at[:, :, :, other], self.land_a, self.sems.at[1], self.sems.at[2], self.spot.by_core),
        ]

    def a_start(self):
        for copy in self.a_copies():
            copy.start()

    def a_wait(self):
        for copy in self.a_copies():
            copy.wait()

        def add(i, carry):
            self.acc[i] = self.acc[i] + self.land_a[i]
            return carry

        lax.fori_loop(0, self.acc.shape[0], add, 0)

    def lanes(self, mine, size):
        side = self.spot.far if mine else 1 - self.spot.far
        return pl.ds(pl.multiple_of(side * size, size), size)

    def b_copy(self):
        spot = self.spot
        if self.along_x:
            out, to = self.acc.at[:, :, :, self.lanes(False, self.land_b.shape[3])], spot.by_far
        else:
            out, to = self.acc.at[:, 1 - spot.parity], spot.by_parity
        return remote(out, self.land_b, self.sems.at[3], self.sems.at[4], to)

    def b_start(self):
        self.b_copy().start()

    def b_wait(self):
        self.b_copy().wait()

        def add(i, carry):
            if self.along_x:
                mine = self.acc[i, :, :, self.lanes(True, self.land_b.shape[3])]
            else:
                mine = self.acc[i, self.spot.parity]
            self.kept[i] = mine + self.land_b[i]
            return carry

        lax.fori_loop(0, self.kept.shape[0], add, 0)

    def bb_copy(self):
        spot = self.spot
        if self.along_x:
            out, to = self.kept.at[:, 1 - spot.parity], spot.by_parity
        else:
            out, to = self.kept.at[:, :, self.lanes(False, self.land_c.shape[2])], spot.by_far
        return remote(out, self.land_c, self.sems.at[5], self.sems.at[6], to)

    def bb_start(self):
        self.bb_copy().start()

    def bb_wait(self):
        self.bb_copy().wait()

        def add(i, carry):
            if self.along_x:
                mine = self.kept[i, self.spot.parity]
            else:
                mine = self.kept[i, :, self.lanes(True, self.land_c.shape[2])]
            self.kept2[i] = mine + self.land_c[i]
            return carry

        lax.fori_loop(0, self.kept2.shape[0], add, 0)

    def base(self):
        return 7

    def c_copy(self, k, arriving):
        spot, half = self.spot, self.spot.n // 2
        row = (spot.row + k) % half
        slot = row if arriving else spot.row
        return remote(self.kept2.at[row], self.slots.at[slot], self.sems.at[self.base() + k], self.sems.at[self.base() + half + slot],
                      (row * 2 + spot.parity, spot.b))

    def c_start(self):
        def step(k, carry):
            self.c_copy(k, False).start()
            return carry

        lax.fori_loop(1, self.spot.n // 2, step, 0)

    def c_wait(self):
        half, row = self.spot.n // 2, self.spot.row

        def step(k, total):
            self.c_copy(k, False).wait_send()
            self.c_copy(k, True).wait_recv()
            return total + self.slots[(row + k) % half].astype(F32)

        total = lax.fori_loop(1, half, step, self.kept2[row].astype(F32))
        self.result[...] = total.astype(BF)

    def d_copies(self, arriving):
        spot, base = self.spot, self.base() + self.spot.n
        made = []
        for k in range(1, spot.m):
            peer = (spot.b + k) % spot.m
            slot = peer if arriving else spot.b
            made.append(remote(self.result, self.gathered.at[slot], self.sems.at[base + k],
                               self.sems.at[base + spot.m + slot], (spot.d, peer)))
        return made

    def d_start(self):
        for copy in self.d_copies(False):
            copy.start()
        self.gathered[self.spot.b] = self.result[...]

    def d_wait(self):
        for copy in self.d_copies(False):
            copy.wait_send()
        for copy in self.d_copies(True):
            copy.wait_recv()


class PairPiece(Piece):
    def __init__(self, spot, sems, source, acc, land_a, quads, kept2, slots, result, gathered):
        super().__init__(spot, True, sems, source, acc, land_a, kept2=kept2, slots=slots, result=result, gathered=gathered)
        self.quads = quads

    def base(self):
        return 11

    def quarter(self, far):
        lanes = self.kept2.shape[2]
        return pl.ds(pl.multiple_of(far * lanes, lanes), lanes)

    def q_copy(self, k, arriving):
        spot = self.spot
        me = spot.far * 2 + spot.parity
        peer = (me + k) % 4
        far, parity = peer // 2, peer % 2
        slot = peer if arriving else me
        return remote(self.acc.at[:, parity, :, self.quarter(far)], self.quads.at[slot], self.sems.at[3 + k],
                      self.sems.at[7 + slot], (spot.row * 2 + parity, spot.core + 2 * far))

    def q_start(self):
        for k in range(1, 4):
            self.q_copy(k, False).start()

    def q_wait(self):
        spot = self.spot
        me = spot.far * 2 + spot.parity
        for k in range(1, 4):
            self.q_copy(k, False).wait_send()
            self.q_copy(k, True).wait_recv()

        def add(i, carry):
            total = self.acc[i, spot.parity, :, self.quarter(spot.far)].astype(F32)
            for k in range(1, 4):
                total = total + self.quads[(me + k) % 4, i].astype(F32)
            self.kept2[i] = total.astype(BF)
            return carry

        lax.fori_loop(0, self.kept2.shape[0], add, 0)


def pair_scratch(n, m, rows, whole):
    vb = lambda shape: pltpu.VMEM(shape, BF)
    first = [vb((n // 2, 2, rows, 512)), vb(half_shape(n, rows)), vb(half_shape(n, rows))] if whole else []
    return first + [vb((4, *last_shape(n, rows))), vb(last_shape(n, rows)), vb(last_shape(n, rows)), vb((rows, 128)),
                    pltpu.SemaphoreType.DMA((11 + n + 2 * m,))]


def piece_sems(n, m):
    return pltpu.SemaphoreType.DMA((7 + n + 2 * m,))


def half_shape(n, rows):
    return (n // 2, 2, rows, 256)


def kept_shape(n, rows, along_x):
    return (n // 2, 2, rows, 128) if along_x else (n // 2, rows, 256)


def last_shape(n, rows):
    return (n // 2, rows, 128)


class VectorSum:
    def __init__(self, spot, v, lands, slots, result, sems):
        self.spot, self.v, self.lands, self.slots, self.result, self.sems = spot, v, lands, slots, result, sems

    def swap(self, step):
        device = (self.spot.by_core, self.spot.by_far, self.spot.by_parity)[step]
        return remote(self.v, self.lands.at[step], self.sems.at[2 * step], self.sems.at[2 * step + 1], device)

    def swap_start(self, step):
        self.swap(step).start()

    def swap_wait(self, step):
        self.swap(step).wait()
        self.v[...] = self.v[...] + self.lands[step]

    def copy(self, k, arriving):
        spot, half = self.spot, self.spot.n // 2
        row = (spot.row + k) % half
        slot = row if arriving else spot.row
        return remote(self.v.at[row * 2 + spot.parity], self.slots.at[slot], self.sems.at[6 + k],
                      self.sems.at[6 + half + slot], (row * 2 + spot.parity, spot.b))

    def c_start(self):
        def step(k, carry):
            self.copy(k, False).start()
            return carry

        lax.fori_loop(1, self.spot.n // 2, step, 0)

    def c_wait(self):
        half, row = self.spot.n // 2, self.spot.row

        def step(k, total):
            self.copy(k, False).wait_send()
            self.copy(k, True).wait_recv()
            return total + self.slots[(row + k) % half]

        self.result[...] = lax.fori_loop(1, half, step, self.v[self.spot.d])


def put(piece, row, value, lane=0):
    halves, two, width = piece.shape[0], piece.shape[1], value.shape[1]
    rows = value.shape[0] // (halves * two)
    piece[:, :, row : row + rows, lane : lane + width] = value.reshape(halves, two, rows, width).astype(BF)


def split_part(raw, parts, p):
    rows = pl.ds(pl.multiple_of(p * 128, 128), 128)
    parts[:, rows, :] = pltpu.einshape("abc->bac", raw[rows])


def tags_forward(n_dp, n_bal, x_h, w_h, ew_h, cw_h, cot_h, gains, shifts,
                 x1, cot, rate, w4_h, ew4_h, cw4_h, qkv_h, ot_h, e_h, a1_h,
                 x, raw, w4, raw_e, ew4, raw_c, cw4, q, k, v, qt, vt, ot, a1, ering, sems, esems, moves):
    spot = Spot(n_dp, n_bal)
    spot.greet(False)
    c = Copies(sems)
    load_w = c.start(w_h, raw)
    load_x = c.start(x_h, x)
    load_e, load_c = c.start(ew_h, raw_e), c.start(cw_h, raw_c)
    load_w.wait()
    split_weights(raw, w4)
    c.out(w4, w4_h)
    load_x.wait()
    project_qkv(x, x, w4, q, qt, k, v, vt)
    n = x.shape[0]
    for i, item in enumerate((q, k, v)):
        c.out(item, qkv_h.at[i])
    spot.await_all(False)
    share = cot_h.shape[0] // n_bal

    def moved(step, arriving):
        peer = (spot.b + step) % n_bal
        slot = peer if arriving else spot.b
        return remote(cot_h.at[pl.ds(peer * share, share)], cot.at[pl.ds(slot * share, share)], moves.at[step],
                      moves.at[n_bal + slot], (spot.d, peer))

    own = pl.ds(spot.b * share, share)
    own_copy = pltpu.make_async_copy(cot_h.at[own], cot.at[own], moves.at[0])
    own_copy.start()
    for step in range(1, n_bal):
        moved(step, False).start()
    load_e.wait()
    load_c.wait()

    def beside(p):
        split_part(raw_e, ew4, p)
        split_part(raw_c, cw4, p)

    tile = 512
    spans = [(start + tile, slice(start, start + tile)) for start in range(0, n, tile)]
    store, drain = out_ring(ering, e_h, esems, spans)
    attend_heads(True, True, tile, qt, k, vt, ot, rate, store, beside)
    drain()
    c.out(ew4, ew4_h)
    c.out(cw4, cw4_h)
    c.out(ot, ot_h)
    for start, size in cut(n):
        part = slice(start, start + size)
        first = x[part].astype(F32) + mm(ot[:, part], w4[3], TN)
        a1[part] = first
        unit, _ = normalise(first)
        x1[part] = (unit * gains[0:1] + shifts[0:1]).astype(BF)
    c.out(a1, a1_h)
    own_copy.wait()
    for step in range(1, n_bal):
        moved(step, False).wait_send()
        moved(step, True).wait_recv()
    c.finish()


def forward(capacity, tag_length, cell_count, destination, slot_index,
            x_h, ew4_h, eup_h, ebias, edown_h, egains, eshifts,
            x1_h, cw4_h, up_h, bias, down_h, gains, shifts, cot_h,
            erate, rate, g_ffn, d_bias, d_gains, d_shifts, y,
            mem_h, eqkv_h, eot_h, ee_h, e1_h, e2_h, zb_h, eact_h, eslope_h,
            da_h, gb_h, q_h, k_h, v_h, ot_h, e_h,
            x, ew4, eup, edown, q, k, v, qt, vt, ot, ering, e1, e2, zb, eact, eslope,
            x1, mem, w4, up, down, unit2, rate2, xb2, act, slope, da, gb, sems, esems):
    cot, dh = y, slope
    c = Copies(sems)
    load_w = c.start(ew4_h, ew4)
    load_x = c.start(x_h, x)
    load_eup = c.start(eup_h, eup)
    load_edown = c.start(edown_h, edown)
    load_w.wait()
    load_x.wait()
    m, n = x.shape[0], x1.shape[0]
    wide = eot_h.shape[1]
    eq, eqt, eot = q.at[pl.ds(0, wide)], qt.at[:, pl.ds(0, wide)], ot.at[:, pl.ds(0, wide)]
    project_qkv(x, x, ew4, eq, eqt, k, v, vt)
    spent = [c.start(item, eqkv_h.at[i]) for i, item in enumerate((q.at[pl.ds(0, m)], k, v))]
    load_w = c.start(cw4_h, w4)
    load_x1 = c.start(x1_h, x1)
    load_up = c.start(up_h, up)
    load_down = c.start(down_h, down)
    load_cot = c.start(cot_h, cot)
    view = ering.at[:, :, pl.ds(0, wide)]
    store, drain = out_ring(view, ee_h, esems, [(m, slice(None))])
    attend(False, wide, eqt, k, vt, eot, erate, store, drain)
    spent.append(c.start(eot, eot_h))
    load_eup.wait()
    load_edown.wait()
    for start, size in cut(m):
        part = slice(start, start + size)
        first = x[part].astype(F32) + mm(ot[:, part], ew4[3], TN)
        e1[part] = first
        unit, _ = normalise(first)
        z = unit * egains[0:1] + eshifts[0:1]
        low = z.astype(BF)
        zb[part] = low
        active, bend = smooth(mm(low, eup[...]) + ebias[...])
        eact[part] = active.astype(BF)
        eslope[part] = bend.astype(BF)
        second = z + mm(eact[part], edown[...]) + eshifts[2:3]
        e2[part] = second
        unit, _ = normalise(second)
        mem[part] = (unit * egains[1:2] + eshifts[1:2]).astype(BF)
    for here, there in ((e1, e1_h), (e2, e2_h), (zb, zb_h), (eact, eact_h), (eslope, eslope_h), (mem, mem_h)):
        c.out(here, there)

    load_w.wait()
    load_x1.wait()
    for copy in spent:
        copy.wait()
    project_qkv(x1, mem, w4, q, qt, k, v, vt)
    for here, there in ((q, q_h), (k, k_h), (v, v_h)):
        c.out(here, there)
    blocks = y.shape[0]
    block = n // blocks
    store, drain = out_ring(ering, e_h, esems, [(m, slice(None))])
    attend(False, n, qt, k, vt, ot, rate, store, drain)
    c.out(ot, ot_h)
    load_up.wait()
    load_down.wait()
    load_cot.wait()
    live = tag_length[0] + cell_count[0]
    places = [destination[0, b] * capacity + slot_index[0, b] for b in range(blocks)]
    zero = jnp.zeros((1, x1.shape[1]), F32)
    gain3, shift3 = zero, zero
    for start, size in cut(n):
        part = slice(start, start + size)
        second = x1[part].astype(F32) + mm(ot[:, part], w4[3], TN)
        unit, pace = normalise(second)
        unit2[part] = unit
        rate2[part] = pace
        x2 = unit * gains[1:2] + shifts[1:2]
        low = x2.astype(BF)
        xb2[part] = low
        active, bend = smooth(mm(low, up[...]) + bias[...])
        act[part] = active.astype(BF)
        slope[part] = bend.astype(BF)
        third = x2 + mm(act[part], down[...]) + shifts[3:4]
        unit, pace = normalise(third)
        row = lax.broadcasted_iota(jnp.int32, (size, 1), 0) + start
        alive = (row < live).astype(F32)
        final = ((unit * gains[2:3] + shifts[2:3]) * alive).astype(BF)
        picked = []
        for b in range(start // block, (start + size) // block):
            picked.append(cot[places[b]])
            y[places[b]] = final[b * block - start : (b + 1) * block - start]
        dy = jnp.concatenate(picked, axis=0).astype(F32) * alive
        gain3 += colsum(dy * unit)
        shift3 += colsum(dy)
        d3 = norm_back(unit, pace, gains[2:3], dy)
        da[part] = d3
        gb[part] = d3.astype(BF)
    d_gains[2:3] = gain3
    d_shifts[2:3] = shift3
    ffn_back(xb2, up, down, act, slope, gb, dh, g_ffn, d_bias, d_shifts, 3)
    gain2, shift2 = zero, zero
    for start, size in cut(n):
        part = slice(start, start + size)
        dx2 = da[part] + mm(dh[part], up[...], NT)
        gain2 += colsum(dx2 * unit2[part])
        shift2 += colsum(dx2)
        d2 = norm_back(unit2[part], rate2[part], gains[1:2], dx2)
        da[part] = d2
        gb[part] = d2.astype(BF)
    d_gains[1:2] = gain2
    d_shifts[1:2] = shift2
    c.out(gb, gb_h)
    c.out(da, da_h)
    c.finish()


def ffn_back(xb, up, down, act, slope, gb, dh, g_ffn, d_bias, d_shifts, row, middle=None):
    n, width = xb.shape
    offset = jnp.zeros((1, up.shape[1]), F32)
    for start, size in cut(n):
        part = slice(start, start + size)
        low = (mm(gb[part], down[...], NT) * slope[part].astype(F32)).astype(BF)
        dh[part] = low
        offset += colsum(low.astype(F32))
    d_bias[...] = offset
    d_shifts[row : row + 1] = colsum(gb[...].astype(F32))
    if middle is not None:
        middle()
    rows = g_ffn.shape[2] // 4
    put(g_ffn, 2 * rows, mm(act[...], gb[...], TN))
    for j in range(up.shape[1] // width):
        put(g_ffn, j * rows, mm(xb[...], dh[:, j * width : (j + 1) * width], TN))


class Room:
    def __init__(self, acc, land, kept, next_, kept_x, next_x, kept2, last, slots, result):
        self.acc, self.land, self.kept, self.next = acc, land, kept, next_
        self.kept_x, self.next_x, self.kept2, self.last, self.slots, self.result = kept_x, next_x, kept2, last, slots, result

    def whole(self, spot, sems, source, gathered):
        return Piece(spot, False, sems, source, self.acc, self.land, self.kept, self.next, self.kept2, self.last,
                     self.slots, self.result, gathered)

    def part(self, spot, sems, source, gathered, along_x, start, size):
        rows, head = pl.ds(start, size), pl.ds(0, size)
        kept = self.kept_x.at[:, :, head] if along_x else self.kept.at[:, rows]
        next_ = self.next_x.at[:, :, head] if along_x else self.next.at[:, rows]
        return Piece(spot, along_x, sems, source, self.acc.at[:, :, rows], self.land.at[:, :, rows], kept, next_,
                     self.kept2.at[:, rows], self.last.at[:, rows], self.slots.at[:, rows], self.result.at[rows], gathered)


def room_scratch(n, rows):
    vb = lambda shape: pltpu.VMEM(shape, BF)
    last, side = vb(last_shape(n, rows)), vb(kept_shape(n, rows // 2, True))
    kept = vb(kept_shape(n, rows, False))
    return [vb(half_shape(n, rows)), vb(half_shape(n, rows)), kept, kept, side, side, last, last, last, vb((rows, 128))]


def backward(n_dp, n_bal,
             da_h, gb_h, x1_h, mem_h, cw4_h, cq_h, ck_h, cv_h, cot_h, ce_h, y_h, g_dffn,
             e2_h, e1_h, zb_h, act_h, slope_h, up_h, down_h, ex_h, ew4_h, eqkv_h, eot_h, ee_h,
             a1_h, tx_h, tw4_h, tqkv_h, tot_h, te_h,
             crate, erate, trate, egains, dgains, d_bias_d, d_gains_d, d_shifts_d,
             dx_enc_h, dx_tags_h, dx1_h, decoded, all_cross, all_dffn, all_effn, all_enc0, all_enc1, *rest_refs):
    all_self, v_total = rest_refs[:4], rest_refs[4]
    (ering, q, k, v, ot, kt, dot_, d_o, rowdot, dqt, dk, dv, ds, gb, da, wide0, wide1, x0, x1,
     wa, wb, g0, g1, d_bias, d_gains, d_shifts, vec, vec_lands, vec_slots, next_effn, next_enc1, *rest) = rest_refs[5:]
    room0, room1 = Room(*rest[:10]), Room(*rest[10:20])
    sems, esems, moves, vsems = rest[20:24]
    psems = rest[24:29]
    early, late = [rest[29:34], rest[34:39]], [rest[39:47], rest[47:55]]
    spot = Spot(n_dp, n_bal)
    spot.greet()
    c = Copies(sems)
    n, width = x0.shape
    m = x1.shape[0]
    wide = eot_h.shape[1]
    hidden = up_h.shape[1]
    size = g0.shape[2] // 2
    rows = size // 2
    half = width // 2
    low, high = pl.ds(0, size), pl.ds(size, size)
    least = all_self[0].shape[1]
    dffn = room0.whole(spot, psems[0], g_dffn, all_dffn)
    cross = room1.whole(spot, psems[1], g0, all_cross)
    effn = room0.whole(spot, psems[2], g1, all_effn)
    effn.land_b = next_effn
    enc0 = room1.part(spot, psems[3], g0.at[:, :, low], all_enc0, True, 0, size)
    enc1 = room1.part(spot, psems[4], g0.at[:, :, high], all_enc1, False, size, size)
    enc1.land_b = next_enc1
    pairs = []
    for i, gathered in enumerate(all_self):
        if i < 2:
            where = pl.ds(i * least, least)
            first = g1.at[:, :, where], room0.acc.at[:, :, where], room0.land.at[:, :, where]
            others = early[i]
        else:
            first, others = late[i - 2][:3], late[i - 2][3:]
        pairs.append(PairPiece(spot, others[4], *first, *others[:4], gathered))
    pair0, pair1, pair2, pair3 = pairs
    vector = VectorSum(spot, vec, vec_lands, vec_slots, v_total, vsems)
    zero = jnp.zeros((1, width), F32)
    pair_ds = ds.at[0], ds.at[1]

    load_gb = c.start(gb_h, gb)
    load_ot = c.start(cot_h, ot)
    load_w = c.start(cw4_h, wa)
    loads = [c.start(a, b) for a, b in ((ck_h, k.at[pl.ds(0, m)]), (cv_h, v.at[pl.ds(0, m)]), (cq_h, q))]
    begin, fetch = in_ring(ering, ce_h, esems.at[0], [(m, slice(0, n))])
    begin()
    last = [c.start(a, b) for a, b in ((x1_h, x0), (mem_h, x1), (da_h, da))]
    load_ew = c.start(ew4_h, wb)
    load_e2 = c.start(e2_h, wide0.at[pl.ds(0, m)])
    load_gb.wait()
    load_ot.wait()
    put(g0, 3 * rows, mm(ot[...], gb[...]))
    load_w.wait()
    back_outputs(gb, wa, ot, crate, dot_, d_o, rowdot)
    for load in loads:
        load.wait()
    kt[:, :m] = k[:m].T
    spot.await_all()
    dffn.a_start()
    share = y_h.shape[0] // n_bal

    def moved(step, arriving):
        peer = (spot.b + step) % n_bal
        slot = peer if arriving else spot.b
        return remote(y_h.at[pl.ds(peer * share, share)], decoded.at[pl.ds(slot * share, share)], moves.at[step],
                      moves.at[n_bal + slot], (spot.d, peer))

    own = pl.ds(spot.b * share, share)
    own_copy = pltpu.make_async_copy(y_h.at[own], decoded.at[own], moves.at[0])
    own_copy.start()
    for step in range(1, n_bal):
        moved(step, False).start()

    def cross1():
        dffn.a_wait()
        dffn.b_start()

    keys = pl.ds(0, m)
    back_heads(False, n, q, kt, v.at[keys], dot_, d_o, rowdot, fetch, pair_ds, dqt, dk.at[keys], dv.at[keys],
               {1: cross1})
    for load in last:
        load.wait()
    put(g0, 0, mm(x0[...], dqt[...], TT))
    put(g0, rows, mm(x1[...], dk[:m], TN))
    put(g0, 2 * rows, mm(x1[...], dv[:m], TN))
    cross.a_start()
    dffn.b_wait()
    dffn.bb_start()
    for start, count in cut(m):
        part = slice(start, start + count)
        wide1[part] = mm(dk[part], wa[1], NT) + mm(dv[part], wa[2], NT)
    for start, count in cut(n):
        part = slice(start, start + count)
        d_o[part] = (da[part] + mm(dqt[:, part], wa[0], TT)).astype(BF)
    save_dx1 = c.start(d_o, dx1_h)
    act, slope = ds.at[0, keys, pl.ds(0, hidden)], ds.at[1, keys, pl.ds(0, hidden)]
    up, down, zb = dqt.at[:, pl.ds(0, hidden)], dk.at[pl.ds(0, hidden)], dv.at[keys]
    load_ffn = [c.start(a, b) for a, b in ((down_h, down), (slope_h, slope), (act_h, act), (zb_h, zb), (up_h, up))]
    queries = pl.ds(0, wide)
    eot, eq = ot.at[:, queries], q.at[queries]
    load_ot = c.start(eot_h, eot)
    loads = [c.start(eqkv_h.at[i], item.at[keys]) for i, item in enumerate((q, k, v))]
    load_x = c.start(ex_h, x1)
    load_tw = c.start(tw4_h, wa)
    load_tx = c.start(tx_h, x0)
    begin, fetch = in_ring(ering, ee_h, esems.at[1], [(m, slice(0, wide))])
    begin()
    q[m:wide] = jnp.zeros((wide - m, width), BF)
    load_e2.wait()
    gain, shift = zero, zero
    for start, count in cut(m):
        part = slice(start, start + count)
        unit, pace = normalise(wide0[part])
        grad = wide1[part]
        gain += colsum(grad * unit)
        shift += colsum(grad)
        d2 = norm_back(unit, pace, egains[1:2], grad)
        da[part] = d2
        gb[part] = d2.astype(BF)
    d_gains[1:2] = gain
    d_shifts[1:2] = shift
    load_e1 = c.start(e1_h, wide1)
    load_a1 = c.start(a1_h, wide0)
    cross.a_wait()
    cross.b_start()
    for load in load_ffn:
        load.wait()
    ffn_back(zb, up, down, act, slope, gb.at[keys], slope, g1, d_bias, d_shifts, 2)
    effn.a_start()
    dffn.bb_wait()
    dffn.c_start()
    load_e1.wait()
    gain, shift = zero, zero
    for start, count in cut(m):
        part = slice(start, start + count)
        unit, pace = normalise(wide1[part])
        dz = da[part] + mm(slope[part], up[...], NT)
        gain += colsum(dz * unit)
        shift += colsum(dz)
        d1 = norm_back(unit, pace, egains[0:1], dz)
        da[part] = d1
        gb[part] = d1.astype(BF)
    d_gains[0:1] = gain
    d_shifts[0:1] = shift

    def enc0_():
        effn.a_wait()
        effn.b_start()

    def enc2():
        cross.b_wait()
        cross.bb_start()
        dffn.c_wait()
        dffn.d_start()

    for load in (load_ew, load_ot, *loads, load_x, save_dx1):
        load.wait()
    kt[:, :m] = k[:m].T
    put(g0, 3 * rows, mm(ot[:, :m], gb[:m]))
    edot, edo, edqt = dot_.at[:, queries], d_o.at[queries], dqt.at[:, queries]
    erowdot = rowdot.at[:, :, queries]
    back_outputs(gb.at[keys], wb, eot, erate, edot, edo, erowdot)
    back_heads(False, wide, eq, kt, v.at[keys], edot, edo, erowdot, fetch, pair_ds, edqt, dk.at[keys], dv.at[keys],
               {0: enc0_, 2: enc2})
    load_dx1 = c.start(dx1_h, d_o)
    cross.bb_wait()
    cross.c_start()
    put(g0, 0, mm(x1[...], dqt[:, :m], TT))
    put(g0, rows, mm(x1[...], dk[:m], TN))
    put(g0, 2 * rows, mm(x1[...], dv[:m], TN))
    enc0.a_start()
    enc1.a_start()
    effn.b_wait()
    effn.bb_start()
    for start, count in cut(m):
        part = slice(start, start + count)
        wide1[part] = da[part] + mm(dqt[:, part], wb[0], TT) + mm(dk[part], wb[1], NT) + mm(dv[part], wb[2], NT)
    c.out(wide1, dx_enc_h)

    load_ot = c.start(tot_h, ot)
    loads = [c.start(tqkv_h.at[i], item) for i, item in enumerate((q, k, v))]
    tile = 512
    spans = [(start + tile, slice(start, start + tile)) for start in range(0, n, tile)]
    begin, fetch = in_ring(ering, te_h, esems.at[2], spans)
    begin()
    load_a1.wait()
    load_dx1.wait()
    gain, shift = zero, zero
    for start, count in cut(n):
        part = slice(start, start + count)
        unit, pace = normalise(wide0[part])
        grad = d_o[part].astype(F32)
        gain += colsum(grad * unit)
        shift += colsum(grad)
        d1 = norm_back(unit, pace, dgains[0:1], grad)
        da[part] = d1
        gb[part] = d1.astype(BF)
    part_lanes = width // n_dp
    vec[...] = jnp.zeros_like(vec)
    for i in range(n_dp):
        lanes = slice(i * part_lanes, (i + 1) * part_lanes)
        for j in range(2):
            wide_lanes = slice((2 * i + j) * part_lanes, (2 * i + j + 1) * part_lanes)
            vec[i, j : j + 1, :part_lanes] = d_bias[:, wide_lanes]
            vec[i, 2 + j : 3 + j, :part_lanes] = d_bias_d[:, wide_lanes]
        vec[i, 4:6, :part_lanes] = d_gains[:, lanes]
        vec[i, 6:9, :part_lanes] = d_shifts[:, lanes]
        vec[i, 9:10, :part_lanes] = gain[:, lanes]
        vec[i, 10:12, :part_lanes] = d_gains_d[1:3, lanes]
        vec[i, 12:13, :part_lanes] = shift[:, lanes]
        vec[i, 13:16, :part_lanes] = d_shifts_d[1:4, lanes]
    vector.swap_start(0)
    enc0.a_wait()
    enc0.b_start()
    enc1.a_wait()
    enc1.b_start()

    quarter = half // 2

    def put_pair(p):
        lanes = slice(p * quarter, (p + 1) * quarter)
        sides = jnp.concatenate([dqt[lanes].T, dk[:, lanes], dv[:, lanes]], axis=1)
        put(pairs[p].source, 0, mm(x0[...], sides, TN))
        pairs[p].a_start()

    def tags0():
        vector.swap_wait(0)
        vector.swap_start(1)
        cross.c_wait()
        cross.d_start()
        effn.bb_wait()
        effn.c_start()

    def tags1():
        put_pair(0)

    def tags2():
        pair0.a_wait()
        pair0.q_start()
        vector.swap_wait(1)
        vector.swap_start(2)

    def tags3():
        put_pair(1)
        enc0.b_wait()
        enc1.b_wait()
        enc0.bb_start()
        enc1.bb_start()

    def tags4():
        pair1.a_wait()
        pair1.q_start()
        dffn.d_wait()
        effn.c_wait()
        effn.d_start()
        vector.swap_wait(2)
        vector.c_start()

    def tags5():
        put_pair(2)

    def tags6():
        pair2.a_wait()
        pair2.q_start()
        pair0.q_wait()
        pair0.c_start()
        enc0.bb_wait()
        enc0.c_start()
        enc1.bb_wait()
        enc1.c_start()

    def tags7():
        put_pair(3)

    for load in (load_ot, load_tw, load_tx, *loads):
        load.wait()
    kt[...] = k[...].T
    out = mm(ot[...], gb[...])
    for i, piece in enumerate(pairs):
        put(piece.source, 0, out[:, i * quarter : (i + 1) * quarter], 3 * quarter)
    back_outputs(gb, wa, ot, trate, dot_, d_o, rowdot)
    back_heads(True, tile, q, kt, v, dot_, d_o, rowdot, fetch, pair_ds, dqt, dk, dv,
               dict(enumerate((tags0, tags1, tags2, tags3, tags4, tags5, tags6, tags7))))
    pair3.a_wait()
    pair3.q_start()
    pair1.q_wait()
    pair1.c_start()
    for i, (start, count) in enumerate(cut(n)):
        part = slice(start, start + count)
        wide0[part] = (da[part] + mm(dqt[:, part], wa[0], TT) + mm(dk[part], wa[1], NT) + mm(dv[part], wa[2], NT))
        if i == 0:
            pair2.q_wait()
            pair2.c_start()
            pair0.c_wait()
            pair0.d_start()
            cross.d_wait()
            enc0.c_wait()
            enc0.d_start()
    c.out(wide0, dx_tags_h)
    pair3.q_wait()
    pair3.c_start()
    enc1.c_wait()
    enc1.d_start()
    pair1.c_wait()
    pair1.d_start()
    pair2.c_wait()
    pair2.d_start()
    vector.c_wait()
    effn.d_wait()
    own_copy.wait()
    for step in range(1, n_bal):
        moved(step, False).wait_send()
        moved(step, True).wait_recv()
    c.finish()
    pair3.c_wait()
    pair3.d_start()
    for piece in (enc0, enc1, *pairs):
        piece.d_wait()


def finish(all_cross, all_dffn, all_effn, all_enc0, all_enc1, all_self0, all_self1, all_self2, all_self3, v_total, decoded_h, patches_h, tags_h,
           o_enc, o_eup, o_ebias, o_edown, o_egains, o_eshifts,
           o_self, o_cross, o_dup, o_dbias, o_ddown, o_dgains, o_dshifts, o_decoded, o_patches, o_tags, tags, patches, decoded, sems):
    c = Copies(sems)
    moves = [(c.start(source, here), here, target) for source, here, target in
             ((tags_h, tags, o_tags), (patches_h, patches, o_patches), (decoded_h, decoded, o_decoded))]
    for load, here, target in moves:
        load.wait()
        c.out(here, target)

    def joined(gathered):
        return jnp.concatenate([gathered[b].astype(F32) for b in (0, 2, 1, 3)], axis=1)

    def layer(out, parts):
        rows = out.shape[0]
        for j in range(4):
            out[:, j, :] = parts[j * rows : (j + 1) * rows]

    def branch(up, down, parts):
        rows, width = up.shape[0], parts.shape[1]
        for j in range(up.shape[1] // width):
            up[:, j * width : (j + 1) * width] = parts[j * rows : (j + 1) * rows]
        down[...] = parts[2 * rows :]

    layer(o_enc, jnp.concatenate([joined(all_enc0), joined(all_enc1)], axis=0))
    layer(o_cross, joined(all_cross))
    branch(o_eup, o_edown, joined(all_effn))
    branch(o_dup, o_ddown, joined(all_dffn))
    rows, _, width = o_self.shape
    half = width // 2
    quarter = half // 2
    for i, gathered in enumerate((all_self0, all_self1, all_self2, all_self3)):
        parts = joined(gathered)
        for j in range(4):
            o_self[:, j, i * quarter : (i + 1) * quarter] = parts[:rows, j * quarter : (j + 1) * quarter]
    share = o_egains.shape[1]
    for j in range(2):
        o_ebias[:, j * share : (j + 1) * share] = v_total[j : j + 1, :share]
        o_dbias[:, j * share : (j + 1) * share] = v_total[2 + j : 3 + j, :share]
    o_egains[...] = v_total[4:6, :share]
    o_eshifts[...] = v_total[6:9, :share]
    o_dgains[...] = v_total[9:12, :share]
    o_dshifts[...] = v_total[12:16, :share]
    c.finish()


def call(kernel, ins, outs, out_specs, scratch, name, params=PARAMS):
    specs = [spec for spec, _ in ins]
    return pl.pallas_call(
        kernel,
        out_shape=outs,
        in_specs=specs,
        out_specs=out_specs,
        scratch_shapes=scratch,
        compiler_params=params,
        name=name,
    )(*[value for _, value in ins])


def talking(number):
    return pltpu.CompilerParams(vmem_limit_bytes=60 << 20, collective_id=number, has_side_effects=True)


def run_tags_forward(n_dp, n_bal, x, w, ew, cw, cot, gains, shifts):
    n, width = x.shape
    bf = lambda *s: Shape(s, BF)
    f32 = lambda *s: Shape(s, F32)
    vb = lambda *s: pltpu.VMEM(s, BF)
    vf = lambda *s: pltpu.VMEM(s, F32)
    line, turned, raw, split = vb(n, width), vb(width, n), vb(width, 4, width), vb(4, width, width)
    weights = bf(4, width, width)
    return call(
        functools.partial(tags_forward, n_dp, n_bal),
        [(ANY, x), (ANY, w), (ANY, ew), (ANY, cw), (ANY, cot), (VM, gains), (VM, shifts)],
        [bf(n, width), bf(*cot.shape), f32(HEADS, 1, n), weights, weights, weights, bf(3, n, width), bf(width, n),
         bf(HEADS, n, n), f32(n, width)],
        [VM, VM, VM] + [ANY] * 7,
        [line, raw, split, raw, split, raw, split, line, line, line, turned, turned, turned, vf(n, width), vb(4, n, n),
         pltpu.SemaphoreType.DMA((20,)), pltpu.SemaphoreType.DMA((4, n // 512)), pltpu.SemaphoreType.DMA((2 * n_bal,))],
        "tags_forward",
        talking(2),
    )


def run_forward(n_dp, n_bal, scalars, x, ew4, eup, ebias, edown, egains, eshifts, x1, cw4, up, bias, down, gains, shifts, cot):
    m, width = x.shape
    n = x1.shape[0]
    hidden = up.shape[1]
    wide = (m + 127) // 128 * 128
    piece = (n_dp // 2, 2, 4 * width // n_dp, width)
    bf = lambda *s: Shape(s, BF)
    f32 = lambda *s: Shape(s, F32)
    vb = lambda *s: pltpu.VMEM(s, BF)
    vf = lambda *s: pltpu.VMEM(s, F32)
    split, first, second = vb(4, width, width), vb(width, hidden), vb(hidden, width)
    short, line = vb(m, width), vb(n, width)
    return call(
        functools.partial(forward, cot.shape[0] // n_bal),
        [(SM, v) for v in scalars]
        + [(ANY, x), (ANY, ew4), (ANY, eup), (VM, ebias), (ANY, edown), (VM, egains), (VM, eshifts),
           (ANY, x1), (ANY, cw4), (ANY, up), (VM, bias), (ANY, down), (VM, gains), (VM, shifts), (ANY, cot)],
        [f32(HEADS, 1, wide), f32(HEADS, 1, n), bf(*piece), f32(1, hidden), f32(3, width), f32(4, width), bf(*cot.shape),
         bf(m, width), bf(3, m, width), bf(width, wide), bf(HEADS, m, wide), f32(m, width), f32(m, width), bf(m, width),
         bf(m, hidden), bf(m, hidden),
         f32(n, width), bf(n, width), bf(n, width), bf(m, width), bf(m, width), bf(width, n), bf(HEADS, m, n)],
        [VM] * 7 + [ANY] * 16,
        [short, split, first, second, line, short, short, vb(width, n), vb(width, m), vb(width, n), vb(4, m, n),
         vf(m, width), vf(m, width), short, vb(m, hidden), vb(m, hidden),
         line, short, split, first, second, vf(n, width), vf(n, 1), line, vb(n, hidden), vb(n, hidden), vf(n, width), line,
         pltpu.SemaphoreType.DMA((40,)), pltpu.SemaphoreType.DMA((4, 1))],
        "forward",
    )


def run_backward(n_dp, n_bal, inputs, vectors, shapes):
    n, m, width, hidden, wide, blocks = shapes
    rows = 4 * width // n_dp
    bf = lambda *s: Shape(s, BF)
    f32 = lambda *s: Shape(s, F32)
    vb = lambda *s: pltpu.VMEM(s, BF)
    vf = lambda *s: pltpu.VMEM(s, F32)
    least = max(rows // 4, 16)
    whole, part, small = bf(n_bal, rows, 128), bf(n_bal, rows // 2, 128), bf(n_bal, least, 128)
    line, turned = vb(n, width), vb(width, n)
    piece = vb(n_dp // 2, 2, rows, width)
    return call(
        functools.partial(backward, n_dp, n_bal),
        [(ANY, item) for item in inputs] + [(VM, item) for item in vectors],
        [f32(m, width), f32(n, width), bf(n, width), bf(*blocks), whole, whole, whole, part, part, small, small, small, small, f32(16, 128)],
        [ANY, ANY, ANY] + [VM] * 11,
        [vb(3, n, n), line, line, line, turned, turned, turned, line, vf(HEADS, 1, n), vb(width, max(n, hidden)), vb(max(n, hidden), width), line,
         vb(2, n, max(n, hidden)), line, vf(n, width), vf(n, width), vf(m, width), line, vb(m, width),
         vb(4, width, width), vb(4, width, width), piece, piece,
         vf(1, hidden), vf(2, width), vf(3, width), vf(n_dp, 16, 128), vf(3, n_dp, 16, 128), vf(n_dp // 2, 16, 128),
         vb(*kept_shape(n_dp, rows, False)), vb(*kept_shape(n_dp, rows // 2, False)),
         *room_scratch(n_dp, rows), *room_scratch(n_dp, rows),
         pltpu.SemaphoreType.DMA((40,)), pltpu.SemaphoreType.DMA((3, 4, n // 512)), pltpu.SemaphoreType.DMA((2 * n_bal,)),
         pltpu.SemaphoreType.DMA((6 + n_dp,)), *[piece_sems(n_dp, n_bal)] * 5,
         *pair_scratch(n_dp, n_bal, least, False) * 2, *pair_scratch(n_dp, n_bal, least, True) * 2],
        "backward",
        pltpu.CompilerParams(vmem_limit_bytes=60 << 20, collective_id=1, has_side_effects=True),
    )


def run_finish(n_dp, hidden, width, gathered, moved):
    share = width // n_dp
    f32 = lambda *s: Shape(s, F32)
    side = [f32(share, 4, width)]
    branch = [f32(share, hidden), f32(1, hidden // n_dp), f32(hidden // n_dp, width)]
    outs = side + branch + [f32(2, share), f32(3, share)] + side + side + branch + [f32(3, share), f32(4, share)]
    return call(finish, [(VM, v) for v in gathered] + [(ANY, v) for v in moved],
                outs + [Shape(v.shape, v.dtype) for v in moved], [VM] * len(outs) + [ANY] * 3,
                [pltpu.VMEM(v.shape, v.dtype) for v in moved[::-1]] + [pltpu.SemaphoreType.DMA((6,))], "finish")


def per_device(
    patches, tag_rows, cotangent, tag_length, cell_count, destination, slot_index,
    encoder_attention, encoder_up, encoder_up_bias, encoder_down, encoder_gains, encoder_shifts,
    decoder_self, decoder_cross, decoder_up, decoder_up_bias, decoder_down, decoder_gains, decoder_shifts,
):
    n_bal, n_dp = lax.axis_size("bal"), lax.axis_size("dp")
    length, width = tag_rows.shape[1:]
    hidden = encoder_up.shape[1]
    blocks = destination.shape[1]
    span = length // blocks
    cot = cotangent[0].reshape(blocks, span, width)
    eg, es, dg, ds = encoder_gains.T, encoder_shifts.T, decoder_gains.T, decoder_shifts.T
    eb, db = encoder_up_bias[None], decoder_up_bias[None]
    x1, cot, srate, sw4, ew4, cw4, sqkv, sot, se, a1 = run_tags_forward(
        n_dp, n_bal, tag_rows[0], decoder_self, encoder_attention, decoder_cross, cot, dg, ds)
    (erate, crate, g_dffn, d_db, d_dg, d_ds, y, memory, eqkv, eot, ee, e1, e2, zb, act, slope, da2, gb2, cq, ck, cv, c_ot,
     ce) = run_forward(
        n_dp, n_bal, (tag_length, cell_count, destination, slot_index), patches[0], ew4, encoder_up, eb, encoder_down,
        eg, es, x1, cw4, decoder_up, db, decoder_down, dg, ds, cot)
    d_patches, d_tags, _, decoded, all_cross, all_dffn, *gathered = run_backward(
        n_dp, n_bal,
        (da2, gb2, x1, memory, cw4, cq, ck, cv, c_ot, ce, y, g_dffn,
         e2, e1, zb, act, slope, encoder_up, encoder_down, patches[0], ew4, eqkv, eot, ee,
         a1, tag_rows[0], sw4, sqkv, sot, se),
        (crate, erate, srate, eg, dg, d_db, d_dg, d_ds),
        (length, patches.shape[1], width, hidden, eot.shape[1], y.shape))
    ew, eu, ebg, ed, egg, esg, sw, cw, du, dbg, dd, dgg, dsg, decoded, d_patches, d_tags = run_finish(
        n_dp, hidden, width, (all_cross, all_dffn, *gathered), (decoded, d_patches, d_tags))
    return (
        decoded.reshape(1, length, width), d_patches[None], d_tags[None],
        ew, eu, ebg.reshape(-1), ed, egg.T, esg.T, sw, cw, du, dbg.reshape(-1), dd, dgg.T, dsg.T,
    )


def solution(mesh):
    split = P(("dp", "bal"))
    in_specs = (split,) * 7 + (P(),) * 13
    out_specs = (split,) * 3 + (P("dp"),) * 13
    return jax.shard_map(per_device, mesh=mesh, in_specs=in_specs, out_specs=out_specs, check_vma=False)
```
